32 devices in a mesh: rows: 8 (over y, x, core), mlp: 4 (over z).
Axes of the slice: x: 2, y: 2, z: 4, core: 2. Of those that a mesh axis runs over, the one named last changes fastest.
Arguments:
- patches: bfloat16 [18576, 768], P('rows'), may hold values from -6 to 6
- w_qkv: bfloat16 [768, 2304], P(None, 'mlp'), may hold values from -0.3125 to 0.3125
- qkv_bias: float32 [2, 768], replicated, may hold values from -2 to 2
- w_out: bfloat16 [768, 768], P('mlp'), may hold values from -0.875 to 0.875
- post_bias: float32 [2, 768], replicated, may hold values from -2 to 2
- w_up: bfloat16 [768, 3072], P(None, 'mlp'), may hold values from -0.21875 to 0.21875
- up_bias: float32 [3072], P('mlp'), may hold values from -2 to 2
- w_down: bfloat16 [3072, 768], P('mlp'), may hold values from -0.15625 to 0.15625
- norm_gains: float32 [2, 768], replicated, may hold values from 0.5 to 1.5
- norm_shifts: float32 [2, 768], replicated, may hold values from -2 to 2
- router: float32 [768], replicated, may hold values from -0.21875 to 0.21875
- picked: int32 [11688], P('rows'), may hold values from 0 to 2321, as said below
- live_slots: int32 [11688], P('rows'), may hold values from 0 to 1, as said below
- cotangent: bfloat16 [18576, 768], P('rows', 'mlp'), may hold values from -6 to 6
Outputs:
- block_out: bfloat16 [18576, 768], P('rows', 'mlp')
- input_grad: bfloat16 [18576, 768], P('rows')
- d_qkv: float32 [768, 2304], P(None, 'mlp')
- d_qkv_bias: float32 [2, 768], P(None, 'mlp')
- d_out: float32 [768, 768], P('mlp')
- d_post_bias: float32 [2, 768], replicated
- d_up: float32 [768, 3072], P(None, 'mlp')
- d_up_bias: float32 [3072], P('mlp')
- d_down: float32 [3072, 768], P('mlp')
- d_gains: float32 [2, 768], replicated
- d_shifts: float32 [2, 768], replicated
- d_router: float32 [768], replicated
The draws below stay inside these ranges and needn't reach their ends.
Inputs may be any that keep to these rules, and one draw needn't show every extreme that they name: `picked`: in each group, slot s < 594 belongs to small image s // 99 and a later slot to large image (s - 594) // 289. The live slots of one image name distinct rows in rising order, all within one run of 197 (small) or 577 (large) rows that holds that image and no other; no row is named by two live slots; slots that are not live name the group's last row. `live_slots`: constant over each image's slots. In each group the live images are the first n large ones and the first 6 - n small ones, 0 <= n <= 3; some group has n = 0 and another n = 3.
All inputs are finite; a program needn't handle non-finite values.
Results may differ from the reference program's by a relative error of at most 0.013.
The reference program's roundings to bfloat16 on the way count: a program that leaves them out, or rounds other values in their place, can miss the bound.
Values may be sent and summed in bfloat16 or wider, within the bound.
No kernel may reach another device: no remote copies, remote signals or barrier semaphores. Data moves between devices by JAX's collectives and lax.ppermute only.
A program may use at most 256 MiB of HBM per device.

```python
import jax
import jax.numpy as jnp
from jax import lax

D = 768
HEADS = 12
HD = 64
FF = 3072
PATCH_S = 197
PATCH_L = 577
IMG_DEV = 6
L_MOST = 3
HALF_S = 99
HALF_L = 289
PICK_DEV = 1461
ROWS_DEV = 2322
ROWS = 18576
PICKED = 11688


def choose_half(one_key, total, keep):
    return jnp.sort(jax.random.permutation(one_key, total)[:keep])


def slot_layout(key):
    groups = PICKED // PICK_DEV
    base_key = jax.random.fold_in(key, 4177)
    count_key, first_key, second_key, small_key, large_key = jax.random.split(base_key, 5)
    large_count = jax.random.randint(count_key, (groups,), 0, L_MOST + 1)
    empty_group = jax.random.randint(first_key, (), 0, groups)
    full_group = (empty_group + 1 + jax.random.randint(second_key, (), 0, groups - 1)) % groups
    group_ids = jnp.arange(groups)
    large_count = jnp.where(group_ids == empty_group, 0, large_count)
    large_count = jnp.where(group_ids == full_group, L_MOST, large_count)
    small_keys = jax.random.split(small_key, groups * IMG_DEV)
    small_pick = jax.vmap(lambda one_key: choose_half(one_key, PATCH_S, HALF_S))(small_keys).reshape(groups, IMG_DEV, HALF_S)
    large_keys = jax.random.split(large_key, groups * L_MOST)
    large_pick = jax.vmap(lambda one_key: choose_half(one_key, PATCH_L, HALF_L))(large_keys).reshape(groups, L_MOST, HALF_L)
    small_image = jnp.arange(IMG_DEV)
    large_image = jnp.arange(L_MOST)
    small_base = large_count[:, None] * PATCH_L + small_image[None, :] * PATCH_S
    small_rows = small_base[:, :, None] + small_pick
    large_rows = large_image[None, :, None] * PATCH_L + large_pick
    small_live = jnp.broadcast_to((small_image[None, :] < IMG_DEV - large_count[:, None])[:, :, None], (groups, IMG_DEV, HALF_S))
    large_live = jnp.broadcast_to((large_image[None, :] < large_count[:, None])[:, :, None], (groups, L_MOST, HALF_L))
    slot_rows = jnp.concatenate([small_rows.reshape(groups, IMG_DEV * HALF_S), large_rows.reshape(groups, L_MOST * HALF_L)], axis=1)
    slot_live = jnp.concatenate([small_live.reshape(groups, IMG_DEV * HALF_S), large_live.reshape(groups, L_MOST * HALF_L)], axis=1).astype(jnp.int32)
    slot_rows = jnp.where(slot_live == 1, slot_rows, ROWS_DEV - 1)
    return (slot_rows.reshape(PICKED).astype(jnp.int32), slot_live.reshape(PICKED).astype(jnp.int32))


def draw_picked(key, part):
    return slot_layout(key)[0]


def draw_live_slots(key, part):
    return slot_layout(key)[1]


def levels(key, dims, pieces, smallest, largest):
    loudness = 1.0
    for dim, parts in pieces:
        heights = jax.random.uniform(jax.random.fold_in(jax.random.fold_in(key, 6), dim), (parts,), jnp.float32, smallest / len(pieces), largest / len(pieces))
        loudness = loudness * jnp.repeat(jnp.exp(heights), dims[dim] // parts).reshape((-1,) + (1,) * (len(dims) - 1 - dim))
    return loudness


def gaussian(stream_key, dims, deviation, most, pieces=(), dtype=jnp.bfloat16):
    values = jax.random.normal(stream_key, dims, jnp.float32) * deviation
    if len(pieces) > 0:
        values = levels(stream_key, dims, pieces, -0.22, 0.18) * values
    return jnp.clip(values, min=-most, max=most).astype(dtype)


def setup_inputs(seed: int = 0) -> dict:
    streams_of = jax.random.split(jax.random.key(seed), 15)
    return {
        "patches": gaussian(streams_of[0], (ROWS, D), 1.0, 6.0, ((0, 8),)),
        "w_qkv": gaussian(streams_of[1], (D, 3 * D), (D // 2) ** -0.5, 0.3125, ((1, 4),)),
        "qkv_bias": gaussian(streams_of[2], (2, D), 0.3, 2.0, (), jnp.float32),
        "w_out": gaussian(streams_of[3], (D, D), (D // 16) ** -0.5, 0.875, ((0, 4),)),
        "post_bias": gaussian(streams_of[4], (2, D), 0.3, 2.0, (), jnp.float32),
        "w_up": gaussian(streams_of[5], (D, FF), D ** -0.5, 0.21875, ((1, 4),)),
        "up_bias": gaussian(streams_of[6], (FF,), 0.3, 2.0, ((0, 4),), jnp.float32),
        "w_down": gaussian(streams_of[7], (FF, D), (FF // 2) ** -0.5, 0.15625, ((0, 4),)),
        "norm_gains": jnp.clip(1.0 + 0.1 * jax.random.normal(streams_of[8], (2, D), jnp.float32), 0.5, 1.5),
        "norm_shifts": gaussian(streams_of[9], (2, D), 0.3, 2.0, (), jnp.float32),
        "router": gaussian(streams_of[10], (D,), D ** -0.5, 0.21875, (), jnp.float32),
        "picked": draw_picked(jax.random.fold_in(streams_of[14], 71), 0),
        "live_slots": draw_live_slots(jax.random.fold_in(streams_of[14], 71), 0),
        "cotangent": gaussian(streams_of[13], (ROWS, D), 1.0, 6.0, ((0, 8), (1, 4))),
    }


@jax.custom_vjp
def low(v):
    return lax.optimization_barrier(v.astype(jnp.bfloat16)).astype(jnp.float32)

@jax.custom_vjp
def low_back(v):
    return v

def low_keep(v):
    return (low(v), None)

def low_pass(kept, grad):
    return (grad,)

def back_keep(v):
    return (v, None)

def back_low(kept, grad):
    return (low(grad),)
low.defvjp(low_keep, low_pass)
low_back.defvjp(back_keep, back_low)
HIGH = lax.Precision.HIGHEST
EPSILON = 1e-06

def layer_norm(values, norm_gain, norm_shift):
    average = lax.optimization_barrier(jnp.mean(values, axis=-1, keepdims=True))
    centred = values - average
    variance = lax.optimization_barrier(jnp.mean(centred * centred, axis=-1, keepdims=True))
    return centred * lax.rsqrt(variance + EPSILON) * norm_gain + norm_shift

def attend(projected, images, length):
    shaped = projected.reshape(images, length, HEADS, 3, HD)
    queries = shaped[:, :, :, 0, :]
    keys = shaped[:, :, :, 1, :]
    values = shaped[:, :, :, 2, :]
    scores = low_back(jnp.einsum('blhd,bmhd->bhlm', queries, keys, precision=HIGH) * HD ** (-0.5))
    probs = low(jax.nn.softmax(scores, axis=-1))
    mixed_heads = jnp.einsum('bhlm,bmhd->blhd', probs, values, precision=HIGH)
    return mixed_heads.reshape(images * length, HEADS * HD)

def group_forward(x_rows, pick_rows, live_rows, weight_set):
    w_qkv, qkv_bias, w_out, post_bias, w_up, up_bias, w_down, norm_gains, norm_shifts, router = weight_set
    picked_rows = x_rows[pick_rows]
    gate_value = jax.nn.sigmoid(jnp.dot(picked_rows, router, precision=HIGH))
    normed_one = low(layer_norm(picked_rows, norm_gains[0], norm_shifts[0]))
    bias_rows = jnp.stack([qkv_bias[0], jnp.zeros_like(qkv_bias[0]), qkv_bias[1]])
    bias_cols = bias_rows.reshape(3, HEADS, HD).transpose(1, 0, 2).reshape(3 * HEADS * HD)
    projected = low(low_back(jnp.dot(normed_one, w_qkv, precision=HIGH) + bias_cols))
    small_slots = IMG_DEV * HALF_S
    head_mix = jnp.concatenate([attend(projected[:small_slots], IMG_DEV, HALF_S), attend(projected[small_slots:], L_MOST, HALF_L)], axis=0)
    head_mix = low(low_back(head_mix))
    attn_out = low_back(jnp.dot(head_mix, w_out, precision=HIGH)) + post_bias[0]
    hidden = picked_rows + attn_out
    normed_two = low(layer_norm(hidden, norm_gains[1], norm_shifts[1]))
    pre_act = low_back(jnp.dot(normed_two, w_up, precision=HIGH) + up_bias)
    activation = low(jax.nn.gelu(pre_act, approximate=False))
    mlp_out = low_back(jnp.dot(activation, w_down, precision=HIGH)) + post_bias[1]
    branch = gate_value[:, None] * (attn_out + mlp_out) * live_rows[:, None]
    return x_rows.at[pick_rows].add(branch)

def reference(patches, w_qkv, qkv_bias, w_out, post_bias, w_up, up_bias, w_down, norm_gains, norm_shifts, router, picked, live_slots, cotangent):
    groups = picked.shape[0] // PICK_DEV
    model_width = patches.shape[1]
    x_groups = patches.astype(jnp.float32).reshape(groups, ROWS_DEV, model_width)
    pick_groups = picked.reshape(groups, PICK_DEV)
    live_groups = live_slots.astype(jnp.float32).reshape(groups, PICK_DEV)
    weight_set = tuple((weight_item.astype(jnp.float32) for weight_item in (w_qkv, qkv_bias, w_out, post_bias, w_up, up_bias, w_down, norm_gains, norm_shifts, router)))

    def forward(x_all, weights_now):

        def one_group(inputs):
            return group_forward(inputs[0], inputs[1], inputs[2], weights_now)
        return lax.map(jax.checkpoint(one_group), (x_all, pick_groups, live_groups))
    out_all, pullback = jax.vjp(forward, x_groups, weight_set)
    grad_x, grad_weights = pullback(cotangent.astype(jnp.float32).reshape(groups, ROWS_DEV, model_width))
    block_out = out_all.reshape(groups * ROWS_DEV, model_width).astype(jnp.bfloat16)
    input_grad = grad_x.reshape(groups * ROWS_DEV, model_width).astype(jnp.bfloat16)
    return (block_out, input_grad, grad_weights[0], grad_weights[1], grad_weights[2], grad_weights[3], grad_weights[4], grad_weights[5], grad_weights[6], grad_weights[7], grad_weights[8], grad_weights[9])
```

```python
import functools

import jax
import jax.numpy as jnp
from jax import lax
from jax.experimental import pallas as pl
from jax.experimental.pallas import tpu as pltpu
from jax.sharding import PartitionSpec as P

HD = 64
IMG_DEV = 6
L_MOST = 3
HALF_S = 99
HALF_L = 289

CHUNK = 304
CHUNKS = 1 + L_MOST
PACKED = CHUNK * CHUNKS
SHARE = 8

EPSILON = 1e-06
LOWER = jnp.bfloat16
FLOAT = jnp.float32
MASKED = -1e30
VMEM_LIMIT = 56 * 1024 * 1024


def nn(a, b):
    return lax.dot_general(a, b, (((1,), (0,)), ((), ())), preferred_element_type=FLOAT)


def nt(a, b):
    return lax.dot_general(a, b, (((1,), (1,)), ((), ())), preferred_element_type=FLOAT)


def tn(a, b):
    return lax.dot_general(a, b, (((0,), (0,)), ((), ())), preferred_element_type=FLOAT)


def params(**kwargs):
    return pltpu.CompilerParams(vmem_limit_bytes=VMEM_LIMIT, **kwargs)


def cost(flops, bytes_accessed, transcendentals=0):
    return pl.CostEstimate(
        flops=flops, bytes_accessed=bytes_accessed, transcendentals=transcendentals
    )


def whole(shape, single=True):
    zeros = (0,) * len(shape)
    if single:
        return pl.BlockSpec(shape, lambda *_: zeros, pipeline_mode=pl.Buffered(1))
    return pl.BlockSpec(shape, lambda *_: zeros)


def rows_spec(width, height=CHUNK):
    return pl.BlockSpec((height, width), lambda c: (c, 0))


def norm_stats(values):
    average = jnp.mean(values, axis=-1, keepdims=True)
    centred = values - average
    variance = jnp.mean(centred * centred, axis=-1, keepdims=True)
    inverse = lax.rsqrt(variance + EPSILON)
    return centred * inverse, inverse


def pick_kernel(patches_ref, idx_ref, gains_ref, shifts_ref, router_ref, x_ref, n_ref, gate_ref):
    rows = patches_ref.shape[0]
    places = lax.broadcasted_iota(jnp.int32, (CHUNK, rows), 1)
    onehot = (places == idx_ref[...]).astype(FLOAT).astype(LOWER)
    x = nn(onehot, patches_ref[...])
    x_ref[...] = x.astype(LOWER)
    scaled, _ = norm_stats(x)
    n_ref[...] = (scaled * gains_ref[0:1, :] + shifts_ref[0:1, :]).astype(LOWER)
    logit = jnp.sum(x * router_ref[...], axis=-1, keepdims=True)
    gate_ref[...] = jax.nn.sigmoid(logit)


def pick_rows(patches, idx_col, gains, shifts, router):
    rows, width = patches.shape
    return pl.pallas_call(
        pick_kernel,
        grid=(CHUNKS,),
        in_specs=[
            whole((rows, width)),
            rows_spec(1),
            whole((2, width)),
            whole((2, width)),
            whole((1, width)),
        ],
        out_specs=[rows_spec(width), rows_spec(width), rows_spec(1)],
        out_shape=[
            jax.ShapeDtypeStruct((PACKED, width), LOWER),
            jax.ShapeDtypeStruct((PACKED, width), LOWER),
            jax.ShapeDtypeStruct((PACKED, 1), FLOAT),
        ],
        compiler_params=params(),
        cost_estimate=cost(2 * PACKED * rows * width, 4 * rows * width),
        name="pick_rows",
    )(patches, idx_col, gains, shifts, router)


def pick_cot_kernel(cot_ref, idx_ref, gate_ref, cot_rows_ref, gated_ref):
    rows = cot_ref.shape[1]
    places = lax.broadcasted_iota(jnp.int32, (CHUNK, rows), 1)
    onehot = (places == idx_ref[...]).astype(FLOAT).astype(LOWER)
    cot_rows = nt(onehot, cot_ref[...])
    cot_rows_ref[...] = cot_rows.astype(LOWER)
    gated_ref[...] = (gate_ref[...] * cot_rows).astype(LOWER)


def pick_cot(cot_t, idx_col, gate):
    width, rows = cot_t.shape
    return pl.pallas_call(
        pick_cot_kernel,
        grid=(CHUNKS,),
        in_specs=[whole((width, rows)), rows_spec(1), rows_spec(1)],
        out_specs=[rows_spec(width), rows_spec(width)],
        out_shape=[jax.ShapeDtypeStruct((PACKED, width), LOWER)] * 2,
        compiler_params=params(),
        cost_estimate=cost(2 * PACKED * rows * width, 4 * rows * width),
        name="pick_cot",
    )(cot_t, idx_col, gate)


def load_attention(gathered_ref, weights):
    part = gathered_ref.shape[2]
    per_kind = SHARE // 4
    places = gathered_ref.shape[1]
    for kind in range(4):
        for place in range(places):
            for piece in range(per_kind):
                start = ((kind * places + place) * per_kind + piece) * part
                weights[start : start + part, :] = gathered_ref[kind * per_kind + piece, place]


def pair_mask(head):
    lanes = lax.broadcasted_iota(jnp.int32, (1, 2 * HD), 1)
    return (lanes < HD) if head % 2 == 0 else (lanes >= HD)


def keep_head(values, head):
    return jnp.where(pair_mask(head), values, jnp.zeros_like(values))


def forward_kernel(
    n_ref,
    x_ref,
    gathered_ref,
    bias_ref,
    seg_col_ref,
    seg_row_ref,
    post_ref,
    gains_ref,
    shifts_ref,
    proj_ref,
    mix_ref,
    lse_ref,
    hidden_ref,
    normed_ref,
    weights,
):
    width = n_ref.shape[1]

    @pl.when(pl.program_id(0) == 0)
    def _():
        load_attention(gathered_ref, weights)

    normed = n_ref[...]
    for kind in range(3):
        cols = slice(kind * width, (kind + 1) * width)
        proj_ref[:, cols] = (nt(normed, weights[cols, :]) + bias_ref[:, cols]).astype(LOWER)
    outside = jnp.where(seg_col_ref[...] == seg_row_ref[0], 0.0, MASKED)
    lse_all = jnp.zeros((CHUNK, 128), FLOAT)
    lanes = lax.broadcasted_iota(jnp.int32, (1, 128), 1)
    for pair in range(width // (2 * HD)):
        cols = slice(pair * 2 * HD, (pair + 1) * 2 * HD)
        q = proj_ref[:, cols] * LOWER(HD**-0.5)
        k = proj_ref[:, width + pair * 2 * HD : width + (pair + 1) * 2 * HD]
        v = proj_ref[:, 2 * width + pair * 2 * HD : 2 * width + (pair + 1) * 2 * HD]
        mixed = None
        for head in (2 * pair, 2 * pair + 1):
            scores = nt(q, keep_head(k, head)) + outside
            largest = jnp.max(scores, axis=-1, keepdims=True)
            powered = jnp.exp(scores - largest)
            total = jnp.sum(powered, axis=-1, keepdims=True)
            probs = (powered * (1.0 / total)).astype(LOWER)
            part = nn(probs, keep_head(v, head))
            mixed = part if mixed is None else mixed + part
            lse_all = jnp.where(lanes == head, largest + jnp.log(total), lse_all)
        mix_ref[:, cols] = mixed.astype(LOWER)
    lse_ref[0] = jnp.transpose(lse_all)[0:16, :]
    attn = nn(mix_ref[...], weights[3 * width :, :]) + post_ref[0:1, :]
    hidden = x_ref[...].astype(FLOAT) + attn
    hidden_ref[...] = hidden
    scaled, _ = norm_stats(hidden)
    normed_ref[...] = (scaled * gains_ref[1:2, :] + shifts_ref[1:2, :]).astype(LOWER)


def forward_attention(normed, x, gathered, bias, seg_col, seg_row, post, gains, shifts):
    width = x.shape[1]
    return pl.pallas_call(
        forward_kernel,
        grid=(CHUNKS,),
        in_specs=[
            rows_spec(width),
            rows_spec(width),
            whole(gathered.shape),
            whole((1, 3 * width)),
            rows_spec(1),
            pl.BlockSpec((1, 1, CHUNK), lambda c: (c, 0, 0)),
            whole((2, width)),
            whole((2, width)),
            whole((2, width)),
        ],
        out_specs=[
            rows_spec(3 * width),
            rows_spec(width),
            pl.BlockSpec((1, 16, CHUNK), lambda c: (c, 0, 0)),
            rows_spec(width),
            rows_spec(width),
        ],
        out_shape=[
            jax.ShapeDtypeStruct((PACKED, 3 * width), LOWER),
            jax.ShapeDtypeStruct((PACKED, width), LOWER),
            jax.ShapeDtypeStruct((CHUNKS, 16, CHUNK), FLOAT),
            jax.ShapeDtypeStruct((PACKED, width), FLOAT),
            jax.ShapeDtypeStruct((PACKED, width), LOWER),
        ],
        scratch_shapes=[pltpu.VMEM((4 * width, width), LOWER)],
        compiler_params=params(),
        cost_estimate=cost(2 * PACKED * width * 8 * width, 20 * PACKED * width),
        name="forward_attention",
    )(normed, x, gathered, bias, seg_col, seg_row, post, gains, shifts)


def gelu_pair(u):
    cdf = 0.5 * (1.0 + lax.erf(u * (0.5**0.5)))
    density = jnp.exp(-0.5 * u * u) * 0.3989422804014327
    return u * cdf, cdf + u * density


def mlp_kernel(
    n_ref,
    gated_ref,
    weights_ref,
    own_down_ref,
    bias_ref,
    act_ref,
    pre_ref,
    grad_ref,
    gate_ref,
    out_ref,
):
    place, chunk = pl.program_id(0), pl.program_id(1)
    width = n_ref.shape[1]
    hidden = bias_ref.shape[2]
    rows = pl.ds(pl.multiple_of(chunk * CHUNK, 16), CHUNK)
    up = weights_ref[:, 0, 0].reshape(width, hidden)
    down = weights_ref[:, 0, 1].reshape(hidden, width)
    normed = n_ref[rows, :]
    gated = gated_ref[rows, :]
    pre_act = nn(normed, up) + bias_ref[0]
    activation, slope = gelu_pair(pre_act)
    activation = activation.astype(LOWER)
    grad_act = nt(gated, down)
    grad_pre = (grad_act * slope).astype(LOWER)
    act_ref[...] = activation
    pre_ref[...] = grad_pre
    grad_part = nt(grad_pre, up)
    gate_part = jnp.sum(activation.astype(FLOAT) * grad_act, axis=-1, keepdims=True)
    out_part = nn(activation, own_down_ref[0])

    @pl.when(place == 0)
    def _():
        grad_ref[rows, :] = grad_part
        gate_ref[rows, :] = gate_part
        out_ref[rows, :] = out_part

    @pl.when(place > 0)
    def _():
        grad_ref[rows, :] += grad_part
        gate_ref[rows, :] += gate_part
        out_ref[rows, :] += out_part


def mlp_both(normed, gated, weights, own_down, bias):
    width = normed.shape[1]
    places, hidden = bias.shape[0], bias.shape[2]
    own = own_down.shape[2]
    share, part = weights.shape[0], weights.shape[3]
    first = lambda j, c: (jnp.where(j == 0, c, CHUNKS), 0)
    return pl.pallas_call(
        mlp_kernel,
        grid=(places, CHUNKS),
        in_specs=[
            whole((PACKED, width)),
            whole((PACKED, width)),
            pl.BlockSpec((share, 1, 2, part, width), lambda j, c: (0, j, 0, 0, 0)),
            pl.BlockSpec((1, hidden, own), lambda j, c: (j, 0, 0)),
            pl.BlockSpec((1, 1, hidden), lambda j, c: (j, 0, 0)),
        ],
        out_specs=[
            pl.BlockSpec((CHUNK, hidden), first),
            pl.BlockSpec((CHUNK, hidden), first),
            whole((PACKED, width), False),
            whole((PACKED, 1), False),
            whole((PACKED, own), False),
        ],
        out_shape=[
            jax.ShapeDtypeStruct((PACKED + CHUNK, hidden), LOWER),
            jax.ShapeDtypeStruct((PACKED + CHUNK, hidden), LOWER),
            jax.ShapeDtypeStruct((PACKED, width), FLOAT),
            jax.ShapeDtypeStruct((PACKED, 1), FLOAT),
            jax.ShapeDtypeStruct((PACKED, own), FLOAT),
        ],
        compiler_params=params(),
        cost_estimate=cost(
            2 * PACKED * places * hidden * (3 * width + own), 4 * places * hidden * width
        ),
        name="mlp_both",
    )(normed, gated, weights, own_down, bias)


def backward_kernel(
    grad_ref,
    gate_part_ref,
    hidden_ref,
    x_ref,
    cot_ref,
    gate_ref,
    proj_ref,
    lse_ref,
    gathered_ref,
    seg_col_ref,
    seg_row_ref,
    post_ref,
    gains_ref,
    gproj_ref,
    ghid_ref,
    glow_ref,
    logit_ref,
    sums_ref,
    weights,
    gmix,
):
    width = x_ref.shape[1]
    chunk = pl.program_id(0)

    @pl.when(chunk == 0)
    def _():
        part = gathered_ref.shape[2]
        per_kind, places = SHARE // 4, gathered_ref.shape[1]
        for place in range(places):
            for piece in range(per_kind):
                start = (place * per_kind + piece) * part
                weights[start : start + part, :] = gathered_ref[3 * per_kind + piece, place]
        sums_ref[...] = jnp.zeros_like(sums_ref)

    hidden = hidden_ref[...]
    scaled, inverse = norm_stats(hidden)
    grad_out = grad_ref[...]
    weighted = grad_out * gains_ref[1:2, :]
    centre_term = jnp.mean(weighted, axis=-1, keepdims=True)
    scale_term = jnp.mean(weighted * scaled, axis=-1, keepdims=True)
    grad_hidden = inverse * (weighted - centre_term - scaled * scale_term)
    gate = gate_ref[...]
    gated = gate * cot_ref[...].astype(FLOAT)
    grad_attn = grad_hidden + gated
    ghid_ref[...] = grad_hidden
    low = grad_attn.astype(LOWER)
    glow_ref[...] = low
    attn = hidden - x_ref[...].astype(FLOAT)
    dotted = jnp.sum(gated * (attn + post_ref[1:2, :]), axis=-1, keepdims=True)
    logit_ref[...] = (1.0 - gate) * (dotted + gate_part_ref[...])
    sums_ref[0:1, :] += jnp.sum(grad_out * scaled, axis=0, keepdims=True)
    sums_ref[1:2, :] += jnp.sum(grad_out, axis=0, keepdims=True)
    sums_ref[2:3, :] += jnp.sum(grad_attn, axis=0, keepdims=True)
    sums_ref[3:4, :] += jnp.sum(gated, axis=0, keepdims=True)
    gmix[...] = nt(low, weights[...]).astype(LOWER)
    outside = jnp.where(seg_col_ref[...] == seg_row_ref[0], 0.0, MASKED)
    for pair in range(width // (2 * HD)):
        cols = slice(pair * 2 * HD, (pair + 1) * 2 * HD)
        k_cols = slice(width + pair * 2 * HD, width + (pair + 1) * 2 * HD)
        v_cols = slice(2 * width + pair * 2 * HD, 2 * width + (pair + 1) * 2 * HD)
        q = proj_ref[:, cols] * LOWER(HD**-0.5)
        k = proj_ref[:, k_cols]
        v = proj_ref[:, v_cols]
        g = gmix[:, cols]
        grad_q, grad_k, grad_v = None, None, None
        for head in (2 * pair, 2 * pair + 1):
            own_k = keep_head(k, head)
            scores = nt(own_k, q) + outside
            probs = jnp.exp(scores - lse_ref[0, head : head + 1, :])
            grad_probs = nt(keep_head(v, head), g)
            inner = jnp.sum(probs * grad_probs, axis=0, keepdims=True)
            grad_scores = (probs * (grad_probs - inner)).astype(LOWER)
            one_v = nn(probs.astype(LOWER), g)
            one_k = nn(grad_scores, q)
            one_q = tn(grad_scores, own_k)
            if head % 2 == 0:
                grad_q, grad_k, grad_v = one_q, one_k, one_v
            else:
                first = pair_mask(0)
                grad_q = grad_q + one_q
                grad_k = jnp.where(first, grad_k, one_k)
                grad_v = jnp.where(first, grad_v, one_v)
        gproj_ref[:, cols] = (grad_q * HD**-0.5).astype(LOWER)
        gproj_ref[:, k_cols] = grad_k.astype(LOWER)
        gproj_ref[:, v_cols] = grad_v.astype(LOWER)


def backward_attention(
    grad, gate_part, hidden, x, cot_rows, gate, proj, lse, gathered, seg_col, seg_row, post, gains
):
    width = x.shape[1]
    return pl.pallas_call(
        backward_kernel,
        grid=(CHUNKS,),
        in_specs=[
            rows_spec(width),
            rows_spec(1),
            rows_spec(width),
            rows_spec(width),
            rows_spec(width),
            rows_spec(1),
            rows_spec(3 * width),
            pl.BlockSpec((1, 16, CHUNK), lambda c: (c, 0, 0)),
            whole(gathered.shape),
            rows_spec(1),
            pl.BlockSpec((1, 1, CHUNK), lambda c: (c, 0, 0)),
            whole((2, width)),
            whole((2, width)),
        ],
        out_specs=[
            rows_spec(3 * width),
            rows_spec(width),
            rows_spec(width),
            rows_spec(1),
            whole((8, width), False),
        ],
        out_shape=[
            jax.ShapeDtypeStruct((PACKED, 3 * width), LOWER),
            jax.ShapeDtypeStruct((PACKED, width), FLOAT),
            jax.ShapeDtypeStruct((PACKED, width), LOWER),
            jax.ShapeDtypeStruct((PACKED, 1), FLOAT),
            jax.ShapeDtypeStruct((8, width), FLOAT),
        ],
        scratch_shapes=[pltpu.VMEM((width, width), LOWER), pltpu.VMEM((CHUNK, width), LOWER)],
        compiler_params=params(),
        cost_estimate=cost(2 * PACKED * width * 14 * width, 20 * PACKED * width),
        name="backward_attention",
    )(grad, gate_part, hidden, x, cot_rows, gate, proj, lse, gathered, seg_col, seg_row, post, gains)


def first_norm_kernel(
    gproj_ref,
    gathered_ref,
    x_ref,
    ghid_ref,
    logit_ref,
    gains_ref,
    router_ref,
    rows_ref,
    sums_ref,
    weights,
):
    width = x_ref.shape[1]

    @pl.when(pl.program_id(0) == 0)
    def _():
        part = gathered_ref.shape[2]
        per_kind, places = SHARE // 4, gathered_ref.shape[1]
        for kind in range(3):
            for place in range(places):
                for piece in range(per_kind):
                    start = ((kind * places + place) * per_kind + piece) * part
                    weights[start : start + part, :] = gathered_ref[kind * per_kind + piece, place]
        sums_ref[...] = jnp.zeros_like(sums_ref)

    grad_out = nn(gproj_ref[...], weights[...])
    x = x_ref[...].astype(FLOAT)
    scaled, inverse = norm_stats(x)
    weighted = grad_out * gains_ref[0:1, :]
    centre_term = jnp.mean(weighted, axis=-1, keepdims=True)
    scale_term = jnp.mean(weighted * scaled, axis=-1, keepdims=True)
    grad_norm = inverse * (weighted - centre_term - scaled * scale_term)
    logit = logit_ref[...]
    rows_ref[...] = (ghid_ref[...] + grad_norm + logit * router_ref[...]).astype(LOWER)
    sums_ref[0:1, :] += jnp.sum(grad_out * scaled, axis=0, keepdims=True)
    sums_ref[1:2, :] += jnp.sum(grad_out, axis=0, keepdims=True)
    sums_ref[2:3, :] += jnp.sum(logit * x, axis=0, keepdims=True)


def first_norm(gproj, gathered, x, ghid, logit, gains, router):
    width = x.shape[1]
    return pl.pallas_call(
        first_norm_kernel,
        grid=(CHUNKS,),
        in_specs=[
            rows_spec(3 * width),
            whole(gathered.shape),
            rows_spec(width),
            rows_spec(width),
            rows_spec(1),
            whole((2, width)),
            whole((1, width)),
        ],
        out_specs=[rows_spec(width), whole((8, width), False)],
        out_shape=[
            jax.ShapeDtypeStruct((PACKED, width), LOWER),
            jax.ShapeDtypeStruct((8, width), FLOAT),
        ],
        scratch_shapes=[pltpu.VMEM((3 * width, width), LOWER)],
        compiler_params=params(),
        cost_estimate=cost(2 * PACKED * width * 3 * width, 16 * PACKED * width),
        name="first_norm",
    )(gproj, gathered, x, ghid, logit, gains, router)


def scatter_kernel(cot_ref, idx_ref, rows_ref, out_ref):
    block = out_ref.shape[0]
    places = lax.broadcasted_iota(jnp.int32, (block, PACKED), 0) + pl.program_id(0) * block
    onehot = (places == idx_ref[...]).astype(FLOAT).astype(LOWER)
    out_ref[...] = (cot_ref[...].astype(FLOAT) + nn(onehot, rows_ref[...])).astype(LOWER)


def scatter_rows(cot, idx_row, rows):
    total, width = cot.shape
    block = 400
    return pl.pallas_call(
        scatter_kernel,
        grid=(pl.cdiv(total, block),),
        in_specs=[
            rows_spec(width, block),
            whole((1, PACKED)),
            whole((PACKED, width)),
        ],
        out_specs=rows_spec(width, block),
        out_shape=jax.ShapeDtypeStruct((total, width), LOWER),
        compiler_params=params(),
        cost_estimate=cost(2 * PACKED * total * width, 4 * total * width),
        name="scatter_rows",
    )(cot, idx_row, rows)


def block_out_kernel(patch_ref, idx_ref, branch_ref, out_ref):
    total = out_ref.shape[1]
    places = lax.broadcasted_iota(jnp.int32, (PACKED, total), 1)
    onehot = (places == idx_ref[...]).astype(FLOAT).astype(LOWER)
    added = nn(branch_ref[...], onehot)
    out_ref[...] = (patch_ref[...].astype(FLOAT) + added).astype(LOWER)


def block_out_rows(patch_t, idx_col, branch_t):
    own, total = patch_t.shape
    return pl.pallas_call(
        block_out_kernel,
        out_shape=jax.ShapeDtypeStruct((own, total), LOWER),
        compiler_params=params(),
        cost_estimate=cost(2 * PACKED * total * own, 4 * total * own),
        name="block_out_rows",
    )(patch_t, idx_col, branch_t)


def share_groups(rows):
    return [list(range(first, first + SHARE)) for first in range(0, rows, SHARE)]


def ring(value, axis, size):
    got = [value]
    step = [(i, (i + 1) % size) for i in range(size)]
    for _ in range(size - 1):
        got.append(lax.ppermute(got[-1], axis, step))
    return got


def turned(values, place):
    size = values.shape[0]
    back = jnp.concatenate([values[:1], values[:0:-1]], axis=0)
    twice = jnp.concatenate([back, back], axis=0)
    return lax.dynamic_slice_in_dim(twice, (size - place) % size, size, 0)


def pack_slots(picked, live_slots):
    small = IMG_DEV * HALF_S
    named = jnp.where(live_slots == 1, picked, -1)

    def padded(parts, fill):
        have = sum(p.shape[0] for p in parts)
        return jnp.concatenate([*parts, jnp.full((CHUNK - have,), fill, jnp.int32)])

    always = IMG_DEV - L_MOST
    idx = [padded([named[: always * HALF_S]], -1)]
    seg = [padded([jnp.repeat(jnp.arange(always, dtype=jnp.int32), HALF_S)], always)]
    for j in range(L_MOST):
        first = small + j * HALF_L
        alive = live_slots[first] == 1
        other = IMG_DEV - 1 - j
        large_idx = padded([named[first : first + HALF_L]], -1)
        small_idx = padded([named[other * HALF_S : (other + 1) * HALF_S]], -1)
        idx.append(jnp.where(alive, large_idx, small_idx))
        length = jnp.where(alive, HALF_L, HALF_S)
        seg.append((jnp.arange(CHUNK, dtype=jnp.int32) >= length).astype(jnp.int32))
    return jnp.concatenate(idx), jnp.concatenate(seg)


def local(
    rows_size,
    mlp_size,
    patches,
    w_qkv,
    qkv_bias,
    w_out,
    post_bias,
    w_up,
    up_bias,
    w_down,
    norm_gains,
    norm_shifts,
    router,
    picked,
    live_slots,
    cotangent,
):
    width = patches.shape[1]
    mlp_index = lax.axis_index("mlp")
    share_index = lax.axis_index("rows") % SHARE
    groups = share_groups(rows_size)
    own = w_out.shape[0]
    heads_here = own // HD
    router_row = router.reshape(1, width)

    attn_shard = jnp.concatenate(
        [
            w_qkv.T.reshape(heads_here, 3, HD, width).transpose(1, 0, 2, 3).reshape(3 * own, width),
            w_out,
        ],
        axis=0,
    )
    part = attn_shard.shape[0] // SHARE
    attn_piece = lax.dynamic_slice_in_dim(attn_shard, share_index * part, part, 0)
    attn_parts = jnp.stack(ring(attn_piece, "mlp", mlp_size), axis=0)
    attn_all = lax.all_gather(attn_parts, "rows", axis_index_groups=groups, axis=0)
    mlp_part = w_up.shape[0] // SHARE
    mlp_piece = jnp.stack(
        [
            lax.dynamic_slice_in_dim(w_up, share_index * mlp_part, mlp_part, 0),
            lax.dynamic_slice_in_dim(w_down, share_index * mlp_part, mlp_part, 0),
        ],
        axis=0,
    )
    mlp_parts = jnp.stack(ring(mlp_piece, "mlp", mlp_size), axis=0)
    mlp_all = lax.all_gather(mlp_parts, "rows", axis_index_groups=groups, axis=0)
    cot_t = lax.all_gather(cotangent.T, "mlp", axis=0, tiled=True)
    up_bias_all = turned(lax.all_gather(up_bias, "mlp", axis=0), mlp_index)[:, None, :]
    kinds = jnp.stack([qkv_bias[0], jnp.zeros_like(qkv_bias[0]), qkv_bias[1]])
    bias = turned(kinds.reshape(3, mlp_size, own).transpose(1, 0, 2), mlp_index)
    bias = bias.transpose(1, 0, 2).reshape(1, 3 * width)

    idx, seg = pack_slots(picked, live_slots)
    idx_col, idx_row = idx.reshape(PACKED, 1), idx.reshape(1, PACKED)
    seg_col, seg_row = seg.reshape(PACKED, 1), seg.reshape(CHUNKS, 1, CHUNK)

    x, normed_one, gate = pick_rows(patches, idx_col, norm_gains, norm_shifts, router_row)
    proj, mix, lse, hidden, normed_two = forward_attention(
        normed_one, x, attn_all, bias, seg_col, seg_row, post_bias, norm_gains, norm_shifts
    )
    cot_rows, gated = pick_cot(cot_t, idx_col, gate)

    feature_start = mlp_index * own
    down_all = mlp_all[:, :, 1].transpose(1, 0, 2, 3).reshape(mlp_size, w_down.shape[0], width)
    own_down = lax.dynamic_slice_in_dim(down_all, feature_start, own, 2)
    act, grad_pre, grad_two, gate_part, mlp_own = mlp_both(
        normed_two, gated, mlp_all, own_down, up_bias_all
    )
    act, grad_pre = act[:PACKED], grad_pre[:PACKED]
    d_down = tn(act, gated).astype(LOWER)
    d_up = tn(normed_two, grad_pre).astype(LOWER)
    d_up_bias = jnp.sum(grad_pre.astype(FLOAT), axis=0)

    attn_own = lax.dynamic_slice_in_dim(hidden - x.astype(FLOAT), feature_start, own, 1)
    bias_own = lax.dynamic_slice_in_dim(post_bias[1], feature_start, own, 0)
    branch = gate * (attn_own + mlp_own + bias_own)
    patch_t = lax.dynamic_slice_in_dim(patches, feature_start, own, 1).T
    block_out = block_out_rows(patch_t, idx_col, branch.astype(LOWER).T).T

    grad_proj, grad_hidden, grad_low, logit, sums_two = backward_attention(
        grad_two,
        gate_part,
        hidden,
        x,
        cot_rows,
        gate,
        proj,
        lse,
        attn_all,
        seg_col,
        seg_row,
        post_bias,
        norm_gains,
    )
    d_out = tn(mix[:, :own], grad_low).astype(LOWER)
    own_proj = jnp.concatenate(
        [grad_proj[:, kind * width : kind * width + own] for kind in range(3)], axis=1
    )
    d_qkv_t = tn(own_proj, normed_one).astype(LOWER)
    bias_grad = jnp.sum(own_proj.astype(FLOAT), axis=0)
    rows_grad, sums_one = first_norm(
        grad_proj, attn_all, x, grad_hidden, logit, norm_gains, router_row
    )
    input_grad = scatter_rows(cot_t.T, idx_row, rows_grad)

    d_down, d_up, d_out, d_qkv_t = lax.psum((d_down, d_up, d_out, d_qkv_t), "rows")
    small = jnp.concatenate(
        [
            sums_two[:4],
            sums_one[:3],
            d_up_bias.reshape(1, width),
            jnp.pad(bias_grad, (0, width - 3 * own)).reshape(1, width),
        ],
        axis=0,
    )
    small = lax.psum(small, "rows")
    d_qkv = (
        d_qkv_t.astype(FLOAT)
        .reshape(3, heads_here, HD, width)
        .transpose(1, 0, 2, 3)
        .reshape(3 * own, width)
        .T
    )
    d_qkv_bias = jnp.stack([small[8, :own], small[8, 2 * own : 3 * own]])
    return (
        block_out,
        input_grad,
        d_qkv,
        d_qkv_bias,
        d_out.astype(FLOAT),
        small[2:4],
        d_up.astype(FLOAT),
        small[7],
        d_down.astype(FLOAT),
        jnp.stack([small[4], small[0]]),
        jnp.stack([small[5], small[1]]),
        small[6],
    )


def solution(mesh):
    in_specs = (
        P("rows", None),
        P(None, "mlp"),
        P(),
        P("mlp", None),
        P(),
        P(None, "mlp"),
        P("mlp"),
        P("mlp", None),
        P(),
        P(),
        P(),
        P("rows"),
        P("rows"),
        P("rows", "mlp"),
    )
    out_specs = (
        P("rows", "mlp"),
        P("rows", None),
        P(None, "mlp"),
        P(None, "mlp"),
        P("mlp", None),
        P(),
        P(None, "mlp"),
        P("mlp"),
        P("mlp", None),
        P(),
        P(),
        P(),
    )
    body = functools.partial(local, mesh.shape["rows"], mesh.shape["mlp"])
    return jax.shard_map(body, mesh=mesh, in_specs=in_specs, out_specs=out_specs, check_vma=False)
```

```python
import functools

import jax
import jax.numpy as jnp
from jax import lax
from jax.experimental import pallas as pl
from jax.experimental.pallas import tpu as pltpu
from jax.sharding import PartitionSpec as P

HD = 64
IMG_DEV = 6
L_MOST = 3
HALF_S = 99
HALF_L = 289

CHUNK = 304
CHUNKS = 1 + L_MOST
PACKED = CHUNK * CHUNKS
SHARE = 8

EPSILON = 1e-06
LOWER = jnp.bfloat16
FLOAT = jnp.float32
MASKED = -1e30


def nn(a, b):
    return lax.dot_general(a, b, (((1,), (0,)), ((), ())), preferred_element_type=FLOAT)


def nt(a, b):
    return lax.dot_general(a, b, (((1,), (1,)), ((), ())), preferred_element_type=FLOAT)


def tn(a, b):
    return lax.dot_general(a, b, (((0,), (0,)), ((), ())), preferred_element_type=FLOAT)


def params(mib):
    return pltpu.CompilerParams(vmem_limit_bytes=mib * 1024 * 1024)


def cost(flops, bytes_accessed, transcendentals=0):
    return pl.CostEstimate(
        flops=flops, bytes_accessed=bytes_accessed, transcendentals=transcendentals
    )


def whole(shape, single=True):
    zeros = (0,) * len(shape)
    if single:
        return pl.BlockSpec(shape, lambda *_: zeros, pipeline_mode=pl.Buffered(1))
    return pl.BlockSpec(shape, lambda *_: zeros)


def rows_spec(width, height=CHUNK):
    return pl.BlockSpec((height, width), lambda c, *_: (c, 0))


def chunk_spec(height, width=CHUNK):
    return pl.BlockSpec((1, height, width), lambda c, *_: (c, 0, 0))


def call(kernel, name, mib, operands, in_specs, outs, scratch=(), flops=0, place=None, grid=None, aliases=None):
    specs = [o[2] for o in outs]
    shapes = [jax.ShapeDtypeStruct(o[0], o[1]) for o in outs]
    moved = sum(x.size * x.dtype.itemsize for x in [*operands, *shapes])
    scalars = () if place is None else (place,)
    made = pl.pallas_call(
        kernel,
        grid_spec=pltpu.PrefetchScalarGridSpec(
            num_scalar_prefetch=len(scalars),
            grid=grid or (CHUNKS,),
            in_specs=in_specs,
            out_specs=specs,
            scratch_shapes=scratch,
        ),
        out_shape=shapes,
        input_output_aliases=aliases or {},
        compiler_params=params(mib),
        cost_estimate=cost(flops, moved),
        name=name,
    )(*scalars, *operands)
    return list(made)


def slot_onehot(slots_ref, rows):
    named = jnp.transpose(slots_ref[0])[:, 0:1].astype(jnp.int32)
    places = lax.broadcasted_iota(jnp.int32, (CHUNK, rows), 1)
    return (places == named).astype(FLOAT).astype(LOWER)


def outside_image(slots_ref):
    image = jnp.transpose(slots_ref[0])[:, 1:2]
    return jnp.where(image == slots_ref[0, 1:2, :], 0.0, MASKED)


def choose_own(place, values, own):
    width = values.shape[1]
    source = lax.broadcasted_iota(jnp.int32, (width, own), 0)
    target = lax.broadcasted_iota(jnp.int32, (width, own), 1)
    onehot = (source == target + place * own).astype(FLOAT).astype(LOWER)
    return nn(values, onehot).astype(LOWER)


def norm_stats(values):
    average = jnp.mean(values, axis=-1, keepdims=True)
    centred = values - average
    variance = jnp.mean(centred * centred, axis=-1, keepdims=True)
    inverse = lax.rsqrt(variance + EPSILON)
    return centred * inverse, inverse


def pick_kernel(
    place_ref,
    patches_ref,
    cot_ref,
    slots_ref,
    gains_ref,
    shifts_ref,
    router_ref,
    x_ref,
    n_ref,
    gate_ref,
    part_ref,
    patch_ref,
):
    onehot = slot_onehot(slots_ref, patches_ref.shape[0])
    part_ref[0] = nt(cot_ref[...], onehot).astype(LOWER)
    x = nn(onehot, patches_ref[...])
    x_ref[...] = x.astype(LOWER)
    scaled, _ = norm_stats(x)
    n_ref[...] = (scaled * gains_ref[0:1, :] + shifts_ref[0:1, :]).astype(LOWER)
    logit = jnp.sum(x * router_ref[...], axis=-1, keepdims=True)
    gate_ref[...] = jnp.broadcast_to(jax.nn.sigmoid(logit), gate_ref.shape)

    @pl.when(pl.program_id(0) == 0)
    def _():
        own, width = patch_ref.shape[0], patches_ref.shape[1]
        source = lax.broadcasted_iota(jnp.int32, (own, width), 1)
        target = lax.broadcasted_iota(jnp.int32, (own, width), 0)
        chosen = (source == target + place_ref[0] * own).astype(FLOAT).astype(LOWER)
        patch_ref[...] = nt(chosen, patches_ref[...]).astype(LOWER)


def pick_rows(place, patches, cot_own, slots, gains, shifts, router):
    rows, width = patches.shape
    own = cot_own.shape[0]
    return call(
        pick_kernel,
        "pick_rows",
        22,
        (patches, cot_own, slots, gains, shifts, router),
        [
            whole((rows, width)),
            whole((own, rows)),
            chunk_spec(8),
            whole((2, width)),
            whole((2, width)),
            whole((1, width)),
        ],
        [
            ((PACKED, width), LOWER, rows_spec(width)),
            ((PACKED, width), LOWER, rows_spec(width)),
            ((PACKED, 128), FLOAT, rows_spec(128)),
            ((CHUNKS, own, CHUNK), LOWER, chunk_spec(own)),
            ((own, rows), LOWER, whole((own, rows))),
        ],
        flops=2 * PACKED * rows * (width + own),
        place=place,
    )


def head_slabs(own):
    slabs = []
    for start in range(0, own, 2 * HD):
        stop = min(start + 2 * HD, own)
        lanes = lax.broadcasted_iota(jnp.int32, (1, stop - start), 1)
        heads = []
        for head in range(start // HD, stop // HD):
            low = head * HD - start
            heads.append((head, (lanes >= low) & (lanes < low + HD)))
        slabs.append((start, stop, heads))
    return slabs


def keep(mask, values):
    return jnp.where(mask, values, jnp.zeros_like(values))


def forward_kernel(kind_ref, n_ref, bias_ref, slots_ref, *refs):
    proj_ref, mix_ref, lse_ref, weights_ref = refs[-4:]
    parts = refs[:-4]
    own = mix_ref.shape[1]

    @pl.when(pl.program_id(0) == 0)
    def _():
        if len(parts) == 1:
            weights_ref[...] = parts[0][...]
        else:
            for other, part_ref in enumerate(parts):
                start = pl.multiple_of((kind_ref[0] ^ other) * own, 64)
                weights_ref[pl.ds(start, own), :] = part_ref[...]

    proj_ref[...] = (nt(n_ref[...], weights_ref[0 : 3 * own, :]) + bias_ref[0]).astype(LOWER)
    outside = outside_image(slots_ref)
    lse_all = jnp.zeros((CHUNK, 128), FLOAT)
    lanes = lax.broadcasted_iota(jnp.int32, (1, 128), 1)
    for start, stop, heads in head_slabs(own):
        q = proj_ref[:, start:stop] * LOWER(HD**-0.5)
        k = proj_ref[:, own + start : own + stop]
        v = proj_ref[:, 2 * own + start : 2 * own + stop]
        mixed = None
        for head, mask in heads:
            scores = nt(q, keep(mask, k)) + outside
            largest = jnp.max(scores, axis=-1, keepdims=True)
            powered = jnp.exp(scores - largest)
            total = jnp.sum(powered, axis=-1, keepdims=True)
            probs = (powered * (1.0 / total)).astype(LOWER)
            part = nn(probs, keep(mask, v))
            mixed = part if mixed is None else mixed + part
            lse_all = jnp.where(lanes == head, largest + jnp.log(total), lse_all)
        mix_ref[:, start:stop] = mixed.astype(LOWER)
    lse_ref[0] = jnp.transpose(lse_all)[0:8, :]


def forward_quarter(kind, normed, biases, slots, parts, j):
    width = normed.shape[1]
    own = biases.shape[2] // 3
    return call(
        forward_kernel,
        "forward_quarter",
        14,
        (normed, biases, slots, *parts),
        [
            rows_spec(width),
            pl.BlockSpec((1, 1, 3 * own), lambda c, *_: (j, 0, 0)),
            chunk_spec(8),
            *[whole(p.shape) for p in parts],
        ],
        [
            ((PACKED, 3 * own), LOWER, rows_spec(3 * own)),
            ((PACKED, own), LOWER, rows_spec(own)),
            ((CHUNKS, 8, CHUNK), FLOAT, chunk_spec(8)),
            ((4 * own, width), LOWER, whole((4 * own, width))),
        ],
        flops=2 * PACKED * width * 8 * own,
        place=kind,
    )


def join_kernel(place_ref, x_ref, post_ref, own_post_ref, gains_ref, shifts_ref, *refs):
    hidden_ref, normed_ref, own_ref, chosen = refs[-4:]
    parts = refs[:-4]
    count = len(parts) // 2
    own = own_ref.shape[1]

    @pl.when(pl.program_id(0) == 0)
    def _():
        for j, out_ref in enumerate(parts[count:]):
            chosen[j * own : (j + 1) * own, :] = choose_own(place_ref[0], out_ref[...], own)

    attn, attn_own = post_ref[0:1, :], own_post_ref[0:1, :]
    for j, (mix_ref, out_ref) in enumerate(zip(parts[:count], parts[count:])):
        attn = attn + nn(mix_ref[...], out_ref[...])
        attn_own = attn_own + nn(mix_ref[...], chosen[j * own : (j + 1) * own, :])
    own_ref[...] = attn_own
    hidden = x_ref[...].astype(FLOAT) + attn
    hidden_ref[...] = hidden
    scaled, _ = norm_stats(hidden)
    normed_ref[...] = (scaled * gains_ref[1:2, :] + shifts_ref[1:2, :]).astype(LOWER)


def out_spec(own, width):
    return pl.BlockSpec((own, width), lambda *_: (3, 0), pipeline_mode=pl.Buffered(1))


def join_quarters(place, x, post, own_post, gains, shifts, mixes, weights):
    width = x.shape[1]
    own = mixes[0].shape[1]
    return call(
        join_kernel,
        "join_quarters",
        14,
        (x, post, own_post, gains, shifts, *mixes, *weights),
        [
            rows_spec(width),
            whole((2, width)),
            whole((2, own)),
            whole((2, width)),
            whole((2, width)),
            *[rows_spec(own) for _ in mixes],
            *[out_spec(own, width) for _ in weights],
        ],
        [
            ((PACKED, width), FLOAT, rows_spec(width)),
            ((PACKED, width), LOWER, rows_spec(width)),
            ((PACKED, own), FLOAT, rows_spec(own)),
        ],
        scratch=[pltpu.VMEM((len(weights) * own, own), LOWER)],
        flops=3 * PACKED * width * width,
        place=place,
    )


def stack_places(place, parts, stacked):
    size = len(parts)
    for j, part in enumerate(parts):
        own = part.shape[0]
        start = pl.multiple_of(lax.rem(place - j + size, size) * own, 64)
        stacked[pl.ds(start, own), :] = part.astype(FLOAT)


def cot_kernel(place_ref, gate_ref, *refs):
    cot_ref, gated_ref, stacked = refs[-3:]
    stack_places(place_ref[0], [r[0] for r in refs[:-3]], stacked)
    cot = jnp.transpose(stacked[...])
    cot_ref[...] = cot.astype(LOWER)
    gated_ref[...] = (gate_ref[:, 0:1] * cot).astype(LOWER)


def cot_chunks(place, gate, parts):
    own = parts[0].shape[1]
    width = own * len(parts)
    return call(
        cot_kernel,
        "cot_chunks",
        10,
        (gate, *parts),
        [rows_spec(128), *[chunk_spec(own) for _ in parts]],
        [((PACKED, width), LOWER, rows_spec(width))] * 2,
        scratch=[pltpu.VMEM((width, CHUNK), FLOAT)],
        flops=PACKED * width,
        place=place,
    )


def gelu_pair(u):
    cdf = 0.5 * (1.0 + lax.erf(u * (0.5**0.5)))
    density = jnp.exp(-0.5 * u * u) * 0.3989422804014327
    return u * cdf, cdf + u * density


def mlp_step(normed, gated, up, down, bias, own_down):
    activation, slope = gelu_pair(nn(normed, up) + bias)
    activation = activation.astype(LOWER)
    grad_act = nt(gated, down)
    grad_pre = (grad_act * slope).astype(LOWER)
    gate_part = jnp.sum(activation.astype(FLOAT) * grad_act, axis=-1, keepdims=True)
    return activation, grad_pre, nt(grad_pre, up), gate_part, nn(activation, own_down)


def own_mlp_kernel(
    place_ref,
    n_ref,
    gated_ref,
    up_ref,
    down_ref,
    bias_ref,
    act_ref,
    pre_ref,
    grad_ref,
    gate_ref,
    out_ref,
    bias_sum_ref,
    own_down,
):
    @pl.when(pl.program_id(0) == 0)
    def _():
        own_down[...] = choose_own(place_ref[0], down_ref[...], own_down.shape[1])
        bias_sum_ref[...] = jnp.zeros_like(bias_sum_ref)

    activation, grad_pre, grad_part, gate_part, out_part = mlp_step(
        n_ref[...], gated_ref[...], up_ref[...], down_ref[...], bias_ref[...], own_down[...]
    )
    act_ref[...] = activation
    pre_ref[...] = grad_pre
    grad_ref[...] = grad_part
    gate_ref[...] = jnp.broadcast_to(gate_part, gate_ref.shape)
    out_ref[...] = out_part
    bias_sum_ref[0:1, :] += jnp.sum(grad_pre.astype(FLOAT), axis=0, keepdims=True)


def own_mlp(place, normed, gated, up, down, bias, own):
    width, hidden = up.shape
    return call(
        own_mlp_kernel,
        "own_mlp",
        24,
        (normed, gated, up, down, bias),
        [
            rows_spec(width),
            rows_spec(width),
            whole((width, hidden)),
            whole((hidden, width)),
            whole((1, hidden)),
        ],
        [
            ((PACKED, hidden), LOWER, rows_spec(hidden)),
            ((PACKED, hidden), LOWER, rows_spec(hidden)),
            ((PACKED, width), FLOAT, rows_spec(width)),
            ((PACKED, 128), FLOAT, rows_spec(128)),
            ((PACKED, own), FLOAT, rows_spec(own)),
            ((8, hidden), FLOAT, whole((8, hidden), False)),
        ],
        scratch=[pltpu.VMEM((hidden, own), LOWER)],
        flops=2 * PACKED * hidden * (3 * width + own),
        place=place,
    )


def other_mlp_kernel(
    last, place_ref, n_ref, gated_ref, grad_in_ref, gate_in_ref, out_in_ref, *refs
):
    grad_ref, gate_ref, out_ref, up, down, own_down = refs[-6:]
    ups, downs = refs[0:4], refs[4:8]
    part = downs[0].shape[2]
    width = up.shape[1]

    @pl.when(pl.program_id(0) == 0)
    def _():
        for side in range(2):
            for c in range(2):
                for near in range(2):
                    to_up = place_ref[1] ^ (4 * side + 2 * near + c)
                    to_down = place_ref[1] ^ (4 * near + 2 * side + c)
                    up_rows = pl.ds(pl.multiple_of(to_up * part, 32), part)
                    down_rows = pl.ds(pl.multiple_of(to_down * part, 32), part)
                    up[up_rows, :] = ups[side + 2 * c][near, 0, 0:part]
                    down[down_rows, :] = downs[side + 2 * c][near, 0]
        own_down[...] = choose_own(place_ref[0], down[...], own_down.shape[1])

    pieces = ups[0][0, 0, part : part + 16].astype(FLOAT)
    bias = pieces[0:1] + (pieces[1:2] + pieces[2:3])
    _, _, grad_part, gate_part, out_part = mlp_step(
        n_ref[...], gated_ref[...], up[...], down[...], bias, own_down[...]
    )
    grad_ref[...] = grad_in_ref[...] + grad_part
    gate_ref[...] = gate_in_ref[...] + gate_part
    if last:
        attn_ref, post_ref, open_ref = refs[8:11]
        total = out_in_ref[...] + out_part + attn_ref[...] + post_ref[1:2, :]
        out_ref[...] = (open_ref[:, 0:1] * total).astype(LOWER)
    else:
        out_ref[...] = out_in_ref[...] + out_part


def other_mlp(places, normed, gated, sums, ups, downs, j, extra=()):
    width = normed.shape[1]
    own = sums[2].shape[1]
    last = len(extra) > 0
    held = lambda array: pl.BlockSpec(
        (2, 1, *array.shape[2:]), lambda c, *_: (0, j, 0, 0), pipeline_mode=pl.Buffered(1)
    )
    extra_specs = [rows_spec(own), whole((2, own)), rows_spec(128)] if last else []
    return call(
        functools.partial(other_mlp_kernel, last),
        "other_mlp",
        26,
        (normed, gated, *sums, *ups, *downs, *extra),
        [
            rows_spec(width),
            rows_spec(width),
            rows_spec(width),
            rows_spec(128),
            rows_spec(own),
            *[held(u) for u in ups],
            *[held(d) for d in downs],
            *extra_specs,
        ],
        [
            ((PACKED, width), FLOAT, rows_spec(width)),
            ((PACKED, 128), FLOAT, rows_spec(128)),
            ((PACKED, own), LOWER if last else FLOAT, rows_spec(own)),
        ],
        scratch=[
            pltpu.VMEM((width, width), LOWER),
            pltpu.VMEM((width, width), LOWER),
            pltpu.VMEM((width, own), LOWER),
        ],
        flops=2 * PACKED * width * (3 * width + own),
        place=places,
    )


def second_norm_kernel(
    grad_ref,
    gate_part_ref,
    hidden_ref,
    x_ref,
    cot_ref,
    gate_ref,
    post_ref,
    gains_ref,
    ghid_ref,
    glow_ref,
    logit_ref,
    sums_ref,
):
    @pl.when(pl.program_id(0) == 0)
    def _():
        sums_ref[...] = jnp.zeros_like(sums_ref)

    hidden = hidden_ref[...]
    scaled, inverse = norm_stats(hidden)
    grad_out = grad_ref[...]
    weighted = grad_out * gains_ref[1:2, :]
    centre_term = jnp.mean(weighted, axis=-1, keepdims=True)
    scale_term = jnp.mean(weighted * scaled, axis=-1, keepdims=True)
    grad_hidden = inverse * (weighted - centre_term - scaled * scale_term)
    gate = gate_ref[:, 0:1]
    gated = gate * cot_ref[...].astype(FLOAT)
    grad_attn = grad_hidden + gated
    ghid_ref[...] = grad_hidden
    glow_ref[...] = grad_attn.astype(LOWER)
    attn = hidden - x_ref[...].astype(FLOAT)
    dotted = jnp.sum(gated * (attn + post_ref[1:2, :]), axis=-1, keepdims=True)
    logit = (1.0 - gate) * (dotted + gate_part_ref[:, 0:1])
    logit_ref[...] = jnp.broadcast_to(logit, logit_ref.shape)
    sums_ref[0:1, :] += jnp.sum(grad_out * scaled, axis=0, keepdims=True)
    sums_ref[1:2, :] += jnp.sum(grad_out, axis=0, keepdims=True)
    sums_ref[2:3, :] += jnp.sum(grad_attn, axis=0, keepdims=True)
    sums_ref[3:4, :] += jnp.sum(gated, axis=0, keepdims=True)


def second_norm(grad, gate_part, hidden, x, cot_rows, gate, post, gains):
    width = x.shape[1]
    return call(
        second_norm_kernel,
        "second_norm",
        20,
        (grad, gate_part, hidden, x, cot_rows, gate, post, gains),
        [
            rows_spec(width),
            rows_spec(128),
            rows_spec(width),
            rows_spec(width),
            rows_spec(width),
            rows_spec(128),
            whole((2, width)),
            whole((2, width)),
        ],
        [
            ((PACKED, width), FLOAT, rows_spec(width)),
            ((PACKED, width), LOWER, rows_spec(width)),
            ((PACKED, 128), FLOAT, rows_spec(128)),
            ((8, width), FLOAT, whole((8, width), False)),
        ],
        flops=20 * PACKED * width,
    )


def backward_kernel(low_ref, slots_ref, proj_ref, lse_ref, out_ref, gproj_ref, sums_ref):
    @pl.when(pl.program_id(0) == 0)
    def _():
        sums_ref[...] = jnp.zeros_like(sums_ref)

    low = low_ref[...]
    outside = outside_image(slots_ref)
    own = out_ref.shape[0]
    gmix = nt(low, out_ref[...]).astype(LOWER)
    for start, stop, heads in head_slabs(own):
        k_cols = slice(own + start, own + stop)
        v_cols = slice(2 * own + start, 2 * own + stop)
        q = proj_ref[:, start:stop] * LOWER(HD**-0.5)
        k = proj_ref[:, k_cols]
        v = proj_ref[:, v_cols]
        g = gmix[:, start:stop]
        grad_q, grad_k, grad_v = None, None, None
        for head, mask in heads:
            own_k = keep(mask, k)
            scores = nt(own_k, q) + outside
            probs = jnp.exp(scores - lse_ref[0, head : head + 1, :])
            grad_probs = nt(keep(mask, v), g)
            inner = jnp.sum(probs * grad_probs, axis=0, keepdims=True)
            grad_scores = (probs * (grad_probs - inner)).astype(LOWER)
            one_v = nn(probs.astype(LOWER), g)
            one_k = nn(grad_scores, q)
            one_q = tn(grad_scores, own_k)
            if grad_q is None:
                grad_q, grad_k, grad_v = one_q, one_k, one_v
            else:
                grad_q = grad_q + one_q
                grad_k = jnp.where(mask, one_k, grad_k)
                grad_v = jnp.where(mask, one_v, grad_v)
        gproj_ref[:, start:stop] = (grad_q * HD**-0.5).astype(LOWER)
        gproj_ref[:, k_cols] = grad_k.astype(LOWER)
        gproj_ref[:, v_cols] = grad_v.astype(LOWER)
    sums_ref[0:1, :] += jnp.sum(gproj_ref[...].astype(FLOAT), axis=0, keepdims=True)


def backward_quarter(low, slots, proj, lse, weights):
    width = low.shape[1]
    own = proj.shape[1] // 3
    return call(
        backward_kernel,
        "backward_quarter",
        18,
        (low, slots, proj, lse, weights),
        [
            rows_spec(width),
            chunk_spec(8),
            rows_spec(3 * own),
            chunk_spec(8),
            out_spec(own, width),
        ],
        [
            ((PACKED, 3 * own), LOWER, rows_spec(3 * own)),
            ((8, 3 * own), FLOAT, whole((8, 3 * own), False)),
        ],
        flops=2 * PACKED * width * 14 * own,
    )


def first_norm_kernel(x_ref, ghid_ref, logit_ref, gains_ref, router_ref, *refs):
    rows_ref, sums_ref = refs[-2:]
    parts = refs[:-2]
    count = len(parts) // 2

    @pl.when(pl.program_id(0) == 0)
    def _():
        sums_ref[...] = jnp.zeros_like(sums_ref)

    grad_out = None
    for gproj_ref, weights_ref in zip(parts[:count], parts[count:]):
        part = nn(gproj_ref[...], weights_ref[0 : gproj_ref.shape[1], :])
        grad_out = part if grad_out is None else grad_out + part
    x = x_ref[...].astype(FLOAT)
    scaled, inverse = norm_stats(x)
    weighted = grad_out * gains_ref[0:1, :]
    centre_term = jnp.mean(weighted, axis=-1, keepdims=True)
    scale_term = jnp.mean(weighted * scaled, axis=-1, keepdims=True)
    grad_norm = inverse * (weighted - centre_term - scaled * scale_term)
    logit = logit_ref[:, 0:1]
    rows_ref[...] = (ghid_ref[...] + grad_norm + logit * router_ref[...]).astype(LOWER)
    sums_ref[0:1, :] += jnp.sum(grad_out * scaled, axis=0, keepdims=True)
    sums_ref[1:2, :] += jnp.sum(grad_out, axis=0, keepdims=True)
    sums_ref[2:3, :] += jnp.sum(logit * x, axis=0, keepdims=True)


def first_norm(x, ghid, logit, gains, router, gprojs, weights):
    width = x.shape[1]
    return call(
        first_norm_kernel,
        "first_norm",
        22,
        (x, ghid, logit, gains, router, *gprojs, *weights),
        [
            rows_spec(width),
            rows_spec(width),
            rows_spec(128),
            whole((2, width)),
            whole((1, width)),
            *[rows_spec(g.shape[1]) for g in gprojs],
            *[whole(w.shape) for w in weights],
        ],
        [
            ((PACKED, width), LOWER, rows_spec(width)),
            ((8, width), FLOAT, whole((8, width), False)),
        ],
        flops=2 * PACKED * width * 3 * width,
    )


def scatter_kernel(place_ref, slots_ref, rows_ref, *refs):
    out_ref, stacked = refs[-2:]
    block = out_ref.shape[0]
    stack_places(place_ref[0], [r[...] for r in refs[:-2]], stacked)
    total = jnp.transpose(stacked[...])
    places = lax.broadcasted_iota(jnp.int32, (block, CHUNK), 0) + pl.program_id(0) * block
    for c in range(CHUNKS):
        onehot = (places == slots_ref[c, 0:1, :].astype(jnp.int32)).astype(FLOAT).astype(LOWER)
        total = total + nn(onehot, rows_ref[c * CHUNK : (c + 1) * CHUNK, :])
    out_ref[...] = total.astype(LOWER)


def scatter_rows(place, cot_parts, slots, rows):
    own, total = cot_parts[0].shape
    width = own * len(cot_parts)
    block = 512
    return call(
        scatter_kernel,
        "scatter_rows",
        16,
        (slots, rows, *cot_parts),
        [
            whole(slots.shape),
            whole((PACKED, width)),
            *[pl.BlockSpec((own, block), lambda c, *_: (0, c)) for _ in cot_parts],
        ],
        [((total, width), LOWER, rows_spec(width, block))],
        scratch=[pltpu.VMEM((width, block), FLOAT)],
        flops=2 * PACKED * total * width,
        place=place,
        grid=(pl.cdiv(total, block),),
    )[0]


def block_out_kernel(patch_ref, slots_ref, branch_ref, out_ref, total_ref):
    chunk = pl.program_id(0)
    added = tn(branch_ref[...], slot_onehot(slots_ref, out_ref.shape[1]))

    @pl.when(chunk == 0)
    def _():
        total_ref[...] = patch_ref[...].astype(FLOAT) + added

    @pl.when(chunk > 0)
    def _():
        total_ref[...] += added

    @pl.when(chunk == CHUNKS - 1)
    def _():
        out_ref[...] = total_ref[...].astype(LOWER)


def block_out_rows(patch_t, slots, branch):
    own, total = patch_t.shape
    return call(
        block_out_kernel,
        "block_out_rows",
        16,
        (patch_t, slots, branch),
        [whole((own, total)), chunk_spec(8), rows_spec(own)],
        [((own, total), LOWER, whole((own, total), False))],
        scratch=[pltpu.VMEM((own, total), FLOAT)],
        flops=2 * PACKED * total * own,
    )[0]


def turned(values, place):
    size = values.shape[0]
    back = jnp.concatenate([values[:1], values[:0:-1]], axis=0)
    twice = jnp.concatenate([back, back], axis=0)
    return lax.dynamic_slice_in_dim(twice, (size - place) % size, size, 0)


def after(value, *others):
    return lax.optimization_barrier((value, *others))[0]


def ring_step(value, size):
    return lax.ppermute(value, "mlp", [(i, (i + 1) % size) for i in range(size)])


def swap(value, bit, size):
    return lax.ppermute(value, "rows", [(i, i ^ (1 << bit)) for i in range(size)])


def bits_of(size):
    return [b for b in range(20) if (1 << b) < size]


def halve(value, rows_index, bit, size):
    pair = value.reshape(2, value.shape[0] // 2, *value.shape[1:])
    mine = (rows_index >> bit) & 1
    send = jnp.where(mine == 0, pair[1], pair[0]).astype(LOWER)
    kept = jnp.where(mine == 0, pair[0], pair[1])
    return kept, swap(send, bit, size)


def rejoin(value, rows_index, bit, size):
    other = swap(value, bit, size)
    mine = (rows_index >> bit) & 1
    return jnp.concatenate(
        [jnp.where(mine == 0, value, other), jnp.where(mine == 0, other, value)], axis=0
    )


def pack_slots(picked, live_slots):
    small = IMG_DEV * HALF_S
    named = jnp.where(live_slots == 1, picked, -1)

    def padded(parts, fill):
        have = sum(p.shape[0] for p in parts)
        return jnp.concatenate([*parts, jnp.full((CHUNK - have,), fill, jnp.int32)])

    always = IMG_DEV - L_MOST
    idx = [padded([named[: always * HALF_S]], -1)]
    seg = [padded([jnp.repeat(jnp.arange(always, dtype=jnp.int32), HALF_S)], always)]
    for j in range(L_MOST):
        first = small + j * HALF_L
        alive = live_slots[first] == 1
        other = IMG_DEV - 1 - j
        large_idx = padded([named[first : first + HALF_L]], -1)
        small_idx = padded([named[other * HALF_S : (other + 1) * HALF_S]], -1)
        idx.append(jnp.where(alive, large_idx, small_idx))
        length = jnp.where(alive, HALF_L, HALF_S)
        seg.append((jnp.arange(CHUNK, dtype=jnp.int32) >= length).astype(jnp.int32))
    idx, seg = jnp.stack(idx).astype(FLOAT), jnp.stack(seg).astype(FLOAT)
    rows = lax.broadcasted_iota(jnp.int32, (1, 8, 1), 1)
    return jnp.where(rows == 0, idx[:, None, :], seg[:, None, :])


def local(
    rows_size,
    mlp_size,
    patches,
    w_qkv,
    qkv_bias,
    w_out,
    post_bias,
    w_up,
    up_bias,
    w_down,
    norm_gains,
    norm_shifts,
    router,
    picked,
    live_slots,
    cotangent,
):
    width = patches.shape[1]
    mlp_index = lax.axis_index("mlp")
    rows_index = lax.axis_index("rows")
    share_index = rows_index % SHARE
    core = rows_index & 1
    place = mlp_index.astype(jnp.int32).reshape(1)
    places = jnp.stack([mlp_index, share_index]).astype(jnp.int32)
    kind = (rows_index % 4).astype(jnp.int32).reshape(1)
    own = w_out.shape[0]
    heads_here = own // HD
    others = mlp_size - 1
    router_row = router.reshape(1, width)

    def swapped(value, bit):
        return swap(value, bit, rows_size)

    own_weights = jnp.concatenate(
        [
            w_qkv.T.reshape(heads_here, 3, HD, width).transpose(1, 0, 2, 3).reshape(3 * own, width),
            w_out,
        ],
        axis=0,
    )
    piece = lax.dynamic_slice_in_dim(own_weights, kind[0] * own, own, 0)
    part = w_up.shape[0] // SHARE
    top = lax.reduce_precision(up_bias, 8, 7)
    middle = lax.reduce_precision(up_bias - top, 8, 7)
    bias_rows = jnp.stack([top, middle, up_bias - top - middle]).astype(LOWER)
    payload = jnp.concatenate(
        [
            piece,
            lax.dynamic_slice_in_dim(w_up, share_index * part, part, 0),
            jnp.pad(bias_rows, ((0, 13), (0, 0))),
            lax.dynamic_slice_in_dim(w_down, share_index * part, part, 0),
        ],
        axis=0,
    )
    came = ring_step(payload, mlp_size)

    kinds = jnp.stack([qkv_bias[0], jnp.zeros_like(qkv_bias[0]), qkv_bias[1]])
    biases = turned(kinds.reshape(3, mlp_size, own).transpose(1, 0, 2), mlp_index)
    biases = biases.reshape(mlp_size, 1, 3 * own)
    own_post = lax.dynamic_slice_in_dim(post_bias, mlp_index * own, own, 1)
    slots = pack_slots(picked, live_slots)
    cot_own = cotangent.T
    x, normed_one, gate, cot_part, patch_t = pick_rows(
        place, patches, cot_own, slots, norm_gains, norm_shifts, router_row
    )
    came = after(came, x)
    quarters, cot_parts, up_parts, down_parts = [], [cot_part], [], []
    parts = [own_weights]
    for j in range(mlp_size):
        normed_one = after(normed_one, came)
        arrived = came
        if j < others:
            up_parts.append(came[own : own + part + 16])
            down_parts.append(came[own + part + 16 :])
            got = came[:own]
            across = swapped(got, 1)
        if j + 1 < others:
            came = ring_step(arrived, mlp_size)
        if j > 0:
            cot_parts.append(ring_step(after(cot_parts[-1], arrived), mlp_size))
        quarters.append(forward_quarter(kind, normed_one, biases, slots, parts, j))
        if j < others:
            across = after(across, quarters[-1][1])
            parts = [got, swapped(got, 0), across, swapped(across, 0)]
            normed_one = after(normed_one, *parts)

    ups, downs = jnp.stack(up_parts), jnp.stack(down_parts)
    ups, downs = jnp.stack([ups, swapped(ups, 1)]), jnp.stack([downs, swapped(downs, 2)])

    projs, mixes, lses, weights = zip(*quarters)
    hidden, normed_two, attn_own = join_quarters(
        place, after(x, ups, downs), post_bias, own_post, norm_gains, norm_shifts, mixes, weights
    )
    ups, downs = [ups, swapped(ups, 2)], [downs, swapped(downs, 1)]
    cot_rows, gated = cot_chunks(place, gate, cot_parts)
    full_parts = [cot_own, ring_step(after(cot_own, gated), mlp_size)]

    act, grad_pre, *sums, up_bias_sum = own_mlp(
        place, normed_two, after(gated, hidden), w_up, w_down, up_bias.reshape(1, -1), own
    )
    sums[0] = after(sums[0], *ups, *downs)
    ups = [*ups, *[swapped(u, 0) for u in ups]]
    downs = [*downs, *[swapped(d, 0) for d in downs]]
    d_up, d_down = tn(normed_two, grad_pre), tn(act, gated)
    d_mlp = jnp.where(core == 0, d_up, d_down) + swapped(
        jnp.where(core == 0, d_down, d_up).astype(LOWER), 0
    ).astype(FLOAT)

    order = bits_of(rows_size)
    halving = [functools.partial(halve, rows_index=rows_index, size=rows_size, bit=b) for b in order]
    joining = [
        functools.partial(rejoin, rows_index=rows_index, size=rows_size, bit=b) for b in order[::-1]
    ]

    def summed(value, step):
        kept, other = step(value)
        return kept + other.astype(FLOAT)

    sums = other_mlp(places, normed_two, gated, sums, ups, downs, 0)
    sums[0] = after(sums[0], d_mlp)
    d_mlp = summed(d_mlp, halving[1])
    full_parts.append(ring_step(after(full_parts[-1], sums[0]), mlp_size))
    sums = other_mlp(places, normed_two, gated, sums, ups, downs, 1)
    for j in range(2, others - 1):
        sums = other_mlp(places, normed_two, gated, sums, ups, downs, j)
    grad_two, gate_part, branch = other_mlp(
        places, normed_two, gated, sums, ups, downs, others - 1, (attn_own, own_post, gate)
    )
    grad_two = after(grad_two, d_mlp)
    for step in halving[2:]:
        d_mlp = summed(d_mlp, step)
    d_mlp = d_mlp.astype(LOWER)
    grad_hidden, grad_low, logit, sums_two = second_norm(
        grad_two, gate_part, hidden, x, cot_rows, gate, post_bias, norm_gains
    )
    own_proj, bias_grad = backward_quarter(grad_low, slots, projs[0], lses[0], weights[0])
    d_attn = jnp.concatenate([tn(own_proj, normed_one), tn(mixes[0], grad_low)], axis=0)
    low = after(grad_low, d_mlp, full_parts[-1])
    full_parts.append(ring_step(after(full_parts[-1], own_proj), mlp_size))
    d_attn = summed(d_attn, halving[0])
    d_mlp = joining[0](d_mlp)
    gprojs = [own_proj]
    for j in range(1, mlp_size):
        low = after(low, d_attn)
        if j == 1:
            d_attn = summed(d_attn, halving[1])
        elif j == 2:
            low = after(low, d_mlp)
            for step in halving[2:]:
                d_attn = summed(d_attn, step)
            d_attn = d_attn.astype(LOWER)
            for step in joining[1:-1]:
                d_mlp = step(d_mlp)
        elif j == 3:
            low = after(low, d_mlp)
            d_attn = joining[0](d_attn)
            other = swapped(d_mlp, 0)
            d_up = jnp.where(core == 0, d_mlp, other).astype(FLOAT)
            d_down = jnp.where(core == 0, other, d_mlp).astype(FLOAT)
        gprojs.append(backward_quarter(low, slots, projs[j], lses[j], weights[j])[0])
    logit = after(logit, d_attn)
    for step in joining[1:-1]:
        d_attn = step(d_attn)
    rows_grad, sums_one = first_norm(
        x, grad_hidden, logit, norm_gains, router_row, gprojs, weights
    )
    branch = after(branch, rows_grad, d_attn)
    d_attn = joining[-1](d_attn)
    small = jnp.concatenate(
        [
            sums_two[:4],
            sums_one[:3],
            up_bias_sum[:1],
            jnp.pad(bias_grad[:1], ((0, 0), (0, width - 3 * own))),
        ],
        axis=0,
    )
    small = small + swapped(small, 0)
    for bit in order[1:-1]:
        small = small + swapped(small, bit)
    block_out = block_out_rows(patch_t, slots, branch).T
    rows_grad = after(rows_grad, block_out, small)
    small = small + swapped(small, order[-1])
    input_grad = scatter_rows(place, full_parts, slots, rows_grad)

    d_qkv = (
        d_attn[: 3 * own]
        .astype(FLOAT)
        .reshape(3, heads_here, HD, width)
        .transpose(1, 0, 2, 3)
        .reshape(3 * own, width)
        .T
    )
    d_qkv_bias = jnp.stack([small[8, :own], small[8, 2 * own : 3 * own]])
    return (
        block_out,
        input_grad,
        d_qkv,
        d_qkv_bias,
        d_attn[3 * own :].astype(FLOAT),
        small[2:4],
        d_up,
        small[7],
        d_down,
        jnp.stack([small[4], small[0]]),
        jnp.stack([small[5], small[1]]),
        small[6],
    )


def solution(mesh):
    in_specs = (
        P("rows", None),
        P(None, "mlp"),
        P(),
        P("mlp", None),
        P(),
        P(None, "mlp"),
        P("mlp"),
        P("mlp", None),
        P(),
        P(),
        P(),
        P("rows"),
        P("rows"),
        P("rows", "mlp"),
    )
    out_specs = (
        P("rows", "mlp"),
        P("rows", None),
        P(None, "mlp"),
        P(None, "mlp"),
        P("mlp", None),
        P(),
        P(None, "mlp"),
        P("mlp"),
        P("mlp", None),
        P(),
        P(),
        P(),
    )
    body = functools.partial(local, mesh.shape["rows"], mesh.shape["mlp"])
    return jax.shard_map(body, mesh=mesh, in_specs=in_specs, out_specs=out_specs, check_vma=False)
```

```python
import functools

import jax
import jax.numpy as jnp
from jax import lax
from jax.experimental import pallas as pl
from jax.experimental.pallas import tpu as pltpu
from jax.sharding import PartitionSpec as P

HD = 64
IMG_DEV = 6
L_MOST = 3
HALF_S = 99
HALF_L = 289

CHUNK = 304
CHUNKS = 1 + L_MOST
PACKED = CHUNK * CHUNKS
SHARE = 8

EPSILON = 1e-06
LOWER = jnp.bfloat16
FLOAT = jnp.float32
MASKED = -1e30


def nn(a, b):
    return lax.dot_general(a, b, (((1,), (0,)), ((), ())), preferred_element_type=FLOAT)


def nt(a, b):
    return lax.dot_general(a, b, (((1,), (1,)), ((), ())), preferred_element_type=FLOAT)


def tn(a, b):
    return lax.dot_general(a, b, (((0,), (0,)), ((), ())), preferred_element_type=FLOAT)


LATER = pltpu.MemorySpace.HBM


def params(mib):
    return pltpu.CompilerParams(vmem_limit_bytes=mib * 1024 * 1024)


def cost(flops, bytes_accessed, transcendentals=0):
    return pl.CostEstimate(
        flops=flops, bytes_accessed=bytes_accessed, transcendentals=transcendentals
    )


def whole(shape, single=True):
    zeros = (0,) * len(shape)
    if single:
        return pl.BlockSpec(shape, lambda *_: zeros, pipeline_mode=pl.Buffered(1))
    return pl.BlockSpec(shape, lambda *_: zeros)


def rows_spec(width, height=CHUNK):
    return pl.BlockSpec((height, width), lambda c, *_: (c, 0))


def chunk_spec(height, width=CHUNK):
    return pl.BlockSpec((1, height, width), lambda c, *_: (c, 0, 0))


def call(kernel, name, mib, operands, in_specs, outs, scratch=(), flops=0, place=None, grid=None, aliases=None):
    specs = [o[2] for o in outs]
    shapes = [o[3](o[0], o[1]) if len(o) > 3 else jax.ShapeDtypeStruct(o[0], o[1]) for o in outs]
    scalars = () if place is None else (place,)
    made = pl.pallas_call(
        kernel,
        grid_spec=pltpu.PrefetchScalarGridSpec(
            num_scalar_prefetch=len(scalars),
            grid=grid or (CHUNKS,),
            in_specs=in_specs,
            out_specs=specs,
            scratch_shapes=scratch,
        ),
        out_shape=shapes,
        input_output_aliases=aliases or {},
        compiler_params=params(mib),
        cost_estimate=cost(flops // 1000000, 1000),
        name=name,
    )(*scalars, *operands)
    return list(made)


def slot_onehot(slots_ref, rows):
    named = jnp.transpose(slots_ref[0])[:, 0:1].astype(jnp.int32)
    places = lax.broadcasted_iota(jnp.int32, (CHUNK, rows), 1)
    return (places == named).astype(FLOAT).astype(LOWER)


def outside_image(slots_ref):
    image = jnp.transpose(slots_ref[0])[:, 1:2]
    return jnp.where(image == slots_ref[0, 1:2, :], 0.0, MASKED)


def choose_own(place, values, own):
    width = values.shape[1]
    source = lax.broadcasted_iota(jnp.int32, (width, own), 0)
    target = lax.broadcasted_iota(jnp.int32, (width, own), 1)
    onehot = (source == target + place * own).astype(FLOAT).astype(LOWER)
    return nn(values, onehot).astype(LOWER)


def norm_stats(values):
    average = jnp.mean(values, axis=-1, keepdims=True)
    centred = values - average
    variance = jnp.mean(centred * centred, axis=-1, keepdims=True)
    inverse = lax.rsqrt(variance + EPSILON)
    return centred * inverse, inverse


def pick_kernel(
    place_ref,
    patches_ref,
    cot_ref,
    slots_ref,
    gains_ref,
    shifts_ref,
    router_ref,
    x_ref,
    n_ref,
    gate_ref,
    part_ref,
    patch_ref,
):
    onehot = slot_onehot(slots_ref, patches_ref.shape[0])
    part_ref[0] = nt(cot_ref[...], onehot).astype(LOWER)
    x = nn(onehot, patches_ref[...])
    x_ref[...] = x.astype(LOWER)
    scaled, _ = norm_stats(x)
    n_ref[...] = (scaled * gains_ref[0:1, :] + shifts_ref[0:1, :]).astype(LOWER)
    logit = jnp.sum(x * router_ref[...], axis=-1, keepdims=True)
    gate_ref[...] = jnp.broadcast_to(jax.nn.sigmoid(logit), gate_ref.shape)

    @pl.when(pl.program_id(0) == 0)
    def _():
        own, width = patch_ref.shape[0], patches_ref.shape[1]
        source = lax.broadcasted_iota(jnp.int32, (own, width), 1)
        target = lax.broadcasted_iota(jnp.int32, (own, width), 0)
        chosen = (source == target + place_ref[0] * own).astype(FLOAT).astype(LOWER)
        patch_ref[...] = nt(chosen, patches_ref[...]).astype(LOWER)


def pick_rows(place, patches, cot_own, slots, gains, shifts, router):
    rows, width = patches.shape
    own = cot_own.shape[0]
    return call(
        pick_kernel,
        "pick_rows",
        22,
        (patches, cot_own, slots, gains, shifts, router),
        [
            whole((rows, width)),
            whole((own, rows)),
            chunk_spec(8),
            whole((2, width)),
            whole((2, width)),
            whole((1, width)),
        ],
        [
            ((PACKED, width), LOWER, rows_spec(width)),
            ((PACKED, width), LOWER, rows_spec(width)),
            ((PACKED, 128), FLOAT, rows_spec(128)),
            ((CHUNKS, own, CHUNK), LOWER, chunk_spec(own)),
            ((own, rows), LOWER, whole((own, rows))),
        ],
        flops=2 * PACKED * rows * (width + own),
        place=place,
    )


def head_slabs(own):
    slabs = []
    for start in range(0, own, 2 * HD):
        stop = min(start + 2 * HD, own)
        lanes = lax.broadcasted_iota(jnp.int32, (1, stop - start), 1)
        heads = []
        for head in range(start // HD, stop // HD):
            low = head * HD - start
            heads.append((head, (lanes >= low) & (lanes < low + HD)))
        slabs.append((start, stop, heads))
    return slabs


def keep(mask, values):
    return jnp.where(mask, values, jnp.zeros_like(values))


def forward_kernel(kind_ref, n_ref, bias_ref, slots_ref, *refs):
    proj_ref, mix_ref, lse_ref, weights_ref = refs[-4:]
    parts = refs[:-4]
    own = mix_ref.shape[1]

    @pl.when(pl.program_id(0) == 0)
    def _():
        if len(parts) == 1:
            weights_ref[...] = parts[0][...]
        else:
            for other, part_ref in enumerate(parts):
                start = pl.multiple_of((kind_ref[0] ^ other) * own, 64)
                weights_ref[pl.ds(start, own), :] = part_ref[...]

    proj_ref[...] = (nt(n_ref[...], weights_ref[0 : 3 * own, :]) + bias_ref[0]).astype(LOWER)
    outside = outside_image(slots_ref)
    lse_all = jnp.zeros((CHUNK, 128), FLOAT)
    lanes = lax.broadcasted_iota(jnp.int32, (1, 128), 1)
    for start, stop, heads in head_slabs(own):
        q = proj_ref[:, start:stop] * LOWER(HD**-0.5)
        k = proj_ref[:, own + start : own + stop]
        v = proj_ref[:, 2 * own + start : 2 * own + stop]
        mixed = None
        for head, mask in heads:
            scores = nt(q, keep(mask, k)) + outside
            largest = jnp.max(scores, axis=-1, keepdims=True)
            powered = jnp.exp(scores - largest)
            total = jnp.sum(powered, axis=-1, keepdims=True)
            probs = (powered * (1.0 / total)).astype(LOWER)
            part = nn(probs, keep(mask, v))
            mixed = part if mixed is None else mixed + part
            lse_all = jnp.where(lanes == head, largest + jnp.log(total), lse_all)
        mix_ref[:, start:stop] = mixed.astype(LOWER)
    lse_ref[0] = jnp.transpose(lse_all)[0:8, :]


def forward_quarter(kind, normed, biases, slots, parts, j):
    width = normed.shape[1]
    own = biases.shape[2] // 3
    return call(
        forward_kernel,
        "forward_quarter",
        14,
        (normed, biases, slots, *parts),
        [
            rows_spec(width),
            pl.BlockSpec((1, 1, 3 * own), lambda c, *_: (j, 0, 0)),
            chunk_spec(8),
            *[whole(p.shape) for p in parts],
        ],
        [
            ((PACKED, 3 * own), LOWER, rows_spec(3 * own)),
            ((PACKED, own), LOWER, rows_spec(own)),
            ((CHUNKS, 8, CHUNK), FLOAT, chunk_spec(8)),
            ((4 * own, width), LOWER, whole((4 * own, width))),
        ],
        flops=2 * PACKED * width * 8 * own,
        place=kind,
    )


def join_kernel(place_ref, x_ref, post_ref, own_post_ref, gains_ref, shifts_ref, *refs):
    hidden_ref, normed_ref, own_ref, chosen = refs[-4:]
    parts = refs[:-4]
    count = len(parts) // 2
    own = own_ref.shape[1]

    @pl.when(pl.program_id(0) == 0)
    def _():
        for j, out_ref in enumerate(parts[count:]):
            chosen[j * own : (j + 1) * own, :] = choose_own(place_ref[0], out_ref[...], own)

    attn, attn_own = post_ref[0:1, :], own_post_ref[0:1, :]
    for j, (mix_ref, out_ref) in enumerate(zip(parts[:count], parts[count:])):
        attn = attn + nn(mix_ref[...], out_ref[...])
        attn_own = attn_own + nn(mix_ref[...], chosen[j * own : (j + 1) * own, :])
    own_ref[...] = attn_own
    hidden = x_ref[...].astype(FLOAT) + attn
    hidden_ref[...] = hidden
    scaled, _ = norm_stats(hidden)
    normed_ref[...] = (scaled * gains_ref[1:2, :] + shifts_ref[1:2, :]).astype(LOWER)


def out_spec(own, width):
    return pl.BlockSpec((own, width), lambda *_: (3, 0), pipeline_mode=pl.Buffered(1))


def join_quarters(place, x, post, own_post, gains, shifts, mixes, weights):
    width = x.shape[1]
    own = mixes[0].shape[1]
    return call(
        join_kernel,
        "join_quarters",
        14,
        (x, post, own_post, gains, shifts, *mixes, *weights),
        [
            rows_spec(width),
            whole((2, width)),
            whole((2, own)),
            whole((2, width)),
            whole((2, width)),
            *[rows_spec(own) for _ in mixes],
            *[out_spec(own, width) for _ in weights],
        ],
        [
            ((PACKED, width), FLOAT, rows_spec(width)),
            ((PACKED, width), LOWER, rows_spec(width)),
            ((PACKED, own), FLOAT, rows_spec(own)),
        ],
        scratch=[pltpu.VMEM((len(weights) * own, own), LOWER)],
        flops=3 * PACKED * width * width,
        place=place,
    )


def stack_places(place, parts, stacked):
    size = len(parts)
    for j, part in enumerate(parts):
        own = part.shape[0]
        start = pl.multiple_of(lax.rem(place - j + size, size) * own, 64)
        stacked[pl.ds(start, own), :] = part.astype(FLOAT)


def cot_kernel(place_ref, gate_ref, *refs):
    cot_ref, gated_ref, stacked = refs[-3:]
    stack_places(place_ref[0], [r[0] for r in refs[:-3]], stacked)
    cot = jnp.transpose(stacked[...])
    cot_ref[...] = cot.astype(LOWER)
    gated_ref[...] = (gate_ref[:, 0:1] * cot).astype(LOWER)


def cot_chunks(place, gate, parts):
    own = parts[0].shape[1]
    width = own * len(parts)
    return call(
        cot_kernel,
        "cot_chunks",
        10,
        (gate, *parts),
        [rows_spec(128), *[chunk_spec(own) for _ in parts]],
        [
            ((PACKED, width), LOWER, rows_spec(width)),
            ((PACKED, width), LOWER, rows_spec(width)),
        ],
        scratch=[pltpu.VMEM((width, CHUNK), FLOAT)],
        flops=PACKED * width,
        place=place,
    )


def gelu_pair(u):
    cdf = 0.5 * (1.0 + lax.erf(u * (0.5**0.5)))
    density = jnp.exp(-0.5 * u * u) * 0.3989422804014327
    return u * cdf, cdf + u * density


def mlp_step(normed, gated, up, down, bias, own_down):
    activation, slope = gelu_pair(nn(normed, up) + bias)
    activation = activation.astype(LOWER)
    grad_act = nt(gated, down)
    grad_pre = (grad_act * slope).astype(LOWER)
    gate_part = jnp.sum(activation.astype(FLOAT) * grad_act, axis=-1, keepdims=True)
    return activation, grad_pre, nt(grad_pre, up), gate_part, nn(activation, own_down)


def own_mlp_kernel(
    place_ref,
    n_ref,
    gated_ref,
    up_ref,
    down_ref,
    bias_ref,
    act_ref,
    pre_ref,
    grad_ref,
    gate_ref,
    out_ref,
    bias_sum_ref,
    own_down,
):
    @pl.when(pl.program_id(0) == 0)
    def _():
        own_down[...] = choose_own(place_ref[0], down_ref[...], own_down.shape[1])
        bias_sum_ref[...] = jnp.zeros_like(bias_sum_ref)

    activation, grad_pre, grad_part, gate_part, out_part = mlp_step(
        n_ref[...], gated_ref[...], up_ref[...], down_ref[...], bias_ref[...], own_down[...]
    )
    act_ref[...] = activation
    pre_ref[...] = grad_pre
    grad_ref[...] = grad_part
    gate_ref[...] = jnp.broadcast_to(gate_part, gate_ref.shape)
    out_ref[...] = out_part
    bias_sum_ref[0:1, :] += jnp.sum(grad_pre.astype(FLOAT), axis=0, keepdims=True)


def own_mlp(place, normed, gated, up, down, bias, own):
    width, hidden = up.shape
    return call(
        own_mlp_kernel,
        "own_mlp",
        24,
        (normed, gated, up, down, bias),
        [
            rows_spec(width),
            rows_spec(width),
            whole((width, hidden)),
            whole((hidden, width)),
            whole((1, hidden)),
        ],
        [
            ((PACKED, hidden), LOWER, rows_spec(hidden)),
            ((PACKED, hidden), LOWER, rows_spec(hidden)),
            ((PACKED, width), FLOAT, rows_spec(width)),
            ((PACKED, 128), FLOAT, rows_spec(128)),
            ((PACKED, own), FLOAT, rows_spec(own)),
            ((8, hidden), FLOAT, whole((8, hidden), False)),
        ],
        scratch=[pltpu.VMEM((hidden, own), LOWER)],
        flops=2 * PACKED * hidden * (3 * width + own),
        place=place,
    )


def own_grads_kernel(core_ref, n_ref, pre_ref, act_ref, gated_ref, kept_ref, sent_ref, up, down):
    chunk = pl.program_id(0)
    grad_up = tn(n_ref[...], pre_ref[...])
    grad_down = tn(act_ref[...], gated_ref[...])

    @pl.when(chunk == 0)
    def _():
        up[...] = grad_up
        down[...] = grad_down

    @pl.when(chunk > 0)
    def _():
        up[...] += grad_up
        down[...] += grad_down

    @pl.when((chunk == CHUNKS - 1) & (core_ref[0] == 0))
    def _():
        kept_ref[...] = up[...]
        sent_ref[...] = down[...].astype(LOWER)

    @pl.when((chunk == CHUNKS - 1) & (core_ref[0] == 1))
    def _():
        kept_ref[...] = down[...]
        sent_ref[...] = up[...].astype(LOWER)


def own_grads(core, normed, grad_pre, act, gated):
    width = normed.shape[1]
    return call(
        own_grads_kernel,
        "own_grads",
        22,
        (normed, grad_pre, act, gated),
        [rows_spec(width)] * 4,
        [
            ((width, width), FLOAT, whole((width, width))),
            ((width, width), LOWER, whole((width, width))),
        ],
        scratch=[pltpu.VMEM((width, width), FLOAT)] * 2,
        flops=4 * PACKED * width * width,
        place=core,
    )


def other_mlp_kernel(
    last, place_ref, n_ref, gated_ref, grad_in_ref, gate_in_ref, out_in_ref, *refs
):
    grad_ref, gate_ref, out_ref, up, down, own_down = refs[-6:]
    ups, downs = refs[0:4], refs[4:8]
    part = downs[0].shape[2]
    width = up.shape[1]

    @pl.when(pl.program_id(0) == 0)
    def _():
        for side in range(2):
            for c in range(2):
                for near in range(2):
                    to_up = place_ref[1] ^ (4 * side + 2 * near + c)
                    to_down = place_ref[1] ^ (4 * near + 2 * side + c)
                    up_rows = pl.ds(pl.multiple_of(to_up * part, 32), part)
                    down_rows = pl.ds(pl.multiple_of(to_down * part, 32), part)
                    up[up_rows, :] = ups[side + 2 * c][near, 0, 0:part]
                    down[down_rows, :] = downs[side + 2 * c][near, 0]
        own_down[...] = choose_own(place_ref[0], down[...], own_down.shape[1])

    pieces = ups[0][0, 0, part : part + 16].astype(FLOAT)
    bias = pieces[0:1] + (pieces[1:2] + pieces[2:3])
    _, _, grad_part, gate_part, out_part = mlp_step(
        n_ref[...], gated_ref[...], up[...], down[...], bias, own_down[...]
    )
    grad_ref[...] = grad_in_ref[...] + grad_part
    gate_ref[...] = gate_in_ref[...] + gate_part
    if last:
        attn_ref, post_ref, open_ref = refs[8:11]
        total = out_in_ref[...] + out_part + attn_ref[...] + post_ref[1:2, :]
        out_ref[...] = (open_ref[:, 0:1] * total).astype(LOWER)
    else:
        out_ref[...] = out_in_ref[...] + out_part


def other_mlp(places, normed, gated, sums, ups, downs, j, extra=()):
    width = normed.shape[1]
    own = sums[2].shape[1]
    last = len(extra) > 0
    held = lambda array: pl.BlockSpec(
        (2, 1, *array.shape[2:]), lambda c, *_: (0, j, 0, 0), pipeline_mode=pl.Buffered(1)
    )
    extra_specs = [rows_spec(own), whole((2, own)), rows_spec(128)] if last else []
    return call(
        functools.partial(other_mlp_kernel, last),
        "other_mlp",
        26,
        (normed, gated, *sums, *ups, *downs, *extra),
        [
            rows_spec(width),
            rows_spec(width),
            rows_spec(width),
            rows_spec(128),
            rows_spec(own),
            *[held(u) for u in ups],
            *[held(d) for d in downs],
            *extra_specs,
        ],
        [
            ((PACKED, width), FLOAT, rows_spec(width)),
            ((PACKED, 128), FLOAT, rows_spec(128)),
            ((PACKED, own), LOWER if last else FLOAT, rows_spec(own)),
        ],
        scratch=[
            pltpu.VMEM((width, width), LOWER),
            pltpu.VMEM((width, width), LOWER),
            pltpu.VMEM((width, own), LOWER),
        ],
        flops=2 * PACKED * width * (3 * width + own),
        place=places,
    )


def second_norm_kernel(
    grad_ref,
    gate_part_ref,
    hidden_ref,
    x_ref,
    cot_ref,
    gate_ref,
    post_ref,
    gains_ref,
    ghid_ref,
    glow_ref,
    logit_ref,
    sums_ref,
):
    @pl.when(pl.program_id(0) == 0)
    def _():
        sums_ref[...] = jnp.zeros_like(sums_ref)

    hidden = hidden_ref[...]
    scaled, inverse = norm_stats(hidden)
    grad_out = grad_ref[...]
    weighted = grad_out * gains_ref[1:2, :]
    centre_term = jnp.mean(weighted, axis=-1, keepdims=True)
    scale_term = jnp.mean(weighted * scaled, axis=-1, keepdims=True)
    grad_hidden = inverse * (weighted - centre_term - scaled * scale_term)
    gate = gate_ref[:, 0:1]
    gated = gate * cot_ref[...].astype(FLOAT)
    grad_attn = grad_hidden + gated
    ghid_ref[...] = grad_hidden
    glow_ref[...] = grad_attn.astype(LOWER)
    attn = hidden - x_ref[...].astype(FLOAT)
    dotted = jnp.sum(gated * (attn + post_ref[1:2, :]), axis=-1, keepdims=True)
    logit = (1.0 - gate) * (dotted + gate_part_ref[:, 0:1])
    logit_ref[...] = jnp.broadcast_to(logit, logit_ref.shape)
    sums_ref[0:1, :] += jnp.sum(grad_out * scaled, axis=0, keepdims=True)
    sums_ref[1:2, :] += jnp.sum(grad_out, axis=0, keepdims=True)
    sums_ref[2:3, :] += jnp.sum(grad_attn, axis=0, keepdims=True)
    sums_ref[3:4, :] += jnp.sum(gated, axis=0, keepdims=True)


def second_norm(grad, gate_part, hidden, x, cot_rows, gate, post, gains):
    width = x.shape[1]
    return call(
        second_norm_kernel,
        "second_norm",
        20,
        (grad, gate_part, hidden, x, cot_rows, gate, post, gains),
        [
            rows_spec(width),
            rows_spec(128),
            rows_spec(width),
            rows_spec(width),
            rows_spec(width),
            rows_spec(128),
            whole((2, width)),
            whole((2, width)),
        ],
        [
            ((PACKED, width), FLOAT, rows_spec(width)),
            ((PACKED, width), LOWER, rows_spec(width)),
            ((PACKED, 128), FLOAT, rows_spec(128)),
            ((8, width), FLOAT, whole((8, width), False)),
        ],
        flops=20 * PACKED * width,
    )


def backward_kernel(own_quarter, core_ref, low_ref, slots_ref, proj_ref, lse_ref, out_ref, *refs):
    if own_quarter:
        normed_ref, mix_ref, gproj_ref, sums_ref, kept_ref, sent_ref, grads = refs
    else:
        (gproj_ref,) = refs
    chunk = pl.program_id(0)
    low = low_ref[...]
    outside = outside_image(slots_ref)
    own = out_ref.shape[0]
    gmix = nt(low, out_ref[...]).astype(LOWER)
    for start, stop, heads in head_slabs(own):
        k_cols = slice(own + start, own + stop)
        v_cols = slice(2 * own + start, 2 * own + stop)
        q = proj_ref[:, start:stop] * LOWER(HD**-0.5)
        k = proj_ref[:, k_cols]
        v = proj_ref[:, v_cols]
        g = gmix[:, start:stop]
        grad_q, grad_k, grad_v = None, None, None
        for head, mask in heads:
            own_k = keep(mask, k)
            scores = nt(own_k, q) + outside
            probs = jnp.exp(scores - lse_ref[0, head : head + 1, :])
            grad_probs = nt(keep(mask, v), g)
            inner = jnp.sum(probs * grad_probs, axis=0, keepdims=True)
            grad_scores = (probs * (grad_probs - inner)).astype(LOWER)
            one_v = nn(probs.astype(LOWER), g)
            one_k = nn(grad_scores, q)
            one_q = tn(grad_scores, own_k)
            if grad_q is None:
                grad_q, grad_k, grad_v = one_q, one_k, one_v
            else:
                grad_q = grad_q + one_q
                grad_k = jnp.where(mask, one_k, grad_k)
                grad_v = jnp.where(mask, one_v, grad_v)
        gproj_ref[:, start:stop] = (grad_q * HD**-0.5).astype(LOWER)
        gproj_ref[:, k_cols] = grad_k.astype(LOWER)
        gproj_ref[:, v_cols] = grad_v.astype(LOWER)
    if own_quarter:
        half = sent_ref.shape[0]
        gproj = gproj_ref[...]
        column_sums = jnp.sum(gproj.astype(FLOAT), axis=0, keepdims=True)
        d_qkv = tn(gproj, normed_ref[...])
        d_out = tn(mix_ref[...], low)

        @pl.when(chunk == 0)
        def _():
            sums_ref[...] = jnp.zeros_like(sums_ref)
            grads[0 : 3 * own, :] = d_qkv
            grads[3 * own :, :] = d_out

        @pl.when(chunk > 0)
        def _():
            grads[0 : 3 * own, :] += d_qkv
            grads[3 * own :, :] += d_out

        sums_ref[0:1, :] += column_sums

        @pl.when(chunk == CHUNKS - 1)
        def _():
            kept = pl.ds(pl.multiple_of(core_ref[0] * half, 16), half)
            sent = pl.ds(pl.multiple_of((1 - core_ref[0]) * half, 16), half)
            kept_ref[...] = grads[kept, :]
            sent_ref[...] = grads[sent, :].astype(LOWER)


def backward_quarter(core, low, slots, proj, lse, weights, extra=()):
    width = low.shape[1]
    own = proj.shape[1] // 3
    own_quarter = len(extra) > 0
    outs = [((PACKED, 3 * own), LOWER, rows_spec(3 * own))]
    if own_quarter:
        half = 2 * own
        outs += [
            ((8, 3 * own), FLOAT, whole((8, 3 * own), False)),
            ((half, width), FLOAT, whole((half, width))),
            ((half, width), LOWER, whole((half, width))),
        ]
    return call(
        functools.partial(backward_kernel, own_quarter),
        "backward_quarter",
        20,
        (low, slots, proj, lse, weights, *extra),
        [
            rows_spec(width),
            chunk_spec(8),
            rows_spec(3 * own),
            chunk_spec(8),
            out_spec(own, width),
            *[rows_spec(e.shape[1]) for e in extra],
        ],
        outs,
        scratch=[pltpu.VMEM((4 * own, width), FLOAT)] if own_quarter else [],
        flops=2 * PACKED * width * 14 * own,
        place=core,
    )


def first_norm_kernel(x_ref, ghid_ref, logit_ref, gains_ref, router_ref, *refs):
    rows_ref, sums_ref = refs[-2:]
    parts = refs[:-2]
    count = len(parts) // 2

    @pl.when(pl.program_id(0) == 0)
    def _():
        sums_ref[...] = jnp.zeros_like(sums_ref)

    grad_out = None
    for gproj_ref, weights_ref in zip(parts[:count], parts[count:]):
        part = nn(gproj_ref[...], weights_ref[0 : gproj_ref.shape[1], :])
        grad_out = part if grad_out is None else grad_out + part
    x = x_ref[...].astype(FLOAT)
    scaled, inverse = norm_stats(x)
    weighted = grad_out * gains_ref[0:1, :]
    centre_term = jnp.mean(weighted, axis=-1, keepdims=True)
    scale_term = jnp.mean(weighted * scaled, axis=-1, keepdims=True)
    grad_norm = inverse * (weighted - centre_term - scaled * scale_term)
    logit = logit_ref[:, 0:1]
    rows_ref[...] = (ghid_ref[...] + grad_norm + logit * router_ref[...]).astype(LOWER)
    sums_ref[0:1, :] += jnp.sum(grad_out * scaled, axis=0, keepdims=True)
    sums_ref[1:2, :] += jnp.sum(grad_out, axis=0, keepdims=True)
    sums_ref[2:3, :] += jnp.sum(logit * x, axis=0, keepdims=True)


def first_norm(x, ghid, logit, gains, router, gprojs, weights):
    width = x.shape[1]
    return call(
        first_norm_kernel,
        "first_norm",
        22,
        (x, ghid, logit, gains, router, *gprojs, *weights),
        [
            rows_spec(width),
            rows_spec(width),
            rows_spec(128),
            whole((2, width)),
            whole((1, width)),
            *[rows_spec(g.shape[1]) for g in gprojs],
            *[whole(w.shape) for w in weights],
        ],
        [
            ((PACKED, width), LOWER, rows_spec(width)),
            ((8, width), FLOAT, whole((8, width), False)),
        ],
        flops=2 * PACKED * width * 3 * width,
    )


def scatter_kernel(place_ref, slots_ref, rows_ref, *refs):
    out_ref, stacked = refs[-2:]
    block = out_ref.shape[0]
    stack_places(place_ref[0], [r[...] for r in refs[:-2]], stacked)
    total = jnp.transpose(stacked[...])
    places = lax.broadcasted_iota(jnp.int32, (block, CHUNK), 0) + pl.program_id(0) * block
    for c in range(CHUNKS):
        onehot = (places == slots_ref[c, 0:1, :].astype(jnp.int32)).astype(FLOAT).astype(LOWER)
        total = total + nn(onehot, rows_ref[c * CHUNK : (c + 1) * CHUNK, :])
    out_ref[...] = total.astype(LOWER)


def scatter_rows(place, cot_parts, slots, rows):
    own, total = cot_parts[0].shape
    width = own * len(cot_parts)
    block = 512
    return call(
        scatter_kernel,
        "scatter_rows",
        16,
        (slots, rows, *cot_parts),
        [
            whole(slots.shape),
            whole((PACKED, width)),
            *[pl.BlockSpec((own, block), lambda c, *_: (0, c)) for _ in cot_parts],
        ],
        [((total, width), LOWER, rows_spec(width, block))],
        scratch=[pltpu.VMEM((width, block), FLOAT)],
        flops=2 * PACKED * total * width,
        place=place,
        grid=(pl.cdiv(total, block),),
    )[0]


def block_out_kernel(patch_ref, slots_ref, branch_ref, out_ref, total_ref):
    chunk = pl.program_id(0)
    added = tn(branch_ref[...], slot_onehot(slots_ref, out_ref.shape[1]))

    @pl.when(chunk == 0)
    def _():
        total_ref[...] = patch_ref[...].astype(FLOAT) + added

    @pl.when(chunk > 0)
    def _():
        total_ref[...] += added

    @pl.when(chunk == CHUNKS - 1)
    def _():
        out_ref[...] = total_ref[...].astype(LOWER)


def block_out_rows(patch_t, slots, branch):
    own, total = patch_t.shape
    return call(
        block_out_kernel,
        "block_out_rows",
        16,
        (patch_t, slots, branch),
        [whole((own, total)), chunk_spec(8), rows_spec(own)],
        [((own, total), LOWER, whole((own, total), False))],
        scratch=[pltpu.VMEM((own, total), FLOAT)],
        flops=2 * PACKED * total * own,
    )[0]


def turned(values, place):
    size = values.shape[0]
    back = jnp.concatenate([values[:1], values[:0:-1]], axis=0)
    twice = jnp.concatenate([back, back], axis=0)
    return lax.dynamic_slice_in_dim(twice, (size - place) % size, size, 0)


def after(value, *others):
    return lax.optimization_barrier((value, *others))[0]


def ring_step(value, size):
    return lax.ppermute(value, "mlp", [(i, (i + 1) % size) for i in range(size)])


def swap(value, bit, size):
    return lax.ppermute(value, "rows", [(i, i ^ (1 << bit)) for i in range(size)])


def bits_of(size):
    return [b for b in range(20) if (1 << b) < size]


def pack_slots(picked, live_slots):
    small = IMG_DEV * HALF_S
    named = jnp.where(live_slots == 1, picked, -1)

    def padded(parts, fill):
        have = sum(p.shape[0] for p in parts)
        return jnp.concatenate([*parts, jnp.full((CHUNK - have,), fill, jnp.int32)])

    always = IMG_DEV - L_MOST
    idx = [padded([named[: always * HALF_S]], -1)]
    seg = [padded([jnp.repeat(jnp.arange(always, dtype=jnp.int32), HALF_S)], always)]
    for j in range(L_MOST):
        first = small + j * HALF_L
        alive = live_slots[first] == 1
        other = IMG_DEV - 1 - j
        large_idx = padded([named[first : first + HALF_L]], -1)
        small_idx = padded([named[other * HALF_S : (other + 1) * HALF_S]], -1)
        idx.append(jnp.where(alive, large_idx, small_idx))
        length = jnp.where(alive, HALF_L, HALF_S)
        seg.append((jnp.arange(CHUNK, dtype=jnp.int32) >= length).astype(jnp.int32))
    idx, seg = jnp.stack(idx).astype(FLOAT), jnp.stack(seg).astype(FLOAT)
    rows = lax.broadcasted_iota(jnp.int32, (1, 8, 1), 1)
    return jnp.where(rows == 0, idx[:, None, :], seg[:, None, :])


def local(
    rows_size,
    mlp_size,
    patches,
    w_qkv,
    qkv_bias,
    w_out,
    post_bias,
    w_up,
    up_bias,
    w_down,
    norm_gains,
    norm_shifts,
    router,
    picked,
    live_slots,
    cotangent,
):
    width = patches.shape[1]
    mlp_index = lax.axis_index("mlp")
    rows_index = lax.axis_index("rows")
    share_index = rows_index % SHARE
    core = rows_index & 1
    place = mlp_index.astype(jnp.int32).reshape(1)
    places = jnp.stack([mlp_index, share_index]).astype(jnp.int32)
    kind = (rows_index % 4).astype(jnp.int32).reshape(1)
    own = w_out.shape[0]
    heads_here = own // HD
    others = mlp_size - 1
    router_row = router.reshape(1, width)

    def swapped(value, bit):
        return swap(value, bit, rows_size)

    own_weights = jnp.concatenate(
        [
            w_qkv.T.reshape(heads_here, 3, HD, width).transpose(1, 0, 2, 3).reshape(3 * own, width),
            w_out,
        ],
        axis=0,
    )
    piece = lax.dynamic_slice_in_dim(own_weights, kind[0] * own, own, 0)
    part = w_up.shape[0] // SHARE
    top = lax.reduce_precision(up_bias, 8, 7)
    middle = lax.reduce_precision(up_bias - top, 8, 7)
    bias_rows = jnp.stack([top, middle, up_bias - top - middle]).astype(LOWER)
    payload = jnp.concatenate(
        [
            piece,
            lax.dynamic_slice_in_dim(w_up, share_index * part, part, 0),
            jnp.pad(bias_rows, ((0, 13), (0, 0))),
            lax.dynamic_slice_in_dim(w_down, share_index * part, part, 0),
        ],
        axis=0,
    )
    def around(value):
        return ring_step(value, mlp_size)

    kinds = jnp.stack([qkv_bias[0], jnp.zeros_like(qkv_bias[0]), qkv_bias[1]])
    biases = turned(kinds.reshape(3, mlp_size, own).transpose(1, 0, 2), mlp_index)
    biases = biases.reshape(mlp_size, 1, 3 * own)
    own_post = lax.dynamic_slice_in_dim(post_bias, mlp_index * own, own, 1)
    slots = pack_slots(picked, live_slots)
    cot_own = cotangent.T
    core_one = core.astype(jnp.int32).reshape(1)

    def split(came):
        return came[:own], came[own : own + part + 16], came[own + part + 16 :]

    def forward(j, normed, parts):
        return forward_quarter(kind, normed, biases, slots, parts, j)

    order = bits_of(rows_size)
    lower = {bit: (rows_index >> bit) & 1 == 0 for bit in order}
    payload, place, places, kind, core_one, lower, own_post, biases = lax.optimization_barrier(
        (payload, place, places, kind, core_one, lower, own_post, biases)
    )
    came = around(payload)
    x, normed_one, gate, cot_part, patch_t = pick_rows(
        place, after(patches, payload), cot_own, slots, norm_gains, norm_shifts, router_row
    )
    quarters, cot_parts, up_parts, down_parts = [], [cot_part], [], []
    parts, before = [own_weights], x
    for j in range(mlp_size):
        if j < others:
            came = after(came, before)
            got, up_part, down_part = split(came)
            up_parts.append(up_part)
            down_parts.append(down_part)
            if j + 1 < others:
                came = around(came)
            across_next, beyond_next = swapped(got, 1), swapped(got, 0)
        if 0 < j < others:
            cot_parts.append(around(after(cot_parts[-1], got)))
        normed_one = after(normed_one, got, before, *parts)
        if j == others:
            normed_one = after(normed_one, *cot_parts[:-1])
            ups, downs = jnp.stack(up_parts), jnp.stack(down_parts)
            ups_x, downs_y = swapped(ups, 1), swapped(downs, 2)
        quarters.append(forward(j, normed_one, parts))
        before = quarters[-1][1]
        if j < others:
            across_next = after(across_next, before)
            parts = [got, beyond_next, across_next, swapped(across_next, 0)]

    projs, mixes, lses, weights = zip(*quarters)
    ups_x, downs_y, cot_last = after(ups_x, before), after(downs_y, before), after(cot_parts[-1], before)
    cot_parts.append(around(cot_last))
    ups, downs = jnp.stack([ups, ups_x]), jnp.stack([downs, downs_y])
    ups_y, downs_x = swapped(ups, 2), swapped(downs, 1)
    hidden, normed_two, attn_own = join_quarters(
        place, after(x, cot_last), post_bias, own_post, norm_gains, norm_shifts, mixes, weights
    )
    cot_rows, gated = cot_chunks(place, after(gate, normed_two), cot_parts)
    full_parts = [cot_own, around(after(cot_own, gated))]
    act, grad_pre, *sums, up_bias_sum = own_mlp(
        place, normed_two, gated, w_up, w_down, up_bias.reshape(1, -1), own
    )
    ups_y, downs_x = after(ups_y, sums[0]), after(downs_x, sums[0])
    more = [swapped(v, 0) for v in (ups, ups_y, downs, downs_x)]
    kept, sent = own_grads(core_one, normed_two, after(grad_pre, ups_y, downs_x), act, gated)
    more = [after(v, kept) for v in more]
    ups, downs = [ups, ups_y, *more[:2]], [downs, downs_x, *more[2:]]
    sent = after(sent, *more)

    turned_order = [order[0], *order[:0:-1]]

    def halves(value, bit):
        pair = value.reshape(2, value.shape[0] // 2, width)
        return (
            jnp.where(lower[bit], pair[0], pair[1]),
            jnp.where(lower[bit], pair[1], pair[0]).astype(LOWER),
        )

    def joined(value, other, bit):
        first, second = jnp.where(lower[bit], value, other), jnp.where(lower[bit], other, value)
        return jnp.concatenate([first, second], axis=0)

    def halve_middle(value, bits):
        for bit in bits[2:-1]:
            kept, sent = halves(value, bit)
            value = kept + swapped(sent, bit).astype(FLOAT)
        return value

    def join_middle(value, bits):
        for bit in bits[-2:1:-1]:
            value = joined(value, swapped(value, bit), bit)
        return value

    came_c = swapped(sent, 0)
    sums[0] = after(sums[0], kept, *more)
    for j in range(others):
        last_quarter = (attn_own, own_post, gate) if j == others - 1 else ()
        sums = other_mlp(places, normed_two, gated, sums, ups, downs, j, last_quarter)
        if j == 0:
            kept, sent = halves(kept + after(came_c, sums[0]).astype(FLOAT), order[1])
            came_x = swapped(sent, order[1])
            sums[0] = after(sums[0], sent)
        if j == 1:
            full_parts.append(around(after(full_parts[-1], sums[0])))
            sums[0] = after(sums[0], full_parts[-2])
    grad_two, gate_part, branch = sums
    came_x = after(came_x, grad_two)
    grad_two = after(grad_two, came_x)
    d_mlp = halve_middle(kept + came_x.astype(FLOAT), order)
    kept, sent = halves(d_mlp, order[-1])
    came_y = swapped(sent, order[-1])
    grad_hidden, grad_low, logit, sums_two = second_norm(
        after(grad_two, kept), gate_part, hidden, x, cot_rows, gate, post_bias, norm_gains
    )
    own_proj, bias_grad, kept_a, sent_a = backward_quarter(
        core_one,
        grad_low,
        slots,
        projs[0],
        lses[0],
        weights[0],
        (normed_one, mixes[0]),
    )
    gprojs = [own_proj]
    came_a = swapped(sent_a, 0)
    d_mlp = (kept + after(came_y, own_proj).astype(FLOAT)).astype(LOWER)
    other = swapped(d_mlp, order[-1])
    full_parts.append(around(after(full_parts[-1], own_proj)))
    low = after(grad_low, own_proj, d_mlp, full_parts[-2])
    gprojs.append(backward_quarter(core_one, low, slots, projs[1], lses[1], weights[1])[0])
    kept_a, sent_a = halves(kept_a + after(came_a, gprojs[-1]).astype(FLOAT), turned_order[1])
    came_a = swapped(sent_a, turned_order[1])
    d_mlp = join_middle(joined(d_mlp, after(other, gprojs[-1]), order[-1]), order)
    other = swapped(d_mlp, order[1])
    low = after(low, gprojs[-1], d_mlp, kept_a)
    gprojs.append(backward_quarter(core_one, low, slots, projs[2], lses[2], weights[2])[0])
    d_attn = halve_middle(kept_a + after(came_a, gprojs[-1]).astype(FLOAT), turned_order)
    kept_a, sent_a = halves(d_attn, turned_order[-1])
    came_a = swapped(sent_a, turned_order[-1])
    low = after(low, gprojs[-1], kept_a)
    for j in range(3, mlp_size):
        gprojs.append(backward_quarter(core_one, low, slots, projs[j], lses[j], weights[j])[0])
    d_attn = (kept_a + after(came_a, gprojs[-1]).astype(FLOAT)).astype(LOWER)
    other_a = swapped(d_attn, turned_order[-1])
    d_mlp = joined(d_mlp, after(other, gprojs[-1]), order[1])
    other = swapped(d_mlp, 0)
    rows_grad, sums_one = first_norm(
        x, grad_hidden, after(logit, gprojs[-1], d_attn, d_mlp), norm_gains, router_row, gprojs, weights
    )
    d_attn = join_middle(joined(d_attn, after(other_a, rows_grad), turned_order[-1]), turned_order)
    other_a = swapped(d_attn, turned_order[1])
    small = jnp.concatenate(
        [
            sums_two[:4],
            sums_one[:3],
            up_bias_sum[:1],
            jnp.pad(bias_grad[:1], ((0, 0), (0, width - 3 * own))),
        ],
        axis=0,
    )
    small = small + swapped(small, 0)
    other_s = swapped(small, order[1])
    input_grad = scatter_rows(place, full_parts, slots, after(rows_grad, small, d_attn))
    d_attn = joined(d_attn, after(other_a, input_grad), turned_order[1])
    other_a = swapped(d_attn, 0)
    small = small + after(other_s, input_grad)
    for bit in order[2:-1]:
        small = small + swapped(small, bit)
    other_s = swapped(small, order[-1])
    branch, other = after(branch, small, d_attn, input_grad), after(other, rows_grad)
    block_out = block_out_rows(patch_t, slots, branch).T
    small = small + other_s
    d_attn = joined(d_attn, other_a, 0)
    d_up = jnp.where(lower[0], d_mlp, other).astype(FLOAT)
    d_down = jnp.where(lower[0], other, d_mlp).astype(FLOAT)

    d_qkv = (
        d_attn[: 3 * own]
        .astype(FLOAT)
        .reshape(3, heads_here, HD, width)
        .transpose(1, 0, 2, 3)
        .reshape(3 * own, width)
        .T
    )
    d_qkv_bias = jnp.stack([small[8, :own], small[8, 2 * own : 3 * own]])
    return (
        block_out,
        input_grad,
        d_qkv,
        d_qkv_bias,
        d_attn[3 * own :].astype(FLOAT),
        small[2:4],
        d_up,
        small[7],
        d_down,
        jnp.stack([small[4], small[0]]),
        jnp.stack([small[5], small[1]]),
        small[6],
    )


def solution(mesh):
    in_specs = (
        P("rows", None),
        P(None, "mlp"),
        P(),
        P("mlp", None),
        P(),
        P(None, "mlp"),
        P("mlp"),
        P("mlp", None),
        P(),
        P(),
        P(),
        P("rows"),
        P("rows"),
        P("rows", "mlp"),
    )
    out_specs = (
        P("rows", "mlp"),
        P("rows", None),
        P(None, "mlp"),
        P(None, "mlp"),
        P("mlp", None),
        P(),
        P(None, "mlp"),
        P("mlp"),
        P("mlp", None),
        P(),
        P(),
        P(),
    )
    body = functools.partial(local, mesh.shape["rows"], mesh.shape["mlp"])
    return jax.shard_map(body, mesh=mesh, in_specs=in_specs, out_specs=out_specs, check_vma=False)
```

```python
import functools

import jax
import jax.numpy as jnp
from jax import lax
from jax.experimental import pallas as pl
from jax.experimental.pallas import tpu as pltpu
from jax.sharding import PartitionSpec as P

HD = 64
IMG_DEV = 6
L_MOST = 3
HALF_S = 99
HALF_L = 289

CHUNK = 304
CHUNKS = 1 + L_MOST
PACKED = CHUNK * CHUNKS
SHARE = 8
PIECES = 4

EPSILON = 1e-06
LOWER = jnp.bfloat16
FLOAT = jnp.float32
MASKED = -1e30


def nn(a, b):
    return lax.dot_general(a, b, (((1,), (0,)), ((), ())), preferred_element_type=FLOAT)


def nt(a, b):
    return lax.dot_general(a, b, (((1,), (1,)), ((), ())), preferred_element_type=FLOAT)


def tn(a, b):
    return lax.dot_general(a, b, (((0,), (0,)), ((), ())), preferred_element_type=FLOAT)


LATER = pltpu.MemorySpace.HBM


def params(mib):
    return pltpu.CompilerParams(vmem_limit_bytes=mib * 1024 * 1024)


def cost(flops, bytes_accessed, transcendentals=0):
    return pl.CostEstimate(
        flops=flops, bytes_accessed=bytes_accessed, transcendentals=transcendentals
    )


def whole(shape, single=True):
    zeros = (0,) * len(shape)
    if single:
        return pl.BlockSpec(shape, lambda *_: zeros, pipeline_mode=pl.Buffered(1))
    return pl.BlockSpec(shape, lambda *_: zeros)


def rows_spec(width, height=CHUNK):
    return pl.BlockSpec((height, width), lambda c, *_: (c, 0))


def chunk_spec(height, width=CHUNK):
    return pl.BlockSpec((1, height, width), lambda c, *_: (c, 0, 0))


def call(kernel, name, mib, operands, in_specs, outs, scratch=(), flops=0, place=None, grid=None, aliases=None):
    specs = [o[2] for o in outs]
    shapes = [o[3](o[0], o[1]) if len(o) > 3 else jax.ShapeDtypeStruct(o[0], o[1]) for o in outs]
    scalars = () if place is None else (place,)
    made = pl.pallas_call(
        kernel,
        grid_spec=pltpu.PrefetchScalarGridSpec(
            num_scalar_prefetch=len(scalars),
            grid=grid or (CHUNKS,),
            in_specs=in_specs,
            out_specs=specs,
            scratch_shapes=scratch,
        ),
        out_shape=shapes,
        input_output_aliases=aliases or {},
        compiler_params=params(mib),
        cost_estimate=cost(flops // 1000000, 1000),
        name=name,
    )(*scalars, *operands)
    return list(made)


def slot_onehot(slots_ref, rows):
    named = jnp.transpose(slots_ref[0])[:, 0:1].astype(jnp.int32)
    places = lax.broadcasted_iota(jnp.int32, (CHUNK, rows), 1)
    return (places == named).astype(FLOAT).astype(LOWER)


def outside_image(slots_ref):
    image = jnp.transpose(slots_ref[0])[:, 1:2]
    return jnp.where(image == slots_ref[0, 1:2, :], 0.0, MASKED)


def choose_own(place, values, own):
    width = values.shape[1]
    source = lax.broadcasted_iota(jnp.int32, (width, own), 0)
    target = lax.broadcasted_iota(jnp.int32, (width, own), 1)
    onehot = (source == target + place * own).astype(FLOAT).astype(LOWER)
    return nn(values, onehot).astype(LOWER)


def norm_stats(values):
    average = jnp.mean(values, axis=-1, keepdims=True)
    centred = values - average
    variance = jnp.mean(centred * centred, axis=-1, keepdims=True)
    inverse = lax.rsqrt(variance + EPSILON)
    return centred * inverse, inverse


def pick_kernel(
    place_ref,
    patches_ref,
    cot_ref,
    slots_ref,
    gains_ref,
    shifts_ref,
    router_ref,
    x_ref,
    n_ref,
    gate_ref,
    part_ref,
    patch_ref,
):
    onehot = slot_onehot(slots_ref, patches_ref.shape[0])
    part_ref[0] = nt(cot_ref[...], onehot).astype(LOWER)
    x = nn(onehot, patches_ref[...])
    x_ref[...] = x.astype(LOWER)
    scaled, _ = norm_stats(x)
    n_ref[...] = (scaled * gains_ref[0:1, :] + shifts_ref[0:1, :]).astype(LOWER)
    logit = jnp.sum(x * router_ref[...], axis=-1, keepdims=True)
    gate_ref[...] = jnp.broadcast_to(jax.nn.sigmoid(logit), gate_ref.shape)

    @pl.when(pl.program_id(0) == 0)
    def _():
        own, width = patch_ref.shape[0], patches_ref.shape[1]
        source = lax.broadcasted_iota(jnp.int32, (own, width), 1)
        target = lax.broadcasted_iota(jnp.int32, (own, width), 0)
        chosen = (source == target + place_ref[0] * own).astype(FLOAT).astype(LOWER)
        patch_ref[...] = nt(chosen, patches_ref[...]).astype(LOWER)


def pick_rows(place, patches, cot_own, slots, gains, shifts, router):
    rows, width = patches.shape
    own = cot_own.shape[0]
    return call(
        pick_kernel,
        "pick_rows",
        22,
        (patches, cot_own, slots, gains, shifts, router),
        [
            whole((rows, width)),
            whole((own, rows)),
            chunk_spec(8),
            whole((2, width)),
            whole((2, width)),
            whole((1, width)),
        ],
        [
            ((PACKED, width), LOWER, rows_spec(width)),
            ((PACKED, width), LOWER, rows_spec(width)),
            ((PACKED, 128), FLOAT, rows_spec(128)),
            ((CHUNKS, own, CHUNK), LOWER, chunk_spec(own)),
            ((own, rows), LOWER, whole((own, rows)), LATER),
        ],
        flops=2 * PACKED * rows * (width + own),
        place=place,
    )


def head_slabs(own):
    slabs = []
    for start in range(0, own, 2 * HD):
        stop = min(start + 2 * HD, own)
        lanes = lax.broadcasted_iota(jnp.int32, (1, stop - start), 1)
        heads = []
        for head in range(start // HD, stop // HD):
            low = head * HD - start
            heads.append((head, (lanes >= low) & (lanes < low + HD)))
        slabs.append((start, stop, heads))
    return slabs


def keep(mask, values):
    return jnp.where(mask, values, jnp.zeros_like(values))


def forward_kernel(kind_ref, n_ref, bias_ref, slots_ref, *refs):
    proj_ref, mix_ref, lse_ref, weights_ref = refs[-4:]
    parts = refs[:-4]
    own = mix_ref.shape[1]

    @pl.when(pl.program_id(0) == 0)
    def _():
        if len(parts) == 1:
            weights_ref[...] = parts[0][...]
        else:
            for other, part_ref in enumerate(parts):
                held = part_ref.shape[0]
                start = pl.multiple_of((kind_ref[0] ^ other) * held, 32)
                weights_ref[pl.ds(start, held), :] = part_ref[...]

    proj_ref[...] = (nt(n_ref[...], weights_ref[0 : 3 * own, :]) + bias_ref[0]).astype(LOWER)
    outside = outside_image(slots_ref)
    lse_all = jnp.zeros((CHUNK, 128), FLOAT)
    lanes = lax.broadcasted_iota(jnp.int32, (1, 128), 1)
    for start, stop, heads in head_slabs(own):
        q = proj_ref[:, start:stop] * LOWER(HD**-0.5)
        k = proj_ref[:, own + start : own + stop]
        v = proj_ref[:, 2 * own + start : 2 * own + stop]
        mixed = None
        for head, mask in heads:
            scores = nt(q, keep(mask, k)) + outside
            largest = jnp.max(scores, axis=-1, keepdims=True)
            powered = jnp.exp(scores - largest)
            total = jnp.sum(powered, axis=-1, keepdims=True)
            probs = (powered * (1.0 / total)).astype(LOWER)
            part = nn(probs, keep(mask, v))
            mixed = part if mixed is None else mixed + part
            lse_all = jnp.where(lanes == head, largest + jnp.log(total), lse_all)
        mix_ref[:, start:stop] = mixed.astype(LOWER)
    lse_ref[0] = jnp.transpose(lse_all)[0:8, :]


def forward_quarter(kind, normed, biases, slots, parts, j):
    width = normed.shape[1]
    own = biases.shape[2] // 3
    return call(
        forward_kernel,
        "forward_quarter",
        11,
        (normed, biases, slots, *parts),
        [
            rows_spec(width),
            pl.BlockSpec((1, 1, 3 * own), lambda c, *_: (j, 0, 0)),
            chunk_spec(8),
            *[whole(p.shape) for p in parts],
        ],
        [
            ((PACKED, 3 * own), LOWER, rows_spec(3 * own), LATER),
            ((PACKED, own), LOWER, rows_spec(own)),
            ((CHUNKS, 8, CHUNK), FLOAT, chunk_spec(8), LATER),
            ((4 * own, width), LOWER, whole((4 * own, width))),
        ],
        flops=2 * PACKED * width * 8 * own,
        place=kind,
    )


def join_kernel(place_ref, x_ref, post_ref, own_post_ref, gains_ref, shifts_ref, *refs):
    hidden_ref, normed_ref, own_ref, chosen = refs[-4:]
    parts = refs[:-4]
    count = len(parts) // 2
    own = own_ref.shape[1]

    @pl.when(pl.program_id(0) == 0)
    def _():
        for j, out_ref in enumerate(parts[count:]):
            chosen[j * own : (j + 1) * own, :] = choose_own(place_ref[0], out_ref[...], own)

    attn, attn_own = post_ref[0:1, :], own_post_ref[0:1, :]
    for j, (mix_ref, out_ref) in enumerate(zip(parts[:count], parts[count:])):
        attn = attn + nn(mix_ref[...], out_ref[...])
        attn_own = attn_own + nn(mix_ref[...], chosen[j * own : (j + 1) * own, :])
    own_ref[...] = attn_own
    hidden = x_ref[...].astype(FLOAT) + attn
    hidden_ref[...] = hidden
    scaled, _ = norm_stats(hidden)
    normed_ref[...] = (scaled * gains_ref[1:2, :] + shifts_ref[1:2, :]).astype(LOWER)


def out_spec(own, width):
    return pl.BlockSpec((own, width), lambda *_: (3, 0), pipeline_mode=pl.Buffered(1))


def join_quarters(place, x, post, own_post, gains, shifts, mixes, weights):
    width = x.shape[1]
    own = mixes[0].shape[1]
    return call(
        join_kernel,
        "join_quarters",
        11,
        (x, post, own_post, gains, shifts, *mixes, *weights),
        [
            rows_spec(width),
            whole((2, width)),
            whole((2, own)),
            whole((2, width)),
            whole((2, width)),
            *[rows_spec(own) for _ in mixes],
            *[out_spec(own, width) for _ in weights],
        ],
        [
            ((PACKED, width), FLOAT, rows_spec(width), LATER),
            ((PACKED, width), LOWER, rows_spec(width)),
            ((PACKED, own), FLOAT, rows_spec(own), LATER),
        ],
        scratch=[pltpu.VMEM((len(weights) * own, own), LOWER)],
        flops=3 * PACKED * width * width,
        place=place,
    )


def stack_places(place, parts, stacked):
    size = len(parts)
    for j, part in enumerate(parts):
        own = part.shape[0]
        start = pl.multiple_of(lax.rem(place - j + size, size) * own, 64)
        stacked[pl.ds(start, own), :] = part.astype(stacked.dtype)


def cot_kernel(place_ref, gate_ref, *refs):
    cot_ref, gated_ref, stacked = refs[-3:]
    stack_places(place_ref[0], [r[0] for r in refs[:-3]], stacked)
    cot = jnp.transpose(stacked[...])
    cot_ref[...] = cot.astype(LOWER)
    gated_ref[...] = (gate_ref[:, 0:1] * cot).astype(LOWER)


def cot_chunks(place, gate, parts):
    own = parts[0].shape[1]
    width = own * len(parts)
    return call(
        cot_kernel,
        "cot_chunks",
        10,
        (gate, *parts),
        [rows_spec(128), *[chunk_spec(own) for _ in parts]],
        [
            ((PACKED, width), LOWER, rows_spec(width), LATER),
            ((PACKED, width), LOWER, rows_spec(width)),
        ],
        scratch=[pltpu.VMEM((width, CHUNK), FLOAT)],
        flops=PACKED * width,
        place=place,
    )


def gelu_pair(u):
    cdf = 0.5 * (1.0 + lax.erf(u * (0.5**0.5)))
    density = jnp.exp(-0.5 * u * u) * 0.3989422804014327
    return u * cdf, cdf + u * density


def mlp_step(normed, gated, up, down, bias, own_down):
    activation, slope = gelu_pair(nn(normed, up) + bias)
    activation = activation.astype(LOWER)
    grad_act = nt(gated, down)
    grad_pre = (grad_act * slope).astype(LOWER)
    gate_part = jnp.sum(activation.astype(FLOAT) * grad_act, axis=-1, keepdims=True)
    return activation, grad_pre, nt(grad_pre, up), gate_part, nn(activation, own_down)


def own_mlp_kernel(
    place_ref,
    n_ref,
    gated_ref,
    up_ref,
    down_ref,
    bias_ref,
    act_ref,
    pre_ref,
    grad_ref,
    gate_ref,
    out_ref,
    bias_sum_ref,
    own_down,
):
    @pl.when(pl.program_id(0) == 0)
    def _():
        own_down[...] = choose_own(place_ref[0], down_ref[...], own_down.shape[1])
        bias_sum_ref[...] = jnp.zeros_like(bias_sum_ref)

    activation, grad_pre, grad_part, gate_part, out_part = mlp_step(
        n_ref[...], gated_ref[...], up_ref[...], down_ref[...], bias_ref[...], own_down[...]
    )
    act_ref[...] = activation
    pre_ref[...] = grad_pre
    grad_ref[...] = grad_part
    gate_ref[...] = jnp.broadcast_to(gate_part, gate_ref.shape)
    out_ref[...] = out_part
    bias_sum_ref[0:1, :] += jnp.sum(grad_pre.astype(FLOAT), axis=0, keepdims=True)


def own_mlp(place, normed, gated, up, down, bias, own):
    width, hidden = up.shape
    return call(
        own_mlp_kernel,
        "own_mlp",
        17,
        (normed, gated, up, down, bias),
        [
            rows_spec(width),
            rows_spec(width),
            whole((width, hidden)),
            whole((hidden, width)),
            whole((1, hidden)),
        ],
        [
            ((PACKED, hidden), LOWER, rows_spec(hidden)),
            ((PACKED, hidden), LOWER, rows_spec(hidden)),
            ((PACKED, width), FLOAT, rows_spec(width)),
            ((PACKED, 128), FLOAT, rows_spec(128)),
            ((PACKED, own), FLOAT, rows_spec(own)),
            ((8, hidden), FLOAT, whole((8, hidden), False)),
        ],
        scratch=[pltpu.VMEM((hidden, own), LOWER)],
        flops=2 * PACKED * hidden * (3 * width + own),
        place=place,
    )


def own_grads_kernel(core_ref, n_ref, pre_ref, act_ref, gated_ref, kept_ref, sent_ref):
    grad_up = tn(n_ref[...], pre_ref[...])
    grad_down = tn(act_ref[...], gated_ref[...])

    @pl.when(core_ref[0] == 0)
    def _():
        kept_ref[...] = grad_up
        sent_ref[...] = grad_down.astype(LOWER)

    @pl.when(core_ref[0] == 1)
    def _():
        kept_ref[...] = grad_down
        sent_ref[...] = grad_up.astype(LOWER)


def own_grads(core, normed, grad_pre, act, gated):
    width = normed.shape[1]
    block = width // 3
    columns = pl.BlockSpec((PACKED, block), lambda c, *_: (0, c))
    return call(
        own_grads_kernel,
        "own_grads",
        16,
        (normed, grad_pre, act, gated),
        [columns, whole((PACKED, width)), columns, whole((PACKED, width))],
        [
            ((width, width), FLOAT, rows_spec(width, block)),
            ((width, width), LOWER, rows_spec(width, block)),
        ],
        flops=4 * PACKED * width * width,
        place=core,
        grid=(3,),
    )


def other_mlp_kernel(
    last, place_ref, n_ref, gated_ref, grad_in_ref, gate_in_ref, out_in_ref, *refs
):
    grad_ref, gate_ref, out_ref, up, down, own_down = refs[-6:]
    ups, downs = refs[0:4], refs[4:8]
    part = downs[0].shape[2]
    width = up.shape[1]

    @pl.when(pl.program_id(0) == 0)
    def _():
        for side in range(2):
            for c in range(2):
                for near in range(2):
                    to_up = place_ref[1] ^ (4 * side + 2 * near + c)
                    to_down = place_ref[1] ^ (4 * near + 2 * side + c)
                    up_rows = pl.ds(pl.multiple_of(to_up * part, 32), part)
                    down_rows = pl.ds(pl.multiple_of(to_down * part, 32), part)
                    up[up_rows, :] = ups[side + 2 * c][near, 0, 0:part]
                    down[down_rows, :] = downs[side + 2 * c][near, 0]
        own_down[...] = choose_own(place_ref[0], down[...], own_down.shape[1])

    pieces = ups[0][0, 0, part : part + 16].astype(FLOAT)
    bias = pieces[0:1] + (pieces[1:2] + pieces[2:3])
    _, _, grad_part, gate_part, out_part = mlp_step(
        n_ref[...], gated_ref[...], up[...], down[...], bias, own_down[...]
    )
    grad_ref[...] = grad_in_ref[...] + grad_part
    gate_ref[...] = gate_in_ref[...] + gate_part
    if last:
        attn_ref, post_ref, open_ref = refs[8:11]
        total = out_in_ref[...] + out_part + attn_ref[...] + post_ref[1:2, :]
        out_ref[...] = open_ref[:, 0:1] * total
    else:
        out_ref[...] = out_in_ref[...] + out_part


def other_mlp(places, normed, gated, sums, ups, downs, j, extra=()):
    width = normed.shape[1]
    own = sums[2].shape[1]
    last = len(extra) > 0
    held = lambda array: pl.BlockSpec(
        (2, 1, *array.shape[2:]), lambda c, *_: (0, j, 0, 0), pipeline_mode=pl.Buffered(1)
    )
    extra_specs = [rows_spec(own), whole((2, own)), rows_spec(128)] if last else []
    return call(
        functools.partial(other_mlp_kernel, last),
        "other_mlp",
        19,
        (normed, gated, *sums, *ups, *downs, *extra),
        [
            rows_spec(width),
            rows_spec(width),
            rows_spec(width),
            rows_spec(128),
            rows_spec(own),
            *[held(u) for u in ups],
            *[held(d) for d in downs],
            *extra_specs,
        ],
        [
            ((PACKED, width), FLOAT, rows_spec(width)),
            ((PACKED, 128), FLOAT, rows_spec(128)),
            ((PACKED, own), FLOAT, rows_spec(own)),
        ],
        scratch=[
            pltpu.VMEM((width, width), LOWER),
            pltpu.VMEM((width, width), LOWER),
            pltpu.VMEM((width, own), LOWER),
        ],
        flops=2 * PACKED * width * (3 * width + own),
        place=places,
    )


def second_norm_kernel(
    grad_ref,
    gate_part_ref,
    hidden_ref,
    x_ref,
    cot_ref,
    gate_ref,
    post_ref,
    gains_ref,
    ghid_ref,
    glow_ref,
    logit_ref,
    sums_ref,
):
    @pl.when(pl.program_id(0) == 0)
    def _():
        sums_ref[...] = jnp.zeros_like(sums_ref)

    hidden = hidden_ref[...]
    scaled, inverse = norm_stats(hidden)
    grad_out = grad_ref[...]
    weighted = grad_out * gains_ref[1:2, :]
    centre_term = jnp.mean(weighted, axis=-1, keepdims=True)
    scale_term = jnp.mean(weighted * scaled, axis=-1, keepdims=True)
    grad_hidden = inverse * (weighted - centre_term - scaled * scale_term)
    gate = gate_ref[:, 0:1]
    gated = gate * cot_ref[...].astype(FLOAT)
    grad_attn = grad_hidden + gated
    ghid_ref[...] = grad_hidden
    glow_ref[...] = grad_attn.astype(LOWER)
    attn = hidden - x_ref[...].astype(FLOAT)
    dotted = jnp.sum(gated * (attn + post_ref[1:2, :]), axis=-1, keepdims=True)
    logit = (1.0 - gate) * (dotted + gate_part_ref[:, 0:1])
    logit_ref[...] = jnp.broadcast_to(logit, logit_ref.shape)
    sums_ref[0:1, :] += jnp.sum(grad_out * scaled, axis=0, keepdims=True)
    sums_ref[1:2, :] += jnp.sum(grad_out, axis=0, keepdims=True)
    sums_ref[2:3, :] += jnp.sum(grad_attn, axis=0, keepdims=True)
    sums_ref[3:4, :] += jnp.sum(gated, axis=0, keepdims=True)


def second_norm(grad, gate_part, hidden, x, cot_rows, gate, post, gains):
    width = x.shape[1]
    return call(
        second_norm_kernel,
        "second_norm",
        15,
        (grad, gate_part, hidden, x, cot_rows, gate, post, gains),
        [
            rows_spec(width),
            rows_spec(128),
            rows_spec(width),
            rows_spec(width),
            rows_spec(width),
            rows_spec(128),
            whole((2, width)),
            whole((2, width)),
        ],
        [
            ((PACKED, width), FLOAT, rows_spec(width)),
            ((PACKED, width), LOWER, rows_spec(width)),
            ((PACKED, 128), FLOAT, rows_spec(128)),
            ((8, width), FLOAT, whole((8, width), False)),
        ],
        flops=20 * PACKED * width,
    )


def backward_kernel(own_quarter, core_ref, low_ref, slots_ref, proj_ref, lse_ref, out_ref, *refs):
    if own_quarter:
        normed_ref, mix_ref, gproj_ref, sums_ref, kept_ref, sent_ref, grads = refs
    else:
        (gproj_ref,) = refs
    chunk = pl.program_id(0)
    low = low_ref[...]
    outside = outside_image(slots_ref)
    own = out_ref.shape[0]
    gmix = nt(low, out_ref[...]).astype(LOWER)
    for start, stop, heads in head_slabs(own):
        k_cols = slice(own + start, own + stop)
        v_cols = slice(2 * own + start, 2 * own + stop)
        q = proj_ref[:, start:stop] * LOWER(HD**-0.5)
        k = proj_ref[:, k_cols]
        v = proj_ref[:, v_cols]
        g = gmix[:, start:stop]
        grad_q, grad_k, grad_v = None, None, None
        for head, mask in heads:
            own_k = keep(mask, k)
            scores = nt(own_k, q) + outside
            probs = jnp.exp(scores - lse_ref[0, head : head + 1, :])
            grad_probs = nt(keep(mask, v), g)
            inner = jnp.sum(probs * grad_probs, axis=0, keepdims=True)
            grad_scores = (probs * (grad_probs - inner)).astype(LOWER)
            one_v = nn(probs.astype(LOWER), g)
            one_k = nn(grad_scores, q)
            one_q = tn(grad_scores, own_k)
            if grad_q is None:
                grad_q, grad_k, grad_v = one_q, one_k, one_v
            else:
                grad_q = grad_q + one_q
                grad_k = jnp.where(mask, one_k, grad_k)
                grad_v = jnp.where(mask, one_v, grad_v)
        gproj_ref[:, start:stop] = (grad_q * HD**-0.5).astype(LOWER)
        gproj_ref[:, k_cols] = grad_k.astype(LOWER)
        gproj_ref[:, v_cols] = grad_v.astype(LOWER)
    if own_quarter:
        half = sent_ref.shape[0]
        gproj = gproj_ref[...]
        column_sums = jnp.sum(gproj.astype(FLOAT), axis=0, keepdims=True)
        d_qkv = tn(gproj, normed_ref[...])
        d_out = tn(mix_ref[...], low)

        @pl.when(chunk == 0)
        def _():
            sums_ref[...] = jnp.zeros_like(sums_ref)
            grads[0 : 3 * own, :] = d_qkv
            grads[3 * own :, :] = d_out

        @pl.when(chunk > 0)
        def _():
            grads[0 : 3 * own, :] += d_qkv
            grads[3 * own :, :] += d_out

        sums_ref[0:1, :] += column_sums

        @pl.when(chunk == CHUNKS - 1)
        def _():
            kept = pl.ds(pl.multiple_of(core_ref[0] * half, 16), half)
            sent = pl.ds(pl.multiple_of((1 - core_ref[0]) * half, 16), half)
            kept_ref[...] = grads[kept, :]
            sent_ref[...] = grads[sent, :].astype(LOWER)


def backward_quarter(core, low, slots, proj, lse, weights, extra=()):
    width = low.shape[1]
    own = proj.shape[1] // 3
    own_quarter = len(extra) > 0
    outs = [((PACKED, 3 * own), LOWER, rows_spec(3 * own))]
    if own_quarter:
        half = 2 * own
        outs += [
            ((8, 3 * own), FLOAT, whole((8, 3 * own), False)),
            ((half, width), FLOAT, whole((half, width))),
            ((half, width), LOWER, whole((half, width))),
        ]
    return call(
        functools.partial(backward_kernel, own_quarter),
        "backward_quarter",
        16,
        (low, slots, proj, lse, weights, *extra),
        [
            rows_spec(width),
            chunk_spec(8),
            rows_spec(3 * own),
            chunk_spec(8),
            out_spec(own, width),
            *[rows_spec(e.shape[1]) for e in extra],
        ],
        outs,
        scratch=[pltpu.VMEM((4 * own, width), FLOAT)] if own_quarter else [],
        flops=2 * PACKED * width * 14 * own,
        place=core,
    )


def first_norm_kernel(x_ref, ghid_ref, logit_ref, gains_ref, router_ref, *refs):
    rows_ref, sums_ref = refs[-2:]
    parts = refs[:-2]
    count = len(parts) // 2

    @pl.when(pl.program_id(0) == 0)
    def _():
        sums_ref[...] = jnp.zeros_like(sums_ref)

    grad_out = None
    for gproj_ref, weights_ref in zip(parts[:count], parts[count:]):
        part = nn(gproj_ref[...], weights_ref[0 : gproj_ref.shape[1], :])
        grad_out = part if grad_out is None else grad_out + part
    x = x_ref[...].astype(FLOAT)
    scaled, inverse = norm_stats(x)
    weighted = grad_out * gains_ref[0:1, :]
    centre_term = jnp.mean(weighted, axis=-1, keepdims=True)
    scale_term = jnp.mean(weighted * scaled, axis=-1, keepdims=True)
    grad_norm = inverse * (weighted - centre_term - scaled * scale_term)
    logit = logit_ref[:, 0:1]
    rows_ref[...] = (ghid_ref[...] + grad_norm + logit * router_ref[...]).astype(LOWER)
    sums_ref[0:1, :] += jnp.sum(grad_out * scaled, axis=0, keepdims=True)
    sums_ref[1:2, :] += jnp.sum(grad_out, axis=0, keepdims=True)
    sums_ref[2:3, :] += jnp.sum(logit * x, axis=0, keepdims=True)


def first_norm(x, ghid, logit, gains, router, gprojs, weights):
    width = x.shape[1]
    return call(
        first_norm_kernel,
        "first_norm",
        18,
        (x, ghid, logit, gains, router, *gprojs, *weights),
        [
            rows_spec(width),
            rows_spec(width),
            rows_spec(128),
            whole((2, width)),
            whole((1, width)),
            *[rows_spec(g.shape[1]) for g in gprojs],
            *[whole(w.shape) for w in weights],
        ],
        [
            ((PACKED, width), LOWER, rows_spec(width)),
            ((8, width), FLOAT, whole((8, width), False)),
        ],
        flops=2 * PACKED * width * 3 * width,
    )


def scatter_kernel(place_ref, named_ref, rows_ref, branch_ref, patch_ref, *refs):
    out_ref, block_ref, stacked, branch_t = refs[-4:]
    block = out_ref.shape[0]

    @pl.when(pl.program_id(0) == 0)
    def _():
        branch_t[...] = jnp.transpose(branch_ref[...]).astype(LOWER)

    stack_places(place_ref[0], [r[...] for r in refs[:-4]], stacked)
    places = lax.broadcasted_iota(jnp.int32, (block, PACKED), 0) + pl.program_id(0) * block
    onehot = (places == named_ref[...]).astype(FLOAT).astype(LOWER)
    out_ref[...] = (jnp.transpose(stacked[...]) + nn(onehot, rows_ref[...])).astype(LOWER)
    block_ref[...] = (patch_ref[...].astype(FLOAT) + nt(branch_t[...], onehot)).astype(LOWER)


def scatter_rows(place, cot_parts, named, rows, branch, patch_t):
    own, total = cot_parts[0].shape
    width = own * len(cot_parts)
    block = 512
    columns = pl.BlockSpec((own, block), lambda c, *_: (0, c))
    return call(
        scatter_kernel,
        "scatter_rows",
        19,
        (named, rows, branch, patch_t, *cot_parts),
        [
            whole(named.shape),
            whole((PACKED, width)),
            whole((PACKED, own)),
            columns,
            *[columns for _ in cot_parts],
        ],
        [
            ((total, width), LOWER, rows_spec(width, block)),
            ((own, total), LOWER, columns),
        ],
        scratch=[pltpu.VMEM((width, block), FLOAT), pltpu.VMEM((own, PACKED), LOWER)],
        flops=2 * PACKED * total * width,
        place=place,
        grid=(pl.cdiv(total, block),),
    )


def halve_kernel(upper_ref, kept_ref, came_ref, half_ref, sent_ref):
    block, half = half_ref.shape[0], kept_ref.shape[0] // 2
    step = pl.program_id(0) * block
    own = pl.ds(pl.multiple_of(upper_ref[0] * half + step, 16), block)
    far = pl.ds(pl.multiple_of((1 - upper_ref[0]) * half + step, 16), block)
    half_ref[...] = kept_ref[own, :] + came_ref[own, :].astype(FLOAT)
    sent_ref[...] = (kept_ref[far, :] + came_ref[far, :].astype(FLOAT)).astype(LOWER)


def halve_sum(upper, kept, came):
    rows, width = kept.shape
    return call(
        halve_kernel,
        "halve_sum",
        10,
        (kept, came),
        [whole((rows, width)), whole((rows, width))],
        [
            ((rows // 2, width), FLOAT, rows_spec(width, rows // 4)),
            ((rows // 2, width), LOWER, rows_spec(width, rows // 4)),
        ],
        place=upper,
        grid=(2,),
    )


def finish_kernel(core_ref, attn_ref, attn_far_ref, mlp_ref, mlp_far_ref, *refs):
    qkv_ref, out_ref, up_ref, down_ref = refs
    own, block = qkv_ref.shape[0], up_ref.shape[0]
    head = pl.program_id(0)
    rows = pl.ds(pl.multiple_of(head * block, 16), block)

    def write(low_ref, high_ref, first_ref, second_ref):
        one = pl.ds(pl.multiple_of(head * HD, HD), HD)
        two = pl.ds(pl.multiple_of(own + head * HD, HD), HD)
        qkv_ref[0:HD, :] = low_ref[one, :].astype(FLOAT)
        qkv_ref[HD : 2 * HD, :] = low_ref[two, :].astype(FLOAT)
        qkv_ref[2 * HD : 3 * HD, :] = high_ref[one, :].astype(FLOAT)
        out_ref[...] = high_ref[two, :].astype(FLOAT)
        up_ref[...] = first_ref[rows, :].astype(FLOAT)
        down_ref[...] = second_ref[rows, :].astype(FLOAT)

    @pl.when(core_ref[0] == 0)
    def _():
        write(attn_ref, attn_far_ref, mlp_ref, mlp_far_ref)

    @pl.when(core_ref[0] == 1)
    def _():
        write(attn_far_ref, attn_ref, mlp_far_ref, mlp_ref)


def finish_grads(core, attn, attn_far, mlp, mlp_far):
    width = mlp.shape[1]
    own = attn.shape[0] // 2
    heads = own // HD
    return call(
        finish_kernel,
        "finish_grads",
        16,
        (attn, attn_far, mlp, mlp_far),
        [whole(attn.shape), whole(attn.shape), whole(mlp.shape), whole(mlp.shape)],
        [
            ((3 * own, width), FLOAT, rows_spec(width, 3 * HD)),
            ((own, width), FLOAT, rows_spec(width, HD)),
            ((width, width), FLOAT, rows_spec(width, width // heads)),
            ((width, width), FLOAT, rows_spec(width, width // heads)),
        ],
        place=core,
        grid=(heads,),
    )


def finish_sums_kernel(own_ref, far_ref, *refs):
    gains_ref, shifts_ref, post_ref, up_ref, router_ref, qkv_ref = refs
    total = own_ref[...] + far_ref[...]
    own = qkv_ref.shape[1]
    gains_ref[0:1, :] = total[4:5]
    gains_ref[1:2, :] = total[0:1]
    shifts_ref[0:1, :] = total[5:6]
    shifts_ref[1:2, :] = total[1:2]
    post_ref[...] = total[2:4]
    up_ref[...] = total[7:8]
    router_ref[...] = total[6:7]
    qkv_ref[0:1, :] = total[8:9, 0:own]
    qkv_ref[1:2, :] = total[8:9, 2 * own : 3 * own]


def finish_sums(small, far, own):
    rows, width = small.shape
    shapes = [(2, width), (2, width), (2, width), (1, width), (1, width), (2, own)]
    return call(
        finish_sums_kernel,
        "finish_sums",
        4,
        (small, far),
        [whole((rows, width)), whole((rows, width))],
        [(shape, FLOAT, whole(shape)) for shape in shapes],
        grid=(1,),
    )


def turned(values, place):
    size = values.shape[0]
    back = jnp.concatenate([values[:1], values[:0:-1]], axis=0)
    twice = jnp.concatenate([back, back], axis=0)
    return lax.dynamic_slice_in_dim(twice, (size - place) % size, size, 0)


def after(value, *others):
    return lax.optimization_barrier((value, *others))[0]


def ring_step(value, size):
    return lax.ppermute(value, "mlp", [(i, (i + 1) % size) for i in range(size)])


def swap(value, bit, size):
    return lax.ppermute(value, "rows", [(i, i ^ (1 << bit)) for i in range(size)])


def bits_of(size):
    return [b for b in range(20) if (1 << b) < size]


def pack_slots(picked, live_slots):
    small = IMG_DEV * HALF_S
    named = jnp.where(live_slots == 1, picked, -1)

    def padded(parts, fill):
        have = sum(p.shape[0] for p in parts)
        return jnp.concatenate([*parts, jnp.full((CHUNK - have,), fill, jnp.int32)])

    always = IMG_DEV - L_MOST
    idx = [padded([named[: always * HALF_S]], -1)]
    seg = [padded([jnp.repeat(jnp.arange(always, dtype=jnp.int32), HALF_S)], always)]
    for j in range(L_MOST):
        first = small + j * HALF_L
        alive = live_slots[first] == 1
        other = IMG_DEV - 1 - j
        large_idx = padded([named[first : first + HALF_L]], -1)
        small_idx = padded([named[other * HALF_S : (other + 1) * HALF_S]], -1)
        idx.append(jnp.where(alive, large_idx, small_idx))
        length = jnp.where(alive, HALF_L, HALF_S)
        seg.append((jnp.arange(CHUNK, dtype=jnp.int32) >= length).astype(jnp.int32))
    named = jnp.concatenate(idx).reshape(1, PACKED)
    idx, seg = jnp.stack(idx).astype(FLOAT), jnp.stack(seg).astype(FLOAT)
    rows = lax.broadcasted_iota(jnp.int32, (1, 8, 1), 1)
    return jnp.where(rows == 0, idx[:, None, :], seg[:, None, :]), named


def local(
    rows_size,
    mlp_size,
    patches,
    w_qkv,
    qkv_bias,
    w_out,
    post_bias,
    w_up,
    up_bias,
    w_down,
    norm_gains,
    norm_shifts,
    router,
    picked,
    live_slots,
    cotangent,
):
    width = patches.shape[1]
    mlp_index = lax.axis_index("mlp")
    rows_index = lax.axis_index("rows")
    share_index = rows_index % SHARE
    core = rows_index & 1
    place = mlp_index.astype(jnp.int32).reshape(1)
    places = jnp.stack([mlp_index, share_index]).astype(jnp.int32)
    kind = (rows_index % PIECES).astype(jnp.int32).reshape(1)
    own = w_out.shape[0]
    heads_here = own // HD
    others = mlp_size - 1
    router_row = router.reshape(1, width)

    def swapped(value, bit):
        return swap(value, bit, rows_size)

    own_weights = jnp.concatenate(
        [
            w_qkv.T.reshape(heads_here, 3, HD, width).transpose(1, 0, 2, 3).reshape(3 * own, width),
            w_out,
        ],
        axis=0,
    )
    held = own_weights.shape[0] // PIECES
    piece = lax.dynamic_slice_in_dim(own_weights, kind[0] * held, held, 0)
    part = w_up.shape[0] // SHARE
    top = lax.reduce_precision(up_bias, 8, 7)
    middle = lax.reduce_precision(up_bias - top, 8, 7)
    bias_rows = jnp.stack([top, middle, up_bias - top - middle]).astype(LOWER)
    payload = jnp.concatenate(
        [
            piece,
            lax.dynamic_slice_in_dim(w_up, share_index * part, part, 0),
            jnp.pad(bias_rows, ((0, 13), (0, 0))),
            lax.dynamic_slice_in_dim(w_down, share_index * part, part, 0),
        ],
        axis=0,
    )
    def around(value):
        return ring_step(value, mlp_size)

    kinds = jnp.stack([qkv_bias[0], jnp.zeros_like(qkv_bias[0]), qkv_bias[1]])
    biases = turned(kinds.reshape(3, mlp_size, own).transpose(1, 0, 2), mlp_index)
    biases = biases.reshape(mlp_size, 1, 3 * own)
    own_post = lax.dynamic_slice_in_dim(post_bias, mlp_index * own, own, 1)
    slots, named = pack_slots(picked, live_slots)
    cot_own = cotangent.T
    core_one = core.astype(jnp.int32).reshape(1)

    def split(came):
        return came[:held], came[held : held + part + 16], came[held + part + 16 :]

    def across(value, mask):
        return lax.ppermute(value, "rows", [(i, i ^ mask) for i in range(rows_size)])

    def forward(j, normed, parts):
        return forward_quarter(kind, normed, biases, slots, parts, j)

    order = bits_of(rows_size)
    lower = {bit: (rows_index >> bit) & 1 == 0 for bit in order}
    upper = {bit: ((rows_index >> bit) & 1).astype(jnp.int32).reshape(1) for bit in order}
    payload, place, places, kind, core_one, lower, upper, own_post, biases = lax.optimization_barrier(
        (payload, place, places, kind, core_one, lower, upper, own_post, biases)
    )
    came = around(payload)
    x, normed_one, gate, cot_part, patch_t = pick_rows(
        place, after(patches, payload), cot_own, slots, norm_gains, norm_shifts, router_row
    )
    quarters, cot_parts, up_parts, down_parts = [], [cot_part], [], []
    parts, before = [own_weights], x
    for j in range(mlp_size):
        if j < others:
            came = after(came, before)
            got, up_part, down_part = split(came)
            up_parts.append(up_part)
            down_parts.append(down_part)
            if j + 1 < others:
                came = around(came)
            spread = [got, *[across(got, mask) for mask in range(2, PIECES, 2)]]
        if 0 < j < others:
            cot_parts.append(around(after(cot_parts[-1], got)))
        normed_one = after(normed_one, got, before, *parts)
        if j == others:
            normed_one = after(normed_one, *cot_parts[:-1])
            ups, downs = jnp.stack(up_parts), jnp.stack(down_parts)
            ups_x, downs_y = swapped(ups, 1), swapped(downs, 2)
        quarters.append(forward(j, normed_one, parts))
        before = quarters[-1][1]
        if j < others:
            spread = [after(v, before) for v in spread]
            parts = [w for v in spread for w in (v, swapped(v, 0))]

    projs, mixes, lses, weights = zip(*quarters)
    cot_last = after(cot_parts[-1], before)
    ups_x, downs_y = after(ups_x, cot_last), after(downs_y, cot_last)
    cot_parts.append(around(cot_last))
    ups, downs = jnp.stack([ups, ups_x]), jnp.stack([downs, downs_y])
    ups_y, downs_x = swapped(ups, 2), swapped(downs, 1)
    hidden, normed_two, attn_own = join_quarters(
        place, after(x, cot_last), post_bias, own_post, norm_gains, norm_shifts, mixes, weights
    )
    cot_rows, gated = cot_chunks(place, after(gate, normed_two), cot_parts)
    full_parts = [cot_own, around(after(cot_own, gated))]

    def full_due(slot, value):
        if slot in ("N2", "B1"):
            full_parts.append(around(after(full_parts[-1], value)))
            return after(value, full_parts[-2])
        return value

    act, grad_pre, *sums, up_bias_sum = own_mlp(
        place, normed_two, gated, w_up, w_down, up_bias.reshape(1, -1), own
    )
    ups_y, downs_x = after(ups_y, sums[0]), after(downs_x, sums[0])
    more = [swapped(v, 0) for v in (ups, ups_y, downs, downs_x)]
    kept, sent = own_grads(core_one, normed_two, after(grad_pre, ups_y, downs_x), act, gated)
    more = [after(v, kept) for v in more]
    ups, downs = [ups, ups_y, *more[:2]], [downs, downs_x, *more[2:]]
    sent = after(sent, *more)

    turned_order = [order[0], *order[:0:-1]]

    def halves(kept, came, bit):
        if kept.shape[0] % 64 == 0:
            return halve_sum(upper[bit], kept, came)
        value = kept + came.astype(FLOAT)
        pair = value.reshape(2, value.shape[0] // 2, width)
        return (
            jnp.where(lower[bit], pair[0], pair[1]),
            jnp.where(lower[bit], pair[1], pair[0]).astype(LOWER),
        )

    def joined(value, other, bit):
        first, second = jnp.where(lower[bit], value, other), jnp.where(lower[bit], other, value)
        return jnp.concatenate([first, second], axis=0)

    def halve_middle(kept, came, bits):
        for bit in bits[2:-1]:
            kept, sent = halves(kept, came, bit)
            came = swapped(sent, bit)
        return halves(kept, came, bits[-1])

    def join_middle(value, bits):
        for bit in bits[-2:1:-1]:
            value = joined(value, swapped(value, bit), bit)
        return value

    came_c = swapped(sent, 0)
    sums[0] = after(sums[0], kept, *more)
    for j in range(others):
        sums[0] = full_due(f"M{j}", sums[0])
        last_quarter = (attn_own, own_post, gate) if j == others - 1 else ()
        sums = other_mlp(places, normed_two, gated, sums, ups, downs, j, last_quarter)
        if j == 0:
            kept, sent = halves(kept, after(came_c, sums[0]), order[1])
            came_x = swapped(sent, order[1])
            sums[0] = after(sums[0], sent)
    grad_two, gate_part, branch = sums
    came_x = after(came_x, grad_two)
    grad_two = full_due("N2", grad_two)
    grad_two = after(grad_two, came_x)
    kept, sent = halve_middle(kept, came_x, order)
    came_y = swapped(sent, order[-1])
    grad_hidden, grad_low, logit, sums_two = second_norm(
        after(grad_two, kept), gate_part, hidden, x, cot_rows, gate, post_bias, norm_gains
    )
    own_proj, bias_grad, kept_a, sent_a = backward_quarter(
        core_one,
        full_due("B0", grad_low),
        slots,
        projs[0],
        lses[0],
        weights[0],
        (normed_one, mixes[0]),
    )
    gprojs = [own_proj]
    came_a = swapped(sent_a, 0)
    d_mlp = (kept + after(came_y, own_proj).astype(FLOAT)).astype(LOWER)
    other = swapped(d_mlp, order[-1])
    low = full_due("B1", after(grad_low, own_proj, d_mlp))
    gprojs.append(backward_quarter(core_one, low, slots, projs[1], lses[1], weights[1])[0])
    kept_a, sent_a = halves(kept_a, after(came_a, gprojs[-1]), turned_order[1])
    came_a = swapped(sent_a, turned_order[1])
    d_mlp = join_middle(joined(d_mlp, after(other, gprojs[-1]), order[-1]), order)
    other = swapped(d_mlp, order[1])
    low = full_due("B2", after(low, gprojs[-1], d_mlp, kept_a))
    gprojs.append(backward_quarter(core_one, low, slots, projs[2], lses[2], weights[2])[0])
    kept_a, sent_a = halve_middle(kept_a, after(came_a, gprojs[-1]), turned_order)
    came_a = swapped(sent_a, turned_order[-1])
    low = full_due("B3", after(low, gprojs[-1], kept_a))
    for j in range(3, mlp_size):
        gprojs.append(backward_quarter(core_one, low, slots, projs[j], lses[j], weights[j])[0])
    d_attn = (kept_a + after(came_a, gprojs[-1]).astype(FLOAT)).astype(LOWER)
    near, far = turned_order[-1], turned_order[-2]
    others_a = [
        lax.ppermute(d_attn, "rows", [(i, i ^ mask) for i in range(rows_size)])
        for mask in (1 << near, 1 << far, (1 << near) | (1 << far))
    ]
    d_mlp = joined(d_mlp, after(other, gprojs[-1]), order[1])
    other = swapped(d_mlp, 0)
    rows_grad, sums_one = first_norm(
        x, grad_hidden, after(logit, gprojs[-1], d_attn, d_mlp), norm_gains, router_row, gprojs, weights
    )
    others_a = [after(v, rows_grad) for v in others_a]
    d_attn = joined(joined(d_attn, others_a[0], near), joined(others_a[1], others_a[2], near), far)
    for bit in turned_order[-3:0:-1]:
        d_attn = joined(d_attn, swapped(d_attn, bit), bit)
    other_a = swapped(d_attn, 0)
    small = jnp.concatenate(
        [
            sums_two[:4],
            sums_one[:3],
            up_bias_sum[:1],
            jnp.pad(bias_grad[:1], ((0, 0), (0, width - 3 * own))),
        ],
        axis=0,
    )
    small = small + swapped(small, 0)
    other_s = swapped(small, order[1])
    input_grad, block_out = scatter_rows(
        place, full_parts, named, after(rows_grad, small, d_attn), branch, patch_t
    )
    block_out = block_out.T
    small = small + after(other_s, input_grad)
    for bit in order[2:-1]:
        small = small + swapped(small, bit)
    other_s = swapped(small, order[-1])
    d_qkv, d_out, d_up, d_down = finish_grads(
        core_one, d_attn, after(other_a, input_grad, small), d_mlp, other
    )
    small, other_s = after(small, d_qkv), after(other_s, d_qkv)
    d_gains, d_shifts, d_post_bias, d_up_bias, d_router, d_qkv_bias = finish_sums(small, other_s, own)
    d_qkv = d_qkv.T
    return (
        block_out,
        input_grad,
        d_qkv,
        d_qkv_bias,
        d_out,
        d_post_bias,
        d_up,
        d_up_bias.reshape(width),
        d_down,
        d_gains,
        d_shifts,
        d_router.reshape(width),
    )


def solution(mesh):
    in_specs = (
        P("rows", None),
        P(None, "mlp"),
        P(),
        P("mlp", None),
        P(),
        P(None, "mlp"),
        P("mlp"),
        P("mlp", None),
        P(),
        P(),
        P(),
        P("rows"),
        P("rows"),
        P("rows", "mlp"),
    )
    out_specs = (
        P("rows", "mlp"),
        P("rows", None),
        P(None, "mlp"),
        P(None, "mlp"),
        P("mlp", None),
        P(),
        P(None, "mlp"),
        P("mlp"),
        P("mlp", None),
        P(),
        P(),
        P(),
    )
    body = functools.partial(local, mesh.shape["rows"], mesh.shape["mlp"])
    return jax.shard_map(body, mesh=mesh, in_specs=in_specs, out_specs=out_specs, check_vma=False)
```

```python
import functools

import jax
import jax.numpy as jnp
from jax import lax
from jax.experimental import pallas as pl
from jax.experimental.pallas import tpu as pltpu
from jax.sharding import PartitionSpec as P

HD = 64
IMG_DEV = 6
L_MOST = 3
HALF_S = 99
HALF_L = 289

CHUNK = 304
CHUNKS = 1 + L_MOST
PACKED = CHUNK * CHUNKS
SHARE = 8
PIECES = 4

EPSILON = 1e-06
LOWER = jnp.bfloat16
FLOAT = jnp.float32
MASKED = -1e30


def nn(a, b):
    return lax.dot_general(a, b, (((1,), (0,)), ((), ())), preferred_element_type=FLOAT)


def nt(a, b):
    return lax.dot_general(a, b, (((1,), (1,)), ((), ())), preferred_element_type=FLOAT)


def tn(a, b):
    return lax.dot_general(a, b, (((0,), (0,)), ((), ())), preferred_element_type=FLOAT)


LATER = pltpu.MemorySpace.HBM


def params(mib):
    return pltpu.CompilerParams(vmem_limit_bytes=mib * 1024 * 1024)


def cost(flops, bytes_accessed, transcendentals=0):
    return pl.CostEstimate(
        flops=flops, bytes_accessed=bytes_accessed, transcendentals=transcendentals
    )


def whole(shape, single=True):
    zeros = (0,) * len(shape)
    if single:
        return pl.BlockSpec(shape, lambda *_: zeros, pipeline_mode=pl.Buffered(1))
    return pl.BlockSpec(shape, lambda *_: zeros)


def rows_spec(width, height=CHUNK):
    return pl.BlockSpec((height, width), lambda c, *_: (c, 0))


def chunk_spec(height, width=CHUNK):
    return pl.BlockSpec((1, height, width), lambda c, *_: (c, 0, 0))


def call(kernel, name, mib, operands, in_specs, outs, scratch=(), flops=0, place=None, grid=None, far=()):
    if far:
        operands = [
            pltpu.with_memory_space_constraint(o, LATER) if i in far else o
            for i, o in enumerate(operands)
        ]
    specs = [o[2] for o in outs]
    shapes = [o[3](o[0], o[1]) if len(o) > 3 else jax.ShapeDtypeStruct(o[0], o[1]) for o in outs]
    scalars = () if place is None else (place,)
    made = pl.pallas_call(
        kernel,
        grid_spec=pltpu.PrefetchScalarGridSpec(
            num_scalar_prefetch=len(scalars),
            grid=grid or (CHUNKS,),
            in_specs=in_specs,
            out_specs=specs,
            scratch_shapes=scratch,
        ),
        out_shape=shapes,
        compiler_params=params(mib),
        cost_estimate=cost(flops // 1000000, 1000),
        name=name,
    )(*scalars, *operands)
    return list(made)


def slot_onehot(slots_ref, rows):
    named = jnp.transpose(slots_ref[0])[:, 0:1].astype(jnp.int32)
    places = lax.broadcasted_iota(jnp.int32, (CHUNK, rows), 1)
    return (places == named).astype(FLOAT).astype(LOWER)


def outside_image(slots_ref):
    image = jnp.transpose(slots_ref[0])[:, 1:2]
    return jnp.where(image == slots_ref[0, 1:2, :], 0.0, MASKED)


def choose_own(place, values, own):
    width = values.shape[1]
    source = lax.broadcasted_iota(jnp.int32, (width, own), 0)
    target = lax.broadcasted_iota(jnp.int32, (width, own), 1)
    onehot = (source == target + place * own).astype(FLOAT).astype(LOWER)
    return nn(values, onehot).astype(LOWER)


def norm_stats(values):
    average = jnp.mean(values, axis=-1, keepdims=True)
    centred = values - average
    variance = jnp.mean(centred * centred, axis=-1, keepdims=True)
    inverse = lax.rsqrt(variance + EPSILON)
    return centred * inverse, inverse


def pick_kernel(
    patches_ref, slots_ref, gains_ref, shifts_ref, router_ref, x_ref, n_ref, gate_ref
):
    x = nn(slot_onehot(slots_ref, patches_ref.shape[0]), patches_ref[...])
    x_ref[...] = x.astype(LOWER)
    scaled, _ = norm_stats(x)
    n_ref[...] = (scaled * gains_ref[0:1, :] + shifts_ref[0:1, :]).astype(LOWER)
    logit = jnp.sum(x * router_ref[...], axis=-1, keepdims=True)
    gate_ref[...] = jnp.broadcast_to(jax.nn.sigmoid(logit), gate_ref.shape)


def pick_rows(patches, slots, gains, shifts, router):
    rows, width = patches.shape
    return call(
        pick_kernel,
        "pick_rows",
        20,
        (patches, slots, gains, shifts, router),
        [
            whole((rows, width)),
            chunk_spec(8),
            whole((2, width)),
            whole((2, width)),
            whole((1, width)),
        ],
        [
            ((PACKED, width), LOWER, rows_spec(width)),
            ((PACKED, width), LOWER, rows_spec(width)),
            ((PACKED, 128), FLOAT, rows_spec(128)),
        ],
        flops=2 * PACKED * rows * width,
    )


def pick_cot_kernel(place_ref, patches_ref, cot_ref, slots_ref, part_ref, patch_ref):
    part_ref[0] = nt(cot_ref[...], slot_onehot(slots_ref, cot_ref.shape[1])).astype(LOWER)

    @pl.when(pl.program_id(0) == 0)
    def _():
        own, width = patch_ref.shape[0], patches_ref.shape[1]
        source = lax.broadcasted_iota(jnp.int32, (own, width), 1)
        target = lax.broadcasted_iota(jnp.int32, (own, width), 0)
        chosen = (source == target + place_ref[0] * own).astype(FLOAT).astype(LOWER)
        patch_ref[...] = nt(chosen, patches_ref[...]).astype(LOWER)


def pick_cot(place, patches, cot_own, slots):
    rows, width = patches.shape
    own = cot_own.shape[0]
    return call(
        pick_cot_kernel,
        "pick_cot",
        18,
        (patches, cot_own, slots),
        [whole((rows, width)), whole((own, rows)), chunk_spec(8)],
        [
            ((CHUNKS, own, CHUNK), LOWER, chunk_spec(own)),
            ((own, rows), LOWER, whole((own, rows)), LATER),
        ],
        flops=2 * PACKED * rows * own,
        place=place,
    )


def head_slabs(own):
    slabs = []
    for start in range(0, own, 2 * HD):
        stop = min(start + 2 * HD, own)
        lanes = lax.broadcasted_iota(jnp.int32, (1, stop - start), 1)
        heads = []
        for head in range(start // HD, stop // HD):
            low = head * HD - start
            heads.append((head, (lanes >= low) & (lanes < low + HD)))
        slabs.append((start, stop, heads))
    return slabs


def keep(mask, values):
    return jnp.where(mask, values, jnp.zeros_like(values))


def forward_kernel(kind_ref, n_ref, bias_ref, slots_ref, *refs):
    proj_ref, mix_ref, lse_ref, weights_ref = refs[-4:]
    parts = refs[:-4]
    own = mix_ref.shape[1]

    @pl.when(pl.program_id(0) == 0)
    def _():
        if len(parts) == 1:
            weights_ref[...] = parts[0][...]
        else:
            for other, part_ref in enumerate(parts):
                held = part_ref.shape[0]
                start = pl.multiple_of((kind_ref[0] ^ other) * held, 32)
                weights_ref[pl.ds(start, held), :] = part_ref[...]

    proj_ref[...] = (nt(n_ref[...], weights_ref[0 : 3 * own, :]) + bias_ref[0]).astype(LOWER)
    outside = outside_image(slots_ref)
    lse_all = jnp.zeros((CHUNK, 128), FLOAT)
    lanes = lax.broadcasted_iota(jnp.int32, (1, 128), 1)
    for start, stop, heads in head_slabs(own):
        q = proj_ref[:, start:stop] * LOWER(HD**-0.5)
        k = proj_ref[:, own + start : own + stop]
        v = proj_ref[:, 2 * own + start : 2 * own + stop]
        mixed = None
        for head, mask in heads:
            scores = nt(q, keep(mask, k)) + outside
            largest = jnp.max(scores, axis=-1, keepdims=True)
            powered = jnp.exp(scores - largest)
            total = jnp.sum(powered, axis=-1, keepdims=True)
            probs = (powered * (1.0 / total)).astype(LOWER)
            part = nn(probs, keep(mask, v))
            mixed = part if mixed is None else mixed + part
            lse_all = jnp.where(lanes == head, largest + jnp.log(total), lse_all)
        mix_ref[:, start:stop] = mixed.astype(LOWER)
    lse_ref[0] = jnp.transpose(lse_all)[0:8, :]


def forward_quarter(kind, normed, biases, slots, parts, j):
    width = normed.shape[1]
    own = biases.shape[2] // 3
    return call(
        forward_kernel,
        "forward_quarter",
        11,
        (normed, biases, slots, *parts),
        [
            rows_spec(width),
            pl.BlockSpec((1, 1, 3 * own), lambda c, *_: (j, 0, 0)),
            chunk_spec(8),
            *[whole(p.shape) for p in parts],
        ],
        [
            ((PACKED, 3 * own), LOWER, rows_spec(3 * own), LATER),
            ((PACKED, own), LOWER, rows_spec(own)),
            ((CHUNKS, 8, CHUNK), FLOAT, chunk_spec(8), LATER),
            ((4 * own, width), LOWER, whole((4 * own, width))),
        ],
        flops=2 * PACKED * width * 8 * own,
        place=kind,
    )


def join_kernel(place_ref, x_ref, post_ref, own_post_ref, gains_ref, shifts_ref, *refs):
    hidden_ref, normed_ref, own_ref, chosen = refs[-4:]
    parts = refs[:-4]
    count = len(parts) // 2
    own = own_ref.shape[1]

    @pl.when(pl.program_id(0) == 0)
    def _():
        for j, out_ref in enumerate(parts[count:]):
            chosen[j * own : (j + 1) * own, :] = choose_own(place_ref[0], out_ref[...], own)

    attn, attn_own = post_ref[0:1, :], own_post_ref[0:1, :]
    for j, (mix_ref, out_ref) in enumerate(zip(parts[:count], parts[count:])):
        attn = attn + nn(mix_ref[...], out_ref[...])
        attn_own = attn_own + nn(mix_ref[...], chosen[j * own : (j + 1) * own, :])
    own_ref[...] = attn_own
    hidden = x_ref[...].astype(FLOAT) + attn
    hidden_ref[...] = hidden
    scaled, _ = norm_stats(hidden)
    normed_ref[...] = (scaled * gains_ref[1:2, :] + shifts_ref[1:2, :]).astype(LOWER)


def out_spec(own, width):
    return pl.BlockSpec((own, width), lambda *_: (3, 0), pipeline_mode=pl.Buffered(1))


def join_quarters(place, x, post, own_post, gains, shifts, mixes, weights):
    width = x.shape[1]
    own = mixes[0].shape[1]
    return call(
        join_kernel,
        "join_quarters",
        11,
        (x, post, own_post, gains, shifts, *mixes, *weights),
        [
            rows_spec(width),
            whole((2, width)),
            whole((2, own)),
            whole((2, width)),
            whole((2, width)),
            *[rows_spec(own) for _ in mixes],
            *[out_spec(own, width) for _ in weights],
        ],
        [
            ((PACKED, width), FLOAT, rows_spec(width), LATER),
            ((PACKED, width), LOWER, rows_spec(width)),
            ((PACKED, own), FLOAT, rows_spec(own), LATER),
        ],
        scratch=[pltpu.VMEM((len(weights) * own, own), LOWER)],
        flops=3 * PACKED * width * width,
        place=place,
    )


def stack_places(place, parts, stacked):
    size = len(parts)
    for j, part in enumerate(parts):
        own = part.shape[0]
        start = pl.multiple_of(lax.rem(place - j + size, size) * own, 64)
        stacked[pl.ds(start, own), :] = part.astype(stacked.dtype)


def cot_kernel(place_ref, gate_ref, *refs):
    cot_ref, gated_ref, stacked = refs[-3:]
    stack_places(place_ref[0], [r[0] for r in refs[:-3]], stacked)
    cot = jnp.transpose(stacked[...])
    cot_ref[...] = cot
    gated_ref[...] = (gate_ref[:, 0:1] * cot.astype(FLOAT)).astype(LOWER)


def cot_chunks(place, gate, parts):
    own = parts[0].shape[1]
    width = own * len(parts)
    return call(
        cot_kernel,
        "cot_chunks",
        10,
        (gate, *parts),
        [rows_spec(128), *[chunk_spec(own) for _ in parts]],
        [
            ((PACKED, width), LOWER, rows_spec(width), LATER),
            ((PACKED, width), LOWER, rows_spec(width)),
        ],
        scratch=[pltpu.VMEM((width, CHUNK), LOWER)],
        flops=PACKED * width,
        place=place,
    )


def gelu_pair(u):
    cdf = 0.5 * (1.0 + lax.erf(u * (0.5**0.5)))
    density = jnp.exp(-0.5 * u * u) * 0.3989422804014327
    return u * cdf, cdf + u * density


def mlp_step(normed, gated, up_ref, down_ref, bias, own_down_ref):
    hidden = up_ref.shape[1]
    block = hidden // 3

    def products(start):
        cols = slice(start, start + block)
        pre_act = nn(normed, up_ref[:, cols]) + bias[:, cols]
        return pre_act, nt(gated, down_ref[cols, :])

    activations, grads, grad, gate, out = [], [], None, None, None
    ahead = products(0)
    for start in range(0, hidden, block):
        cols = slice(start, start + block)
        pre_act, grad_act = ahead
        if start + block < hidden:
            ahead = products(start + block)
        activation, slope = gelu_pair(pre_act)
        activation = activation.astype(LOWER)
        grad_pre = (grad_act * slope).astype(LOWER)
        gate_part = jnp.sum(activation.astype(FLOAT) * grad_act, axis=-1, keepdims=True)
        grad_part = nt(grad_pre, up_ref[:, cols])
        out_part = nn(activation, own_down_ref[cols, :])
        activations.append(activation)
        grads.append(grad_pre)
        grad = grad_part if grad is None else grad + grad_part
        gate = gate_part if gate is None else gate + gate_part
        out = out_part if out is None else out + out_part
    return activations, grads, grad, gate, out


def own_mlp_kernel(
    place_ref,
    n_ref,
    gated_ref,
    up_ref,
    down_ref,
    bias_ref,
    act_ref,
    pre_ref,
    grad_ref,
    gate_ref,
    out_ref,
    bias_sum_ref,
    own_down,
):
    @pl.when(pl.program_id(0) == 0)
    def _():
        own_down[...] = choose_own(place_ref[0], down_ref[...], own_down.shape[1])
        bias_sum_ref[...] = jnp.zeros_like(bias_sum_ref)

    activation, grad_pre, grad_part, gate_part, out_part = mlp_step(
        n_ref[...], gated_ref[...], up_ref, down_ref, bias_ref[...], own_down
    )
    block = activation[0].shape[1]
    for i, (act, pre) in enumerate(zip(activation, grad_pre)):
        act_ref[:, i * block : (i + 1) * block] = act
        pre_ref[:, i * block : (i + 1) * block] = pre
    grad_ref[...] = grad_part
    gate_ref[...] = jnp.broadcast_to(gate_part, gate_ref.shape)
    out_ref[...] = out_part
    bias_sum_ref[0:1, :] += jnp.sum(pre_ref[...].astype(FLOAT), axis=0, keepdims=True)


def own_mlp(place, normed, gated, up, down, bias, own):
    width, hidden = up.shape
    return call(
        own_mlp_kernel,
        "own_mlp",
        17,
        (normed, gated, up, down, bias),
        [
            rows_spec(width),
            rows_spec(width),
            whole((width, hidden)),
            whole((hidden, width)),
            whole((1, hidden)),
        ],
        [
            ((PACKED, hidden), LOWER, rows_spec(hidden)),
            ((PACKED, hidden), LOWER, rows_spec(hidden)),
            ((PACKED, width), FLOAT, rows_spec(width)),
            ((PACKED, 128), FLOAT, rows_spec(128)),
            ((PACKED, own), FLOAT, rows_spec(own)),
            ((8, hidden), FLOAT, whole((8, hidden), False)),
        ],
        scratch=[pltpu.VMEM((hidden, own), LOWER)],
        flops=2 * PACKED * hidden * (3 * width + own),
        place=place,
    )


def own_grads_kernel(core_ref, n_ref, pre_ref, act_ref, gated_ref, kept_ref, sent_ref):
    grad_up = tn(n_ref[...], pre_ref[...])
    grad_down = tn(act_ref[...], gated_ref[...])

    @pl.when(core_ref[0] == 0)
    def _():
        kept_ref[...] = grad_up
        sent_ref[...] = grad_down.astype(LOWER)

    @pl.when(core_ref[0] == 1)
    def _():
        kept_ref[...] = grad_down
        sent_ref[...] = grad_up.astype(LOWER)


def own_grads(core, normed, grad_pre, act, gated):
    width = normed.shape[1]
    block = width // 3
    columns = pl.BlockSpec((PACKED, block), lambda c, *_: (0, c))
    return call(
        own_grads_kernel,
        "own_grads",
        16,
        (normed, grad_pre, act, gated),
        [columns, whole((PACKED, width)), columns, whole((PACKED, width))],
        [
            ((width, width), FLOAT, rows_spec(width, block)),
            ((width, width), LOWER, rows_spec(width, block)),
        ],
        flops=4 * PACKED * width * width,
        place=core,
        grid=(3,),
    )


def other_mlp_kernel(
    last, place_ref, n_ref, gated_ref, grad_in_ref, gate_in_ref, out_in_ref, *refs
):
    grad_ref, gate_ref, out_ref, up, down, own_down = refs[-6:]
    ups, downs = refs[0:4], refs[4:8]
    part = downs[0].shape[2]
    width = up.shape[1]

    @pl.when(pl.program_id(0) == 0)
    def _():
        for side in range(2):
            for c in range(2):
                for near in range(2):
                    to_up = place_ref[1] ^ (4 * side + 2 * near + c)
                    to_down = place_ref[1] ^ (4 * near + 2 * side + c)
                    up_rows = pl.ds(pl.multiple_of(to_up * part, 32), part)
                    down_rows = pl.ds(pl.multiple_of(to_down * part, 32), part)
                    up[up_rows, :] = ups[side + 2 * c][near, 0, 0:part]
                    down[down_rows, :] = downs[side + 2 * c][near, 0]
        own_down[...] = choose_own(place_ref[0], down[...], own_down.shape[1])

    pieces = ups[0][0, 0, part : part + 16].astype(FLOAT)
    bias = pieces[0:1] + (pieces[1:2] + pieces[2:3])
    _, _, grad_part, gate_part, out_part = mlp_step(
        n_ref[...], gated_ref[...], up, down, bias, own_down
    )
    grad_ref[...] = grad_in_ref[...] + grad_part
    gate_ref[...] = gate_in_ref[...] + gate_part
    if last:
        attn_ref, post_ref, open_ref = refs[8:11]
        total = out_in_ref[...] + out_part + attn_ref[...] + post_ref[1:2, :]
        out_ref[...] = open_ref[:, 0:1] * total
    else:
        out_ref[...] = out_in_ref[...] + out_part


def other_mlp(places, normed, gated, sums, ups, downs, j, extra=()):
    width = normed.shape[1]
    own = sums[2].shape[1]
    last = len(extra) > 0
    held = lambda array: pl.BlockSpec(
        (2, 1, *array.shape[2:]), lambda c, *_: (0, j, 0, 0), pipeline_mode=pl.Buffered(1)
    )
    extra_specs = [rows_spec(own), whole((2, own)), rows_spec(128)] if last else []
    return call(
        functools.partial(other_mlp_kernel, last),
        "other_mlp",
        19,
        (normed, gated, *sums, *ups, *downs, *extra),
        [
            rows_spec(width),
            rows_spec(width),
            rows_spec(width),
            rows_spec(128),
            rows_spec(own),
            *[held(u) for u in ups],
            *[held(d) for d in downs],
            *extra_specs,
        ],
        [
            ((PACKED, width), FLOAT, rows_spec(width)),
            ((PACKED, 128), FLOAT, rows_spec(128)),
            ((PACKED, own), FLOAT, rows_spec(own)),
        ],
        scratch=[
            pltpu.VMEM((width, width), LOWER),
            pltpu.VMEM((width, width), LOWER),
            pltpu.VMEM((width, own), LOWER),
        ],
        flops=2 * PACKED * width * (3 * width + own),
        place=places,
    )


def second_norm_kernel(
    grad_ref,
    gate_part_ref,
    hidden_ref,
    x_ref,
    cot_ref,
    gate_ref,
    post_ref,
    gains_ref,
    ghid_ref,
    glow_ref,
    logit_ref,
    sums_ref,
):
    @pl.when(pl.program_id(0) == 0)
    def _():
        sums_ref[...] = jnp.zeros_like(sums_ref)

    hidden = hidden_ref[...]
    scaled, inverse = norm_stats(hidden)
    grad_out = grad_ref[...]
    weighted = grad_out * gains_ref[1:2, :]
    centre_term = jnp.mean(weighted, axis=-1, keepdims=True)
    scale_term = jnp.mean(weighted * scaled, axis=-1, keepdims=True)
    grad_hidden = inverse * (weighted - centre_term - scaled * scale_term)
    gate = gate_ref[:, 0:1]
    gated = gate * cot_ref[...].astype(FLOAT)
    grad_attn = grad_hidden + gated
    ghid_ref[...] = grad_hidden
    glow_ref[...] = grad_attn.astype(LOWER)
    attn = hidden - x_ref[...].astype(FLOAT)
    dotted = jnp.sum(gated * (attn + post_ref[1:2, :]), axis=-1, keepdims=True)
    logit = (1.0 - gate) * (dotted + gate_part_ref[:, 0:1])
    logit_ref[...] = jnp.broadcast_to(logit, logit_ref.shape)
    sums_ref[0:1, :] += jnp.sum(grad_out * scaled, axis=0, keepdims=True)
    sums_ref[1:2, :] += jnp.sum(grad_out, axis=0, keepdims=True)
    sums_ref[2:3, :] += jnp.sum(grad_attn, axis=0, keepdims=True)
    sums_ref[3:4, :] += jnp.sum(gated, axis=0, keepdims=True)


def second_norm(grad, gate_part, hidden, x, cot_rows, gate, post, gains):
    width = x.shape[1]
    return call(
        second_norm_kernel,
        "second_norm",
        15,
        (grad, gate_part, hidden, x, cot_rows, gate, post, gains),
        [
            rows_spec(width),
            rows_spec(128),
            rows_spec(width),
            rows_spec(width),
            rows_spec(width),
            rows_spec(128),
            whole((2, width)),
            whole((2, width)),
        ],
        [
            ((PACKED, width), FLOAT, rows_spec(width)),
            ((PACKED, width), LOWER, rows_spec(width)),
            ((PACKED, 128), FLOAT, rows_spec(128)),
            ((8, width), FLOAT, whole((8, width), False)),
        ],
        flops=20 * PACKED * width,
    )


def backward_kernel(low_ref, slots_ref, proj_ref, lse_ref, out_ref, gproj_ref, sums_ref):
    @pl.when(pl.program_id(0) == 0)
    def _():
        sums_ref[...] = jnp.zeros_like(sums_ref)

    outside = outside_image(slots_ref)
    own = out_ref.shape[0]
    heads = own // HD
    g = nt(low_ref[...], out_ref[...]).astype(LOWER)
    q = proj_ref[:, 0:own] * LOWER(HD**-0.5)
    k = proj_ref[:, own : 2 * own]
    v = proj_ref[:, 2 * own : 3 * own]
    lanes = lax.broadcasted_iota(jnp.int32, (1, own), 1) // HD
    keys = jnp.concatenate([keep(lanes == head, k) for head in range(heads)], axis=0)
    values = jnp.concatenate([keep(lanes == head, v) for head in range(heads)], axis=0)
    scores = nt(keys, q)
    grad_probs = nt(values, g)
    probs, grad_scores = [], []
    for head in range(heads):
        rows = slice(head * CHUNK, (head + 1) * CHUNK)
        prob = jnp.exp(scores[rows] + outside - lse_ref[0, head : head + 1, :])
        inner = jnp.sum(prob * grad_probs[rows], axis=0, keepdims=True)
        grad_scores.append((prob * (grad_probs[rows] - inner)).astype(LOWER))
        probs.append(prob.astype(LOWER))
    grad_scores = jnp.concatenate(grad_scores, axis=0)
    all_v = nn(jnp.concatenate(probs, axis=0), g)
    all_k = nn(grad_scores, q)
    grad_q = tn(grad_scores, keys)
    grad_k, grad_v = all_k[0:CHUNK], all_v[0:CHUNK]
    for head in range(1, heads):
        rows = slice(head * CHUNK, (head + 1) * CHUNK)
        grad_k = jnp.where(lanes == head, all_k[rows], grad_k)
        grad_v = jnp.where(lanes == head, all_v[rows], grad_v)
    gproj_ref[:, 0:own] = (grad_q * HD**-0.5).astype(LOWER)
    gproj_ref[:, own : 2 * own] = grad_k.astype(LOWER)
    gproj_ref[:, 2 * own : 3 * own] = grad_v.astype(LOWER)
    sums_ref[0:1, :] += jnp.sum(gproj_ref[...].astype(FLOAT), axis=0, keepdims=True)


def backward_quarter(low, slots, proj, lse, weights):
    width = low.shape[1]
    own = proj.shape[1] // 3
    return call(
        backward_kernel,
        "backward_quarter",
        20,
        (low, slots, proj, lse, weights),
        [
            rows_spec(width),
            chunk_spec(8),
            rows_spec(3 * own),
            chunk_spec(8),
            out_spec(own, width),
        ],
        [
            ((PACKED, 3 * own), LOWER, rows_spec(3 * own)),
            ((8, 3 * own), FLOAT, whole((8, 3 * own), False)),
        ],
        flops=2 * PACKED * width * 14 * own,
    )


def attn_grads_kernel(core_ref, gproj_ref, normed_ref, mix_ref, low_ref, kept_ref, sent_ref):
    half = kept_ref.shape[0]
    rest = gproj_ref.shape[1] - half
    normed = normed_ref[...]
    first = tn(gproj_ref[:, 0:half], normed)
    second = tn(gproj_ref[:, half:], normed)
    third = tn(mix_ref[...], low_ref[...])

    @pl.when(core_ref[0] == 0)
    def _():
        kept_ref[...] = first
        sent_ref[0:rest, :] = second.astype(LOWER)
        sent_ref[rest:half, :] = third.astype(LOWER)

    @pl.when(core_ref[0] == 1)
    def _():
        kept_ref[0:rest, :] = second
        kept_ref[rest:half, :] = third
        sent_ref[...] = first.astype(LOWER)


def attn_grads(core, gproj, normed, mix, low):
    width, own = normed.shape[1], mix.shape[1]
    operands = (gproj, normed, mix, low)
    return call(
        attn_grads_kernel,
        "attn_grads",
        18,
        operands,
        [whole(o.shape) for o in operands],
        [
            ((2 * own, width), FLOAT, whole((2 * own, width))),
            ((2 * own, width), LOWER, whole((2 * own, width))),
        ],
        place=core,
        grid=(1,),
    )


def first_norm_kernel(x_ref, ghid_ref, logit_ref, gains_ref, router_ref, *refs):
    rows_ref, sums_ref = refs[-2:]
    parts = refs[:-2]
    count = len(parts) // 2

    @pl.when(pl.program_id(0) == 0)
    def _():
        sums_ref[...] = jnp.zeros_like(sums_ref)

    grad_out = None
    for gproj_ref, weights_ref in zip(parts[:count], parts[count:]):
        part = nn(gproj_ref[...], weights_ref[0 : gproj_ref.shape[1], :])
        grad_out = part if grad_out is None else grad_out + part
    x = x_ref[...].astype(FLOAT)
    scaled, inverse = norm_stats(x)
    weighted = grad_out * gains_ref[0:1, :]
    centre_term = jnp.mean(weighted, axis=-1, keepdims=True)
    scale_term = jnp.mean(weighted * scaled, axis=-1, keepdims=True)
    grad_norm = inverse * (weighted - centre_term - scaled * scale_term)
    logit = logit_ref[:, 0:1]
    rows_ref[...] = (ghid_ref[...] + grad_norm + logit * router_ref[...]).astype(LOWER)
    sums_ref[0:1, :] += jnp.sum(grad_out * scaled, axis=0, keepdims=True)
    sums_ref[1:2, :] += jnp.sum(grad_out, axis=0, keepdims=True)
    sums_ref[2:3, :] += jnp.sum(logit * x, axis=0, keepdims=True)


def first_norm(x, ghid, logit, gains, router, gprojs, weights):
    width = x.shape[1]
    return call(
        first_norm_kernel,
        "first_norm",
        18,
        (x, ghid, logit, gains, router, *gprojs, *weights),
        [
            rows_spec(width),
            rows_spec(width),
            rows_spec(128),
            whole((2, width)),
            whole((1, width)),
            *[rows_spec(g.shape[1]) for g in gprojs],
            *[whole(w.shape) for w in weights],
        ],
        [
            ((PACKED, width), LOWER, rows_spec(width)),
            ((8, width), FLOAT, whole((8, width), False)),
        ],
        flops=2 * PACKED * width * 3 * width,
    )


def scatter_kernel(place_ref, named_ref, rows_ref, branch_ref, patch_ref, *refs):
    out_ref, block_ref, stacked, branch_t, total, own_total = refs[-6:]
    block = out_ref.shape[0]
    first = pl.program_id(0) * block

    @pl.when(pl.program_id(0) == 0)
    def _():
        for c in range(CHUNKS):
            part = branch_ref[c * CHUNK : (c + 1) * CHUNK, :]
            branch_t[c] = jnp.transpose(part).astype(LOWER)

    stack_places(place_ref[0], [r[...] for r in refs[:-6]], stacked)
    total[...] = jnp.transpose(stacked[...]).astype(FLOAT)
    own_total[...] = patch_ref[...].astype(FLOAT)
    for c in range(CHUNKS):
        low, high = place_ref[1 + 2 * c], place_ref[2 + 2 * c]

        @pl.when((low < first + block) & (high >= first))
        def _():
            places = lax.broadcasted_iota(jnp.int32, (block, CHUNK), 0) + first
            onehot = (places == named_ref[c, 0:1, :].astype(jnp.int32)).astype(FLOAT).astype(LOWER)
            total[...] += nn(onehot, rows_ref[c * CHUNK : (c + 1) * CHUNK, :])
            own_total[...] += nt(branch_t[c], onehot)

    out_ref[...] = total[...].astype(LOWER)
    block_ref[...] = own_total[...].astype(LOWER)


def scatter_rows(places, cot_parts, slots, rows, branch, patch_t):
    own, total = cot_parts[0].shape
    width = own * len(cot_parts)
    block = 512
    columns = pl.BlockSpec((own, block), lambda c, *_: (0, c))
    return call(
        scatter_kernel,
        "scatter_rows",
        19,
        (slots, rows, branch, patch_t, *cot_parts),
        [
            whole(slots.shape),
            whole((PACKED, width)),
            whole((PACKED, own)),
            columns,
            *[columns for _ in cot_parts],
        ],
        [
            ((total, width), LOWER, rows_spec(width, block)),
            ((own, total), LOWER, columns),
        ],
        scratch=[
            pltpu.VMEM((width, block), LOWER),
            pltpu.VMEM((CHUNKS, own, CHUNK), LOWER),
            pltpu.VMEM((block, width), FLOAT),
            pltpu.VMEM((own, block), FLOAT),
        ],
        flops=2 * PACKED * total * width,
        place=places,
        grid=(pl.cdiv(total, block),),
        far=range(3, 4 + len(cot_parts)),
    )


def halve_kernel(upper_ref, kept_ref, came_ref, half_ref, sent_ref):
    block, half = half_ref.shape[0], kept_ref.shape[0] // 2
    step = pl.program_id(0) * block
    own = pl.ds(pl.multiple_of(upper_ref[0] * half + step, 16), block)
    far = pl.ds(pl.multiple_of((1 - upper_ref[0]) * half + step, 16), block)
    half_ref[...] = kept_ref[own, :] + came_ref[own, :].astype(FLOAT)
    sent_ref[...] = (kept_ref[far, :] + came_ref[far, :].astype(FLOAT)).astype(LOWER)


def halve_sum(upper, kept, came):
    rows, width = kept.shape
    return call(
        halve_kernel,
        "halve_sum",
        10,
        (kept, came),
        [whole((rows, width)), whole((rows, width))],
        [
            ((rows // 2, width), FLOAT, rows_spec(width, rows // 4)),
            ((rows // 2, width), LOWER, rows_spec(width, rows // 4)),
        ],
        place=upper,
        grid=(2,),
    )


def finish_kernel(core_ref, attn_ref, attn_far_ref, mlp_ref, mlp_far_ref, *refs):
    qkv_ref, out_ref, up_ref, down_ref = refs
    own, block = qkv_ref.shape[0], up_ref.shape[0]
    head = pl.program_id(0)
    rows = pl.ds(pl.multiple_of(head * block, 16), block)

    def write(low_ref, high_ref, first_ref, second_ref):
        one = pl.ds(pl.multiple_of(head * HD, HD), HD)
        two = pl.ds(pl.multiple_of(own + head * HD, HD), HD)
        qkv_ref[0:HD, :] = low_ref[one, :].astype(FLOAT)
        qkv_ref[HD : 2 * HD, :] = low_ref[two, :].astype(FLOAT)
        qkv_ref[2 * HD : 3 * HD, :] = high_ref[one, :].astype(FLOAT)
        out_ref[...] = high_ref[two, :].astype(FLOAT)
        up_ref[...] = first_ref[rows, :].astype(FLOAT)
        down_ref[...] = second_ref[rows, :].astype(FLOAT)

    @pl.when(core_ref[0] == 0)
    def _():
        write(attn_ref, attn_far_ref, mlp_ref, mlp_far_ref)

    @pl.when(core_ref[0] == 1)
    def _():
        write(attn_far_ref, attn_ref, mlp_far_ref, mlp_ref)


def finish_grads(core, attn, attn_far, mlp, mlp_far):
    width = mlp.shape[1]
    own = attn.shape[0] // 2
    heads = own // HD
    return call(
        finish_kernel,
        "finish_grads",
        16,
        (attn, attn_far, mlp, mlp_far),
        [whole(attn.shape), whole(attn.shape), whole(mlp.shape), whole(mlp.shape)],
        [
            ((3 * own, width), FLOAT, rows_spec(width, 3 * HD)),
            ((own, width), FLOAT, rows_spec(width, HD)),
            ((width, width), FLOAT, rows_spec(width, width // heads)),
            ((width, width), FLOAT, rows_spec(width, width // heads)),
        ],
        place=core,
        grid=(heads,),
    )


def finish_sums_kernel(own_ref, far_ref, *refs):
    gains_ref, shifts_ref, post_ref, up_ref, router_ref, qkv_ref = refs
    total = own_ref[...] + far_ref[...]
    own = qkv_ref.shape[1]
    gains_ref[0:1, :] = total[4:5]
    gains_ref[1:2, :] = total[0:1]
    shifts_ref[0:1, :] = total[5:6]
    shifts_ref[1:2, :] = total[1:2]
    post_ref[...] = total[2:4]
    up_ref[...] = total[7:8]
    router_ref[...] = total[6:7]
    qkv_ref[0:1, :] = total[8:9, 0:own]
    qkv_ref[1:2, :] = total[8:9, 2 * own : 3 * own]


def finish_sums(small, far, own):
    rows, width = small.shape
    shapes = [(2, width), (2, width), (2, width), (1, width), (1, width), (2, own)]
    return call(
        finish_sums_kernel,
        "finish_sums",
        4,
        (small, far),
        [whole((rows, width)), whole((rows, width))],
        [(shape, FLOAT, whole(shape)) for shape in shapes],
        grid=(1,),
    )


def turned(values, place):
    size = values.shape[0]
    back = jnp.concatenate([values[:1], values[:0:-1]], axis=0)
    twice = jnp.concatenate([back, back], axis=0)
    return lax.dynamic_slice_in_dim(twice, (size - place) % size, size, 0)


def after(value, *others):
    return lax.optimization_barrier((value, *others))[0]


def ring_step(value, size):
    return lax.ppermute(value, "mlp", [(i, (i + 1) % size) for i in range(size)])


def swap(value, bit, size):
    return lax.ppermute(value, "rows", [(i, i ^ (1 << bit)) for i in range(size)])


def bits_of(size):
    return [b for b in range(20) if (1 << b) < size]


def pack_slots(picked, live_slots):
    small = IMG_DEV * HALF_S
    named = jnp.where(live_slots == 1, picked, -1)

    def padded(parts, fill):
        have = sum(p.shape[0] for p in parts)
        return jnp.concatenate([*parts, jnp.full((CHUNK - have,), fill, jnp.int32)])

    always = IMG_DEV - L_MOST
    idx = [padded([named[: always * HALF_S]], -1)]
    seg = [padded([jnp.repeat(jnp.arange(always, dtype=jnp.int32), HALF_S)], always)]
    for j in range(L_MOST):
        first = small + j * HALF_L
        alive = live_slots[first] == 1
        other = IMG_DEV - 1 - j
        large_idx = padded([named[first : first + HALF_L]], -1)
        small_idx = padded([named[other * HALF_S : (other + 1) * HALF_S]], -1)
        idx.append(jnp.where(alive, large_idx, small_idx))
        length = jnp.where(alive, HALF_L, HALF_S)
        seg.append((jnp.arange(CHUNK, dtype=jnp.int32) >= length).astype(jnp.int32))
    named = jnp.stack(idx)
    low = jnp.min(jnp.where(named < 0, 1 << 24, named), axis=1)
    bounds = jnp.stack([low, jnp.max(named, axis=1)], axis=1).reshape(2 * CHUNKS)
    idx, seg = jnp.stack(idx).astype(FLOAT), jnp.stack(seg).astype(FLOAT)
    rows = lax.broadcasted_iota(jnp.int32, (1, 8, 1), 1)
    return jnp.where(rows == 0, idx[:, None, :], seg[:, None, :]), bounds


def local(
    rows_size,
    mlp_size,
    patches,
    w_qkv,
    qkv_bias,
    w_out,
    post_bias,
    w_up,
    up_bias,
    w_down,
    norm_gains,
    norm_shifts,
    router,
    picked,
    live_slots,
    cotangent,
):
    width = patches.shape[1]
    mlp_index = lax.axis_index("mlp")
    rows_index = lax.axis_index("rows")
    share_index = rows_index % SHARE
    core = rows_index & 1
    place = mlp_index.astype(jnp.int32).reshape(1)
    places = jnp.stack([mlp_index, share_index]).astype(jnp.int32)
    kind = (rows_index % PIECES).astype(jnp.int32).reshape(1)
    own = w_out.shape[0]
    heads_here = own // HD
    others = mlp_size - 1
    router_row = router.reshape(1, width)

    def swapped(value, bit):
        return swap(value, bit, rows_size)

    own_weights = jnp.concatenate(
        [
            w_qkv.T.reshape(heads_here, 3, HD, width).transpose(1, 0, 2, 3).reshape(3 * own, width),
            w_out,
        ],
        axis=0,
    )
    held = own_weights.shape[0] // PIECES
    piece = lax.dynamic_slice_in_dim(own_weights, kind[0] * held, held, 0)
    part = w_up.shape[0] // SHARE
    top = lax.reduce_precision(up_bias, 8, 7)
    middle = lax.reduce_precision(up_bias - top, 8, 7)
    bias_rows = jnp.stack([top, middle, up_bias - top - middle]).astype(LOWER)
    payload = jnp.concatenate(
        [
            piece,
            lax.dynamic_slice_in_dim(w_up, share_index * part, part, 0),
            jnp.pad(bias_rows, ((0, 13), (0, 0))),
            lax.dynamic_slice_in_dim(w_down, share_index * part, part, 0),
        ],
        axis=0,
    )
    def around(value):
        return ring_step(value, mlp_size)

    kinds = jnp.stack([qkv_bias[0], jnp.zeros_like(qkv_bias[0]), qkv_bias[1]])
    biases = turned(kinds.reshape(3, mlp_size, own).transpose(1, 0, 2), mlp_index)
    biases = biases.reshape(mlp_size, 1, 3 * own)
    own_post = lax.dynamic_slice_in_dim(post_bias, mlp_index * own, own, 1)
    slots, bounds = pack_slots(picked, live_slots)
    bounds = jnp.concatenate([place, bounds])
    cot_own = cotangent.T
    core_one = core.astype(jnp.int32).reshape(1)

    def split(came):
        return came[:held], came[held : held + part + 16], came[held + part + 16 :]

    def across(value, mask):
        return lax.ppermute(value, "rows", [(i, i ^ mask) for i in range(rows_size)])

    def forward(j, normed, parts):
        return forward_quarter(kind, normed, biases, slots, parts, j)

    order = bits_of(rows_size)
    lower = {bit: (rows_index >> bit) & 1 == 0 for bit in order}
    upper = {bit: ((rows_index >> bit) & 1).astype(jnp.int32).reshape(1) for bit in order}
    payload, place, places, kind, core_one, lower, upper, own_post, biases = lax.optimization_barrier(
        (payload, place, places, kind, core_one, lower, upper, own_post, biases)
    )
    came = around(payload)
    patches, bounds = lax.optimization_barrier((after(patches, payload), bounds))
    x, normed_one, gate = pick_rows(
        patches, slots, norm_gains, norm_shifts, router_row
    )
    came = after(came, x)
    cot_part, patch_t = pick_cot(place, after(patches, came), cot_own, slots)
    normed_one = after(normed_one, cot_part)
    quarters, cot_parts, up_parts, down_parts = [], [cot_part], [], []
    parts, before = [own_weights], x
    for j in range(mlp_size):
        if j < others:
            came = after(came, before)
            got, up_part, down_part = split(came)
            up_parts.append(up_part)
            down_parts.append(down_part)
            if j + 1 < others:
                came = around(came)
            spread = [got, *[across(got, mask) for mask in range(2, PIECES, 2)]]
        if 0 < j < others:
            cot_parts.append(around(after(cot_parts[-1], got)))
        normed_one = after(normed_one, got, before, *parts)
        if j == others:
            normed_one = after(normed_one, *cot_parts[:-1])
            ups, downs = jnp.stack(up_parts), jnp.stack(down_parts)
            ups_x, downs_y = swapped(ups, 1), swapped(downs, 2)
        quarters.append(forward(j, normed_one, parts))
        before = quarters[-1][1]
        if j < others:
            spread = [after(v, before) for v in spread]
            parts = [w for v in spread for w in (v, swapped(v, 0))]

    projs, mixes, lses, weights = zip(*quarters)
    cot_last = after(cot_parts[-1], before)
    ups_x, downs_y = after(ups_x, cot_last), after(downs_y, cot_last)
    cot_parts.append(around(cot_last))
    ups, downs = jnp.stack([ups, ups_x]), jnp.stack([downs, downs_y])
    ups_y, downs_x = swapped(ups, 2), swapped(downs, 1)
    hidden, normed_two, attn_own = join_quarters(
        place, after(x, cot_last), post_bias, own_post, norm_gains, norm_shifts, mixes, weights
    )
    cot_rows, gated = cot_chunks(place, after(gate, normed_two), cot_parts)
    full_parts = [cot_own, around(after(cot_own, gated))]

    def full_due(slot, value):
        if slot in ("N2", "B2"):
            full_parts.append(around(after(full_parts[-1], value)))
            return after(value, full_parts[-2])
        return value

    act, grad_pre, *sums, up_bias_sum = own_mlp(
        place, normed_two, gated, w_up, w_down, up_bias.reshape(1, -1), own
    )
    ups_y, downs_x = after(ups_y, sums[0]), after(downs_x, sums[0])
    more = [swapped(v, 0) for v in (ups, ups_y, downs, downs_x)]
    kept, sent = own_grads(core_one, normed_two, after(grad_pre, ups_y, downs_x), act, gated)
    more = [after(v, kept) for v in more]
    ups, downs = [ups, ups_y, *more[:2]], [downs, downs_x, *more[2:]]
    sent = after(sent, *more)

    turned_order = [order[0], *order[:0:-1]]

    def halves(kept, came, bit):
        if kept.shape[0] % 64 == 0:
            return halve_sum(upper[bit], kept, came)
        value = kept + came.astype(FLOAT)
        pair = value.reshape(2, value.shape[0] // 2, width)
        return (
            jnp.where(lower[bit], pair[0], pair[1]),
            jnp.where(lower[bit], pair[1], pair[0]).astype(LOWER),
        )

    def joined(value, other, bit):
        first, second = jnp.where(lower[bit], value, other), jnp.where(lower[bit], other, value)
        return jnp.concatenate([first, second], axis=0)

    def halve_middle(kept, came, bits):
        for bit in bits[2:-1]:
            kept, sent = halves(kept, came, bit)
            came = swapped(sent, bit)
        return halves(kept, came, bits[-1])

    def join_middle(value, bits):
        for bit in bits[-2:1:-1]:
            value = joined(value, swapped(value, bit), bit)
        return value

    came_c = swapped(sent, 0)
    sums[0] = after(sums[0], kept, *more)
    for j in range(others):
        sums[0] = full_due(f"M{j}", sums[0])
        last_quarter = (attn_own, own_post, gate) if j == others - 1 else ()
        sums = other_mlp(places, normed_two, gated, sums, ups, downs, j, last_quarter)
        if j == 0:
            kept, sent = halves(kept, after(came_c, sums[0]), order[1])
            came_x = swapped(sent, order[1])
            sums[0] = after(sums[0], sent)
    grad_two, gate_part, branch = sums
    came_x = after(came_x, grad_two)
    grad_two = full_due("N2", grad_two)
    grad_two = after(grad_two, came_x)
    kept, sent = halve_middle(kept, came_x, order)
    came_y = swapped(sent, order[-1])
    grad_hidden, grad_low, logit, sums_two = second_norm(
        after(grad_two, kept), gate_part, hidden, x, cot_rows, gate, post_bias, norm_gains
    )
    own_proj, bias_grad = backward_quarter(
        full_due("B0", grad_low), slots, projs[0], lses[0], weights[0]
    )
    kept_a, sent_a = attn_grads(core_one, own_proj, normed_one, mixes[0], grad_low)
    gprojs = [own_proj]
    came_a = swapped(sent_a, 0)
    d_mlp = (kept + after(came_y, kept_a).astype(FLOAT)).astype(LOWER)
    other = swapped(d_mlp, order[-1])
    low = full_due("B1", after(grad_low, kept_a, d_mlp))
    gprojs.append(backward_quarter(low, slots, projs[1], lses[1], weights[1])[0])
    kept_a, sent_a = halves(kept_a, after(came_a, gprojs[-1]), turned_order[1])
    came_a = swapped(sent_a, turned_order[1])
    d_mlp = join_middle(joined(d_mlp, after(other, gprojs[-1]), order[-1]), order)
    other = swapped(d_mlp, order[1])
    low = full_due("B2", after(low, gprojs[-1], d_mlp, kept_a))
    gprojs.append(backward_quarter(low, slots, projs[2], lses[2], weights[2])[0])
    kept_a, sent_a = halve_middle(kept_a, after(came_a, gprojs[-1]), turned_order)
    came_a = swapped(sent_a, turned_order[-1])
    low = full_due("B3", after(low, gprojs[-1], kept_a))
    for j in range(3, mlp_size):
        gprojs.append(backward_quarter(low, slots, projs[j], lses[j], weights[j])[0])
    d_attn = (kept_a + after(came_a, gprojs[-1]).astype(FLOAT)).astype(LOWER)
    near, far = turned_order[-1], turned_order[-2]
    others_a = [
        lax.ppermute(d_attn, "rows", [(i, i ^ mask) for i in range(rows_size)])
        for mask in (1 << near, 1 << far, (1 << near) | (1 << far))
    ]
    d_mlp = joined(d_mlp, after(other, gprojs[-1]), order[1])
    other = swapped(d_mlp, 0)
    rows_grad, sums_one = first_norm(
        x, grad_hidden, after(logit, gprojs[-1], d_attn, d_mlp), norm_gains, router_row, gprojs, weights
    )
    others_a = [after(v, rows_grad) for v in others_a]
    d_attn = joined(joined(d_attn, others_a[0], near), joined(others_a[1], others_a[2], near), far)
    for bit in turned_order[-3:0:-1]:
        d_attn = joined(d_attn, swapped(d_attn, bit), bit)
    other_a = swapped(d_attn, 0)
    small = jnp.concatenate(
        [
            sums_two[:4],
            sums_one[:3],
            up_bias_sum[:1],
            jnp.pad(bias_grad[:1], ((0, 0), (0, width - 3 * own))),
        ],
        axis=0,
    )
    small = small + swapped(small, 0)
    other_s = swapped(small, order[1])
    input_grad, block_out = scatter_rows(
        bounds, full_parts, slots, after(rows_grad, small, d_attn), branch, patch_t
    )
    block_out = block_out.T
    small = small + after(other_s, input_grad)
    for bit in order[2:-1]:
        small = small + swapped(small, bit)
    other_s = swapped(small, order[-1])
    d_qkv, d_out, d_up, d_down = finish_grads(
        core_one, d_attn, after(other_a, input_grad, small), d_mlp, other
    )
    small, other_s = after(small, d_qkv), after(other_s, d_qkv)
    d_gains, d_shifts, d_post_bias, d_up_bias, d_router, d_qkv_bias = finish_sums(small, other_s, own)
    d_qkv = d_qkv.T
    return (
        block_out,
        input_grad,
        d_qkv,
        d_qkv_bias,
        d_out,
        d_post_bias,
        d_up,
        d_up_bias.reshape(width),
        d_down,
        d_gains,
        d_shifts,
        d_router.reshape(width),
    )


def solution(mesh):
    in_specs = (
        P("rows", None),
        P(None, "mlp"),
        P(),
        P("mlp", None),
        P(),
        P(None, "mlp"),
        P("mlp"),
        P("mlp", None),
        P(),
        P(),
        P(),
        P("rows"),
        P("rows"),
        P("rows", "mlp"),
    )
    out_specs = (
        P("rows", "mlp"),
        P("rows", None),
        P(None, "mlp"),
        P(None, "mlp"),
        P("mlp", None),
        P(),
        P(None, "mlp"),
        P("mlp"),
        P("mlp", None),
        P(),
        P(),
        P(),
    )
    body = functools.partial(local, mesh.shape["rows"], mesh.shape["mlp"])
    return jax.shard_map(body, mesh=mesh, in_specs=in_specs, out_specs=out_specs, check_vma=False)
```

```python
import functools

import jax
import jax.numpy as jnp
from jax import lax
from jax.experimental import pallas as pl
from jax.experimental.pallas import tpu as pltpu
from jax.sharding import PartitionSpec as P

HD = 64
IMG_DEV = 6
L_MOST = 3
HALF_S = 99
HALF_L = 289

CHUNK = 304
CHUNKS = 1 + L_MOST
PACKED = CHUNK * CHUNKS
SHARE = 8
PIECES = 4

EPSILON = 1e-06
LOWER = jnp.bfloat16
FLOAT = jnp.float32
MASKED = -1e30


def nn(a, b):
    return lax.dot_general(a, b, (((1,), (0,)), ((), ())), preferred_element_type=FLOAT)


def nt(a, b):
    return lax.dot_general(a, b, (((1,), (1,)), ((), ())), preferred_element_type=FLOAT)


def tn(a, b):
    return lax.dot_general(a, b, (((0,), (0,)), ((), ())), preferred_element_type=FLOAT)


LATER = pltpu.MemorySpace.HBM


def params(mib):
    return pltpu.CompilerParams(vmem_limit_bytes=mib * 1024 * 1024)


def cost(flops, bytes_accessed, transcendentals=0):
    return pl.CostEstimate(
        flops=flops, bytes_accessed=bytes_accessed, transcendentals=transcendentals
    )


def whole(shape, single=True):
    zeros = (0,) * len(shape)
    if single:
        return pl.BlockSpec(shape, lambda *_: zeros, pipeline_mode=pl.Buffered(1))
    return pl.BlockSpec(shape, lambda *_: zeros)


def rows_spec(width, height=CHUNK):
    return pl.BlockSpec((height, width), lambda c, *_: (c, 0))


def chunk_spec(height, width=CHUNK):
    return pl.BlockSpec((1, height, width), lambda c, *_: (c, 0, 0))


def call(kernel, name, mib, operands, in_specs, outs, scratch=(), flops=0, place=None, grid=None, far=()):
    if far:
        operands = [
            pltpu.with_memory_space_constraint(o, LATER) if i in far else o
            for i, o in enumerate(operands)
        ]
    specs = [o[2] for o in outs]
    shapes = [o[3](o[0], o[1]) if len(o) > 3 else jax.ShapeDtypeStruct(o[0], o[1]) for o in outs]
    scalars = () if place is None else (place,)
    made = pl.pallas_call(
        kernel,
        grid_spec=pltpu.PrefetchScalarGridSpec(
            num_scalar_prefetch=len(scalars),
            grid=grid or (CHUNKS,),
            in_specs=in_specs,
            out_specs=specs,
            scratch_shapes=scratch,
        ),
        out_shape=shapes,
        compiler_params=params(mib),
        cost_estimate=cost(flops // 1000000, 1000),
        name=name,
    )(*scalars, *operands)
    return list(made)


def slot_onehot(slots_ref, rows, chunk=0):
    named = jnp.transpose(slots_ref[chunk])[:, 0:1].astype(jnp.int32)
    places = lax.broadcasted_iota(jnp.int32, (CHUNK, rows), 1)
    return (places == named).astype(FLOAT).astype(LOWER)


def outside_image(slots_ref):
    image = jnp.transpose(slots_ref[0])[:, 1:2]
    return jnp.where(image == slots_ref[0, 1:2, :], 0.0, MASKED)


def choose_own(place, values, own):
    width = values.shape[1]
    source = lax.broadcasted_iota(jnp.int32, (width, own), 0)
    target = lax.broadcasted_iota(jnp.int32, (width, own), 1)
    onehot = (source == target + place * own).astype(FLOAT).astype(LOWER)
    return nn(values, onehot).astype(LOWER)


def norm_stats(values):
    average = jnp.mean(values, axis=-1, keepdims=True)
    centred = values - average
    variance = jnp.mean(centred * centred, axis=-1, keepdims=True)
    inverse = lax.rsqrt(variance + EPSILON)
    return centred * inverse, inverse


def pick_kernel(
    patches_ref, slots_ref, gains_ref, shifts_ref, router_ref, x_ref, n_ref, gate_ref
):
    x = nn(slot_onehot(slots_ref, patches_ref.shape[0]), patches_ref[...])
    x_ref[...] = x.astype(LOWER)
    scaled, _ = norm_stats(x)
    n_ref[...] = (scaled * gains_ref[0:1, :] + shifts_ref[0:1, :]).astype(LOWER)
    logit = jnp.sum(x * router_ref[...], axis=-1, keepdims=True)
    gate_ref[...] = jnp.broadcast_to(jax.nn.sigmoid(logit), gate_ref.shape)


def pick_rows(patches, slots, gains, shifts, router):
    rows, width = patches.shape
    return call(
        pick_kernel,
        "pick_rows",
        20,
        (patches, slots, gains, shifts, router),
        [
            whole((rows, width)),
            chunk_spec(8),
            whole((2, width)),
            whole((2, width)),
            whole((1, width)),
        ],
        [
            ((PACKED, width), LOWER, rows_spec(width)),
            ((PACKED, width), LOWER, rows_spec(width)),
            ((PACKED, 128), FLOAT, rows_spec(128)),
        ],
        flops=2 * PACKED * rows * width,
    )


def pick_cot_kernel(cot_ref, slots_ref, part_ref):
    for c in range(CHUNKS):
        onehot = slot_onehot(slots_ref, cot_ref.shape[1], c)
        part_ref[:, c * CHUNK : (c + 1) * CHUNK] = nt(cot_ref[...], onehot).astype(LOWER)


def pick_cot(cot_own, slots):
    own, rows = cot_own.shape
    return call(
        pick_cot_kernel,
        "pick_cot",
        24,
        (cot_own, slots),
        [whole((own, rows)), whole(slots.shape)],
        [((own, PACKED), LOWER, whole((own, PACKED)))],
        flops=2 * PACKED * rows * own,
        grid=(1,),
    )[0]


def own_columns_kernel(place_ref, patches_ref, patch_ref):
    own, width = patch_ref.shape[0], patches_ref.shape[1]
    source = lax.broadcasted_iota(jnp.int32, (own, width), 1)
    target = lax.broadcasted_iota(jnp.int32, (own, width), 0)
    chosen = (source == target + place_ref[0] * own).astype(FLOAT).astype(LOWER)
    patch_ref[...] = nt(chosen, patches_ref[...]).astype(LOWER)


def own_columns(place, patches, own):
    rows, width = patches.shape
    return call(
        own_columns_kernel,
        "own_columns",
        12,
        (patches,),
        [whole((rows, width))],
        [((own, rows), LOWER, whole((own, rows)), LATER)],
        flops=2 * own * rows * width,
        place=place,
        grid=(1,),
        far=(0,),
    )[0]


def head_slabs(own):
    slabs = []
    for start in range(0, own, 2 * HD):
        stop = min(start + 2 * HD, own)
        lanes = lax.broadcasted_iota(jnp.int32, (1, stop - start), 1)
        heads = []
        for head in range(start // HD, stop // HD):
            low = head * HD - start
            heads.append((head, (lanes >= low) & (lanes < low + HD)))
        slabs.append((start, stop, heads))
    return slabs


def keep(mask, values):
    return jnp.where(mask, values, jnp.zeros_like(values))


def forward_kernel(kind_ref, n_ref, bias_ref, slots_ref, *refs):
    proj_ref, mix_ref, lse_ref, weights_ref = refs[-4:]
    parts = refs[:-4]
    own = mix_ref.shape[1]

    @pl.when(pl.program_id(0) == 0)
    def _():
        if len(parts) == 1:
            weights_ref[...] = parts[0][...]
        else:
            for other, part_ref in enumerate(parts):
                held = part_ref.shape[0]
                start = pl.multiple_of((kind_ref[0] ^ other) * held, 32)
                weights_ref[pl.ds(start, held), :] = part_ref[...]

    proj_ref[...] = (nt(n_ref[...], weights_ref[0 : 3 * own, :]) + bias_ref[0]).astype(LOWER)
    outside = outside_image(slots_ref)
    lse_all = jnp.zeros((CHUNK, 128), FLOAT)
    lanes = lax.broadcasted_iota(jnp.int32, (1, 128), 1)
    for start, stop, heads in head_slabs(own):
        q = proj_ref[:, start:stop] * LOWER(HD**-0.5)
        k = proj_ref[:, own + start : own + stop]
        v = proj_ref[:, 2 * own + start : 2 * own + stop]
        mixed = None
        for head, mask in heads:
            scores = nt(q, keep(mask, k)) + outside
            largest = jnp.max(scores, axis=-1, keepdims=True)
            powered = jnp.exp(scores - largest)
            total = jnp.sum(powered, axis=-1, keepdims=True)
            probs = (powered * (1.0 / total)).astype(LOWER)
            part = nn(probs, keep(mask, v))
            mixed = part if mixed is None else mixed + part
            lse_all = jnp.where(lanes == head, largest + jnp.log(total), lse_all)
        mix_ref[:, start:stop] = mixed.astype(LOWER)
    lse_ref[0] = jnp.transpose(lse_all)[0:8, :]


def forward_quarter(kind, normed, biases, slots, parts, j):
    width = normed.shape[1]
    own = biases.shape[2] // 3
    return call(
        forward_kernel,
        "forward_quarter",
        11,
        (normed, biases, slots, *parts),
        [
            rows_spec(width),
            pl.BlockSpec((1, 1, 3 * own), lambda c, *_: (j, 0, 0)),
            chunk_spec(8),
            *[whole(p.shape) for p in parts],
        ],
        [
            ((PACKED, 3 * own), LOWER, rows_spec(3 * own), LATER),
            ((PACKED, own), LOWER, rows_spec(own)),
            ((CHUNKS, 8, CHUNK), FLOAT, chunk_spec(8), LATER),
            ((4 * own, width), LOWER, whole((4 * own, width))),
        ],
        flops=2 * PACKED * width * 8 * own,
        place=kind,
    )


def join_kernel(place_ref, x_ref, post_ref, own_post_ref, gains_ref, shifts_ref, *refs):
    hidden_ref, normed_ref, own_ref, chosen = refs[-4:]
    parts = refs[:-4]
    count = len(parts) // 2
    own = own_ref.shape[1]

    @pl.when(pl.program_id(0) == 0)
    def _():
        for j, out_ref in enumerate(parts[count:]):
            chosen[j * own : (j + 1) * own, :] = choose_own(place_ref[0], out_ref[...], own)

    attn, attn_own = post_ref[0:1, :], own_post_ref[0:1, :]
    for j, (mix_ref, out_ref) in enumerate(zip(parts[:count], parts[count:])):
        attn = attn + nn(mix_ref[...], out_ref[...])
        attn_own = attn_own + nn(mix_ref[...], chosen[j * own : (j + 1) * own, :])
    own_ref[...] = attn_own
    hidden = x_ref[...].astype(FLOAT) + attn
    hidden_ref[...] = hidden
    scaled, _ = norm_stats(hidden)
    normed_ref[...] = (scaled * gains_ref[1:2, :] + shifts_ref[1:2, :]).astype(LOWER)


def out_spec(own, width):
    return pl.BlockSpec((own, width), lambda *_: (3, 0), pipeline_mode=pl.Buffered(1))


def join_quarters(place, x, post, own_post, gains, shifts, mixes, weights):
    width = x.shape[1]
    own = mixes[0].shape[1]
    return call(
        join_kernel,
        "join_quarters",
        11,
        (x, post, own_post, gains, shifts, *mixes, *weights),
        [
            rows_spec(width),
            whole((2, width)),
            whole((2, own)),
            whole((2, width)),
            whole((2, width)),
            *[rows_spec(own) for _ in mixes],
            *[out_spec(own, width) for _ in weights],
        ],
        [
            ((PACKED, width), FLOAT, rows_spec(width), LATER),
            ((PACKED, width), LOWER, rows_spec(width)),
            ((PACKED, own), FLOAT, rows_spec(own), LATER),
        ],
        scratch=[pltpu.VMEM((len(weights) * own, own), LOWER)],
        flops=3 * PACKED * width * width,
        place=place,
    )


def stack_places(place, parts, stacked):
    size = len(parts)
    for j, part in enumerate(parts):
        own = part.shape[0]
        start = pl.multiple_of(lax.rem(place - j + size, size) * own, 64)
        stacked[pl.ds(start, own), :] = part.astype(stacked.dtype)


def cot_kernel(place_ref, gate_ref, *refs):
    cot_ref, gated_ref, stacked = refs[-3:]
    stack_places(place_ref[0], [r[...] for r in refs[:-3]], stacked)
    cot = jnp.transpose(stacked[...])
    cot_ref[...] = cot
    gated_ref[...] = (gate_ref[:, 0:1] * cot.astype(FLOAT)).astype(LOWER)


def cot_chunks(place, gate, parts):
    own = parts[0].shape[0]
    width = own * len(parts)
    return call(
        cot_kernel,
        "cot_chunks",
        20,
        (gate, *parts),
        [whole((PACKED, 128)), *[whole(p.shape) for p in parts]],
        [
            ((PACKED, width), LOWER, whole((PACKED, width)), LATER),
            ((PACKED, width), LOWER, whole((PACKED, width))),
        ],
        scratch=[pltpu.VMEM((width, PACKED), LOWER)],
        flops=PACKED * width,
        place=place,
        grid=(1,),
    )


def gelu_pair(u):
    cdf = 0.5 * (1.0 + lax.erf(u * (0.5**0.5)))
    density = jnp.exp(-0.5 * u * u) * 0.3989422804014327
    return u * cdf, cdf + u * density


def mlp_step(normed, gated, up_ref, down_ref, bias, own_down_ref):
    hidden = up_ref.shape[1]
    block = hidden // 3

    def products(start):
        cols = slice(start, start + block)
        pre_act = nn(normed, up_ref[:, cols]) + bias[:, cols]
        return pre_act, nt(gated, down_ref[cols, :])

    activations, grads, grad, gate, out = [], [], None, None, None
    ahead = products(0)
    for start in range(0, hidden, block):
        cols = slice(start, start + block)
        pre_act, grad_act = ahead
        if start + block < hidden:
            ahead = products(start + block)
        activation, slope = gelu_pair(pre_act)
        activation = activation.astype(LOWER)
        grad_pre = (grad_act * slope).astype(LOWER)
        gate_part = jnp.sum(activation.astype(FLOAT) * grad_act, axis=-1, keepdims=True)
        grad_part = nt(grad_pre, up_ref[:, cols])
        out_part = nn(activation, own_down_ref[cols, :])
        activations.append(activation)
        grads.append(grad_pre)
        grad = grad_part if grad is None else grad + grad_part
        gate = gate_part if gate is None else gate + gate_part
        out = out_part if out is None else out + out_part
    return activations, grads, grad, gate, out


def own_mlp_kernel(
    place_ref,
    n_ref,
    gated_ref,
    up_ref,
    down_ref,
    bias_ref,
    act_ref,
    pre_ref,
    grad_ref,
    gate_ref,
    out_ref,
    bias_sum_ref,
    own_down,
):
    @pl.when(pl.program_id(0) == 0)
    def _():
        own_down[...] = choose_own(place_ref[0], down_ref[...], own_down.shape[1])
        bias_sum_ref[...] = jnp.zeros_like(bias_sum_ref)

    activation, grad_pre, grad_part, gate_part, out_part = mlp_step(
        n_ref[...], gated_ref[...], up_ref, down_ref, bias_ref[...], own_down
    )
    block = activation[0].shape[1]
    for i, (act, pre) in enumerate(zip(activation, grad_pre)):
        act_ref[:, i * block : (i + 1) * block] = act
        pre_ref[:, i * block : (i + 1) * block] = pre
    grad_ref[...] = grad_part
    gate_ref[...] = jnp.broadcast_to(gate_part, gate_ref.shape)
    out_ref[...] = out_part
    bias_sum_ref[0:1, :] += jnp.sum(pre_ref[...].astype(FLOAT), axis=0, keepdims=True)


def own_mlp(place, normed, gated, up, down, bias, own):
    width, hidden = up.shape
    return call(
        own_mlp_kernel,
        "own_mlp",
        17,
        (normed, gated, up, down, bias),
        [
            rows_spec(width),
            rows_spec(width),
            whole((width, hidden)),
            whole((hidden, width)),
            whole((1, hidden)),
        ],
        [
            ((PACKED, hidden), LOWER, rows_spec(hidden)),
            ((PACKED, hidden), LOWER, rows_spec(hidden)),
            ((PACKED, width), FLOAT, rows_spec(width), LATER),
            ((PACKED, 128), FLOAT, rows_spec(128)),
            ((PACKED, own), FLOAT, rows_spec(own)),
            ((8, hidden), FLOAT, whole((8, hidden), False)),
        ],
        scratch=[pltpu.VMEM((hidden, own), LOWER)],
        flops=2 * PACKED * hidden * (3 * width + own),
        place=place,
    )


def own_grads_kernel(core_ref, n_ref, pre_ref, act_ref, gated_ref, kept_ref, sent_ref):
    grad_up = tn(n_ref[...], pre_ref[...])
    grad_down = tn(act_ref[...], gated_ref[...])

    @pl.when(core_ref[0] == 0)
    def _():
        kept_ref[...] = grad_up
        sent_ref[...] = grad_down.astype(LOWER)

    @pl.when(core_ref[0] == 1)
    def _():
        kept_ref[...] = grad_down
        sent_ref[...] = grad_up.astype(LOWER)


def own_grads(core, normed, grad_pre, act, gated):
    width = normed.shape[1]
    block = width // 3
    columns = pl.BlockSpec((PACKED, block), lambda c, *_: (0, c))
    return call(
        own_grads_kernel,
        "own_grads",
        16,
        (normed, grad_pre, act, gated),
        [columns, whole((PACKED, width)), columns, whole((PACKED, width))],
        [
            ((width, width), FLOAT, rows_spec(width, block)),
            ((width, width), LOWER, rows_spec(width, block)),
        ],
        flops=4 * PACKED * width * width,
        place=core,
        grid=(3,),
    )


def other_mlp_kernel(
    last, place_ref, n_ref, gated_ref, grad_in_ref, gate_in_ref, out_in_ref, *refs
):
    grad_ref, gate_ref, out_ref, up, down, own_down = refs[-6:]
    ups, downs = refs[0:4], refs[4:8]
    part = downs[0].shape[2]
    width = up.shape[1]

    @pl.when(pl.program_id(0) == 0)
    def _():
        for side in range(2):
            for c in range(2):
                for near in range(2):
                    to_up = place_ref[1] ^ (4 * side + 2 * near + c)
                    to_down = place_ref[1] ^ (4 * near + 2 * side + c)
                    up_rows = pl.ds(pl.multiple_of(to_up * part, 32), part)
                    down_rows = pl.ds(pl.multiple_of(to_down * part, 32), part)
                    up[up_rows, :] = ups[side + 2 * c][near, 0, 0:part]
                    down[down_rows, :] = downs[side + 2 * c][near, 0]
        own_down[...] = choose_own(place_ref[0], down[...], own_down.shape[1])

    pieces = ups[0][0, 0, part : part + 16].astype(FLOAT)
    bias = pieces[0:1] + (pieces[1:2] + pieces[2:3])
    _, _, grad_part, gate_part, out_part = mlp_step(
        n_ref[...], gated_ref[...], up, down, bias, own_down
    )
    grad_ref[...] = grad_in_ref[...] + grad_part
    gate_ref[...] = gate_in_ref[...] + gate_part
    if last:
        attn_ref, post_ref, open_ref = refs[8:11]
        total = out_in_ref[...] + out_part + attn_ref[...] + post_ref[1:2, :]
        out_ref[...] = open_ref[:, 0:1] * total
    else:
        out_ref[...] = out_in_ref[...] + out_part


def other_mlp(places, normed, gated, sums, ups, downs, j, extra=()):
    width = normed.shape[1]
    own = sums[2].shape[1]
    last = len(extra) > 0
    held = lambda array: pl.BlockSpec(
        (2, 1, *array.shape[2:]), lambda c, *_: (0, j, 0, 0), pipeline_mode=pl.Buffered(1)
    )
    extra_specs = [rows_spec(own), whole((2, own)), rows_spec(128)] if last else []
    return call(
        functools.partial(other_mlp_kernel, last),
        "other_mlp",
        19,
        (normed, gated, *sums, *ups, *downs, *extra),
        [
            rows_spec(width),
            rows_spec(width),
            rows_spec(width),
            rows_spec(128),
            rows_spec(own),
            *[held(u) for u in ups],
            *[held(d) for d in downs],
            *extra_specs,
        ],
        [
            ((PACKED, width), FLOAT, rows_spec(width)),
            ((PACKED, 128), FLOAT, rows_spec(128)),
            ((PACKED, own), FLOAT, rows_spec(own)),
        ],
        scratch=[
            pltpu.VMEM((width, width), LOWER),
            pltpu.VMEM((width, width), LOWER),
            pltpu.VMEM((width, own), LOWER),
        ],
        flops=2 * PACKED * width * (3 * width + own),
        place=places,
    )


def second_norm_kernel(
    grad_ref,
    gate_part_ref,
    hidden_ref,
    x_ref,
    cot_ref,
    gate_ref,
    post_ref,
    gains_ref,
    ghid_ref,
    glow_ref,
    logit_ref,
    sums_ref,
):
    @pl.when(pl.program_id(0) == 0)
    def _():
        sums_ref[...] = jnp.zeros_like(sums_ref)

    hidden = hidden_ref[...]
    scaled, inverse = norm_stats(hidden)
    grad_out = grad_ref[...]
    weighted = grad_out * gains_ref[1:2, :]
    centre_term = jnp.mean(weighted, axis=-1, keepdims=True)
    scale_term = jnp.mean(weighted * scaled, axis=-1, keepdims=True)
    grad_hidden = inverse * (weighted - centre_term - scaled * scale_term)
    gate = gate_ref[:, 0:1]
    gated = gate * cot_ref[...].astype(FLOAT)
    grad_attn = grad_hidden + gated
    ghid_ref[...] = grad_hidden
    glow_ref[...] = grad_attn.astype(LOWER)
    attn = hidden - x_ref[...].astype(FLOAT)
    dotted = jnp.sum(gated * (attn + post_ref[1:2, :]), axis=-1, keepdims=True)
    logit = (1.0 - gate) * (dotted + gate_part_ref[:, 0:1])
    logit_ref[...] = jnp.broadcast_to(logit, logit_ref.shape)
    sums_ref[0:1, :] += jnp.sum(grad_out * scaled, axis=0, keepdims=True)
    sums_ref[1:2, :] += jnp.sum(grad_out, axis=0, keepdims=True)
    sums_ref[2:3, :] += jnp.sum(grad_attn, axis=0, keepdims=True)
    sums_ref[3:4, :] += jnp.sum(gated, axis=0, keepdims=True)


def second_norm(grad, gate_part, hidden, x, cot_rows, gate, post, gains):
    width = x.shape[1]
    return call(
        second_norm_kernel,
        "second_norm",
        15,
        (grad, gate_part, hidden, x, cot_rows, gate, post, gains),
        [
            rows_spec(width),
            rows_spec(128),
            rows_spec(width),
            rows_spec(width),
            rows_spec(width),
            rows_spec(128),
            whole((2, width)),
            whole((2, width)),
        ],
        [
            ((PACKED, width), FLOAT, rows_spec(width)),
            ((PACKED, width), LOWER, rows_spec(width)),
            ((PACKED, 128), FLOAT, rows_spec(128)),
            ((8, width), FLOAT, whole((8, width), False)),
        ],
        flops=20 * PACKED * width,
    )


def backward_kernel(low_ref, slots_ref, proj_ref, lse_ref, out_ref, gproj_ref, sums_ref):
    @pl.when(pl.program_id(0) == 0)
    def _():
        sums_ref[...] = jnp.zeros_like(sums_ref)

    outside = outside_image(slots_ref)
    own = out_ref.shape[0]
    heads = own // HD
    g = nt(low_ref[...], out_ref[...]).astype(LOWER)
    q = proj_ref[:, 0:own] * LOWER(HD**-0.5)
    k = proj_ref[:, own : 2 * own]
    v = proj_ref[:, 2 * own : 3 * own]
    lanes = lax.broadcasted_iota(jnp.int32, (1, own), 1) // HD
    keys = jnp.concatenate([keep(lanes == head, k) for head in range(heads)], axis=0)
    values = jnp.concatenate([keep(lanes == head, v) for head in range(heads)], axis=0)
    scores = nt(keys, q)
    grad_probs = nt(values, g)
    probs, grad_scores = [], []
    for head in range(heads):
        rows = slice(head * CHUNK, (head + 1) * CHUNK)
        prob = jnp.exp(scores[rows] + outside - lse_ref[0, head : head + 1, :])
        inner = jnp.sum(prob * grad_probs[rows], axis=0, keepdims=True)
        grad_scores.append((prob * (grad_probs[rows] - inner)).astype(LOWER))
        probs.append(prob.astype(LOWER))
    grad_scores = jnp.concatenate(grad_scores, axis=0)
    all_v = nn(jnp.concatenate(probs, axis=0), g)
    all_k = nn(grad_scores, q)
    grad_q = tn(grad_scores, keys)
    grad_k, grad_v = all_k[0:CHUNK], all_v[0:CHUNK]
    for head in range(1, heads):
        rows = slice(head * CHUNK, (head + 1) * CHUNK)
        grad_k = jnp.where(lanes == head, all_k[rows], grad_k)
        grad_v = jnp.where(lanes == head, all_v[rows], grad_v)
    gproj_ref[:, 0:own] = (grad_q * HD**-0.5).astype(LOWER)
    gproj_ref[:, own : 2 * own] = grad_k.astype(LOWER)
    gproj_ref[:, 2 * own : 3 * own] = grad_v.astype(LOWER)
    sums_ref[0:1, :] += jnp.sum(gproj_ref[...].astype(FLOAT), axis=0, keepdims=True)


def backward_quarter(low, slots, proj, lse, weights):
    width = low.shape[1]
    own = proj.shape[1] // 3
    return call(
        backward_kernel,
        "backward_quarter",
        20,
        (low, slots, proj, lse, weights),
        [
            rows_spec(width),
            chunk_spec(8),
            rows_spec(3 * own),
            chunk_spec(8),
            out_spec(own, width),
        ],
        [
            ((PACKED, 3 * own), LOWER, rows_spec(3 * own)),
            ((8, 3 * own), FLOAT, whole((8, 3 * own), False)),
        ],
        flops=2 * PACKED * width * 14 * own,
    )


def attn_grads_kernel(core_ref, gproj_ref, normed_ref, mix_ref, low_ref, kept_ref, sent_ref):
    half = kept_ref.shape[0]
    rest = gproj_ref.shape[1] - half
    normed = normed_ref[...]
    first = tn(gproj_ref[:, 0:half], normed)
    second = tn(gproj_ref[:, half:], normed)
    third = tn(mix_ref[...], low_ref[...])

    @pl.when(core_ref[0] == 0)
    def _():
        kept_ref[...] = first
        sent_ref[0:rest, :] = second.astype(LOWER)
        sent_ref[rest:half, :] = third.astype(LOWER)

    @pl.when(core_ref[0] == 1)
    def _():
        kept_ref[0:rest, :] = second
        kept_ref[rest:half, :] = third
        sent_ref[...] = first.astype(LOWER)


def attn_grads(core, gproj, normed, mix, low):
    width, own = normed.shape[1], mix.shape[1]
    operands = (gproj, normed, mix, low)
    return call(
        attn_grads_kernel,
        "attn_grads",
        18,
        operands,
        [whole(o.shape) for o in operands],
        [
            ((2 * own, width), FLOAT, whole((2 * own, width))),
            ((2 * own, width), LOWER, whole((2 * own, width))),
        ],
        place=core,
        grid=(1,),
    )


def first_norm_kernel(x_ref, ghid_ref, logit_ref, gains_ref, router_ref, *refs):
    rows_ref, sums_ref = refs[-2:]
    parts = refs[:-2]
    count = len(parts) // 2

    @pl.when(pl.program_id(0) == 0)
    def _():
        sums_ref[...] = jnp.zeros_like(sums_ref)

    grad_out = None
    for gproj_ref, weights_ref in zip(parts[:count], parts[count:]):
        part = nn(gproj_ref[...], weights_ref[0 : gproj_ref.shape[1], :])
        grad_out = part if grad_out is None else grad_out + part
    x = x_ref[...].astype(FLOAT)
    scaled, inverse = norm_stats(x)
    weighted = grad_out * gains_ref[0:1, :]
    centre_term = jnp.mean(weighted, axis=-1, keepdims=True)
    scale_term = jnp.mean(weighted * scaled, axis=-1, keepdims=True)
    grad_norm = inverse * (weighted - centre_term - scaled * scale_term)
    logit = logit_ref[:, 0:1]
    rows_ref[...] = (ghid_ref[...] + grad_norm + logit * router_ref[...]).astype(LOWER)
    sums_ref[0:1, :] += jnp.sum(grad_out * scaled, axis=0, keepdims=True)
    sums_ref[1:2, :] += jnp.sum(grad_out, axis=0, keepdims=True)
    sums_ref[2:3, :] += jnp.sum(logit * x, axis=0, keepdims=True)


def first_norm(x, ghid, logit, gains, router, gprojs, weights):
    width = x.shape[1]
    return call(
        first_norm_kernel,
        "first_norm",
        18,
        (x, ghid, logit, gains, router, *gprojs, *weights),
        [
            rows_spec(width),
            rows_spec(width),
            rows_spec(128),
            whole((2, width)),
            whole((1, width)),
            *[rows_spec(g.shape[1]) for g in gprojs],
            *[whole(w.shape) for w in weights],
        ],
        [
            ((PACKED, width), LOWER, rows_spec(width)),
            ((8, width), FLOAT, whole((8, width), False)),
        ],
        flops=2 * PACKED * width * 3 * width,
    )


def scatter_kernel(place_ref, named_ref, rows_ref, branch_ref, patch_ref, *refs):
    out_ref, block_ref, stacked, branch_t, total, own_total = refs[-6:]
    block = out_ref.shape[0]
    first = pl.program_id(0) * block

    @pl.when(pl.program_id(0) == 0)
    def _():
        for c in range(CHUNKS):
            part = branch_ref[c * CHUNK : (c + 1) * CHUNK, :]
            branch_t[c] = jnp.transpose(part).astype(LOWER)

    stack_places(place_ref[0], [r[...] for r in refs[:-6]], stacked)
    total[...] = jnp.transpose(stacked[...]).astype(FLOAT)
    own_total[...] = patch_ref[...].astype(FLOAT)
    for c in range(CHUNKS):
        low, high = place_ref[1 + 2 * c], place_ref[2 + 2 * c]

        @pl.when((low < first + block) & (high >= first))
        def _():
            places = lax.broadcasted_iota(jnp.int32, (block, CHUNK), 0) + first
            onehot = (places == named_ref[c, 0:1, :].astype(jnp.int32)).astype(FLOAT).astype(LOWER)
            total[...] += nn(onehot, rows_ref[c * CHUNK : (c + 1) * CHUNK, :])
            own_total[...] += nt(branch_t[c], onehot)

    out_ref[...] = total[...].astype(LOWER)
    block_ref[...] = own_total[...].astype(LOWER)


def scatter_rows(places, cot_parts, slots, rows, branch, patch_t):
    own, total = cot_parts[0].shape
    width = own * len(cot_parts)
    block = 512
    columns = pl.BlockSpec((own, block), lambda c, *_: (0, c))
    return call(
        scatter_kernel,
        "scatter_rows",
        19,
        (slots, rows, branch, patch_t, *cot_parts),
        [
            whole(slots.shape),
            whole((PACKED, width)),
            whole((PACKED, own)),
            columns,
            *[columns for _ in cot_parts],
        ],
        [
            ((total, width), LOWER, rows_spec(width, block), LATER),
            ((own, total), LOWER, columns, LATER),
        ],
        scratch=[
            pltpu.VMEM((width, block), LOWER),
            pltpu.VMEM((CHUNKS, own, CHUNK), LOWER),
            pltpu.VMEM((block, width), FLOAT),
            pltpu.VMEM((own, block), FLOAT),
        ],
        flops=2 * PACKED * total * width,
        place=places,
        grid=(pl.cdiv(total, block),),
        far=range(3, 4 + len(cot_parts)),
    )


def halve_kernel(upper_ref, kept_ref, came_ref, half_ref, sent_ref):
    block, half = half_ref.shape[0], kept_ref.shape[0] // 2
    step = pl.program_id(0) * block
    own = pl.ds(pl.multiple_of(upper_ref[0] * half + step, 16), block)
    far = pl.ds(pl.multiple_of((1 - upper_ref[0]) * half + step, 16), block)
    half_ref[...] = kept_ref[own, :] + came_ref[own, :].astype(FLOAT)
    sent_ref[...] = (kept_ref[far, :] + came_ref[far, :].astype(FLOAT)).astype(LOWER)


def halve_sum(upper, kept, came):
    rows, width = kept.shape
    return call(
        halve_kernel,
        "halve_sum",
        10,
        (kept, came),
        [whole((rows, width)), whole((rows, width))],
        [
            ((rows // 2, width), FLOAT, rows_spec(width, rows // 4)),
            ((rows // 2, width), LOWER, rows_spec(width, rows // 4)),
        ],
        place=upper,
        grid=(2,),
    )


def finish_kernel(core_ref, attn_ref, attn_far_ref, mlp_ref, mlp_far_ref, *refs):
    qkv_ref, out_ref, up_ref, down_ref = refs
    own, block = qkv_ref.shape[0], up_ref.shape[0]
    head = pl.program_id(0)
    rows = pl.ds(pl.multiple_of(head * block, 16), block)

    def write(low_ref, high_ref, first_ref, second_ref):
        one = pl.ds(pl.multiple_of(head * HD, HD), HD)
        two = pl.ds(pl.multiple_of(own + head * HD, HD), HD)
        qkv_ref[0:HD, :] = low_ref[one, :].astype(FLOAT)
        qkv_ref[HD : 2 * HD, :] = low_ref[two, :].astype(FLOAT)
        qkv_ref[2 * HD : 3 * HD, :] = high_ref[one, :].astype(FLOAT)
        out_ref[...] = high_ref[two, :].astype(FLOAT)
        up_ref[...] = first_ref[rows, :].astype(FLOAT)
        down_ref[...] = second_ref[rows, :].astype(FLOAT)

    @pl.when(core_ref[0] == 0)
    def _():
        write(attn_ref, attn_far_ref, mlp_ref, mlp_far_ref)

    @pl.when(core_ref[0] == 1)
    def _():
        write(attn_far_ref, attn_ref, mlp_far_ref, mlp_ref)


def finish_grads(core, attn, attn_far, mlp, mlp_far):
    width = mlp.shape[1]
    own = attn.shape[0] // 2
    heads = own // HD
    return call(
        finish_kernel,
        "finish_grads",
        16,
        (attn, attn_far, mlp, mlp_far),
        [whole(attn.shape), whole(attn.shape), whole(mlp.shape), whole(mlp.shape)],
        [
            ((3 * own, width), FLOAT, rows_spec(width, 3 * HD)),
            ((own, width), FLOAT, rows_spec(width, HD)),
            ((width, width), FLOAT, rows_spec(width, width // heads)),
            ((width, width), FLOAT, rows_spec(width, width // heads)),
        ],
        place=core,
        grid=(heads,),
    )


def finish_sums_kernel(own_ref, far_ref, *refs):
    gains_ref, shifts_ref, post_ref, up_ref, router_ref, qkv_ref = refs
    total = own_ref[...] + far_ref[...]
    own = qkv_ref.shape[1]
    gains_ref[0:1, :] = total[4:5]
    gains_ref[1:2, :] = total[0:1]
    shifts_ref[0:1, :] = total[5:6]
    shifts_ref[1:2, :] = total[1:2]
    post_ref[...] = total[2:4]
    up_ref[...] = total[7]
    router_ref[...] = total[6]
    qkv_ref[0:1, :] = total[8:9, 0:own]
    qkv_ref[1:2, :] = total[8:9, 2 * own : 3 * own]


def finish_sums(small, far, own):
    rows, width = small.shape
    shapes = [(2, width), (2, width), (2, width), (width,), (width,), (2, own)]
    return call(
        finish_sums_kernel,
        "finish_sums",
        4,
        (small, far),
        [whole((rows, width)), whole((rows, width))],
        [(shape, FLOAT, whole(shape)) for shape in shapes],
        grid=(1,),
    )


def turned(values, place):
    size = values.shape[0]
    back = jnp.concatenate([values[:1], values[:0:-1]], axis=0)
    twice = jnp.concatenate([back, back], axis=0)
    return lax.dynamic_slice_in_dim(twice, (size - place) % size, size, 0)


def after(value, *others):
    return lax.optimization_barrier((value, *others))[0]


def ring_step(value, size):
    return lax.ppermute(value, "mlp", [(i, (i + 1) % size) for i in range(size)])


def swap(value, bit, size):
    return lax.ppermute(value, "rows", [(i, i ^ (1 << bit)) for i in range(size)])


def bits_of(size):
    return [b for b in range(20) if (1 << b) < size]


def pack_slots(picked, live_slots):
    small = IMG_DEV * HALF_S
    named = jnp.where(live_slots == 1, picked, -1)

    def padded(parts, fill):
        have = sum(p.shape[0] for p in parts)
        return jnp.concatenate([*parts, jnp.full((CHUNK - have,), fill, jnp.int32)])

    always = IMG_DEV - L_MOST
    idx = [padded([named[: always * HALF_S]], -1)]
    seg = [padded([jnp.repeat(jnp.arange(always, dtype=jnp.int32), HALF_S)], always)]
    for j in range(L_MOST):
        first = small + j * HALF_L
        alive = live_slots[first] == 1
        other = IMG_DEV - 1 - j
        large_idx = padded([named[first : first + HALF_L]], -1)
        small_idx = padded([named[other * HALF_S : (other + 1) * HALF_S]], -1)
        idx.append(jnp.where(alive, large_idx, small_idx))
        length = jnp.where(alive, HALF_L, HALF_S)
        seg.append((jnp.arange(CHUNK, dtype=jnp.int32) >= length).astype(jnp.int32))
    named = jnp.stack(idx)
    low = jnp.min(jnp.where(named < 0, 1 << 24, named), axis=1)
    bounds = jnp.stack([low, jnp.max(named, axis=1)], axis=1).reshape(2 * CHUNKS)
    idx, seg = jnp.stack(idx).astype(FLOAT), jnp.stack(seg).astype(FLOAT)
    rows = lax.broadcasted_iota(jnp.int32, (1, 8, 1), 1)
    return jnp.where(rows == 0, idx[:, None, :], seg[:, None, :]), bounds


def local(
    rows_size,
    mlp_size,
    patches,
    w_qkv,
    qkv_bias,
    w_out,
    post_bias,
    w_up,
    up_bias,
    w_down,
    norm_gains,
    norm_shifts,
    router,
    picked,
    live_slots,
    cotangent,
):
    width = patches.shape[1]
    mlp_index = lax.axis_index("mlp")
    rows_index = lax.axis_index("rows")
    share_index = rows_index % SHARE
    core = rows_index & 1
    place = mlp_index.astype(jnp.int32).reshape(1)
    places = jnp.stack([mlp_index, share_index]).astype(jnp.int32)
    kind = (rows_index % PIECES).astype(jnp.int32).reshape(1)
    own = w_out.shape[0]
    heads_here = own // HD
    others = mlp_size - 1
    router_row = router.reshape(1, width)

    def swapped(value, bit):
        return swap(value, bit, rows_size)

    own_weights = jnp.concatenate(
        [
            w_qkv.T.reshape(heads_here, 3, HD, width).transpose(1, 0, 2, 3).reshape(3 * own, width),
            w_out,
        ],
        axis=0,
    )
    held = own_weights.shape[0] // PIECES
    piece = lax.dynamic_slice_in_dim(own_weights, kind[0] * held, held, 0)
    part = w_up.shape[0] // SHARE
    top = lax.reduce_precision(up_bias, 8, 7)
    middle = lax.reduce_precision(up_bias - top, 8, 7)
    bias_rows = jnp.stack([top, middle, up_bias - top - middle]).astype(LOWER)
    payload = jnp.concatenate(
        [
            piece,
            lax.dynamic_slice_in_dim(w_up, share_index * part, part, 0),
            jnp.pad(bias_rows, ((0, 13), (0, 0))),
            lax.dynamic_slice_in_dim(w_down, share_index * part, part, 0),
        ],
        axis=0,
    )
    def around(value):
        return ring_step(value, mlp_size)

    kinds = jnp.stack([qkv_bias[0], jnp.zeros_like(qkv_bias[0]), qkv_bias[1]])
    biases = turned(kinds.reshape(3, mlp_size, own).transpose(1, 0, 2), mlp_index)
    biases = biases.reshape(mlp_size, 1, 3 * own)
    own_post = lax.dynamic_slice_in_dim(post_bias, mlp_index * own, own, 1)
    slots, bounds = pack_slots(picked, live_slots)
    bounds = jnp.concatenate([place, bounds])
    cot_own = cotangent.T
    core_one = core.astype(jnp.int32).reshape(1)

    def split(came):
        return came[:held], came[held : held + part + 16], came[held + part + 16 :]

    def across(value, mask):
        return lax.ppermute(value, "rows", [(i, i ^ mask) for i in range(rows_size)])

    def forward(j, normed, parts):
        return forward_quarter(kind, normed, biases, slots, parts, j)

    order = bits_of(rows_size)
    lower = {bit: (rows_index >> bit) & 1 == 0 for bit in order}
    upper = {bit: ((rows_index >> bit) & 1).astype(jnp.int32).reshape(1) for bit in order}
    payload, place, places, kind, core_one, lower, upper, own_post, biases = lax.optimization_barrier(
        (payload, place, places, kind, core_one, lower, upper, own_post, biases)
    )
    came = around(payload)
    patches, bounds = lax.optimization_barrier((after(patches, payload), bounds))
    x, normed_one, gate = pick_rows(
        patches, slots, norm_gains, norm_shifts, router_row
    )
    came = after(came, x)
    cot_part = pick_cot(after(cot_own, came), slots)
    normed_one = after(normed_one, cot_part)
    quarters, cot_parts, up_parts, down_parts = [], [cot_part], [], []
    parts, before = [own_weights], x
    for j in range(mlp_size):
        if j < others:
            came = after(came, before)
            got, up_part, down_part = split(came)
            up_parts.append(up_part)
            down_parts.append(down_part)
            if j + 1 < others:
                came = around(came)
            spread = [got, *[across(got, mask) for mask in range(2, PIECES, 2)]]
        if 0 < j < others:
            cot_parts.append(around(after(cot_parts[-1], got)))
        normed_one = after(normed_one, got, before, *parts)
        if j == others:
            normed_one = after(normed_one, *cot_parts[:-1])
            ups, downs = jnp.stack(up_parts), jnp.stack(down_parts)
            ups_x, downs_y = swapped(ups, 1), swapped(downs, 2)
        quarters.append(forward(j, normed_one, parts))
        before = quarters[-1][1]
        if j < others:
            spread = [after(v, before) for v in spread]
            parts = [w for v in spread for w in (v, swapped(v, 0))]

    projs, mixes, lses, weights = zip(*quarters)
    cot_last = after(cot_parts[-1], before)
    ups_x, downs_y = after(ups_x, cot_last), after(downs_y, cot_last)
    cot_parts.append(around(cot_last))
    ups, downs = jnp.stack([ups, ups_x]), jnp.stack([downs, downs_y])
    ups_y, downs_x = swapped(ups, 2), swapped(downs, 1)
    hidden, normed_two, attn_own = join_quarters(
        place, after(x, cot_last), post_bias, own_post, norm_gains, norm_shifts, mixes, weights
    )
    patch_t = own_columns(place, after(patches, normed_two), own)
    cot_rows, gated = cot_chunks(place, after(gate, normed_two, patch_t), cot_parts)
    full_parts = [cot_own, around(after(cot_own, gated))]

    def full_due(slot, value):
        if slot in ("N2", "B2"):
            full_parts.append(around(after(full_parts[-1], value)))
            return after(value, full_parts[-2])
        return value

    act, grad_pre, *sums, up_bias_sum = own_mlp(
        place, normed_two, gated, w_up, w_down, up_bias.reshape(1, -1), own
    )
    ups_y, downs_x = after(ups_y, sums[0]), after(downs_x, sums[0])
    more = [swapped(v, 0) for v in (ups, ups_y, downs, downs_x)]
    kept, sent = own_grads(core_one, normed_two, after(grad_pre, ups_y, downs_x), act, gated)
    more = [after(v, kept) for v in more]
    ups, downs = [ups, ups_y, *more[:2]], [downs, downs_x, *more[2:]]
    sent = after(sent, *more)

    turned_order = [order[0], *order[:0:-1]]

    def halves(kept, came, bit):
        if kept.shape[0] % 64 == 0:
            return halve_sum(upper[bit], kept, came)
        value = kept + came.astype(FLOAT)
        pair = value.reshape(2, value.shape[0] // 2, width)
        return (
            jnp.where(lower[bit], pair[0], pair[1]),
            jnp.where(lower[bit], pair[1], pair[0]).astype(LOWER),
        )

    def joined(value, other, bit):
        first, second = jnp.where(lower[bit], value, other), jnp.where(lower[bit], other, value)
        return jnp.concatenate([first, second], axis=0)

    def halve_middle(kept, came, bits):
        for bit in bits[2:-1]:
            kept, sent = halves(kept, came, bit)
            came = swapped(sent, bit)
        return halves(kept, came, bits[-1])

    def join_middle(value, bits):
        for bit in bits[-2:1:-1]:
            value = joined(value, swapped(value, bit), bit)
        return value

    came_c = swapped(sent, 0)
    sums[0] = after(sums[0], kept, *more)
    for j in range(others):
        sums[0] = full_due(f"M{j}", sums[0])
        last_quarter = (attn_own, own_post, gate) if j == others - 1 else ()
        sums = other_mlp(places, normed_two, gated, sums, ups, downs, j, last_quarter)
        if j == 0:
            kept, sent = halves(kept, after(came_c, sums[0]), order[1])
            came_x = swapped(sent, order[1])
            sums[0] = after(sums[0], sent)
    grad_two, gate_part, branch = sums
    came_x = after(came_x, grad_two)
    grad_two = full_due("N2", grad_two)
    grad_two = after(grad_two, came_x)
    kept, sent = halve_middle(kept, came_x, order)
    came_y = swapped(sent, order[-1])
    grad_hidden, grad_low, logit, sums_two = second_norm(
        after(grad_two, kept), gate_part, hidden, x, cot_rows, gate, post_bias, norm_gains
    )
    own_proj, bias_grad = backward_quarter(
        full_due("B0", grad_low), slots, projs[0], lses[0], weights[0]
    )
    kept_a, sent_a = attn_grads(core_one, own_proj, normed_one, mixes[0], grad_low)
    gprojs = [own_proj]
    came_a = swapped(sent_a, 0)
    d_mlp = (kept + after(came_y, kept_a).astype(FLOAT)).astype(LOWER)
    other = swapped(d_mlp, order[-1])
    low = full_due("B1", after(grad_low, kept_a, d_mlp))
    gprojs.append(backward_quarter(low, slots, projs[1], lses[1], weights[1])[0])
    kept_a, sent_a = halves(kept_a, after(came_a, gprojs[-1]), turned_order[1])
    came_a = swapped(sent_a, turned_order[1])
    d_mlp = join_middle(joined(d_mlp, after(other, gprojs[-1]), order[-1]), order)
    other = swapped(d_mlp, order[1])
    low = full_due("B2", after(low, gprojs[-1], d_mlp, kept_a))
    gprojs.append(backward_quarter(low, slots, projs[2], lses[2], weights[2])[0])
    kept_a, sent_a = halve_middle(kept_a, after(came_a, gprojs[-1]), turned_order)
    came_a = swapped(sent_a, turned_order[-1])
    low = full_due("B3", after(low, gprojs[-1], kept_a))
    for j in range(3, mlp_size):
        gprojs.append(backward_quarter(low, slots, projs[j], lses[j], weights[j])[0])
    d_attn = (kept_a + after(came_a, gprojs[-1]).astype(FLOAT)).astype(LOWER)
    near, far = turned_order[-1], turned_order[-2]
    others_a = [
        lax.ppermute(d_attn, "rows", [(i, i ^ mask) for i in range(rows_size)])
        for mask in (1 << near, 1 << far, (1 << near) | (1 << far))
    ]
    d_mlp = joined(d_mlp, after(other, gprojs[-1]), order[1])
    other = swapped(d_mlp, 0)
    rows_grad, sums_one = first_norm(
        x, grad_hidden, after(logit, gprojs[-1], d_attn, d_mlp), norm_gains, router_row, gprojs, weights
    )
    others_a = [after(v, rows_grad) for v in others_a]
    d_attn = joined(joined(d_attn, others_a[0], near), joined(others_a[1], others_a[2], near), far)
    for bit in turned_order[-3:0:-1]:
        d_attn = joined(d_attn, swapped(d_attn, bit), bit)
    other_a = swapped(d_attn, 0)
    small = jnp.concatenate(
        [
            sums_two[:4],
            sums_one[:3],
            up_bias_sum[:1],
            jnp.pad(bias_grad[:1], ((0, 0), (0, width - 3 * own))),
        ],
        axis=0,
    )
    small = small + swapped(small, 0)
    other_s = swapped(small, order[1])
    input_grad, block_out = scatter_rows(
        bounds, full_parts, slots, after(rows_grad, small, d_attn), branch, patch_t
    )
    block_out = block_out.T
    small = small + after(other_s, input_grad)
    for bit in order[2:-1]:
        small = small + swapped(small, bit)
    other_s = swapped(small, order[-1])
    d_qkv, d_out, d_up, d_down = finish_grads(
        core_one, d_attn, after(other_a, input_grad, small), d_mlp, other
    )
    small, other_s = after(small, d_qkv), after(other_s, d_qkv)
    d_gains, d_shifts, d_post_bias, d_up_bias, d_router, d_qkv_bias = finish_sums(small, other_s, own)
    d_qkv = d_qkv.T
    return (
        block_out,
        input_grad,
        d_qkv,
        d_qkv_bias,
        d_out,
        d_post_bias,
        d_up,
        d_up_bias,
        d_down,
        d_gains,
        d_shifts,
        d_router,
    )


def solution(mesh):
    in_specs = (
        P("rows", None),
        P(None, "mlp"),
        P(),
        P("mlp", None),
        P(),
        P(None, "mlp"),
        P("mlp"),
        P("mlp", None),
        P(),
        P(),
        P(),
        P("rows"),
        P("rows"),
        P("rows", "mlp"),
    )
    out_specs = (
        P("rows", "mlp"),
        P("rows", None),
        P(None, "mlp"),
        P(None, "mlp"),
        P("mlp", None),
        P(),
        P(None, "mlp"),
        P("mlp"),
        P("mlp", None),
        P(),
        P(),
        P(),
    )
    body = functools.partial(local, mesh.shape["rows"], mesh.shape["mlp"])
    return jax.shard_map(body, mesh=mesh, in_specs=in_specs, out_specs=out_specs, check_vma=False)
```

```python
import functools

import jax
import jax.numpy as jnp
from jax import lax
from jax.experimental import pallas as pl
from jax.experimental.pallas import tpu as pltpu
from jax.sharding import PartitionSpec as P

HD = 64
IMG_DEV = 6
L_MOST = 3
HALF_S = 99
HALF_L = 289

CHUNK = 304
CHUNKS = 1 + L_MOST
PACKED = CHUNK * CHUNKS
SHARE = 8
PIECES = 4

EPSILON = 1e-06
LOWER = jnp.bfloat16
FLOAT = jnp.float32
MASKED = -1e30


def nn(a, b):
    return lax.dot_general(a, b, (((1,), (0,)), ((), ())), preferred_element_type=FLOAT)


def nt(a, b):
    return lax.dot_general(a, b, (((1,), (1,)), ((), ())), preferred_element_type=FLOAT)


def tn(a, b):
    return lax.dot_general(a, b, (((0,), (0,)), ((), ())), preferred_element_type=FLOAT)


LATER = pltpu.MemorySpace.HBM


def params(mib):
    return pltpu.CompilerParams(vmem_limit_bytes=mib * 1024 * 1024)


def cost(flops, bytes_accessed, transcendentals=0):
    return pl.CostEstimate(
        flops=flops, bytes_accessed=bytes_accessed, transcendentals=transcendentals
    )


def whole(shape, single=True):
    zeros = (0,) * len(shape)
    if single:
        return pl.BlockSpec(shape, lambda *_: zeros, pipeline_mode=pl.Buffered(1))
    return pl.BlockSpec(shape, lambda *_: zeros)


def rows_spec(width, height=CHUNK):
    return pl.BlockSpec((height, width), lambda c, *_: (c, 0))


def chunk_spec(height, width=CHUNK):
    return pl.BlockSpec((1, height, width), lambda c, *_: (c, 0, 0))


def call(kernel, name, mib, operands, in_specs, outs, scratch=(), flops=0, place=None, grid=None, far=()):
    if far:
        operands = [
            pltpu.with_memory_space_constraint(o, LATER) if i in far else o
            for i, o in enumerate(operands)
        ]
    specs = [o[2] for o in outs]
    shapes = [o[3](o[0], o[1]) if len(o) > 3 else jax.ShapeDtypeStruct(o[0], o[1]) for o in outs]
    scalars = () if place is None else (place,)
    made = pl.pallas_call(
        kernel,
        grid_spec=pltpu.PrefetchScalarGridSpec(
            num_scalar_prefetch=len(scalars),
            grid=grid or (CHUNKS,),
            in_specs=in_specs,
            out_specs=specs,
            scratch_shapes=scratch,
        ),
        out_shape=shapes,
        compiler_params=params(mib),
        cost_estimate=cost(flops // 1000000, 1000),
        name=name,
    )(*scalars, *operands)
    return list(made)


def slot_onehot(slots_ref, rows, chunk=0):
    named = jnp.transpose(slots_ref[chunk])[:, 0:1].astype(jnp.int32)
    places = lax.broadcasted_iota(jnp.int32, (CHUNK, rows), 1)
    return (places == named).astype(FLOAT).astype(LOWER)


def outside_image(slots_ref):
    image = jnp.transpose(slots_ref[0])[:, 1:2]
    return jnp.where(image == slots_ref[0, 1:2, :], 0.0, MASKED)


def choose_own(place, values, own):
    width = values.shape[1]
    source = lax.broadcasted_iota(jnp.int32, (width, own), 0)
    target = lax.broadcasted_iota(jnp.int32, (width, own), 1)
    onehot = (source == target + place * own).astype(FLOAT).astype(LOWER)
    return nn(values, onehot).astype(LOWER)


def norm_stats(values):
    average = jnp.mean(values, axis=-1, keepdims=True)
    centred = values - average
    variance = jnp.mean(centred * centred, axis=-1, keepdims=True)
    inverse = lax.rsqrt(variance + EPSILON)
    return centred * inverse, inverse


def pick_kernel(
    patches_ref, slots_ref, gains_ref, shifts_ref, router_ref, x_ref, n_ref, gate_ref
):
    x = nn(slot_onehot(slots_ref, patches_ref.shape[0]), patches_ref[...])
    x_ref[...] = x.astype(LOWER)
    scaled, _ = norm_stats(x)
    n_ref[...] = (scaled * gains_ref[0:1, :] + shifts_ref[0:1, :]).astype(LOWER)
    logit = jnp.sum(x * router_ref[...], axis=-1, keepdims=True)
    gate_ref[...] = jnp.broadcast_to(jax.nn.sigmoid(logit), gate_ref.shape)


def pick_rows(patches, slots, gains, shifts, router):
    rows, width = patches.shape
    return call(
        pick_kernel,
        "pick_rows",
        20,
        (patches, slots, gains, shifts, router),
        [
            whole((rows, width)),
            chunk_spec(8),
            whole((2, width)),
            whole((2, width)),
            whole((1, width)),
        ],
        [
            ((PACKED, width), LOWER, rows_spec(width)),
            ((PACKED, width), LOWER, rows_spec(width)),
            ((PACKED, 128), FLOAT, rows_spec(128)),
        ],
        flops=2 * PACKED * rows * width,
    )


def pick_cot_kernel(cot_ref, slots_ref, part_ref):
    for c in range(CHUNKS):
        onehot = slot_onehot(slots_ref, cot_ref.shape[1], c)
        part_ref[:, c * CHUNK : (c + 1) * CHUNK] = nt(cot_ref[...], onehot).astype(LOWER)


def pick_cot(cot_own, slots):
    own, rows = cot_own.shape
    return call(
        pick_cot_kernel,
        "pick_cot",
        24,
        (cot_own, slots),
        [whole((own, rows)), whole(slots.shape)],
        [((own, PACKED), LOWER, whole((own, PACKED)))],
        flops=2 * PACKED * rows * own,
        grid=(1,),
    )[0]


def own_columns_kernel(place_ref, patches_ref, patch_ref):
    own, width = patch_ref.shape[0], patches_ref.shape[1]
    source = lax.broadcasted_iota(jnp.int32, (own, width), 1)
    target = lax.broadcasted_iota(jnp.int32, (own, width), 0)
    chosen = (source == target + place_ref[0] * own).astype(FLOAT).astype(LOWER)
    patch_ref[...] = nt(chosen, patches_ref[...]).astype(LOWER)


def own_columns(place, patches, own):
    rows, width = patches.shape
    return call(
        own_columns_kernel,
        "own_columns",
        12,
        (patches,),
        [whole((rows, width))],
        [((own, rows), LOWER, whole((own, rows)), LATER)],
        flops=2 * own * rows * width,
        place=place,
        grid=(1,),
        far=(0,),
    )[0]


def head_slabs(own):
    slabs = []
    for start in range(0, own, 2 * HD):
        stop = min(start + 2 * HD, own)
        lanes = lax.broadcasted_iota(jnp.int32, (1, stop - start), 1)
        heads = []
        for head in range(start // HD, stop // HD):
            low = head * HD - start
            heads.append((head, (lanes >= low) & (lanes < low + HD)))
        slabs.append((start, stop, heads))
    return slabs


def keep(mask, values):
    return jnp.where(mask, values, jnp.zeros_like(values))


def forward_kernel(kind_ref, n_ref, bias_ref, slots_ref, *refs):
    proj_ref, mix_ref, lse_ref, weights_ref = refs[-4:]
    parts = refs[:-4]
    own = mix_ref.shape[1]

    @pl.when(pl.program_id(0) == 0)
    def _():
        if len(parts) == 1:
            weights_ref[...] = parts[0][...]
        else:
            for other, part_ref in enumerate(parts):
                held = part_ref.shape[0]
                start = pl.multiple_of((kind_ref[0] ^ other) * held, 32)
                weights_ref[pl.ds(start, held), :] = part_ref[...]

    proj_ref[...] = (nt(n_ref[...], weights_ref[0 : 3 * own, :]) + bias_ref[0]).astype(LOWER)
    outside = outside_image(slots_ref)
    lse_all = jnp.zeros((CHUNK, 128), FLOAT)
    lanes = lax.broadcasted_iota(jnp.int32, (1, 128), 1)
    for start, stop, heads in head_slabs(own):
        q = proj_ref[:, start:stop] * LOWER(HD**-0.5)
        k = proj_ref[:, own + start : own + stop]
        v = proj_ref[:, 2 * own + start : 2 * own + stop]
        mixed = None
        for head, mask in heads:
            scores = nt(q, keep(mask, k)) + outside
            largest = jnp.max(scores, axis=-1, keepdims=True)
            powered = jnp.exp(scores - largest)
            total = jnp.sum(powered, axis=-1, keepdims=True)
            probs = (powered * (1.0 / total)).astype(LOWER)
            part = nn(probs, keep(mask, v))
            mixed = part if mixed is None else mixed + part
            lse_all = jnp.where(lanes == head, largest + jnp.log(total), lse_all)
        mix_ref[:, start:stop] = mixed.astype(LOWER)
    lse_ref[0] = jnp.transpose(lse_all)[0:8, :]


def forward_quarter(kind, normed, biases, slots, parts, j):
    width = normed.shape[1]
    own = biases.shape[2] // 3
    return call(
        forward_kernel,
        "forward_quarter",
        11,
        (normed, biases, slots, *parts),
        [
            rows_spec(width),
            pl.BlockSpec((1, 1, 3 * own), lambda c, *_: (j, 0, 0)),
            chunk_spec(8),
            *[whole(p.shape) for p in parts],
        ],
        [
            ((PACKED, 3 * own), LOWER, rows_spec(3 * own), LATER),
            ((PACKED, own), LOWER, rows_spec(own)),
            ((CHUNKS, 8, CHUNK), FLOAT, chunk_spec(8), LATER),
            ((4 * own, width), LOWER, whole((4 * own, width))),
        ],
        flops=2 * PACKED * width * 8 * own,
        place=kind,
    )


def join_kernel(place_ref, x_ref, post_ref, own_post_ref, gains_ref, shifts_ref, *refs):
    hidden_ref, normed_ref, own_ref, chosen = refs[-4:]
    parts = refs[:-4]
    count = len(parts) // 2
    own = own_ref.shape[1]

    @pl.when(pl.program_id(0) == 0)
    def _():
        for j, out_ref in enumerate(parts[count:]):
            chosen[j * own : (j + 1) * own, :] = choose_own(place_ref[0], out_ref[...], own)

    attn, attn_own = post_ref[0:1, :], own_post_ref[0:1, :]
    for j, (mix_ref, out_ref) in enumerate(zip(parts[:count], parts[count:])):
        attn = attn + nn(mix_ref[...], out_ref[...])
        attn_own = attn_own + nn(mix_ref[...], chosen[j * own : (j + 1) * own, :])
    own_ref[...] = attn_own
    hidden = x_ref[...].astype(FLOAT) + attn
    hidden_ref[...] = hidden
    scaled, _ = norm_stats(hidden)
    normed_ref[...] = (scaled * gains_ref[1:2, :] + shifts_ref[1:2, :]).astype(LOWER)


def out_spec(own, width):
    return pl.BlockSpec((own, width), lambda *_: (3, 0), pipeline_mode=pl.Buffered(1))


def join_quarters(place, x, post, own_post, gains, shifts, mixes, weights):
    width = x.shape[1]
    own = mixes[0].shape[1]
    return call(
        join_kernel,
        "join_quarters",
        11,
        (x, post, own_post, gains, shifts, *mixes, *weights),
        [
            rows_spec(width),
            whole((2, width)),
            whole((2, own)),
            whole((2, width)),
            whole((2, width)),
            *[rows_spec(own) for _ in mixes],
            *[out_spec(own, width) for _ in weights],
        ],
        [
            ((PACKED, width), FLOAT, rows_spec(width), LATER),
            ((PACKED, width), LOWER, rows_spec(width)),
            ((PACKED, own), FLOAT, rows_spec(own), LATER),
        ],
        scratch=[pltpu.VMEM((len(weights) * own, own), LOWER)],
        flops=3 * PACKED * width * width,
        place=place,
    )


def stack_places(place, parts, stacked):
    size = len(parts)
    for j, part in enumerate(parts):
        own = part.shape[0]
        start = pl.multiple_of(lax.rem(place - j + size, size) * own, 64)
        stacked[pl.ds(start, own), :] = part.astype(stacked.dtype)


def cot_kernel(place_ref, gate_ref, *refs):
    cot_ref, gated_ref, stacked = refs[-3:]
    stack_places(place_ref[0], [r[...] for r in refs[:-3]], stacked)
    cot = jnp.transpose(stacked[...])
    cot_ref[...] = cot
    gated_ref[...] = (gate_ref[:, 0:1] * cot.astype(FLOAT)).astype(LOWER)


def cot_chunks(place, gate, parts):
    own = parts[0].shape[0]
    width = own * len(parts)
    return call(
        cot_kernel,
        "cot_chunks",
        20,
        (gate, *parts),
        [whole((PACKED, 128)), *[whole(p.shape) for p in parts]],
        [
            ((PACKED, width), LOWER, whole((PACKED, width)), LATER),
            ((PACKED, width), LOWER, whole((PACKED, width))),
        ],
        scratch=[pltpu.VMEM((width, PACKED), LOWER)],
        flops=PACKED * width,
        place=place,
        grid=(1,),
    )


def gelu_pair(u):
    cdf = 0.5 * (1.0 + lax.erf(u * (0.5**0.5)))
    density = jnp.exp(-0.5 * u * u) * 0.3989422804014327
    return u * cdf, cdf + u * density


def mlp_step(normed, gated, up_ref, down_ref, bias, own_down_ref):
    hidden = up_ref.shape[1]
    block = hidden // 3

    def products(start):
        cols = slice(start, start + block)
        pre_act = nn(normed, up_ref[:, cols]) + bias[:, cols]
        return pre_act, nt(gated, down_ref[cols, :])

    activations, grads, grad, gate, out = [], [], None, None, None
    ahead = products(0)
    for start in range(0, hidden, block):
        cols = slice(start, start + block)
        pre_act, grad_act = ahead
        if start + block < hidden:
            ahead = products(start + block)
        activation, slope = gelu_pair(pre_act)
        activation = activation.astype(LOWER)
        grad_pre = (grad_act * slope).astype(LOWER)
        gate_part = jnp.sum(activation.astype(FLOAT) * grad_act, axis=-1, keepdims=True)
        grad_part = nt(grad_pre, up_ref[:, cols])
        out_part = nn(activation, own_down_ref[cols, :])
        activations.append(activation)
        grads.append(grad_pre)
        grad = grad_part if grad is None else grad + grad_part
        gate = gate_part if gate is None else gate + gate_part
        out = out_part if out is None else out + out_part
    return activations, grads, grad, gate, out


def own_mlp_kernel(
    place_ref,
    n_ref,
    gated_ref,
    up_ref,
    down_ref,
    bias_ref,
    act_ref,
    pre_ref,
    grad_ref,
    gate_ref,
    out_ref,
    bias_sum_ref,
    own_down,
):
    @pl.when(pl.program_id(0) == 0)
    def _():
        own_down[...] = choose_own(place_ref[0], down_ref[...], own_down.shape[1])
        bias_sum_ref[...] = jnp.zeros_like(bias_sum_ref)

    activation, grad_pre, grad_part, gate_part, out_part = mlp_step(
        n_ref[...], gated_ref[...], up_ref, down_ref, bias_ref[...], own_down
    )
    block = activation[0].shape[1]
    for i, (act, pre) in enumerate(zip(activation, grad_pre)):
        act_ref[:, i * block : (i + 1) * block] = act
        pre_ref[:, i * block : (i + 1) * block] = pre
    grad_ref[...] = grad_part
    gate_ref[...] = jnp.broadcast_to(gate_part, gate_ref.shape)
    out_ref[...] = out_part
    bias_sum_ref[0:1, :] += jnp.sum(pre_ref[...].astype(FLOAT), axis=0, keepdims=True)


def own_mlp(place, normed, gated, up, down, bias, own):
    width, hidden = up.shape
    return call(
        own_mlp_kernel,
        "own_mlp",
        17,
        (normed, gated, up, down, bias),
        [
            rows_spec(width),
            rows_spec(width),
            whole((width, hidden)),
            whole((hidden, width)),
            whole((1, hidden)),
        ],
        [
            ((PACKED, hidden), LOWER, rows_spec(hidden)),
            ((PACKED, hidden), LOWER, rows_spec(hidden)),
            ((PACKED, width), FLOAT, rows_spec(width), LATER),
            ((PACKED, 128), FLOAT, rows_spec(128)),
            ((PACKED, own), FLOAT, rows_spec(own)),
            ((8, hidden), FLOAT, whole((8, hidden), False)),
        ],
        scratch=[pltpu.VMEM((hidden, own), LOWER)],
        flops=2 * PACKED * hidden * (3 * width + own),
        place=place,
    )


def own_grads_kernel(core_ref, n_ref, pre_ref, act_ref, gated_ref, kept_ref, sent_ref):
    grad_up = tn(n_ref[...], pre_ref[...])
    grad_down = tn(act_ref[...], gated_ref[...])

    @pl.when(core_ref[0] == 0)
    def _():
        kept_ref[...] = grad_up
        sent_ref[...] = grad_down.astype(LOWER)

    @pl.when(core_ref[0] == 1)
    def _():
        kept_ref[...] = grad_down
        sent_ref[...] = grad_up.astype(LOWER)


def own_grads(core, normed, grad_pre, act, gated):
    width = normed.shape[1]
    block = width // 3
    columns = pl.BlockSpec((PACKED, block), lambda c, *_: (0, c))
    return call(
        own_grads_kernel,
        "own_grads",
        16,
        (normed, grad_pre, act, gated),
        [columns, whole((PACKED, width)), columns, whole((PACKED, width))],
        [
            ((width, width), FLOAT, rows_spec(width, block)),
            ((width, width), LOWER, rows_spec(width, block)),
        ],
        flops=4 * PACKED * width * width,
        place=core,
        grid=(3,),
    )


def other_mlp_kernel(
    last, place_ref, n_ref, gated_ref, grad_in_ref, gate_in_ref, out_in_ref, *refs
):
    grad_ref, gate_ref, out_ref, up, down, own_down = refs[-6:]
    ups, downs = refs[0:4], refs[4:8]
    part = downs[0].shape[2]
    width = up.shape[1]

    @pl.when(pl.program_id(0) == 0)
    def _():
        for side in range(2):
            for c in range(2):
                for near in range(2):
                    to_up = place_ref[1] ^ (4 * side + 2 * near + c)
                    to_down = place_ref[1] ^ (4 * near + 2 * side + c)
                    up_rows = pl.ds(pl.multiple_of(to_up * part, 32), part)
                    down_rows = pl.ds(pl.multiple_of(to_down * part, 32), part)
                    up[up_rows, :] = ups[side + 2 * c][near, 0, 0:part]
                    down[down_rows, :] = downs[side + 2 * c][near, 0]
        own_down[...] = choose_own(place_ref[0], down[...], own_down.shape[1])

    pieces = ups[0][0, 0, part : part + 16].astype(FLOAT)
    bias = pieces[0:1] + (pieces[1:2] + pieces[2:3])
    _, _, grad_part, gate_part, out_part = mlp_step(
        n_ref[...], gated_ref[...], up, down, bias, own_down
    )
    grad_ref[...] = grad_in_ref[...] + grad_part
    gate_ref[...] = gate_in_ref[...] + gate_part
    if last:
        attn_ref, post_ref, open_ref = refs[8:11]
        total = out_in_ref[...] + out_part + attn_ref[...] + post_ref[1:2, :]
        out_ref[...] = open_ref[:, 0:1] * total
    else:
        out_ref[...] = out_in_ref[...] + out_part


def other_mlp(places, normed, gated, sums, ups, downs, j, extra=()):
    width = normed.shape[1]
    own = sums[2].shape[1]
    last = len(extra) > 0
    held = lambda array: pl.BlockSpec(
        (2, 1, *array.shape[2:]), lambda c, *_: (0, j, 0, 0), pipeline_mode=pl.Buffered(1)
    )
    extra_specs = [rows_spec(own), whole((2, own)), rows_spec(128)] if last else []
    return call(
        functools.partial(other_mlp_kernel, last),
        "other_mlp",
        19,
        (normed, gated, *sums, *ups, *downs, *extra),
        [
            rows_spec(width),
            rows_spec(width),
            rows_spec(width),
            rows_spec(128),
            rows_spec(own),
            *[held(u) for u in ups],
            *[held(d) for d in downs],
            *extra_specs,
        ],
        [
            ((PACKED, width), FLOAT, rows_spec(width)),
            ((PACKED, 128), FLOAT, rows_spec(128)),
            ((PACKED, own), FLOAT, rows_spec(own)),
        ],
        scratch=[
            pltpu.VMEM((width, width), LOWER),
            pltpu.VMEM((width, width), LOWER),
            pltpu.VMEM((width, own), LOWER),
        ],
        flops=2 * PACKED * width * (3 * width + own),
        place=places,
    )


def second_norm_kernel(
    grad_ref,
    gate_part_ref,
    hidden_ref,
    x_ref,
    cot_ref,
    gate_ref,
    post_ref,
    gains_ref,
    ghid_ref,
    glow_ref,
    logit_ref,
    sums_ref,
):
    @pl.when(pl.program_id(0) == 0)
    def _():
        sums_ref[...] = jnp.zeros_like(sums_ref)

    hidden = hidden_ref[...]
    scaled, inverse = norm_stats(hidden)
    grad_out = grad_ref[...]
    weighted = grad_out * gains_ref[1:2, :]
    centre_term = jnp.mean(weighted, axis=-1, keepdims=True)
    scale_term = jnp.mean(weighted * scaled, axis=-1, keepdims=True)
    grad_hidden = inverse * (weighted - centre_term - scaled * scale_term)
    gate = gate_ref[:, 0:1]
    gated = gate * cot_ref[...].astype(FLOAT)
    grad_attn = grad_hidden + gated
    ghid_ref[...] = grad_hidden
    glow_ref[...] = grad_attn.astype(LOWER)
    attn = hidden - x_ref[...].astype(FLOAT)
    dotted = jnp.sum(gated * (attn + post_ref[1:2, :]), axis=-1, keepdims=True)
    logit = (1.0 - gate) * (dotted + gate_part_ref[:, 0:1])
    logit_ref[...] = jnp.broadcast_to(logit, logit_ref.shape)
    sums_ref[0:1, :] += jnp.sum(grad_out * scaled, axis=0, keepdims=True)
    sums_ref[1:2, :] += jnp.sum(grad_out, axis=0, keepdims=True)
    sums_ref[2:3, :] += jnp.sum(grad_attn, axis=0, keepdims=True)
    sums_ref[3:4, :] += jnp.sum(gated, axis=0, keepdims=True)


def second_norm(grad, gate_part, hidden, x, cot_rows, gate, post, gains):
    width = x.shape[1]
    return call(
        second_norm_kernel,
        "second_norm",
        15,
        (grad, gate_part, hidden, x, cot_rows, gate, post, gains),
        [
            rows_spec(width),
            rows_spec(128),
            rows_spec(width),
            rows_spec(width),
            rows_spec(width),
            rows_spec(128),
            whole((2, width)),
            whole((2, width)),
        ],
        [
            ((PACKED, width), FLOAT, rows_spec(width)),
            ((PACKED, width), LOWER, rows_spec(width)),
            ((PACKED, 128), FLOAT, rows_spec(128)),
            ((8, width), FLOAT, whole((8, width), False)),
        ],
        flops=20 * PACKED * width,
    )


def backward_kernel(low_ref, slots_ref, proj_ref, lse_ref, out_ref, gproj_ref, sums_ref):
    @pl.when(pl.program_id(0) == 0)
    def _():
        sums_ref[...] = jnp.zeros_like(sums_ref)

    outside = outside_image(slots_ref)
    own = out_ref.shape[0]
    heads = own // HD
    g = nt(low_ref[...], out_ref[...]).astype(LOWER)
    q = proj_ref[:, 0:own] * LOWER(HD**-0.5)
    k = proj_ref[:, own : 2 * own]
    v = proj_ref[:, 2 * own : 3 * own]
    lanes = lax.broadcasted_iota(jnp.int32, (1, own), 1) // HD
    keys = jnp.concatenate([keep(lanes == head, k) for head in range(heads)], axis=0)
    values = jnp.concatenate([keep(lanes == head, v) for head in range(heads)], axis=0)
    scores = nt(keys, q)
    grad_probs = nt(values, g)
    probs, grad_scores = [], []
    for head in range(heads):
        rows = slice(head * CHUNK, (head + 1) * CHUNK)
        prob = jnp.exp(scores[rows] + outside - lse_ref[0, head : head + 1, :])
        inner = jnp.sum(prob * grad_probs[rows], axis=0, keepdims=True)
        grad_scores.append((prob * (grad_probs[rows] - inner)).astype(LOWER))
        probs.append(prob.astype(LOWER))
    grad_scores = jnp.concatenate(grad_scores, axis=0)
    all_v = nn(jnp.concatenate(probs, axis=0), g)
    all_k = nn(grad_scores, q)
    grad_q = tn(grad_scores, keys)
    grad_k, grad_v = all_k[0:CHUNK], all_v[0:CHUNK]
    for head in range(1, heads):
        rows = slice(head * CHUNK, (head + 1) * CHUNK)
        grad_k = jnp.where(lanes == head, all_k[rows], grad_k)
        grad_v = jnp.where(lanes == head, all_v[rows], grad_v)
    gproj_ref[:, 0:own] = (grad_q * HD**-0.5).astype(LOWER)
    gproj_ref[:, own : 2 * own] = grad_k.astype(LOWER)
    gproj_ref[:, 2 * own : 3 * own] = grad_v.astype(LOWER)
    sums_ref[0:1, :] += jnp.sum(gproj_ref[...].astype(FLOAT), axis=0, keepdims=True)


def backward_quarter(low, slots, proj, lse, weights):
    width = low.shape[1]
    own = proj.shape[1] // 3
    return call(
        backward_kernel,
        "backward_quarter",
        20,
        (low, slots, proj, lse, weights),
        [
            rows_spec(width),
            chunk_spec(8),
            rows_spec(3 * own),
            chunk_spec(8),
            out_spec(own, width),
        ],
        [
            ((PACKED, 3 * own), LOWER, rows_spec(3 * own)),
            ((8, 3 * own), FLOAT, whole((8, 3 * own), False)),
        ],
        flops=2 * PACKED * width * 14 * own,
    )


def attn_grads_kernel(core_ref, gproj_ref, normed_ref, mix_ref, low_ref, kept_ref, sent_ref):
    half = kept_ref.shape[0]
    rest = gproj_ref.shape[1] - half
    normed = normed_ref[...]
    first = tn(gproj_ref[:, 0:half], normed)
    second = tn(gproj_ref[:, half:], normed)
    third = tn(mix_ref[...], low_ref[...])

    @pl.when(core_ref[0] == 0)
    def _():
        kept_ref[...] = first
        sent_ref[0:rest, :] = second.astype(LOWER)
        sent_ref[rest:half, :] = third.astype(LOWER)

    @pl.when(core_ref[0] == 1)
    def _():
        kept_ref[0:rest, :] = second
        kept_ref[rest:half, :] = third
        sent_ref[...] = first.astype(LOWER)


def attn_grads(core, gproj, normed, mix, low):
    width, own = normed.shape[1], mix.shape[1]
    operands = (gproj, normed, mix, low)
    return call(
        attn_grads_kernel,
        "attn_grads",
        18,
        operands,
        [whole(o.shape) for o in operands],
        [
            ((2 * own, width), FLOAT, whole((2 * own, width))),
            ((2 * own, width), LOWER, whole((2 * own, width))),
        ],
        place=core,
        grid=(1,),
    )


def first_norm_kernel(x_ref, ghid_ref, logit_ref, gains_ref, router_ref, *refs):
    rows_ref, sums_ref, gprojs, weights = refs[-4:]
    parts = refs[:-4]
    count = len(parts) // 2
    held = parts[0].shape[1]

    @pl.when(pl.program_id(0) == 0)
    def _():
        sums_ref[...] = jnp.zeros_like(sums_ref)
        for j, weights_ref in enumerate(parts[count:]):
            weights[j * held : (j + 1) * held, :] = weights_ref[0:held, :]

    for j, gproj_ref in enumerate(parts[:count]):
        gprojs[:, j * held : (j + 1) * held] = gproj_ref[...]
    grad_out = nn(gprojs[...], weights[...])
    x = x_ref[...].astype(FLOAT)
    scaled, inverse = norm_stats(x)
    weighted = grad_out * gains_ref[0:1, :]
    centre_term = jnp.mean(weighted, axis=-1, keepdims=True)
    scale_term = jnp.mean(weighted * scaled, axis=-1, keepdims=True)
    grad_norm = inverse * (weighted - centre_term - scaled * scale_term)
    logit = logit_ref[:, 0:1]
    rows_ref[...] = (ghid_ref[...] + grad_norm + logit * router_ref[...]).astype(LOWER)
    sums_ref[0:1, :] += jnp.sum(grad_out * scaled, axis=0, keepdims=True)
    sums_ref[1:2, :] += jnp.sum(grad_out, axis=0, keepdims=True)
    sums_ref[2:3, :] += jnp.sum(logit * x, axis=0, keepdims=True)


def first_norm(x, ghid, logit, gains, router, gprojs, weights):
    width = x.shape[1]
    return call(
        first_norm_kernel,
        "first_norm",
        24,
        (x, ghid, logit, gains, router, *gprojs, *weights),
        [
            rows_spec(width),
            rows_spec(width),
            rows_spec(128),
            whole((2, width)),
            whole((1, width)),
            *[rows_spec(g.shape[1]) for g in gprojs],
            *[whole(w.shape) for w in weights],
        ],
        [
            ((PACKED, width), LOWER, rows_spec(width)),
            ((8, width), FLOAT, whole((8, width), False)),
        ],
        scratch=[pltpu.VMEM((CHUNK, 3 * width), LOWER), pltpu.VMEM((3 * width, width), LOWER)],
        flops=2 * PACKED * width * 3 * width,
    )


def scatter_kernel(place_ref, named_ref, rows_ref, branch_ref, patch_ref, *refs):
    out_ref, block_ref, stacked, branch_t = refs[-4:]
    block = out_ref.shape[0]

    @pl.when(pl.program_id(0) == 0)
    def _():
        branch_t[...] = jnp.transpose(branch_ref[...].astype(LOWER))

    stack_places(place_ref[0], [r[...] for r in refs[:-4]], stacked)
    places = lax.broadcasted_iota(jnp.int32, (block, PACKED), 0) + pl.program_id(0) * block
    onehot = (places == named_ref[...]).astype(FLOAT).astype(LOWER)
    cot = jnp.transpose(stacked[...]).astype(FLOAT)
    out_ref[...] = (cot + nn(onehot, rows_ref[...])).astype(LOWER)
    block_ref[...] = (patch_ref[...].astype(FLOAT) + nt(branch_t[...], onehot)).astype(LOWER)


def scatter_rows(place, cot_parts, named, rows, branch, patch_t):
    own, total = cot_parts[0].shape
    width = own * len(cot_parts)
    block = 512
    columns = pl.BlockSpec((own, block), lambda c, *_: (0, c))
    return call(
        scatter_kernel,
        "scatter_rows",
        19,
        (named, rows, branch, patch_t, *cot_parts),
        [
            whole(named.shape),
            whole((PACKED, width)),
            whole((PACKED, own)),
            columns,
            *[columns for _ in cot_parts],
        ],
        [
            ((total, width), LOWER, rows_spec(width, block), LATER),
            ((own, total), LOWER, columns, LATER),
        ],
        scratch=[
            pltpu.VMEM((width, block), LOWER),
            pltpu.VMEM((own, PACKED), LOWER),
        ],
        flops=2 * PACKED * total * width,
        place=place,
        grid=(pl.cdiv(total, block),),
        far=range(3, 4 + len(cot_parts)),
    )


def halve_kernel(upper_ref, kept_ref, came_ref, half_ref, sent_ref):
    block, half = half_ref.shape[0], kept_ref.shape[0] // 2
    step = pl.program_id(0) * block
    own = pl.ds(pl.multiple_of(upper_ref[0] * half + step, 16), block)
    far = pl.ds(pl.multiple_of((1 - upper_ref[0]) * half + step, 16), block)
    half_ref[...] = kept_ref[own, :] + came_ref[own, :].astype(FLOAT)
    sent_ref[...] = (kept_ref[far, :] + came_ref[far, :].astype(FLOAT)).astype(LOWER)


def halve_sum(upper, kept, came):
    rows, width = kept.shape
    return call(
        halve_kernel,
        "halve_sum",
        10,
        (kept, came),
        [whole((rows, width)), whole((rows, width))],
        [
            ((rows // 2, width), FLOAT, rows_spec(width, rows // 4)),
            ((rows // 2, width), LOWER, rows_spec(width, rows // 4)),
        ],
        place=upper,
        grid=(2,),
    )


def finish_kernel(core_ref, attn_ref, attn_far_ref, mlp_ref, mlp_far_ref, *refs):
    qkv_ref, out_ref, up_ref, down_ref = refs
    own, block = qkv_ref.shape[0], up_ref.shape[0]
    head = pl.program_id(0)
    rows = pl.ds(pl.multiple_of(head * block, 16), block)

    def write(low_ref, high_ref, first_ref, second_ref):
        one = pl.ds(pl.multiple_of(head * HD, HD), HD)
        two = pl.ds(pl.multiple_of(own + head * HD, HD), HD)
        qkv_ref[0:HD, :] = low_ref[one, :].astype(FLOAT)
        qkv_ref[HD : 2 * HD, :] = low_ref[two, :].astype(FLOAT)
        qkv_ref[2 * HD : 3 * HD, :] = high_ref[one, :].astype(FLOAT)
        out_ref[...] = high_ref[two, :].astype(FLOAT)
        up_ref[...] = first_ref[rows, :].astype(FLOAT)
        down_ref[...] = second_ref[rows, :].astype(FLOAT)

    @pl.when(core_ref[0] == 0)
    def _():
        write(attn_ref, attn_far_ref, mlp_ref, mlp_far_ref)

    @pl.when(core_ref[0] == 1)
    def _():
        write(attn_far_ref, attn_ref, mlp_far_ref, mlp_ref)


def finish_grads(core, attn, attn_far, mlp, mlp_far):
    width = mlp.shape[1]
    own = attn.shape[0] // 2
    heads = own // HD
    return call(
        finish_kernel,
        "finish_grads",
        16,
        (attn, attn_far, mlp, mlp_far),
        [whole(attn.shape), whole(attn.shape), whole(mlp.shape), whole(mlp.shape)],
        [
            ((3 * own, width), FLOAT, rows_spec(width, 3 * HD)),
            ((own, width), FLOAT, rows_spec(width, HD)),
            ((width, width), FLOAT, rows_spec(width, width // heads)),
            ((width, width), FLOAT, rows_spec(width, width // heads)),
        ],
        place=core,
        grid=(heads,),
    )


def finish_sums_kernel(own_ref, far_ref, *refs):
    gains_ref, shifts_ref, post_ref, up_ref, router_ref, qkv_ref = refs
    total = own_ref[...] + far_ref[...]
    own = qkv_ref.shape[1]
    gains_ref[0:1, :] = total[4:5]
    gains_ref[1:2, :] = total[0:1]
    shifts_ref[0:1, :] = total[5:6]
    shifts_ref[1:2, :] = total[1:2]
    post_ref[...] = total[2:4]
    up_ref[...] = total[7]
    router_ref[...] = total[6]
    qkv_ref[0:1, :] = total[8:9, 0:own]
    qkv_ref[1:2, :] = total[8:9, 2 * own : 3 * own]


def finish_sums(small, far, own):
    rows, width = small.shape
    shapes = [(2, width), (2, width), (2, width), (width,), (width,), (2, own)]
    return call(
        finish_sums_kernel,
        "finish_sums",
        4,
        (small, far),
        [whole((rows, width)), whole((rows, width))],
        [(shape, FLOAT, whole(shape)) for shape in shapes],
        grid=(1,),
    )


def turned(values, place):
    size = values.shape[0]
    back = jnp.concatenate([values[:1], values[:0:-1]], axis=0)
    twice = jnp.concatenate([back, back], axis=0)
    return lax.dynamic_slice_in_dim(twice, (size - place) % size, size, 0)


def after(value, *others):
    return lax.optimization_barrier((value, *others))[0]


def ring_step(value, size):
    return lax.ppermute(value, "mlp", [(i, (i + 1) % size) for i in range(size)])


def swap(value, bit, size):
    return lax.ppermute(value, "rows", [(i, i ^ (1 << bit)) for i in range(size)])


def bits_of(size):
    return [b for b in range(20) if (1 << b) < size]


def pack_slots(picked, live_slots):
    small = IMG_DEV * HALF_S
    named = jnp.where(live_slots == 1, picked, -1)

    def padded(parts, fill):
        have = sum(p.shape[0] for p in parts)
        return jnp.concatenate([*parts, jnp.full((CHUNK - have,), fill, jnp.int32)])

    always = IMG_DEV - L_MOST
    idx = [padded([named[: always * HALF_S]], -1)]
    seg = [padded([jnp.repeat(jnp.arange(always, dtype=jnp.int32), HALF_S)], always)]
    for j in range(L_MOST):
        first = small + j * HALF_L
        alive = live_slots[first] == 1
        other = IMG_DEV - 1 - j
        large_idx = padded([named[first : first + HALF_L]], -1)
        small_idx = padded([named[other * HALF_S : (other + 1) * HALF_S]], -1)
        idx.append(jnp.where(alive, large_idx, small_idx))
        length = jnp.where(alive, HALF_L, HALF_S)
        seg.append((jnp.arange(CHUNK, dtype=jnp.int32) >= length).astype(jnp.int32))
    named = jnp.concatenate(idx).reshape(1, PACKED)
    idx, seg = jnp.stack(idx).astype(FLOAT), jnp.stack(seg).astype(FLOAT)
    rows = lax.broadcasted_iota(jnp.int32, (1, 8, 1), 1)
    return jnp.where(rows == 0, idx[:, None, :], seg[:, None, :]), named


def local(
    rows_size,
    mlp_size,
    patches,
    w_qkv,
    qkv_bias,
    w_out,
    post_bias,
    w_up,
    up_bias,
    w_down,
    norm_gains,
    norm_shifts,
    router,
    picked,
    live_slots,
    cotangent,
):
    width = patches.shape[1]
    mlp_index = lax.axis_index("mlp")
    rows_index = lax.axis_index("rows")
    share_index = rows_index % SHARE
    core = rows_index & 1
    place = mlp_index.astype(jnp.int32).reshape(1)
    places = jnp.stack([mlp_index, share_index]).astype(jnp.int32)
    kind = (rows_index % PIECES).astype(jnp.int32).reshape(1)
    own = w_out.shape[0]
    heads_here = own // HD
    others = mlp_size - 1
    router_row = router.reshape(1, width)

    def swapped(value, bit):
        return swap(value, bit, rows_size)

    own_weights = jnp.concatenate(
        [
            w_qkv.T.reshape(heads_here, 3, HD, width).transpose(1, 0, 2, 3).reshape(3 * own, width),
            w_out,
        ],
        axis=0,
    )
    held = own_weights.shape[0] // PIECES
    piece = lax.dynamic_slice_in_dim(own_weights, kind[0] * held, held, 0)
    part = w_up.shape[0] // SHARE
    top = lax.reduce_precision(up_bias, 8, 7)
    middle = lax.reduce_precision(up_bias - top, 8, 7)
    bias_rows = jnp.stack([top, middle, up_bias - top - middle]).astype(LOWER)
    payload = jnp.concatenate(
        [
            piece,
            lax.dynamic_slice_in_dim(w_up, share_index * part, part, 0),
            jnp.pad(bias_rows, ((0, 13), (0, 0))),
            lax.dynamic_slice_in_dim(w_down, share_index * part, part, 0),
        ],
        axis=0,
    )
    def around(value):
        return ring_step(value, mlp_size)

    kinds = jnp.stack([qkv_bias[0], jnp.zeros_like(qkv_bias[0]), qkv_bias[1]])
    biases = turned(kinds.reshape(3, mlp_size, own).transpose(1, 0, 2), mlp_index)
    biases = biases.reshape(mlp_size, 1, 3 * own)
    own_post = lax.dynamic_slice_in_dim(post_bias, mlp_index * own, own, 1)
    slots, named = pack_slots(picked, live_slots)
    cot_own = cotangent.T
    core_one = core.astype(jnp.int32).reshape(1)

    def split(came):
        return came[:held], came[held : held + part + 16], came[held + part + 16 :]

    def across(value, mask):
        return lax.ppermute(value, "rows", [(i, i ^ mask) for i in range(rows_size)])

    def forward(j, normed, parts):
        return forward_quarter(kind, normed, biases, slots, parts, j)

    order = bits_of(rows_size)
    lower = {bit: (rows_index >> bit) & 1 == 0 for bit in order}
    upper = {bit: ((rows_index >> bit) & 1).astype(jnp.int32).reshape(1) for bit in order}
    payload, place, places, kind, core_one, lower, upper = lax.optimization_barrier(
        (payload, place, places, kind, core_one, lower, upper)
    )
    came = around(payload)
    patches, named, own_post, biases = lax.optimization_barrier(
        (after(patches, payload), named, own_post, biases)
    )
    x, normed_one, gate = pick_rows(
        patches, slots, norm_gains, norm_shifts, router_row
    )
    came = after(came, x)
    cot_part = pick_cot(after(cot_own, came), slots)
    normed_one = after(normed_one, cot_part)
    quarters, cot_parts, up_parts, down_parts = [], [cot_part], [], []
    parts, before = [own_weights], x
    for j in range(mlp_size):
        if j < others:
            came = after(came, before)
            got, up_part, down_part = split(came)
            up_parts.append(up_part)
            down_parts.append(down_part)
            if j + 1 < others:
                came = around(came)
            spread = [got, *[across(got, mask) for mask in range(2, PIECES, 2)]]
        if 0 < j < others:
            cot_parts.append(around(after(cot_parts[-1], got)))
        normed_one = after(normed_one, got, before, *parts)
        if j == others:
            normed_one = after(normed_one, *cot_parts[:-1])
            ups, downs = jnp.stack(up_parts), jnp.stack(down_parts)
            ups_x, downs_y = swapped(ups, 1), swapped(downs, 2)
        quarters.append(forward(j, normed_one, parts))
        before = quarters[-1][1]
        if j < others:
            spread = [after(v, before) for v in spread]
            parts = [w for v in spread for w in (v, swapped(v, 0))]

    projs, mixes, lses, weights = zip(*quarters)
    cot_last = after(cot_parts[-1], before)
    ups_x, downs_y = after(ups_x, cot_last), after(downs_y, cot_last)
    cot_parts.append(around(cot_last))
    ups, downs = jnp.stack([ups, ups_x]), jnp.stack([downs, downs_y])
    ups_y, downs_x = swapped(ups, 2), swapped(downs, 1)
    hidden, normed_two, attn_own = join_quarters(
        place, after(x, cot_last), post_bias, own_post, norm_gains, norm_shifts, mixes, weights
    )
    patch_t = own_columns(place, after(patches, normed_two), own)
    cot_rows, gated = cot_chunks(place, after(gate, normed_two, patch_t), cot_parts)
    full_parts = [cot_own, around(after(cot_own, gated))]

    def full_due(slot, value):
        if slot in ("N2", "B2"):
            full_parts.append(around(after(full_parts[-1], value)))
            return after(value, full_parts[-2])
        return value

    act, grad_pre, *sums, up_bias_sum = own_mlp(
        place, normed_two, gated, w_up, w_down, up_bias.reshape(1, -1), own
    )
    ups_y, downs_x = after(ups_y, sums[0]), after(downs_x, sums[0])
    more = [swapped(v, 0) for v in (ups, ups_y, downs, downs_x)]
    kept, sent = own_grads(core_one, normed_two, after(grad_pre, ups_y, downs_x), act, gated)
    more = [after(v, kept) for v in more]
    ups, downs = [ups, ups_y, *more[:2]], [downs, downs_x, *more[2:]]
    sent = after(sent, *more)

    turned_order = [order[0], *order[:0:-1]]

    def halves(kept, came, bit):
        if kept.shape[0] % 64 == 0:
            return halve_sum(upper[bit], kept, came)
        value = kept + came.astype(FLOAT)
        pair = value.reshape(2, value.shape[0] // 2, width)
        return (
            jnp.where(lower[bit], pair[0], pair[1]),
            jnp.where(lower[bit], pair[1], pair[0]).astype(LOWER),
        )

    def joined(value, other, bit):
        first, second = jnp.where(lower[bit], value, other), jnp.where(lower[bit], other, value)
        return jnp.concatenate([first, second], axis=0)

    def halve_middle(kept, came, bits):
        for bit in bits[2:-1]:
            kept, sent = halves(kept, came, bit)
            came = swapped(sent, bit)
        return halves(kept, came, bits[-1])

    def join_middle(value, bits):
        for bit in bits[-2:1:-1]:
            value = joined(value, swapped(value, bit), bit)
        return value

    came_c = swapped(sent, 0)
    sums[0] = after(sums[0], kept, *more)
    for j in range(others):
        sums[0] = full_due(f"M{j}", sums[0])
        last_quarter = (attn_own, own_post, gate) if j == others - 1 else ()
        sums = other_mlp(places, normed_two, gated, sums, ups, downs, j, last_quarter)
        if j == 0:
            kept, sent = halves(kept, after(came_c, sums[0]), order[1])
            came_x = swapped(sent, order[1])
            sums[0] = after(sums[0], sent)
    grad_two, gate_part, branch = sums
    came_x = after(came_x, grad_two)
    grad_two = full_due("N2", grad_two)
    grad_two = after(grad_two, came_x)
    kept, sent = halve_middle(kept, came_x, order)
    came_y = swapped(sent, order[-1])
    grad_hidden, grad_low, logit, sums_two = second_norm(
        after(grad_two, kept), gate_part, hidden, x, cot_rows, gate, post_bias, norm_gains
    )
    own_proj, bias_grad = backward_quarter(
        full_due("B0", grad_low), slots, projs[0], lses[0], weights[0]
    )
    kept_a, sent_a = attn_grads(core_one, own_proj, normed_one, mixes[0], grad_low)
    gprojs = [own_proj]
    came_a = swapped(sent_a, 0)
    d_mlp = (kept + after(came_y, kept_a).astype(FLOAT)).astype(LOWER)
    other = swapped(d_mlp, order[-1])
    low = full_due("B1", after(grad_low, kept_a, d_mlp))
    gprojs.append(backward_quarter(low, slots, projs[1], lses[1], weights[1])[0])
    kept_a, sent_a = halves(kept_a, after(came_a, gprojs[-1]), turned_order[1])
    came_a = swapped(sent_a, turned_order[1])
    d_mlp = join_middle(joined(d_mlp, after(other, gprojs[-1]), order[-1]), order)
    other = swapped(d_mlp, order[1])
    low = full_due("B2", after(low, gprojs[-1], d_mlp, kept_a))
    gprojs.append(backward_quarter(low, slots, projs[2], lses[2], weights[2])[0])
    kept_a, sent_a = halve_middle(kept_a, after(came_a, gprojs[-1]), turned_order)
    came_a = swapped(sent_a, turned_order[-1])
    low = full_due("B3", after(low, gprojs[-1], kept_a))
    for j in range(3, mlp_size):
        gprojs.append(backward_quarter(low, slots, projs[j], lses[j], weights[j])[0])
    d_attn = (kept_a + after(came_a, gprojs[-1]).astype(FLOAT)).astype(LOWER)
    near, far = turned_order[-1], turned_order[-2]
    others_a = [
        lax.ppermute(d_attn, "rows", [(i, i ^ mask) for i in range(rows_size)])
        for mask in (1 << near, 1 << far, (1 << near) | (1 << far))
    ]
    d_mlp = joined(d_mlp, after(other, gprojs[-1]), order[1])
    other = swapped(d_mlp, 0)
    rows_grad, sums_one = first_norm(
        x, grad_hidden, after(logit, gprojs[-1], d_attn, d_mlp), norm_gains, router_row, gprojs, weights
    )
    others_a = [after(v, rows_grad) for v in others_a]
    d_attn = joined(joined(d_attn, others_a[0], near), joined(others_a[1], others_a[2], near), far)
    for bit in turned_order[-3:0:-1]:
        d_attn = joined(d_attn, swapped(d_attn, bit), bit)
    other_a = swapped(d_attn, 0)
    small = jnp.concatenate(
        [
            sums_two[:4],
            sums_one[:3],
            up_bias_sum[:1],
            jnp.pad(bias_grad[:1], ((0, 0), (0, width - 3 * own))),
        ],
        axis=0,
    )
    small = small + swapped(small, 0)
    other_s = swapped(small, order[1])
    input_grad, block_out = scatter_rows(
        place, full_parts, named, after(rows_grad, small, d_attn), branch, patch_t
    )
    block_out = block_out.T
    small = small + after(other_s, input_grad)
    for bit in order[2:-1]:
        small = small + swapped(small, bit)
    other_s = swapped(small, order[-1])
    d_qkv, d_out, d_up, d_down = finish_grads(
        core_one, d_attn, after(other_a, input_grad, small), d_mlp, other
    )
    small, other_s = after(small, d_qkv), after(other_s, d_qkv)
    d_gains, d_shifts, d_post_bias, d_up_bias, d_router, d_qkv_bias = finish_sums(small, other_s, own)
    d_qkv = d_qkv.T
    return (
        block_out,
        input_grad,
        d_qkv,
        d_qkv_bias,
        d_out,
        d_post_bias,
        d_up,
        d_up_bias,
        d_down,
        d_gains,
        d_shifts,
        d_router,
    )


def solution(mesh):
    in_specs = (
        P("rows", None),
        P(None, "mlp"),
        P(),
        P("mlp", None),
        P(),
        P(None, "mlp"),
        P("mlp"),
        P("mlp", None),
        P(),
        P(),
        P(),
        P("rows"),
        P("rows"),
        P("rows", "mlp"),
    )
    out_specs = (
        P("rows", "mlp"),
        P("rows", None),
        P(None, "mlp"),
        P(None, "mlp"),
        P("mlp", None),
        P(),
        P(None, "mlp"),
        P("mlp"),
        P("mlp", None),
        P(),
        P(),
        P(),
    )
    body = functools.partial(local, mesh.shape["rows"], mesh.shape["mlp"])
    return jax.shard_map(body, mesh=mesh, in_specs=in_specs, out_specs=out_specs, check_vma=False)
```

```python
import functools

import jax
import jax.numpy as jnp
from jax import lax
from jax.experimental import pallas as pl
from jax.experimental.pallas import tpu as pltpu
from jax.sharding import PartitionSpec as P

HD = 64
IMG_DEV = 6
L_MOST = 3
HALF_S = 99
HALF_L = 289

CHUNK = 304
CHUNKS = 1 + L_MOST
PACKED = CHUNK * CHUNKS
SHARE = 8
PIECES = 4

EPSILON = 1e-06
LOWER = jnp.bfloat16
FLOAT = jnp.float32
MASKED = -1e30


def nn(a, b):
    return lax.dot_general(a, b, (((1,), (0,)), ((), ())), preferred_element_type=FLOAT)


def nt(a, b):
    return lax.dot_general(a, b, (((1,), (1,)), ((), ())), preferred_element_type=FLOAT)


def tn(a, b):
    return lax.dot_general(a, b, (((0,), (0,)), ((), ())), preferred_element_type=FLOAT)


LATER = pltpu.MemorySpace.HBM


def params(mib):
    return pltpu.CompilerParams(vmem_limit_bytes=mib * 1024 * 1024)


def cost(flops, bytes_accessed, transcendentals=0):
    return pl.CostEstimate(
        flops=flops, bytes_accessed=bytes_accessed, transcendentals=transcendentals
    )


def whole(shape, single=True):
    zeros = (0,) * len(shape)
    if single:
        return pl.BlockSpec(shape, lambda *_: zeros, pipeline_mode=pl.Buffered(1))
    return pl.BlockSpec(shape, lambda *_: zeros)


def rows_spec(width, height=CHUNK):
    return pl.BlockSpec((height, width), lambda c, *_: (c, 0))


def chunk_spec(height, width=CHUNK):
    return pl.BlockSpec((1, height, width), lambda c, *_: (c, 0, 0))


def call(kernel, name, mib, operands, in_specs, outs, scratch=(), flops=0, place=None, grid=None, far=()):
    if far:
        operands = [
            pltpu.with_memory_space_constraint(o, LATER) if i in far else o
            for i, o in enumerate(operands)
        ]
    specs = [o[2] for o in outs]
    shapes = [o[3](o[0], o[1]) if len(o) > 3 else jax.ShapeDtypeStruct(o[0], o[1]) for o in outs]
    scalars = () if place is None else (place,)
    made = pl.pallas_call(
        kernel,
        grid_spec=pltpu.PrefetchScalarGridSpec(
            num_scalar_prefetch=len(scalars),
            grid=grid or (CHUNKS,),
            in_specs=in_specs,
            out_specs=specs,
            scratch_shapes=scratch,
        ),
        out_shape=shapes,
        compiler_params=params(mib),
        cost_estimate=cost(flops // 1000000, 1000),
        name=name,
    )(*scalars, *operands)
    return list(made)


def slot_onehot(slots_ref, rows, chunk=0):
    named = jnp.transpose(slots_ref[chunk])[:, 0:1].astype(jnp.int32)
    places = lax.broadcasted_iota(jnp.int32, (CHUNK, rows), 1)
    return (places == named).astype(FLOAT).astype(LOWER)


def outside_image(slots_ref):
    image = jnp.transpose(slots_ref[0])[:, 1:2]
    return jnp.where(image == slots_ref[0, 1:2, :], 0.0, MASKED)


def choose_own(place, values, own):
    width = values.shape[1]
    source = lax.broadcasted_iota(jnp.int32, (width, own), 0)
    target = lax.broadcasted_iota(jnp.int32, (width, own), 1)
    onehot = (source == target + place * own).astype(FLOAT).astype(LOWER)
    return nn(values, onehot).astype(LOWER)


def norm_stats(values):
    average = jnp.mean(values, axis=-1, keepdims=True)
    centred = values - average
    variance = jnp.mean(centred * centred, axis=-1, keepdims=True)
    inverse = lax.rsqrt(variance + EPSILON)
    return centred * inverse, inverse


def pick_kernel(
    patches_ref, slots_ref, gains_ref, shifts_ref, router_ref, x_ref, n_ref, gate_ref
):
    x = nn(slot_onehot(slots_ref, patches_ref.shape[0]), patches_ref[...])
    x_ref[...] = x.astype(LOWER)
    scaled, _ = norm_stats(x)
    n_ref[...] = (scaled * gains_ref[0:1, :] + shifts_ref[0:1, :]).astype(LOWER)
    logit = jnp.sum(x * router_ref[...], axis=-1, keepdims=True)
    gate_ref[...] = jnp.broadcast_to(jax.nn.sigmoid(logit), gate_ref.shape)


def pick_rows(patches, slots, gains, shifts, router):
    rows, width = patches.shape
    return call(
        pick_kernel,
        "pick_rows",
        20,
        (patches, slots, gains, shifts, router),
        [
            whole((rows, width)),
            chunk_spec(8),
            whole((2, width)),
            whole((2, width)),
            whole((1, width)),
        ],
        [
            ((PACKED, width), LOWER, rows_spec(width)),
            ((PACKED, width), LOWER, rows_spec(width)),
            ((PACKED, 128), FLOAT, rows_spec(128)),
        ],
        flops=2 * PACKED * rows * width,
    )


def pick_cot_kernel(cot_ref, slots_ref, part_ref):
    for c in range(CHUNKS):
        onehot = slot_onehot(slots_ref, cot_ref.shape[1], c)
        part_ref[:, c * CHUNK : (c + 1) * CHUNK] = nt(cot_ref[...], onehot).astype(LOWER)


def pick_cot(cot_own, slots):
    own, rows = cot_own.shape
    return call(
        pick_cot_kernel,
        "pick_cot",
        24,
        (cot_own, slots),
        [whole((own, rows)), whole(slots.shape)],
        [((own, PACKED), LOWER, whole((own, PACKED)))],
        flops=2 * PACKED * rows * own,
        grid=(1,),
    )[0]


def own_columns_kernel(place_ref, patches_ref, patch_ref):
    own, width = patch_ref.shape[0], patches_ref.shape[1]
    source = lax.broadcasted_iota(jnp.int32, (own, width), 1)
    target = lax.broadcasted_iota(jnp.int32, (own, width), 0)
    chosen = (source == target + place_ref[0] * own).astype(FLOAT).astype(LOWER)
    patch_ref[...] = nt(chosen, patches_ref[...]).astype(LOWER)


def own_columns(place, patches, own):
    rows, width = patches.shape
    return call(
        own_columns_kernel,
        "own_columns",
        12,
        (patches,),
        [whole((rows, width))],
        [((own, rows), LOWER, whole((own, rows)), LATER)],
        flops=2 * own * rows * width,
        place=place,
        grid=(1,),
        far=(0,),
    )[0]


def head_slabs(own):
    slabs = []
    for start in range(0, own, 2 * HD):
        stop = min(start + 2 * HD, own)
        lanes = lax.broadcasted_iota(jnp.int32, (1, stop - start), 1)
        heads = []
        for head in range(start // HD, stop // HD):
            low = head * HD - start
            heads.append((head, (lanes >= low) & (lanes < low + HD)))
        slabs.append((start, stop, heads))
    return slabs


def keep(mask, values):
    return jnp.where(mask, values, jnp.zeros_like(values))


def forward_kernel(kind_ref, n_ref, bias_ref, slots_ref, *refs):
    proj_ref, mix_ref, lse_ref, weights_ref = refs[-4:]
    parts = refs[:-4]
    own = mix_ref.shape[1]

    @pl.when(pl.program_id(0) == 0)
    def _():
        if len(parts) == 1:
            weights_ref[...] = parts[0][...]
        else:
            for other, part_ref in enumerate(parts):
                held = part_ref.shape[0]
                start = pl.multiple_of((kind_ref[0] ^ other) * held, 32)
                weights_ref[pl.ds(start, held), :] = part_ref[...]

    proj_ref[...] = (nt(n_ref[...], weights_ref[0 : 3 * own, :]) + bias_ref[0]).astype(LOWER)
    outside = outside_image(slots_ref)
    lse_all = jnp.zeros((CHUNK, 128), FLOAT)
    lanes = lax.broadcasted_iota(jnp.int32, (1, 128), 1)
    for start, stop, heads in head_slabs(own):
        q = proj_ref[:, start:stop] * LOWER(HD**-0.5)
        k = proj_ref[:, own + start : own + stop]
        v = proj_ref[:, 2 * own + start : 2 * own + stop]
        mixed = None
        for head, mask in heads:
            scores = nt(q, keep(mask, k)) + outside
            largest = jnp.max(scores, axis=-1, keepdims=True)
            powered = jnp.exp(scores - largest)
            total = jnp.sum(powered, axis=-1, keepdims=True)
            probs = (powered * (1.0 / total)).astype(LOWER)
            part = nn(probs, keep(mask, v))
            mixed = part if mixed is None else mixed + part
            lse_all = jnp.where(lanes == head, largest + jnp.log(total), lse_all)
        mix_ref[:, start:stop] = mixed.astype(LOWER)
    lse_ref[0] = jnp.transpose(lse_all)[0:8, :]


def forward_quarter(kind, normed, biases, slots, parts, j):
    width = normed.shape[1]
    own = biases.shape[2] // 3
    return call(
        forward_kernel,
        "forward_quarter",
        11,
        (normed, biases, slots, *parts),
        [
            rows_spec(width),
            pl.BlockSpec((1, 1, 3 * own), lambda c, *_: (j, 0, 0)),
            chunk_spec(8),
            *[whole(p.shape) for p in parts],
        ],
        [
            ((PACKED, 3 * own), LOWER, rows_spec(3 * own), LATER),
            ((PACKED, own), LOWER, rows_spec(own)),
            ((CHUNKS, 8, CHUNK), FLOAT, chunk_spec(8), LATER),
            ((4 * own, width), LOWER, whole((4 * own, width))),
        ],
        flops=2 * PACKED * width * 8 * own,
        place=kind,
    )


def join_kernel(place_ref, x_ref, post_ref, own_post_ref, gains_ref, shifts_ref, *refs):
    hidden_ref, normed_ref, own_ref, chosen = refs[-4:]
    parts = refs[:-4]
    count = len(parts) // 2
    own = own_ref.shape[1]

    @pl.when(pl.program_id(0) == 0)
    def _():
        for j, out_ref in enumerate(parts[count:]):
            chosen[j * own : (j + 1) * own, :] = choose_own(place_ref[0], out_ref[...], own)

    attn, attn_own = post_ref[0:1, :], own_post_ref[0:1, :]
    for j, (mix_ref, out_ref) in enumerate(zip(parts[:count], parts[count:])):
        attn = attn + nn(mix_ref[...], out_ref[...])
        attn_own = attn_own + nn(mix_ref[...], chosen[j * own : (j + 1) * own, :])
    own_ref[...] = attn_own
    hidden = x_ref[...].astype(FLOAT) + attn
    hidden_ref[...] = hidden
    scaled, _ = norm_stats(hidden)
    normed_ref[...] = (scaled * gains_ref[1:2, :] + shifts_ref[1:2, :]).astype(LOWER)


def out_spec(own, width):
    return pl.BlockSpec((own, width), lambda *_: (3, 0), pipeline_mode=pl.Buffered(1))


def join_quarters(place, x, post, own_post, gains, shifts, mixes, weights):
    width = x.shape[1]
    own = mixes[0].shape[1]
    return call(
        join_kernel,
        "join_quarters",
        11,
        (x, post, own_post, gains, shifts, *mixes, *weights),
        [
            rows_spec(width),
            whole((2, width)),
            whole((2, own)),
            whole((2, width)),
            whole((2, width)),
            *[rows_spec(own) for _ in mixes],
            *[out_spec(own, width) for _ in weights],
        ],
        [
            ((PACKED, width), FLOAT, rows_spec(width), LATER),
            ((PACKED, width), LOWER, rows_spec(width)),
            ((PACKED, own), FLOAT, rows_spec(own), LATER),
        ],
        scratch=[pltpu.VMEM((len(weights) * own, own), LOWER)],
        flops=3 * PACKED * width * width,
        place=place,
    )


def stack_places(place, parts, stacked):
    size = len(parts)
    for j, part in enumerate(parts):
        own = part.shape[0]
        start = pl.multiple_of(lax.rem(place - j + size, size) * own, 64)
        stacked[pl.ds(start, own), :] = part.astype(stacked.dtype)


def cot_kernel(place_ref, gate_ref, *refs):
    cot_ref, gated_ref, stacked = refs[-3:]
    stack_places(place_ref[0], [r[...] for r in refs[:-3]], stacked)
    cot = jnp.transpose(stacked[...])
    cot_ref[...] = cot
    gated_ref[...] = (gate_ref[:, 0:1] * cot.astype(FLOAT)).astype(LOWER)


def cot_chunks(place, gate, parts):
    own = parts[0].shape[0]
    width = own * len(parts)
    return call(
        cot_kernel,
        "cot_chunks",
        20,
        (gate, *parts),
        [whole((PACKED, 128)), *[whole(p.shape) for p in parts]],
        [
            ((PACKED, width), LOWER, whole((PACKED, width)), LATER),
            ((PACKED, width), LOWER, whole((PACKED, width))),
        ],
        scratch=[pltpu.VMEM((width, PACKED), LOWER)],
        flops=PACKED * width,
        place=place,
        grid=(1,),
    )


def gelu_pair(u):
    cdf = 0.5 * (1.0 + lax.erf(u * (0.5**0.5)))
    density = jnp.exp(-0.5 * u * u) * 0.3989422804014327
    return u * cdf, cdf + u * density


def mlp_step(normed, gated, up_ref, down_ref, bias, own_down_ref):
    hidden = up_ref.shape[1]
    block = hidden // 3

    def products(start):
        cols = slice(start, start + block)
        pre_act = nn(normed, up_ref[:, cols]) + bias[:, cols]
        return pre_act, nt(gated, down_ref[cols, :])

    activations, grads, grad, gate, out = [], [], None, None, None
    ahead = products(0)
    for start in range(0, hidden, block):
        cols = slice(start, start + block)
        pre_act, grad_act = ahead
        if start + block < hidden:
            ahead = products(start + block)
        activation, slope = gelu_pair(pre_act)
        activation = activation.astype(LOWER)
        grad_pre = (grad_act * slope).astype(LOWER)
        gate_part = jnp.sum(activation.astype(FLOAT) * grad_act, axis=-1, keepdims=True)
        grad_part = nt(grad_pre, up_ref[:, cols])
        out_part = nn(activation, own_down_ref[cols, :])
        activations.append(activation)
        grads.append(grad_pre)
        grad = grad_part if grad is None else grad + grad_part
        gate = gate_part if gate is None else gate + gate_part
        out = out_part if out is None else out + out_part
    return activations, grads, grad, gate, out


def own_mlp_kernel(
    place_ref,
    n_ref,
    gated_ref,
    up_ref,
    down_ref,
    bias_ref,
    act_ref,
    pre_ref,
    grad_ref,
    gate_ref,
    out_ref,
    bias_sum_ref,
    own_down,
):
    @pl.when(pl.program_id(0) == 0)
    def _():
        own_down[...] = choose_own(place_ref[0], down_ref[...], own_down.shape[1])
        bias_sum_ref[...] = jnp.zeros_like(bias_sum_ref)

    activation, grad_pre, grad_part, gate_part, out_part = mlp_step(
        n_ref[...], gated_ref[...], up_ref, down_ref, bias_ref[...], own_down
    )
    block = activation[0].shape[1]
    for i, (act, pre) in enumerate(zip(activation, grad_pre)):
        act_ref[:, i * block : (i + 1) * block] = act
        pre_ref[:, i * block : (i + 1) * block] = pre
    grad_ref[...] = grad_part
    gate_ref[...] = jnp.broadcast_to(gate_part, gate_ref.shape)
    out_ref[...] = out_part
    bias_sum_ref[0:1, :] += jnp.sum(pre_ref[...].astype(FLOAT), axis=0, keepdims=True)


def own_mlp(place, normed, gated, up, down, bias, own):
    width, hidden = up.shape
    return call(
        own_mlp_kernel,
        "own_mlp",
        17,
        (normed, gated, up, down, bias),
        [
            rows_spec(width),
            rows_spec(width),
            whole((width, hidden)),
            whole((hidden, width)),
            whole((1, hidden)),
        ],
        [
            ((PACKED, hidden), LOWER, rows_spec(hidden)),
            ((PACKED, hidden), LOWER, rows_spec(hidden)),
            ((PACKED, width), FLOAT, rows_spec(width), LATER),
            ((PACKED, 128), FLOAT, rows_spec(128)),
            ((PACKED, own), FLOAT, rows_spec(own)),
            ((8, hidden), FLOAT, whole((8, hidden), False)),
        ],
        scratch=[pltpu.VMEM((hidden, own), LOWER)],
        flops=2 * PACKED * hidden * (3 * width + own),
        place=place,
    )


def own_grads_kernel(core_ref, n_ref, pre_ref, act_ref, gated_ref, kept_ref, sent_ref):
    grad_up = tn(n_ref[...], pre_ref[...])
    grad_down = tn(act_ref[...], gated_ref[...])

    @pl.when(core_ref[0] == 0)
    def _():
        kept_ref[...] = grad_up
        sent_ref[...] = grad_down.astype(LOWER)

    @pl.when(core_ref[0] == 1)
    def _():
        kept_ref[...] = grad_down
        sent_ref[...] = grad_up.astype(LOWER)


def own_grads(core, normed, grad_pre, act, gated):
    width = normed.shape[1]
    block = width // 3
    columns = pl.BlockSpec((PACKED, block), lambda c, *_: (0, c))
    return call(
        own_grads_kernel,
        "own_grads",
        16,
        (normed, grad_pre, act, gated),
        [columns, whole((PACKED, width)), columns, whole((PACKED, width))],
        [
            ((width, width), FLOAT, rows_spec(width, block)),
            ((width, width), LOWER, rows_spec(width, block)),
        ],
        flops=4 * PACKED * width * width,
        place=core,
        grid=(3,),
    )


def other_mlp_kernel(
    last, place_ref, n_ref, gated_ref, grad_in_ref, gate_in_ref, out_in_ref, *refs
):
    grad_ref, gate_ref, out_ref, up, down, own_down = refs[-6:]
    ups, downs = refs[0:4], refs[4:8]
    part = downs[0].shape[2]
    width = up.shape[1]

    @pl.when(pl.program_id(0) == 0)
    def _():
        for side in range(2):
            for c in range(2):
                for near in range(2):
                    to_up = place_ref[1] ^ (4 * side + 2 * near + c)
                    to_down = place_ref[1] ^ (4 * near + 2 * side + c)
                    up_rows = pl.ds(pl.multiple_of(to_up * part, 32), part)
                    down_rows = pl.ds(pl.multiple_of(to_down * part, 32), part)
                    up[up_rows, :] = ups[side + 2 * c][near, 0, 0:part]
                    down[down_rows, :] = downs[side + 2 * c][near, 0]
        own_down[...] = choose_own(place_ref[0], down[...], own_down.shape[1])

    pieces = ups[0][0, 0, part : part + 16].astype(FLOAT)
    bias = pieces[0:1] + (pieces[1:2] + pieces[2:3])
    _, _, grad_part, gate_part, out_part = mlp_step(
        n_ref[...], gated_ref[...], up, down, bias, own_down
    )
    grad_ref[...] = grad_in_ref[...] + grad_part
    gate_ref[...] = gate_in_ref[...] + gate_part
    if last:
        attn_ref, post_ref, open_ref = refs[8:11]
        total = out_in_ref[...] + out_part + attn_ref[...] + post_ref[1:2, :]
        out_ref[...] = open_ref[:, 0:1] * total
    else:
        out_ref[...] = out_in_ref[...] + out_part


def other_mlp(places, normed, gated, sums, ups, downs, j, extra=()):
    width = normed.shape[1]
    own = sums[2].shape[1]
    last = len(extra) > 0
    held = lambda array: pl.BlockSpec(
        (2, 1, *array.shape[2:]), lambda c, *_: (0, j, 0, 0), pipeline_mode=pl.Buffered(1)
    )
    extra_specs = [rows_spec(own), whole((2, own)), rows_spec(128)] if last else []
    return call(
        functools.partial(other_mlp_kernel, last),
        "other_mlp",
        17,
        (normed, gated, *sums, *ups, *downs, *extra),
        [
            rows_spec(width),
            rows_spec(width),
            rows_spec(width),
            rows_spec(128),
            rows_spec(own),
            *[held(u) for u in ups],
            *[held(d) for d in downs],
            *extra_specs,
        ],
        [
            ((PACKED, width), FLOAT, rows_spec(width)),
            ((PACKED, 128), FLOAT, rows_spec(128)),
            ((PACKED, own), FLOAT, rows_spec(own)),
        ],
        scratch=[
            pltpu.VMEM((width, width), LOWER),
            pltpu.VMEM((width, width), LOWER),
            pltpu.VMEM((width, own), LOWER),
        ],
        flops=2 * PACKED * width * (3 * width + own),
        place=places,
    )


def second_norm_kernel(
    grad_ref,
    gate_part_ref,
    hidden_ref,
    x_ref,
    cot_ref,
    gate_ref,
    post_ref,
    gains_ref,
    ghid_ref,
    glow_ref,
    logit_ref,
    sums_ref,
):
    @pl.when(pl.program_id(0) == 0)
    def _():
        sums_ref[...] = jnp.zeros_like(sums_ref)

    hidden = hidden_ref[...]
    scaled, inverse = norm_stats(hidden)
    grad_out = grad_ref[...]
    weighted = grad_out * gains_ref[1:2, :]
    centre_term = jnp.mean(weighted, axis=-1, keepdims=True)
    scale_term = jnp.mean(weighted * scaled, axis=-1, keepdims=True)
    grad_hidden = inverse * (weighted - centre_term - scaled * scale_term)
    gate = gate_ref[:, 0:1]
    gated = gate * cot_ref[...].astype(FLOAT)
    grad_attn = grad_hidden + gated
    ghid_ref[...] = grad_hidden
    glow_ref[...] = grad_attn.astype(LOWER)
    attn = hidden - x_ref[...].astype(FLOAT)
    dotted = jnp.sum(gated * (attn + post_ref[1:2, :]), axis=-1, keepdims=True)
    logit = (1.0 - gate) * (dotted + gate_part_ref[:, 0:1])
    logit_ref[...] = jnp.broadcast_to(logit, logit_ref.shape)
    sums_ref[0:1, :] += jnp.sum(grad_out * scaled, axis=0, keepdims=True)
    sums_ref[1:2, :] += jnp.sum(grad_out, axis=0, keepdims=True)
    sums_ref[2:3, :] += jnp.sum(grad_attn, axis=0, keepdims=True)
    sums_ref[3:4, :] += jnp.sum(gated, axis=0, keepdims=True)


def second_norm(grad, gate_part, hidden, x, cot_rows, gate, post, gains):
    width = x.shape[1]
    return call(
        second_norm_kernel,
        "second_norm",
        14,
        (grad, gate_part, hidden, x, cot_rows, gate, post, gains),
        [
            rows_spec(width),
            rows_spec(128),
            rows_spec(width),
            rows_spec(width),
            rows_spec(width),
            rows_spec(128),
            whole((2, width)),
            whole((2, width)),
        ],
        [
            ((PACKED, width), FLOAT, rows_spec(width)),
            ((PACKED, width), LOWER, rows_spec(width)),
            ((PACKED, 128), FLOAT, rows_spec(128)),
            ((8, width), FLOAT, whole((8, width), False)),
        ],
        flops=20 * PACKED * width,
    )


def backward_kernel(low_ref, slots_ref, proj_ref, lse_ref, out_ref, gproj_ref, sums_ref):
    @pl.when(pl.program_id(0) == 0)
    def _():
        sums_ref[...] = jnp.zeros_like(sums_ref)

    outside = outside_image(slots_ref)
    own = out_ref.shape[0]
    heads = own // HD
    g = nt(low_ref[...], out_ref[...]).astype(LOWER)
    q = proj_ref[:, 0:own] * LOWER(HD**-0.5)
    k = proj_ref[:, own : 2 * own]
    v = proj_ref[:, 2 * own : 3 * own]
    lanes = lax.broadcasted_iota(jnp.int32, (1, own), 1) // HD
    keys = jnp.concatenate([keep(lanes == head, k) for head in range(heads)], axis=0)
    values = jnp.concatenate([keep(lanes == head, v) for head in range(heads)], axis=0)
    scores = nt(keys, q)
    grad_probs = nt(values, g)
    probs, grad_scores = [], []
    for head in range(heads):
        rows = slice(head * CHUNK, (head + 1) * CHUNK)
        prob = jnp.exp(scores[rows] + outside - lse_ref[0, head : head + 1, :])
        inner = jnp.sum(prob * grad_probs[rows], axis=0, keepdims=True)
        grad_scores.append((prob * (grad_probs[rows] - inner)).astype(LOWER))
        probs.append(prob.astype(LOWER))
    grad_scores = jnp.concatenate(grad_scores, axis=0)
    all_v = nn(jnp.concatenate(probs, axis=0), g)
    all_k = nn(grad_scores, q)
    grad_q = tn(grad_scores, keys)
    grad_k, grad_v = all_k[0:CHUNK], all_v[0:CHUNK]
    for head in range(1, heads):
        rows = slice(head * CHUNK, (head + 1) * CHUNK)
        grad_k = jnp.where(lanes == head, all_k[rows], grad_k)
        grad_v = jnp.where(lanes == head, all_v[rows], grad_v)
    gproj_ref[:, 0:own] = (grad_q * HD**-0.5).astype(LOWER)
    gproj_ref[:, own : 2 * own] = grad_k.astype(LOWER)
    gproj_ref[:, 2 * own : 3 * own] = grad_v.astype(LOWER)
    sums_ref[0:1, :] += jnp.sum(gproj_ref[...].astype(FLOAT), axis=0, keepdims=True)


def backward_quarter(low, slots, proj, lse, weights):
    width = low.shape[1]
    own = proj.shape[1] // 3
    return call(
        backward_kernel,
        "backward_quarter",
        16,
        (low, slots, proj, lse, weights),
        [
            rows_spec(width),
            chunk_spec(8),
            rows_spec(3 * own),
            chunk_spec(8),
            out_spec(own, width),
        ],
        [
            ((PACKED, 3 * own), LOWER, rows_spec(3 * own)),
            ((8, 3 * own), FLOAT, whole((8, 3 * own), False)),
        ],
        flops=2 * PACKED * width * 14 * own,
    )


def attn_grads_kernel(core_ref, gproj_ref, normed_ref, mix_ref, low_ref, kept_ref, sent_ref):
    half = kept_ref.shape[0]
    rest = gproj_ref.shape[1] - half
    normed = normed_ref[...]
    first = tn(gproj_ref[:, 0:half], normed)
    second = tn(gproj_ref[:, half:], normed)
    third = tn(mix_ref[...], low_ref[...])

    @pl.when(core_ref[0] == 0)
    def _():
        kept_ref[...] = first
        sent_ref[0:rest, :] = second.astype(LOWER)
        sent_ref[rest:half, :] = third.astype(LOWER)

    @pl.when(core_ref[0] == 1)
    def _():
        kept_ref[0:rest, :] = second
        kept_ref[rest:half, :] = third
        sent_ref[...] = first.astype(LOWER)


def attn_grads(core, gproj, normed, mix, low):
    width, own = normed.shape[1], mix.shape[1]
    operands = (gproj, normed, mix, low)
    return call(
        attn_grads_kernel,
        "attn_grads",
        18,
        operands,
        [whole(o.shape) for o in operands],
        [
            ((2 * own, width), FLOAT, whole((2 * own, width))),
            ((2 * own, width), LOWER, whole((2 * own, width))),
        ],
        place=core,
        grid=(1,),
    )


def first_norm_kernel(x_ref, ghid_ref, logit_ref, gains_ref, router_ref, *refs):
    rows_ref, sums_ref, gprojs, weights = refs[-4:]
    parts = refs[:-4]
    count = len(parts) // 2
    held = parts[0].shape[1]

    @pl.when(pl.program_id(0) == 0)
    def _():
        sums_ref[...] = jnp.zeros_like(sums_ref)
        for j, weights_ref in enumerate(parts[count:]):
            weights[j * held : (j + 1) * held, :] = weights_ref[0:held, :]

    for j, gproj_ref in enumerate(parts[:count]):
        gprojs[:, j * held : (j + 1) * held] = gproj_ref[...]
    grad_out = nn(gprojs[...], weights[...])
    x = x_ref[...].astype(FLOAT)
    scaled, inverse = norm_stats(x)
    weighted = grad_out * gains_ref[0:1, :]
    centre_term = jnp.mean(weighted, axis=-1, keepdims=True)
    scale_term = jnp.mean(weighted * scaled, axis=-1, keepdims=True)
    grad_norm = inverse * (weighted - centre_term - scaled * scale_term)
    logit = logit_ref[:, 0:1]
    rows_ref[...] = (ghid_ref[...] + grad_norm + logit * router_ref[...]).astype(LOWER)
    sums_ref[0:1, :] += jnp.sum(grad_out * scaled, axis=0, keepdims=True)
    sums_ref[1:2, :] += jnp.sum(grad_out, axis=0, keepdims=True)
    sums_ref[2:3, :] += jnp.sum(logit * x, axis=0, keepdims=True)


def first_norm(x, ghid, logit, gains, router, gprojs, weights):
    width = x.shape[1]
    return call(
        first_norm_kernel,
        "first_norm",
        24,
        (x, ghid, logit, gains, router, *gprojs, *weights),
        [
            rows_spec(width),
            rows_spec(width),
            rows_spec(128),
            whole((2, width)),
            whole((1, width)),
            *[rows_spec(g.shape[1]) for g in gprojs],
            *[whole(w.shape) for w in weights],
        ],
        [
            ((PACKED, width), LOWER, rows_spec(width)),
            ((8, width), FLOAT, whole((8, width), False)),
        ],
        scratch=[pltpu.VMEM((CHUNK, 3 * width), LOWER), pltpu.VMEM((3 * width, width), LOWER)],
        flops=2 * PACKED * width * 3 * width,
    )


def scatter_kernel(place_ref, named_ref, rows_ref, branch_ref, patch_ref, *refs):
    out_ref, block_ref, stacked, branch_t = refs[-4:]
    block = out_ref.shape[0]

    @pl.when(pl.program_id(0) == 0)
    def _():
        branch_t[...] = jnp.transpose(branch_ref[...].astype(LOWER))

    stack_places(place_ref[0], [r[...] for r in refs[:-4]], stacked)
    places = lax.broadcasted_iota(jnp.int32, (block, PACKED), 0) + pl.program_id(0) * block
    onehot = (places == named_ref[...]).astype(FLOAT).astype(LOWER)
    cot = jnp.transpose(stacked[...]).astype(FLOAT)
    out_ref[...] = (cot + nn(onehot, rows_ref[...])).astype(LOWER)
    block_ref[...] = (patch_ref[...].astype(FLOAT) + nt(branch_t[...], onehot)).astype(LOWER)


def scatter_rows(place, cot_parts, named, rows, branch, patch_t):
    own, total = cot_parts[0].shape
    width = own * len(cot_parts)
    block = 512
    columns = pl.BlockSpec((own, block), lambda c, *_: (0, c))
    return call(
        scatter_kernel,
        "scatter_rows",
        19,
        (named, rows, branch, patch_t, *cot_parts),
        [
            whole(named.shape),
            whole((PACKED, width)),
            whole((PACKED, own)),
            columns,
            *[columns for _ in cot_parts],
        ],
        [
            ((total, width), LOWER, rows_spec(width, block), LATER),
            ((own, total), LOWER, columns, LATER),
        ],
        scratch=[
            pltpu.VMEM((width, block), LOWER),
            pltpu.VMEM((own, PACKED), LOWER),
        ],
        flops=2 * PACKED * total * width,
        place=place,
        grid=(pl.cdiv(total, block),),
        far=range(3, 4 + len(cot_parts)),
    )


def halve_kernel(upper_ref, kept_ref, came_ref, half_ref, sent_ref):
    block, half = half_ref.shape[0], kept_ref.shape[0] // 2
    step = pl.program_id(0) * block
    own = pl.ds(pl.multiple_of(upper_ref[0] * half + step, 16), block)
    far = pl.ds(pl.multiple_of((1 - upper_ref[0]) * half + step, 16), block)
    half_ref[...] = kept_ref[own, :] + came_ref[own, :].astype(FLOAT)
    sent_ref[...] = (kept_ref[far, :] + came_ref[far, :].astype(FLOAT)).astype(LOWER)


def halve_sum(upper, kept, came):
    rows, width = kept.shape
    return call(
        halve_kernel,
        "halve_sum",
        10,
        (kept, came),
        [whole((rows, width)), whole((rows, width))],
        [
            ((rows // 2, width), FLOAT, rows_spec(width, rows // 4)),
            ((rows // 2, width), LOWER, rows_spec(width, rows // 4)),
        ],
        place=upper,
        grid=(2,),
    )


def finish_kernel(core_ref, attn_ref, attn_far_ref, mlp_ref, mlp_far_ref, *refs):
    qkv_ref, out_ref, up_ref, down_ref = refs
    own, block = qkv_ref.shape[0], up_ref.shape[0]
    head = pl.program_id(0)
    rows = pl.ds(pl.multiple_of(head * block, 16), block)

    def write(low_ref, high_ref, first_ref, second_ref):
        one = pl.ds(pl.multiple_of(head * HD, HD), HD)
        two = pl.ds(pl.multiple_of(own + head * HD, HD), HD)
        qkv_ref[0:HD, :] = low_ref[one, :].astype(FLOAT)
        qkv_ref[HD : 2 * HD, :] = low_ref[two, :].astype(FLOAT)
        qkv_ref[2 * HD : 3 * HD, :] = high_ref[one, :].astype(FLOAT)
        out_ref[...] = high_ref[two, :].astype(FLOAT)
        up_ref[...] = first_ref[rows, :].astype(FLOAT)
        down_ref[...] = second_ref[rows, :].astype(FLOAT)

    @pl.when(core_ref[0] == 0)
    def _():
        write(attn_ref, attn_far_ref, mlp_ref, mlp_far_ref)

    @pl.when(core_ref[0] == 1)
    def _():
        write(attn_far_ref, attn_ref, mlp_far_ref, mlp_ref)


def finish_grads(core, attn, attn_far, mlp, mlp_far):
    width = mlp.shape[1]
    own = attn.shape[0] // 2
    heads = own // HD
    return call(
        finish_kernel,
        "finish_grads",
        16,
        (attn, attn_far, mlp, mlp_far),
        [whole(attn.shape), whole(attn.shape), whole(mlp.shape), whole(mlp.shape)],
        [
            ((3 * own, width), FLOAT, rows_spec(width, 3 * HD)),
            ((own, width), FLOAT, rows_spec(width, HD)),
            ((width, width), FLOAT, rows_spec(width, width // heads)),
            ((width, width), FLOAT, rows_spec(width, width // heads)),
        ],
        place=core,
        grid=(heads,),
    )


def finish_sums_kernel(own_ref, far_ref, *refs):
    gains_ref, shifts_ref, post_ref, up_ref, router_ref, qkv_ref = refs
    total = own_ref[...] + far_ref[...]
    own = qkv_ref.shape[1]
    gains_ref[0:1, :] = total[4:5]
    gains_ref[1:2, :] = total[0:1]
    shifts_ref[0:1, :] = total[5:6]
    shifts_ref[1:2, :] = total[1:2]
    post_ref[...] = total[2:4]
    up_ref[...] = total[7]
    router_ref[...] = total[6]
    qkv_ref[0:1, :] = total[8:9, 0:own]
    qkv_ref[1:2, :] = total[8:9, 2 * own : 3 * own]


def finish_sums(small, far, own):
    rows, width = small.shape
    shapes = [(2, width), (2, width), (2, width), (width,), (width,), (2, own)]
    return call(
        finish_sums_kernel,
        "finish_sums",
        4,
        (small, far),
        [whole((rows, width)), whole((rows, width))],
        [(shape, FLOAT, whole(shape)) for shape in shapes],
        grid=(1,),
    )


def turned(values, place):
    size = values.shape[0]
    back = jnp.concatenate([values[:1], values[:0:-1]], axis=0)
    twice = jnp.concatenate([back, back], axis=0)
    return lax.dynamic_slice_in_dim(twice, (size - place) % size, size, 0)


def after(value, *others):
    return lax.optimization_barrier((value, *others))[0]


def ring_step(value, size):
    return lax.ppermute(value, "mlp", [(i, (i + 1) % size) for i in range(size)])


def swap(value, bit, size):
    return lax.ppermute(value, "rows", [(i, i ^ (1 << bit)) for i in range(size)])


def bits_of(size):
    return [b for b in range(20) if (1 << b) < size]


def pack_slots(picked, live_slots):
    small = IMG_DEV * HALF_S
    named = jnp.where(live_slots == 1, picked, -1)

    def padded(parts, fill):
        have = sum(p.shape[0] for p in parts)
        return jnp.concatenate([*parts, jnp.full((CHUNK - have,), fill, jnp.int32)])

    always = IMG_DEV - L_MOST
    idx = [padded([named[: always * HALF_S]], -1)]
    seg = [padded([jnp.repeat(jnp.arange(always, dtype=jnp.int32), HALF_S)], always)]
    for j in range(L_MOST):
        first = small + j * HALF_L
        alive = live_slots[first] == 1
        other = IMG_DEV - 1 - j
        large_idx = padded([named[first : first + HALF_L]], -1)
        small_idx = padded([named[other * HALF_S : (other + 1) * HALF_S]], -1)
        idx.append(jnp.where(alive, large_idx, small_idx))
        length = jnp.where(alive, HALF_L, HALF_S)
        seg.append((jnp.arange(CHUNK, dtype=jnp.int32) >= length).astype(jnp.int32))
    named = jnp.concatenate(idx).reshape(1, PACKED)
    idx, seg = jnp.stack(idx).astype(FLOAT), jnp.stack(seg).astype(FLOAT)
    rows = lax.broadcasted_iota(jnp.int32, (1, 8, 1), 1)
    return jnp.where(rows == 0, idx[:, None, :], seg[:, None, :]), named


def local(
    rows_size,
    mlp_size,
    patches,
    w_qkv,
    qkv_bias,
    w_out,
    post_bias,
    w_up,
    up_bias,
    w_down,
    norm_gains,
    norm_shifts,
    router,
    picked,
    live_slots,
    cotangent,
):
    width = patches.shape[1]
    mlp_index = lax.axis_index("mlp")
    rows_index = lax.axis_index("rows")
    share_index = rows_index % SHARE
    core = rows_index & 1
    place = mlp_index.astype(jnp.int32).reshape(1)
    places = jnp.stack([mlp_index, share_index]).astype(jnp.int32)
    kind = (rows_index % PIECES).astype(jnp.int32).reshape(1)
    own = w_out.shape[0]
    heads_here = own // HD
    others = mlp_size - 1
    router_row = router.reshape(1, width)

    def swapped(value, bit):
        return swap(value, bit, rows_size)

    own_weights = jnp.concatenate(
        [
            w_qkv.T.reshape(heads_here, 3, HD, width).transpose(1, 0, 2, 3).reshape(3 * own, width),
            w_out,
        ],
        axis=0,
    )
    held = own_weights.shape[0] // PIECES
    piece = lax.dynamic_slice_in_dim(own_weights, kind[0] * held, held, 0)
    part = w_up.shape[0] // SHARE
    top = lax.reduce_precision(up_bias, 8, 7)
    middle = lax.reduce_precision(up_bias - top, 8, 7)
    bias_rows = jnp.stack([top, middle, up_bias - top - middle]).astype(LOWER)
    payload = jnp.concatenate(
        [
            piece,
            lax.dynamic_slice_in_dim(w_up, share_index * part, part, 0),
            jnp.pad(bias_rows, ((0, 13), (0, 0))),
            lax.dynamic_slice_in_dim(w_down, share_index * part, part, 0),
        ],
        axis=0,
    )
    def around(value):
        return ring_step(value, mlp_size)

    kinds = jnp.stack([qkv_bias[0], jnp.zeros_like(qkv_bias[0]), qkv_bias[1]])
    biases = turned(kinds.reshape(3, mlp_size, own).transpose(1, 0, 2), mlp_index)
    biases = biases.reshape(mlp_size, 1, 3 * own)
    own_post = lax.dynamic_slice_in_dim(post_bias, mlp_index * own, own, 1)
    slots, named = pack_slots(picked, live_slots)
    cot_own = cotangent.T
    core_one = core.astype(jnp.int32).reshape(1)

    def split(came):
        return came[:held], came[held : held + part + 16], came[held + part + 16 :]

    def across(value, mask):
        return lax.ppermute(value, "rows", [(i, i ^ mask) for i in range(rows_size)])

    def forward(j, normed, parts):
        return forward_quarter(kind, normed, biases, slots, parts, j)

    order = bits_of(rows_size)
    lower = {bit: (rows_index >> bit) & 1 == 0 for bit in order}
    upper = {bit: ((rows_index >> bit) & 1).astype(jnp.int32).reshape(1) for bit in order}
    payload, place, places, kind, core_one, lower, upper = lax.optimization_barrier(
        (payload, place, places, kind, core_one, lower, upper)
    )
    came = around(payload)
    patches, named, own_post, biases = lax.optimization_barrier(
        (after(patches, payload), named, own_post, biases)
    )
    x, normed_one, gate = pick_rows(
        patches, slots, norm_gains, norm_shifts, router_row
    )
    came = after(came, x)
    cot_part = pick_cot(after(cot_own, came), slots)
    normed_one = after(normed_one, cot_part)
    quarters, cot_parts, up_parts, down_parts = [], [cot_part], [], []
    parts, before = [own_weights], x
    for j in range(mlp_size):
        if j < others:
            came = after(came, before)
            got, up_part, down_part = split(came)
            up_parts.append(up_part)
            down_parts.append(down_part)
            if j + 1 < others:
                came = around(came)
            spread = [got, *[across(got, mask) for mask in range(2, PIECES, 2)]]
        if 0 < j < others:
            cot_parts.append(around(after(cot_parts[-1], got)))
        normed_one = after(normed_one, got, before, *parts)
        if j == others:
            normed_one = after(normed_one, *cot_parts[:-1])
            ups, downs = jnp.stack(up_parts), jnp.stack(down_parts)
            ups_x, downs_y = swapped(ups, 1), swapped(downs, 2)
        quarters.append(forward(j, normed_one, parts))
        before = quarters[-1][1]
        if j < others:
            spread = [after(v, before) for v in spread]
            parts = [w for v in spread for w in (v, swapped(v, 0))]

    projs, mixes, lses, weights = zip(*quarters)
    cot_last = after(cot_parts[-1], before)
    ups_x, downs_y = after(ups_x, cot_last), after(downs_y, cot_last)
    cot_parts.append(around(cot_last))
    ups, downs = jnp.stack([ups, ups_x]), jnp.stack([downs, downs_y])
    ups_y, downs_x = swapped(ups, 2), swapped(downs, 1)
    hidden, normed_two, attn_own = join_quarters(
        place, after(x, cot_last), post_bias, own_post, norm_gains, norm_shifts, mixes, weights
    )
    patch_t = own_columns(place, after(patches, normed_two), own)
    cot_rows, gated = cot_chunks(place, after(gate, normed_two, patch_t), cot_parts)
    full_parts = [cot_own, around(after(cot_own, gated))]

    def full_due(slot, value):
        if slot in ("N2", "B2"):
            full_parts.append(around(after(full_parts[-1], value)))
            return after(value, full_parts[-2])
        return value

    act, grad_pre, *sums, up_bias_sum = own_mlp(
        place, normed_two, gated, w_up, w_down, up_bias.reshape(1, -1), own
    )
    ups_y, downs_x = after(ups_y, sums[0]), after(downs_x, sums[0])
    more = [swapped(v, 0) for v in (ups, ups_y, downs, downs_x)]
    kept, sent = own_grads(core_one, normed_two, after(grad_pre, ups_y, downs_x), act, gated)
    more = [after(v, kept) for v in more]
    ups, downs = [ups, ups_y, *more[:2]], [downs, downs_x, *more[2:]]
    sent = after(sent, *more)

    turned_order = [order[0], *order[:0:-1]]

    def halves(kept, came, bit):
        if kept.shape[0] % 64 == 0:
            return halve_sum(upper[bit], kept, came)
        value = kept + came.astype(FLOAT)
        pair = value.reshape(2, value.shape[0] // 2, width)
        return (
            jnp.where(lower[bit], pair[0], pair[1]),
            jnp.where(lower[bit], pair[1], pair[0]).astype(LOWER),
        )

    def joined(value, other, bit):
        first, second = jnp.where(lower[bit], value, other), jnp.where(lower[bit], other, value)
        return jnp.concatenate([first, second], axis=0)

    def halve_middle(kept, came, bits):
        for bit in bits[2:-1]:
            kept, sent = halves(kept, came, bit)
            came = swapped(sent, bit)
        return halves(kept, came, bits[-1])

    def join_middle(value, bits):
        for bit in bits[-2:1:-1]:
            value = joined(value, swapped(value, bit), bit)
        return value

    came_c = swapped(sent, 0)
    sums[0] = after(sums[0], kept, *more)
    for j in range(others):
        sums[0] = full_due(f"M{j}", sums[0])
        last_quarter = (attn_own, own_post, gate) if j == others - 1 else ()
        sums = other_mlp(places, normed_two, gated, sums, ups, downs, j, last_quarter)
        if j == 0:
            kept, sent = halves(kept, after(came_c, sums[0]), order[1])
            came_x = swapped(sent, order[1])
            sums[0] = after(sums[0], sent)
    grad_two, gate_part, branch = sums
    came_x = after(came_x, grad_two)
    grad_two = full_due("N2", grad_two)
    grad_two = after(grad_two, came_x)
    kept, sent = halve_middle(kept, came_x, order)
    came_y = swapped(sent, order[-1])
    grad_hidden, grad_low, logit, sums_two = second_norm(
        after(grad_two, kept), gate_part, hidden, x, cot_rows, gate, post_bias, norm_gains
    )
    own_proj, bias_grad = backward_quarter(
        full_due("B0", grad_low), slots, projs[0], lses[0], weights[0]
    )
    kept_a, sent_a = attn_grads(core_one, own_proj, normed_one, mixes[0], grad_low)
    gprojs = [own_proj]
    came_a = swapped(sent_a, 0)
    d_mlp = (kept + after(came_y, kept_a).astype(FLOAT)).astype(LOWER)
    other = swapped(d_mlp, order[-1])
    low = full_due("B1", after(grad_low, kept_a, d_mlp))
    gprojs.append(backward_quarter(low, slots, projs[1], lses[1], weights[1])[0])
    kept_a, sent_a = halves(kept_a, after(came_a, gprojs[-1]), turned_order[1])
    came_a = swapped(sent_a, turned_order[1])
    d_mlp = join_middle(joined(d_mlp, after(other, gprojs[-1]), order[-1]), order)
    other = swapped(d_mlp, order[1])
    low = full_due("B2", after(low, gprojs[-1], d_mlp, kept_a))
    gprojs.append(backward_quarter(low, slots, projs[2], lses[2], weights[2])[0])
    kept_a, sent_a = halve_middle(kept_a, after(came_a, gprojs[-1]), turned_order)
    came_a = swapped(sent_a, turned_order[-1])
    low = full_due("B3", after(low, gprojs[-1], kept_a))
    for j in range(3, mlp_size):
        gprojs.append(backward_quarter(low, slots, projs[j], lses[j], weights[j])[0])
    d_attn = (kept_a + after(came_a, gprojs[-1]).astype(FLOAT)).astype(LOWER)
    near, far = turned_order[-1], turned_order[-2]
    others_a = [
        lax.ppermute(d_attn, "rows", [(i, i ^ mask) for i in range(rows_size)])
        for mask in (1 << near, 1 << far, (1 << near) | (1 << far))
    ]
    d_mlp = joined(d_mlp, after(other, gprojs[-1]), order[1])
    other = swapped(d_mlp, 0)
    rows_grad, sums_one = first_norm(
        x, grad_hidden, after(logit, gprojs[-1], d_attn, d_mlp), norm_gains, router_row, gprojs, weights
    )
    others_a = [after(v, rows_grad) for v in others_a]
    d_attn = joined(joined(d_attn, others_a[0], near), joined(others_a[1], others_a[2], near), far)
    for bit in turned_order[-3:0:-1]:
        d_attn = joined(d_attn, swapped(d_attn, bit), bit)
    other_a = swapped(d_attn, 0)
    small = jnp.concatenate(
        [
            sums_two[:4],
            sums_one[:3],
            up_bias_sum[:1],
            jnp.pad(bias_grad[:1], ((0, 0), (0, width - 3 * own))),
        ],
        axis=0,
    )
    small = small + swapped(small, 0)
    other_s = swapped(small, order[1])
    input_grad, block_out = scatter_rows(
        place, full_parts, named, after(rows_grad, small, d_attn), branch, patch_t
    )
    block_out = block_out.T
    small = small + after(other_s, input_grad)
    for bit in order[2:-1]:
        small = small + swapped(small, bit)
    other_s = swapped(small, order[-1])
    d_qkv, d_out, d_up, d_down = finish_grads(
        core_one, d_attn, after(other_a, input_grad, small), d_mlp, other
    )
    small, other_s = after(small, d_qkv), after(other_s, d_qkv)
    d_gains, d_shifts, d_post_bias, d_up_bias, d_router, d_qkv_bias = finish_sums(small, other_s, own)
    d_qkv = d_qkv.T
    return (
        block_out,
        input_grad,
        d_qkv,
        d_qkv_bias,
        d_out,
        d_post_bias,
        d_up,
        d_up_bias,
        d_down,
        d_gains,
        d_shifts,
        d_router,
    )


def solution(mesh):
    in_specs = (
        P("rows", None),
        P(None, "mlp"),
        P(),
        P("mlp", None),
        P(),
        P(None, "mlp"),
        P("mlp"),
        P("mlp", None),
        P(),
        P(),
        P(),
        P("rows"),
        P("rows"),
        P("rows", "mlp"),
    )
    out_specs = (
        P("rows", "mlp"),
        P("rows", None),
        P(None, "mlp"),
        P(None, "mlp"),
        P("mlp", None),
        P(),
        P(None, "mlp"),
        P("mlp"),
        P("mlp", None),
        P(),
        P(),
        P(),
    )
    body = functools.partial(local, mesh.shape["rows"], mesh.shape["mlp"])
    return jax.shard_map(body, mesh=mesh, in_specs=in_specs, out_specs=out_specs, check_vma=False)
```

```python
import functools

import jax
import jax.numpy as jnp
from jax import lax
from jax.experimental import pallas as pl
from jax.experimental.pallas import tpu as pltpu
from jax.sharding import PartitionSpec as P

HD = 64
IMG_DEV = 6
L_MOST = 3
HALF_S = 99
HALF_L = 289

CHUNK = 304
CHUNKS = 1 + L_MOST
PACKED = CHUNK * CHUNKS
SHARE = 8
PIECES = 4

EPSILON = 1e-06
LOWER = jnp.bfloat16
FLOAT = jnp.float32
MASKED = -1e30


def nn(a, b):
    return lax.dot_general(a, b, (((1,), (0,)), ((), ())), preferred_element_type=FLOAT)


def nt(a, b):
    return lax.dot_general(a, b, (((1,), (1,)), ((), ())), preferred_element_type=FLOAT)


def tn(a, b):
    return lax.dot_general(a, b, (((0,), (0,)), ((), ())), preferred_element_type=FLOAT)


LATER = pltpu.MemorySpace.HBM


def params(mib):
    return pltpu.CompilerParams(vmem_limit_bytes=mib * 1024 * 1024)


def cost(flops, bytes_accessed, transcendentals=0):
    return pl.CostEstimate(
        flops=flops, bytes_accessed=bytes_accessed, transcendentals=transcendentals
    )


def whole(shape, single=True):
    zeros = (0,) * len(shape)
    if single:
        return pl.BlockSpec(shape, lambda *_: zeros, pipeline_mode=pl.Buffered(1))
    return pl.BlockSpec(shape, lambda *_: zeros)


def rows_spec(width, height=CHUNK):
    return pl.BlockSpec((height, width), lambda c, *_: (c, 0))


def chunk_spec(height, width=CHUNK):
    return pl.BlockSpec((1, height, width), lambda c, *_: (c, 0, 0))


def call(kernel, name, mib, operands, in_specs, outs, scratch=(), flops=0, place=None, grid=None, far=()):
    if far:
        operands = [
            pltpu.with_memory_space_constraint(o, LATER) if i in far else o
            for i, o in enumerate(operands)
        ]
    specs = [o[2] for o in outs]
    shapes = [o[3](o[0], o[1]) if len(o) > 3 else jax.ShapeDtypeStruct(o[0], o[1]) for o in outs]
    scalars = () if place is None else (place,)
    made = pl.pallas_call(
        kernel,
        grid_spec=pltpu.PrefetchScalarGridSpec(
            num_scalar_prefetch=len(scalars),
            grid=grid or (CHUNKS,),
            in_specs=in_specs,
            out_specs=specs,
            scratch_shapes=scratch,
        ),
        out_shape=shapes,
        compiler_params=params(mib),
        cost_estimate=cost(flops // 1000000, 1000),
        name=name,
    )(*scalars, *operands)
    return list(made)


def slot_onehot(slots_ref, rows, chunk=0):
    named = jnp.transpose(slots_ref[chunk])[:, 0:1].astype(jnp.int32)
    places = lax.broadcasted_iota(jnp.int32, (CHUNK, rows), 1)
    return (places == named).astype(FLOAT).astype(LOWER)


def outside_image(slots_ref):
    image = jnp.transpose(slots_ref[0])[:, 1:2]
    return jnp.where(image == slots_ref[0, 1:2, :], 0.0, MASKED)


def choose_own(place, values, own):
    width = values.shape[1]
    source = lax.broadcasted_iota(jnp.int32, (width, own), 0)
    target = lax.broadcasted_iota(jnp.int32, (width, own), 1)
    onehot = (source == target + place * own).astype(FLOAT).astype(LOWER)
    return nn(values, onehot).astype(LOWER)


def norm_stats(values):
    average = jnp.mean(values, axis=-1, keepdims=True)
    centred = values - average
    variance = jnp.mean(centred * centred, axis=-1, keepdims=True)
    inverse = lax.rsqrt(variance + EPSILON)
    return centred * inverse, inverse


def pick_kernel(
    patches_ref, slots_ref, gains_ref, shifts_ref, router_ref, x_ref, n_ref, gate_ref
):
    x = nn(slot_onehot(slots_ref, patches_ref.shape[0]), patches_ref[...])
    x_ref[...] = x.astype(LOWER)
    scaled, _ = norm_stats(x)
    n_ref[...] = (scaled * gains_ref[0:1, :] + shifts_ref[0:1, :]).astype(LOWER)
    logit = jnp.sum(x * router_ref[...], axis=-1, keepdims=True)
    gate_ref[...] = jnp.broadcast_to(jax.nn.sigmoid(logit), gate_ref.shape)


def pick_rows(patches, slots, gains, shifts, router):
    rows, width = patches.shape
    return call(
        pick_kernel,
        "pick_rows",
        20,
        (patches, slots, gains, shifts, router),
        [
            whole((rows, width)),
            chunk_spec(8),
            whole((2, width)),
            whole((2, width)),
            whole((1, width)),
        ],
        [
            ((PACKED, width), LOWER, rows_spec(width)),
            ((PACKED, width), LOWER, rows_spec(width)),
            ((PACKED, 128), FLOAT, rows_spec(128)),
        ],
        flops=2 * PACKED * rows * width,
    )


def pick_cot_kernel(cot_ref, slots_ref, part_ref):
    for c in range(CHUNKS):
        onehot = slot_onehot(slots_ref, cot_ref.shape[1], c)
        part_ref[:, c * CHUNK : (c + 1) * CHUNK] = nt(cot_ref[...], onehot).astype(LOWER)


def pick_cot(cot_own, slots):
    own, rows = cot_own.shape
    return call(
        pick_cot_kernel,
        "pick_cot",
        24,
        (cot_own, slots),
        [whole((own, rows)), whole(slots.shape)],
        [((own, PACKED), LOWER, whole((own, PACKED)))],
        flops=2 * PACKED * rows * own,
        grid=(1,),
    )[0]


def own_columns_kernel(place_ref, patches_ref, patch_ref):
    own, width = patch_ref.shape[0], patches_ref.shape[1]
    source = lax.broadcasted_iota(jnp.int32, (own, width), 1)
    target = lax.broadcasted_iota(jnp.int32, (own, width), 0)
    chosen = (source == target + place_ref[0] * own).astype(FLOAT).astype(LOWER)
    patch_ref[...] = nt(chosen, patches_ref[...]).astype(LOWER)


def own_columns(place, patches, own):
    rows, width = patches.shape
    return call(
        own_columns_kernel,
        "own_columns",
        12,
        (patches,),
        [whole((rows, width))],
        [((own, rows), LOWER, whole((own, rows)), LATER)],
        flops=2 * own * rows * width,
        place=place,
        grid=(1,),
        far=(0,),
    )[0]


def head_slabs(own):
    slabs = []
    for start in range(0, own, 2 * HD):
        stop = min(start + 2 * HD, own)
        lanes = lax.broadcasted_iota(jnp.int32, (1, stop - start), 1)
        heads = []
        for head in range(start // HD, stop // HD):
            low = head * HD - start
            heads.append((head, (lanes >= low) & (lanes < low + HD)))
        slabs.append((start, stop, heads))
    return slabs


def keep(mask, values):
    return jnp.where(mask, values, jnp.zeros_like(values))


def forward_kernel(kind_ref, n_ref, bias_ref, slots_ref, *refs):
    proj_ref, mix_ref, lse_ref, weights_ref = refs[-4:]
    parts = refs[:-4]
    own = mix_ref.shape[1]

    @pl.when(pl.program_id(0) == 0)
    def _():
        if len(parts) == 1:
            weights_ref[...] = parts[0][...]
        else:
            for other, part_ref in enumerate(parts):
                held = part_ref.shape[0]
                start = pl.multiple_of((kind_ref[0] ^ other) * held, 32)
                weights_ref[pl.ds(start, held), :] = part_ref[...]

    proj_ref[...] = (nt(n_ref[...], weights_ref[0 : 3 * own, :]) + bias_ref[0]).astype(LOWER)
    outside = outside_image(slots_ref)
    lse_all = jnp.zeros((CHUNK, 128), FLOAT)
    lanes = lax.broadcasted_iota(jnp.int32, (1, 128), 1)
    for start, stop, heads in head_slabs(own):
        q = proj_ref[:, start:stop] * LOWER(HD**-0.5)
        k = proj_ref[:, own + start : own + stop]
        v = proj_ref[:, 2 * own + start : 2 * own + stop]
        mixed = None
        for head, mask in heads:
            scores = nt(q, keep(mask, k)) + outside
            largest = jnp.max(scores, axis=-1, keepdims=True)
            powered = jnp.exp(scores - largest)
            total = jnp.sum(powered, axis=-1, keepdims=True)
            probs = (powered * (1.0 / total)).astype(LOWER)
            part = nn(probs, keep(mask, v))
            mixed = part if mixed is None else mixed + part
            lse_all = jnp.where(lanes == head, largest + jnp.log(total), lse_all)
        mix_ref[:, start:stop] = mixed.astype(LOWER)
    lse_ref[0] = jnp.transpose(lse_all)[0:8, :]


def forward_quarter(kind, normed, biases, slots, parts, j):
    width = normed.shape[1]
    own = biases.shape[2] // 3
    return call(
        forward_kernel,
        "forward_quarter",
        11,
        (normed, biases, slots, *parts),
        [
            rows_spec(width),
            pl.BlockSpec((1, 1, 3 * own), lambda c, *_: (j, 0, 0)),
            chunk_spec(8),
            *[whole(p.shape) for p in parts],
        ],
        [
            ((PACKED, 3 * own), LOWER, rows_spec(3 * own), LATER),
            ((PACKED, own), LOWER, rows_spec(own)),
            ((CHUNKS, 8, CHUNK), FLOAT, chunk_spec(8), LATER),
            ((4 * own, width), LOWER, whole((4 * own, width))),
        ],
        flops=2 * PACKED * width * 8 * own,
        place=kind,
    )


def join_kernel(place_ref, x_ref, post_ref, own_post_ref, gains_ref, shifts_ref, *refs):
    hidden_ref, normed_ref, own_ref, chosen = refs[-4:]
    parts = refs[:-4]
    count = len(parts) // 2
    own = own_ref.shape[1]

    @pl.when(pl.program_id(0) == 0)
    def _():
        for j, out_ref in enumerate(parts[count:]):
            chosen[j * own : (j + 1) * own, :] = choose_own(place_ref[0], out_ref[...], own)

    attn, attn_own = post_ref[0:1, :], own_post_ref[0:1, :]
    for j, (mix_ref, out_ref) in enumerate(zip(parts[:count], parts[count:])):
        attn = attn + nn(mix_ref[...], out_ref[...])
        attn_own = attn_own + nn(mix_ref[...], chosen[j * own : (j + 1) * own, :])
    own_ref[...] = attn_own
    hidden = x_ref[...].astype(FLOAT) + attn
    hidden_ref[...] = hidden
    scaled, _ = norm_stats(hidden)
    normed_ref[...] = (scaled * gains_ref[1:2, :] + shifts_ref[1:2, :]).astype(LOWER)


def out_spec(own, width):
    return pl.BlockSpec((own, width), lambda *_: (3, 0), pipeline_mode=pl.Buffered(1))


def join_quarters(place, x, post, own_post, gains, shifts, mixes, weights):
    width = x.shape[1]
    own = mixes[0].shape[1]
    return call(
        join_kernel,
        "join_quarters",
        11,
        (x, post, own_post, gains, shifts, *mixes, *weights),
        [
            rows_spec(width),
            whole((2, width)),
            whole((2, own)),
            whole((2, width)),
            whole((2, width)),
            *[rows_spec(own) for _ in mixes],
            *[out_spec(own, width) for _ in weights],
        ],
        [
            ((PACKED, width), FLOAT, rows_spec(width), LATER),
            ((PACKED, width), LOWER, rows_spec(width)),
            ((PACKED, own), FLOAT, rows_spec(own), LATER),
        ],
        scratch=[pltpu.VMEM((len(weights) * own, own), LOWER)],
        flops=3 * PACKED * width * width,
        place=place,
    )


def stack_places(place, parts, stacked):
    size = len(parts)
    for j, part in enumerate(parts):
        own = part.shape[0]
        start = pl.multiple_of(lax.rem(place - j + size, size) * own, 64)
        stacked[pl.ds(start, own), :] = part.astype(stacked.dtype)


def cot_kernel(place_ref, gate_ref, *refs):
    cot_ref, gated_ref, stacked = refs[-3:]
    stack_places(place_ref[0], [r[...] for r in refs[:-3]], stacked)
    cot = jnp.transpose(stacked[...])
    cot_ref[...] = cot
    gated_ref[...] = (gate_ref[:, 0:1] * cot.astype(FLOAT)).astype(LOWER)


def cot_chunks(place, gate, parts):
    own = parts[0].shape[0]
    width = own * len(parts)
    return call(
        cot_kernel,
        "cot_chunks",
        20,
        (gate, *parts),
        [whole((PACKED, 128)), *[whole(p.shape) for p in parts]],
        [
            ((PACKED, width), LOWER, whole((PACKED, width)), LATER),
            ((PACKED, width), LOWER, whole((PACKED, width))),
        ],
        scratch=[pltpu.VMEM((width, PACKED), LOWER)],
        flops=PACKED * width,
        place=place,
        grid=(1,),
    )


def gelu_pair(u):
    cdf = 0.5 * (1.0 + lax.erf(u * (0.5**0.5)))
    density = jnp.exp(-0.5 * u * u) * 0.3989422804014327
    return u * cdf, cdf + u * density


def mlp_step(normed, gated, up_ref, down_ref, bias, own_down_ref):
    hidden = up_ref.shape[1]
    block = hidden // 3

    def products(start):
        cols = slice(start, start + block)
        pre_act = nn(normed, up_ref[:, cols]) + bias[:, cols]
        return pre_act, nt(gated, down_ref[cols, :])

    activations, grads, grad, gate, out = [], [], None, None, None
    ahead = products(0)
    for start in range(0, hidden, block):
        cols = slice(start, start + block)
        pre_act, grad_act = ahead
        if start + block < hidden:
            ahead = products(start + block)
        activation, slope = gelu_pair(pre_act)
        activation = activation.astype(LOWER)
        grad_pre = (grad_act * slope).astype(LOWER)
        gate_part = jnp.sum(activation.astype(FLOAT) * grad_act, axis=-1, keepdims=True)
        grad_part = nt(grad_pre, up_ref[:, cols])
        out_part = nn(activation, own_down_ref[cols, :])
        activations.append(activation)
        grads.append(grad_pre)
        grad = grad_part if grad is None else grad + grad_part
        gate = gate_part if gate is None else gate + gate_part
        out = out_part if out is None else out + out_part
    return activations, grads, grad, gate, out


def own_mlp_kernel(
    place_ref,
    n_ref,
    gated_ref,
    up_ref,
    down_ref,
    bias_ref,
    act_ref,
    pre_ref,
    grad_ref,
    gate_ref,
    out_ref,
    bias_sum_ref,
    own_down,
):
    @pl.when(pl.program_id(0) == 0)
    def _():
        own_down[...] = choose_own(place_ref[0], down_ref[...], own_down.shape[1])
        bias_sum_ref[...] = jnp.zeros_like(bias_sum_ref)

    activation, grad_pre, grad_part, gate_part, out_part = mlp_step(
        n_ref[...], gated_ref[...], up_ref, down_ref, bias_ref[...], own_down
    )
    block = activation[0].shape[1]
    for i, (act, pre) in enumerate(zip(activation, grad_pre)):
        act_ref[:, i * block : (i + 1) * block] = act
        pre_ref[:, i * block : (i + 1) * block] = pre
    grad_ref[...] = grad_part
    gate_ref[...] = jnp.broadcast_to(gate_part, gate_ref.shape)
    out_ref[...] = out_part
    bias_sum_ref[0:1, :] += jnp.sum(pre_ref[...].astype(FLOAT), axis=0, keepdims=True)


def own_mlp(place, normed, gated, up, down, bias, own):
    width, hidden = up.shape
    return call(
        own_mlp_kernel,
        "own_mlp",
        17,
        (normed, gated, up, down, bias),
        [
            rows_spec(width),
            rows_spec(width),
            whole((width, hidden)),
            whole((hidden, width)),
            whole((1, hidden)),
        ],
        [
            ((PACKED, hidden), LOWER, rows_spec(hidden)),
            ((PACKED, hidden), LOWER, rows_spec(hidden)),
            ((PACKED, width), FLOAT, rows_spec(width), LATER),
            ((PACKED, 128), FLOAT, rows_spec(128)),
            ((PACKED, own), FLOAT, rows_spec(own)),
            ((8, hidden), FLOAT, whole((8, hidden), False)),
        ],
        scratch=[pltpu.VMEM((hidden, own), LOWER)],
        flops=2 * PACKED * hidden * (3 * width + own),
        place=place,
    )


def own_grads_kernel(core_ref, n_ref, pre_ref, act_ref, gated_ref, kept_ref, sent_ref):
    grad_up = tn(n_ref[...], pre_ref[...])
    grad_down = tn(act_ref[...], gated_ref[...])

    @pl.when(core_ref[0] == 0)
    def _():
        kept_ref[...] = grad_up
        sent_ref[...] = grad_down.astype(LOWER)

    @pl.when(core_ref[0] == 1)
    def _():
        kept_ref[...] = grad_down
        sent_ref[...] = grad_up.astype(LOWER)


def own_grads(core, normed, grad_pre, act, gated):
    width = normed.shape[1]
    block = width // 3
    columns = pl.BlockSpec((PACKED, block), lambda c, *_: (0, c))
    return call(
        own_grads_kernel,
        "own_grads",
        16,
        (normed, grad_pre, act, gated),
        [columns, whole((PACKED, width)), columns, whole((PACKED, width))],
        [
            ((width, width), FLOAT, rows_spec(width, block)),
            ((width, width), LOWER, rows_spec(width, block)),
        ],
        flops=4 * PACKED * width * width,
        place=core,
        grid=(3,),
    )


def other_mlp_kernel(
    last, place_ref, n_ref, gated_ref, grad_in_ref, gate_in_ref, out_in_ref, *refs
):
    grad_ref, gate_ref, out_ref, up, down, own_down = refs[-6:]
    ups, downs = refs[0:4], refs[4:8]
    part = downs[0].shape[2]
    width = up.shape[1]

    @pl.when(pl.program_id(0) == 0)
    def _():
        for side in range(2):
            for c in range(2):
                for near in range(2):
                    to_up = place_ref[1] ^ (4 * side + 2 * near + c)
                    to_down = place_ref[1] ^ (4 * near + 2 * side + c)
                    up_rows = pl.ds(pl.multiple_of(to_up * part, 32), part)
                    down_rows = pl.ds(pl.multiple_of(to_down * part, 32), part)
                    up[up_rows, :] = ups[side + 2 * c][near, 0, 0:part]
                    down[down_rows, :] = downs[side + 2 * c][near, 0]
        own_down[...] = choose_own(place_ref[0], down[...], own_down.shape[1])

    pieces = ups[0][0, 0, part : part + 16].astype(FLOAT)
    bias = pieces[0:1] + (pieces[1:2] + pieces[2:3])
    _, _, grad_part, gate_part, out_part = mlp_step(
        n_ref[...], gated_ref[...], up, down, bias, own_down
    )
    grad_ref[...] = grad_in_ref[...] + grad_part
    gate_ref[...] = gate_in_ref[...] + gate_part
    if last:
        attn_ref, post_ref, open_ref = refs[8:11]
        total = out_in_ref[...] + out_part + attn_ref[...] + post_ref[1:2, :]
        out_ref[...] = open_ref[:, 0:1] * total
    else:
        out_ref[...] = out_in_ref[...] + out_part


def other_mlp(places, normed, gated, sums, ups, downs, j, extra=()):
    width = normed.shape[1]
    own = sums[2].shape[1]
    last = len(extra) > 0
    held = lambda array: pl.BlockSpec(
        (2, 1, *array.shape[2:]), lambda c, *_: (0, j, 0, 0), pipeline_mode=pl.Buffered(1)
    )
    extra_specs = [rows_spec(own), whole((2, own)), rows_spec(128)] if last else []
    return call(
        functools.partial(other_mlp_kernel, last),
        "other_mlp",
        17,
        (normed, gated, *sums, *ups, *downs, *extra),
        [
            rows_spec(width),
            rows_spec(width),
            rows_spec(width),
            rows_spec(128),
            rows_spec(own),
            *[held(u) for u in ups],
            *[held(d) for d in downs],
            *extra_specs,
        ],
        [
            ((PACKED, width), FLOAT, rows_spec(width)),
            ((PACKED, 128), FLOAT, rows_spec(128)),
            ((PACKED, own), FLOAT, rows_spec(own)),
        ],
        scratch=[
            pltpu.VMEM((width, width), LOWER),
            pltpu.VMEM((width, width), LOWER),
            pltpu.VMEM((width, own), LOWER),
        ],
        flops=2 * PACKED * width * (3 * width + own),
        place=places,
    )


def second_norm_kernel(
    grad_ref,
    gate_part_ref,
    hidden_ref,
    x_ref,
    cot_ref,
    gate_ref,
    post_ref,
    gains_ref,
    ghid_ref,
    glow_ref,
    logit_ref,
    sums_ref,
):
    @pl.when(pl.program_id(0) == 0)
    def _():
        sums_ref[...] = jnp.zeros_like(sums_ref)

    hidden = hidden_ref[...]
    scaled, inverse = norm_stats(hidden)
    grad_out = grad_ref[...]
    weighted = grad_out * gains_ref[1:2, :]
    centre_term = jnp.mean(weighted, axis=-1, keepdims=True)
    scale_term = jnp.mean(weighted * scaled, axis=-1, keepdims=True)
    grad_hidden = inverse * (weighted - centre_term - scaled * scale_term)
    gate = gate_ref[:, 0:1]
    gated = gate * cot_ref[...].astype(FLOAT)
    grad_attn = grad_hidden + gated
    ghid_ref[...] = grad_hidden
    glow_ref[...] = grad_attn.astype(LOWER)
    attn = hidden - x_ref[...].astype(FLOAT)
    dotted = jnp.sum(gated * (attn + post_ref[1:2, :]), axis=-1, keepdims=True)
    logit = (1.0 - gate) * (dotted + gate_part_ref[:, 0:1])
    logit_ref[...] = jnp.broadcast_to(logit, logit_ref.shape)
    sums_ref[0:1, :] += jnp.sum(grad_out * scaled, axis=0, keepdims=True)
    sums_ref[1:2, :] += jnp.sum(grad_out, axis=0, keepdims=True)
    sums_ref[2:3, :] += jnp.sum(grad_attn, axis=0, keepdims=True)
    sums_ref[3:4, :] += jnp.sum(gated, axis=0, keepdims=True)


def second_norm(grad, gate_part, hidden, x, cot_rows, gate, post, gains):
    width = x.shape[1]
    return call(
        second_norm_kernel,
        "second_norm",
        14,
        (grad, gate_part, hidden, x, cot_rows, gate, post, gains),
        [
            rows_spec(width),
            rows_spec(128),
            rows_spec(width),
            rows_spec(width),
            rows_spec(width),
            rows_spec(128),
            whole((2, width)),
            whole((2, width)),
        ],
        [
            ((PACKED, width), FLOAT, rows_spec(width)),
            ((PACKED, width), LOWER, rows_spec(width)),
            ((PACKED, 128), FLOAT, rows_spec(128)),
            ((8, width), FLOAT, whole((8, width), False)),
        ],
        flops=20 * PACKED * width,
    )


def backward_kernel(low_ref, slots_ref, proj_ref, lse_ref, out_ref, gproj_ref, sums_ref):
    @pl.when(pl.program_id(0) == 0)
    def _():
        sums_ref[...] = jnp.zeros_like(sums_ref)

    outside = outside_image(slots_ref)
    own = out_ref.shape[0]
    heads = own // HD
    g = nt(low_ref[...], out_ref[...]).astype(LOWER)
    q = proj_ref[:, 0:own] * LOWER(HD**-0.5)
    k = proj_ref[:, own : 2 * own]
    v = proj_ref[:, 2 * own : 3 * own]
    lanes = lax.broadcasted_iota(jnp.int32, (1, own), 1) // HD
    keys = jnp.concatenate([keep(lanes == head, k) for head in range(heads)], axis=0)
    values = jnp.concatenate([keep(lanes == head, v) for head in range(heads)], axis=0)
    scores = nt(keys, q)
    grad_probs = nt(values, g)
    probs, grad_scores = [], []
    for head in range(heads):
        rows = slice(head * CHUNK, (head + 1) * CHUNK)
        prob = jnp.exp(scores[rows] + outside - lse_ref[0, head : head + 1, :])
        inner = jnp.sum(prob * grad_probs[rows], axis=0, keepdims=True)
        grad_scores.append((prob * (grad_probs[rows] - inner)).astype(LOWER))
        probs.append(prob.astype(LOWER))
    grad_scores = jnp.concatenate(grad_scores, axis=0)
    all_v = nn(jnp.concatenate(probs, axis=0), g)
    all_k = nn(grad_scores, q)
    grad_q = tn(grad_scores, keys)
    grad_k, grad_v = all_k[0:CHUNK], all_v[0:CHUNK]
    for head in range(1, heads):
        rows = slice(head * CHUNK, (head + 1) * CHUNK)
        grad_k = jnp.where(lanes == head, all_k[rows], grad_k)
        grad_v = jnp.where(lanes == head, all_v[rows], grad_v)
    gproj_ref[:, 0:own] = (grad_q * HD**-0.5).astype(LOWER)
    gproj_ref[:, own : 2 * own] = grad_k.astype(LOWER)
    gproj_ref[:, 2 * own : 3 * own] = grad_v.astype(LOWER)
    sums_ref[0:1, :] += jnp.sum(gproj_ref[...].astype(FLOAT), axis=0, keepdims=True)


def backward_quarter(low, slots, proj, lse, weights):
    width = low.shape[1]
    own = proj.shape[1] // 3
    return call(
        backward_kernel,
        "backward_quarter",
        16,
        (low, slots, proj, lse, weights),
        [
            rows_spec(width),
            chunk_spec(8),
            rows_spec(3 * own),
            chunk_spec(8),
            out_spec(own, width),
        ],
        [
            ((PACKED, 3 * own), LOWER, rows_spec(3 * own)),
            ((8, 3 * own), FLOAT, whole((8, 3 * own), False)),
        ],
        flops=2 * PACKED * width * 14 * own,
    )


def attn_grads_kernel(core_ref, gproj_ref, normed_ref, mix_ref, low_ref, kept_ref, sent_ref):
    half = kept_ref.shape[0]
    rest = gproj_ref.shape[1] - half
    normed = normed_ref[...]
    first = tn(gproj_ref[:, 0:half], normed)
    second = tn(gproj_ref[:, half:], normed)
    third = tn(mix_ref[...], low_ref[...])

    @pl.when(core_ref[0] == 0)
    def _():
        kept_ref[...] = first
        sent_ref[0:rest, :] = second.astype(LOWER)
        sent_ref[rest:half, :] = third.astype(LOWER)

    @pl.when(core_ref[0] == 1)
    def _():
        kept_ref[0:rest, :] = second
        kept_ref[rest:half, :] = third
        sent_ref[...] = first.astype(LOWER)


def attn_grads(core, gproj, normed, mix, low):
    width, own = normed.shape[1], mix.shape[1]
    operands = (gproj, normed, mix, low)
    return call(
        attn_grads_kernel,
        "attn_grads",
        18,
        operands,
        [whole(o.shape) for o in operands],
        [
            ((2 * own, width), FLOAT, whole((2 * own, width))),
            ((2 * own, width), LOWER, whole((2 * own, width))),
        ],
        place=core,
        grid=(1,),
    )


def first_norm_kernel(x_ref, ghid_ref, logit_ref, gains_ref, router_ref, *refs):
    rows_ref, sums_ref, gprojs, weights = refs[-4:]
    parts = refs[:-4]
    count = len(parts) // 2
    held = parts[0].shape[1]

    @pl.when(pl.program_id(0) == 0)
    def _():
        sums_ref[...] = jnp.zeros_like(sums_ref)
        for j, weights_ref in enumerate(parts[count:]):
            weights[j * held : (j + 1) * held, :] = weights_ref[0:held, :]

    for j, gproj_ref in enumerate(parts[:count]):
        gprojs[:, j * held : (j + 1) * held] = gproj_ref[...]
    grad_out = nn(gprojs[...], weights[...])
    x = x_ref[...].astype(FLOAT)
    scaled, inverse = norm_stats(x)
    weighted = grad_out * gains_ref[0:1, :]
    centre_term = jnp.mean(weighted, axis=-1, keepdims=True)
    scale_term = jnp.mean(weighted * scaled, axis=-1, keepdims=True)
    grad_norm = inverse * (weighted - centre_term - scaled * scale_term)
    logit = logit_ref[:, 0:1]
    rows_ref[...] = (ghid_ref[...] + grad_norm + logit * router_ref[...]).astype(LOWER)
    sums_ref[0:1, :] += jnp.sum(grad_out * scaled, axis=0, keepdims=True)
    sums_ref[1:2, :] += jnp.sum(grad_out, axis=0, keepdims=True)
    sums_ref[2:3, :] += jnp.sum(logit * x, axis=0, keepdims=True)


def first_norm(x, ghid, logit, gains, router, gprojs, weights):
    width = x.shape[1]
    return call(
        first_norm_kernel,
        "first_norm",
        20,
        (x, ghid, logit, gains, router, *gprojs, *weights),
        [
            rows_spec(width),
            rows_spec(width),
            rows_spec(128),
            whole((2, width)),
            whole((1, width)),
            *[rows_spec(g.shape[1]) for g in gprojs],
            *[whole(w.shape) for w in weights],
        ],
        [
            ((PACKED, width), LOWER, rows_spec(width)),
            ((8, width), FLOAT, whole((8, width), False)),
        ],
        scratch=[pltpu.VMEM((CHUNK, 3 * width), LOWER), pltpu.VMEM((3 * width, width), LOWER)],
        flops=2 * PACKED * width * 3 * width,
    )


def scatter_kernel(place_ref, named_ref, rows_ref, branch_ref, patch_ref, *refs):
    out_ref, block_ref, stacked, branch_t = refs[-4:]
    block = out_ref.shape[0]

    @pl.when(pl.program_id(0) == 0)
    def _():
        branch_t[...] = jnp.transpose(branch_ref[...].astype(LOWER))

    stack_places(place_ref[0], [r[...] for r in refs[:-4]], stacked)
    places = lax.broadcasted_iota(jnp.int32, (block, PACKED), 0) + pl.program_id(0) * block
    onehot = (places == named_ref[...]).astype(FLOAT).astype(LOWER)
    cot = jnp.transpose(stacked[...]).astype(FLOAT)
    out_ref[...] = (cot + nn(onehot, rows_ref[...])).astype(LOWER)
    block_ref[...] = (patch_ref[...].astype(FLOAT) + nt(branch_t[...], onehot)).astype(LOWER)


def scatter_rows(place, cot_parts, named, rows, branch, patch_t):
    own, total = cot_parts[0].shape
    width = own * len(cot_parts)
    block = 512
    columns = pl.BlockSpec((own, block), lambda c, *_: (0, c))
    return call(
        scatter_kernel,
        "scatter_rows",
        16,
        (named, rows, branch, patch_t, *cot_parts),
        [
            whole(named.shape),
            whole((PACKED, width)),
            whole((PACKED, own)),
            columns,
            *[columns for _ in cot_parts],
        ],
        [
            ((total, width), LOWER, rows_spec(width, block), LATER),
            ((own, total), LOWER, columns, LATER),
        ],
        scratch=[
            pltpu.VMEM((width, block), LOWER),
            pltpu.VMEM((own, PACKED), LOWER),
        ],
        flops=2 * PACKED * total * width,
        place=place,
        grid=(pl.cdiv(total, block),),
        far=range(3, 4 + len(cot_parts)),
    )


def halve_kernel(upper_ref, kept_ref, came_ref, half_ref, sent_ref):
    block, half = half_ref.shape[0], kept_ref.shape[0] // 2
    step = pl.program_id(0) * block
    own = pl.ds(pl.multiple_of(upper_ref[0] * half + step, 16), block)
    far = pl.ds(pl.multiple_of((1 - upper_ref[0]) * half + step, 16), block)
    half_ref[...] = kept_ref[own, :] + came_ref[own, :].astype(FLOAT)
    sent_ref[...] = (kept_ref[far, :] + came_ref[far, :].astype(FLOAT)).astype(LOWER)


def halve_sum(upper, kept, came):
    rows, width = kept.shape
    return call(
        halve_kernel,
        "halve_sum",
        10,
        (kept, came),
        [whole((rows, width)), whole((rows, width))],
        [
            ((rows // 2, width), FLOAT, rows_spec(width, rows // 4)),
            ((rows // 2, width), LOWER, rows_spec(width, rows // 4)),
        ],
        place=upper,
        grid=(2,),
    )


def finish_kernel(core_ref, attn_ref, attn_far_ref, mlp_ref, mlp_far_ref, *refs):
    qkv_ref, out_ref, up_ref, down_ref = refs
    own, block = qkv_ref.shape[0], up_ref.shape[0]
    head = pl.program_id(0)
    rows = pl.ds(pl.multiple_of(head * block, 16), block)

    def write(low_ref, high_ref, first_ref, second_ref):
        one = pl.ds(pl.multiple_of(head * HD, HD), HD)
        two = pl.ds(pl.multiple_of(own + head * HD, HD), HD)
        qkv_ref[0:HD, :] = low_ref[one, :].astype(FLOAT)
        qkv_ref[HD : 2 * HD, :] = low_ref[two, :].astype(FLOAT)
        qkv_ref[2 * HD : 3 * HD, :] = high_ref[one, :].astype(FLOAT)
        out_ref[...] = high_ref[two, :].astype(FLOAT)
        up_ref[...] = first_ref[rows, :].astype(FLOAT)
        down_ref[...] = second_ref[rows, :].astype(FLOAT)

    @pl.when(core_ref[0] == 0)
    def _():
        write(attn_ref, attn_far_ref, mlp_ref, mlp_far_ref)

    @pl.when(core_ref[0] == 1)
    def _():
        write(attn_far_ref, attn_ref, mlp_far_ref, mlp_ref)


def finish_grads(core, attn, attn_far, mlp, mlp_far):
    width = mlp.shape[1]
    own = attn.shape[0] // 2
    heads = own // HD
    return call(
        finish_kernel,
        "finish_grads",
        16,
        (attn, attn_far, mlp, mlp_far),
        [whole(attn.shape), whole(attn.shape), whole(mlp.shape), whole(mlp.shape)],
        [
            ((3 * own, width), FLOAT, rows_spec(width, 3 * HD)),
            ((own, width), FLOAT, rows_spec(width, HD)),
            ((width, width), FLOAT, rows_spec(width, width // heads)),
            ((width, width), FLOAT, rows_spec(width, width // heads)),
        ],
        place=core,
        grid=(heads,),
    )


def finish_sums_kernel(own_ref, far_ref, *refs):
    gains_ref, shifts_ref, post_ref, up_ref, router_ref, qkv_ref = refs
    total = own_ref[...] + far_ref[...]
    own = qkv_ref.shape[1]
    gains_ref[0:1, :] = total[4:5]
    gains_ref[1:2, :] = total[0:1]
    shifts_ref[0:1, :] = total[5:6]
    shifts_ref[1:2, :] = total[1:2]
    post_ref[...] = total[2:4]
    up_ref[...] = total[7]
    router_ref[...] = total[6]
    qkv_ref[0:1, :] = total[8:9, 0:own]
    qkv_ref[1:2, :] = total[8:9, 2 * own : 3 * own]


def finish_sums(small, far, own):
    rows, width = small.shape
    shapes = [(2, width), (2, width), (2, width), (width,), (width,), (2, own)]
    return call(
        finish_sums_kernel,
        "finish_sums",
        4,
        (small, far),
        [whole((rows, width)), whole((rows, width))],
        [(shape, FLOAT, whole(shape)) for shape in shapes],
        grid=(1,),
    )


def turned(values, place):
    size = values.shape[0]
    back = jnp.concatenate([values[:1], values[:0:-1]], axis=0)
    twice = jnp.concatenate([back, back], axis=0)
    return lax.dynamic_slice_in_dim(twice, (size - place) % size, size, 0)


def after(value, *others):
    return lax.optimization_barrier((value, *others))[0]


def ring_step(value, size):
    return lax.ppermute(value, "mlp", [(i, (i + 1) % size) for i in range(size)])


def swap(value, bit, size):
    return lax.ppermute(value, "rows", [(i, i ^ (1 << bit)) for i in range(size)])


def bits_of(size):
    return [b for b in range(20) if (1 << b) < size]


def pack_slots(picked, live_slots):
    small = IMG_DEV * HALF_S
    named = jnp.where(live_slots == 1, picked, -1)

    def padded(parts, fill):
        have = sum(p.shape[0] for p in parts)
        return jnp.concatenate([*parts, jnp.full((CHUNK - have,), fill, jnp.int32)])

    always = IMG_DEV - L_MOST
    idx = [padded([named[: always * HALF_S]], -1)]
    seg = [padded([jnp.repeat(jnp.arange(always, dtype=jnp.int32), HALF_S)], always)]
    for j in range(L_MOST):
        first = small + j * HALF_L
        alive = live_slots[first] == 1
        other = IMG_DEV - 1 - j
        large_idx = padded([named[first : first + HALF_L]], -1)
        small_idx = padded([named[other * HALF_S : (other + 1) * HALF_S]], -1)
        idx.append(jnp.where(alive, large_idx, small_idx))
        length = jnp.where(alive, HALF_L, HALF_S)
        seg.append((jnp.arange(CHUNK, dtype=jnp.int32) >= length).astype(jnp.int32))
    named = jnp.concatenate(idx).reshape(1, PACKED)
    idx, seg = jnp.stack(idx).astype(FLOAT), jnp.stack(seg).astype(FLOAT)
    rows = lax.broadcasted_iota(jnp.int32, (1, 8, 1), 1)
    return jnp.where(rows == 0, idx[:, None, :], seg[:, None, :]), named


def local(
    rows_size,
    mlp_size,
    patches,
    w_qkv,
    qkv_bias,
    w_out,
    post_bias,
    w_up,
    up_bias,
    w_down,
    norm_gains,
    norm_shifts,
    router,
    picked,
    live_slots,
    cotangent,
):
    width = patches.shape[1]
    mlp_index = lax.axis_index("mlp")
    rows_index = lax.axis_index("rows")
    share_index = rows_index % SHARE
    core = rows_index & 1
    place = mlp_index.astype(jnp.int32).reshape(1)
    places = jnp.stack([mlp_index, share_index]).astype(jnp.int32)
    kind = (rows_index % PIECES).astype(jnp.int32).reshape(1)
    own = w_out.shape[0]
    heads_here = own // HD
    others = mlp_size - 1
    router_row = router.reshape(1, width)

    def swapped(value, bit):
        return swap(value, bit, rows_size)

    own_weights = jnp.concatenate(
        [
            w_qkv.T.reshape(heads_here, 3, HD, width).transpose(1, 0, 2, 3).reshape(3 * own, width),
            w_out,
        ],
        axis=0,
    )
    held = own_weights.shape[0] // PIECES
    piece = lax.dynamic_slice_in_dim(own_weights, kind[0] * held, held, 0)
    part = w_up.shape[0] // SHARE
    top = lax.reduce_precision(up_bias, 8, 7)
    middle = lax.reduce_precision(up_bias - top, 8, 7)
    bias_rows = jnp.stack([top, middle, up_bias - top - middle]).astype(LOWER)
    payload = jnp.concatenate(
        [
            piece,
            lax.dynamic_slice_in_dim(w_up, share_index * part, part, 0),
            jnp.pad(bias_rows, ((0, 13), (0, 0))),
            lax.dynamic_slice_in_dim(w_down, share_index * part, part, 0),
        ],
        axis=0,
    )
    def around(value):
        return ring_step(value, mlp_size)

    kinds = jnp.stack([qkv_bias[0], jnp.zeros_like(qkv_bias[0]), qkv_bias[1]])
    biases = turned(kinds.reshape(3, mlp_size, own).transpose(1, 0, 2), mlp_index)
    biases = biases.reshape(mlp_size, 1, 3 * own)
    own_post = lax.dynamic_slice_in_dim(post_bias, mlp_index * own, own, 1)
    slots, named = pack_slots(picked, live_slots)
    cot_own = cotangent.T
    core_one = core.astype(jnp.int32).reshape(1)

    def split(came):
        return came[:held], came[held : held + part + 16], came[held + part + 16 :]

    def across(value, mask):
        return lax.ppermute(value, "rows", [(i, i ^ mask) for i in range(rows_size)])

    def forward(j, normed, parts):
        return forward_quarter(kind, normed, biases, slots, parts, j)

    order = bits_of(rows_size)
    lower = {bit: (rows_index >> bit) & 1 == 0 for bit in order}
    upper = {bit: ((rows_index >> bit) & 1).astype(jnp.int32).reshape(1) for bit in order}
    payload, place, places, kind, core_one, lower, upper = lax.optimization_barrier(
        (payload, place, places, kind, core_one, lower, upper)
    )
    came = around(payload)
    patches, named, own_post, biases = lax.optimization_barrier(
        (after(patches, payload), named, own_post, biases)
    )
    x, normed_one, gate = pick_rows(
        patches, slots, norm_gains, norm_shifts, router_row
    )
    came = after(came, x)
    cot_part = pick_cot(after(cot_own, came), slots)
    normed_one = after(normed_one, cot_part)
    quarters, cot_parts, up_parts, down_parts = [], [cot_part], [], []
    parts, before = [own_weights], x
    for j in range(mlp_size):
        if j < others:
            came = after(came, before)
            got, up_part, down_part = split(came)
            up_parts.append(up_part)
            down_parts.append(down_part)
            if j + 1 < others:
                came = around(came)
            spread = [got, *[across(got, mask) for mask in range(2, PIECES, 2)]]
        if 0 < j < others:
            cot_parts.append(around(after(cot_parts[-1], got)))
        normed_one = after(normed_one, got, before, *parts)
        if j == others:
            normed_one = after(normed_one, *cot_parts[:-1])
            ups, downs = jnp.stack(up_parts), jnp.stack(down_parts)
            ups_x, downs_y = swapped(ups, 1), swapped(downs, 2)
        quarters.append(forward(j, normed_one, parts))
        before = quarters[-1][1]
        if j < others:
            spread = [after(v, before) for v in spread]
            parts = [w for v in spread for w in (v, swapped(v, 0))]

    projs, mixes, lses, weights = zip(*quarters)
    cot_last = after(cot_parts[-1], before)
    ups_x, downs_y = after(ups_x, cot_last), after(downs_y, cot_last)
    cot_parts.append(around(cot_last))
    ups, downs = jnp.stack([ups, ups_x]), jnp.stack([downs, downs_y])
    ups_y, downs_x = swapped(ups, 2), swapped(downs, 1)
    hidden, normed_two, attn_own = join_quarters(
        place, after(x, cot_last), post_bias, own_post, norm_gains, norm_shifts, mixes, weights
    )
    patch_t = own_columns(place, after(patches, normed_two), own)
    cot_rows, gated = cot_chunks(place, after(gate, normed_two, patch_t), cot_parts)
    full_parts = [cot_own, around(after(cot_own, gated))]

    def full_due(slot, value):
        if slot in ("N2", "B2"):
            full_parts.append(around(after(full_parts[-1], value)))
            return after(value, full_parts[-2])
        return value

    act, grad_pre, *sums, up_bias_sum = own_mlp(
        place, normed_two, gated, w_up, w_down, up_bias.reshape(1, -1), own
    )
    ups_y, downs_x = after(ups_y, sums[0]), after(downs_x, sums[0])
    more = [swapped(v, 0) for v in (ups, ups_y, downs, downs_x)]
    kept, sent = own_grads(core_one, normed_two, after(grad_pre, ups_y, downs_x), act, gated)
    more = [after(v, kept) for v in more]
    ups, downs = [ups, ups_y, *more[:2]], [downs, downs_x, *more[2:]]
    sent = after(sent, *more)

    turned_order = [order[0], *order[:0:-1]]

    def halves(kept, came, bit):
        if kept.shape[0] % 64 == 0:
            return halve_sum(upper[bit], kept, came)
        value = kept + came.astype(FLOAT)
        pair = value.reshape(2, value.shape[0] // 2, width)
        return (
            jnp.where(lower[bit], pair[0], pair[1]),
            jnp.where(lower[bit], pair[1], pair[0]).astype(LOWER),
        )

    def joined(value, other, bit):
        first, second = jnp.where(lower[bit], value, other), jnp.where(lower[bit], other, value)
        return jnp.concatenate([first, second], axis=0)

    def halve_middle(kept, came, bits):
        for bit in bits[2:-1]:
            kept, sent = halves(kept, came, bit)
            came = swapped(sent, bit)
        return halves(kept, came, bits[-1])

    def join_middle(value, bits):
        for bit in bits[-2:1:-1]:
            value = joined(value, swapped(value, bit), bit)
        return value

    came_c = swapped(sent, 0)
    sums[0] = after(sums[0], kept, *more)
    for j in range(others):
        sums[0] = full_due(f"M{j}", sums[0])
        last_quarter = (attn_own, own_post, gate) if j == others - 1 else ()
        sums = other_mlp(places, normed_two, gated, sums, ups, downs, j, last_quarter)
        if j == 0:
            kept, sent = halves(kept, after(came_c, sums[0]), order[1])
            came_x = swapped(sent, order[1])
            sums[0] = after(sums[0], sent)
    grad_two, gate_part, branch = sums
    came_x = after(came_x, grad_two)
    grad_two = full_due("N2", grad_two)
    grad_two = after(grad_two, came_x)
    kept, sent = halve_middle(kept, came_x, order)
    came_y = swapped(sent, order[-1])
    grad_hidden, grad_low, logit, sums_two = second_norm(
        after(grad_two, kept), gate_part, hidden, x, cot_rows, gate, post_bias, norm_gains
    )
    own_proj, bias_grad = backward_quarter(
        full_due("B0", grad_low), slots, projs[0], lses[0], weights[0]
    )
    kept_a, sent_a = attn_grads(core_one, own_proj, normed_one, mixes[0], grad_low)
    gprojs = [own_proj]
    came_a = swapped(sent_a, 0)
    d_mlp = (kept + after(came_y, kept_a).astype(FLOAT)).astype(LOWER)
    other = swapped(d_mlp, order[-1])
    low = full_due("B1", after(grad_low, kept_a, d_mlp))
    gprojs.append(backward_quarter(low, slots, projs[1], lses[1], weights[1])[0])
    kept_a, sent_a = halves(kept_a, after(came_a, gprojs[-1]), turned_order[1])
    came_a = swapped(sent_a, turned_order[1])
    d_mlp = join_middle(joined(d_mlp, after(other, gprojs[-1]), order[-1]), order)
    other = swapped(d_mlp, order[1])
    low = full_due("B2", after(low, gprojs[-1], d_mlp, kept_a))
    gprojs.append(backward_quarter(low, slots, projs[2], lses[2], weights[2])[0])
    kept_a, sent_a = halve_middle(kept_a, after(came_a, gprojs[-1]), turned_order)
    came_a = swapped(sent_a, turned_order[-1])
    low = full_due("B3", after(low, gprojs[-1], kept_a))
    for j in range(3, mlp_size):
        gprojs.append(backward_quarter(low, slots, projs[j], lses[j], weights[j])[0])
    d_attn = (kept_a + after(came_a, gprojs[-1]).astype(FLOAT)).astype(LOWER)
    near, far = turned_order[-1], turned_order[-2]
    others_a = [
        lax.ppermute(d_attn, "rows", [(i, i ^ mask) for i in range(rows_size)])
        for mask in (1 << near, 1 << far, (1 << near) | (1 << far))
    ]
    d_mlp = joined(d_mlp, after(other, gprojs[-1]), order[1])
    other = swapped(d_mlp, 0)
    rows_grad, sums_one = first_norm(
        x, grad_hidden, after(logit, gprojs[-1], d_attn, d_mlp), norm_gains, router_row, gprojs, weights
    )
    others_a = [after(v, rows_grad) for v in others_a]
    d_attn = joined(joined(d_attn, others_a[0], near), joined(others_a[1], others_a[2], near), far)
    for bit in turned_order[-3:0:-1]:
        d_attn = joined(d_attn, swapped(d_attn, bit), bit)
    other_a = swapped(d_attn, 0)
    small = jnp.concatenate(
        [
            sums_two[:4],
            sums_one[:3],
            up_bias_sum[:1],
            jnp.pad(bias_grad[:1], ((0, 0), (0, width - 3 * own))),
        ],
        axis=0,
    )
    small = small + swapped(small, 0)
    other_s = swapped(small, order[1])
    input_grad, block_out = scatter_rows(
        place, full_parts, named, after(rows_grad, small, d_attn), branch, patch_t
    )
    block_out = block_out.T
    small = small + after(other_s, input_grad)
    for bit in order[2:-1]:
        small = small + swapped(small, bit)
    other_s = swapped(small, order[-1])
    d_qkv, d_out, d_up, d_down = finish_grads(
        core_one, d_attn, after(other_a, input_grad, small), d_mlp, other
    )
    small, other_s = after(small, d_qkv), after(other_s, d_qkv)
    d_gains, d_shifts, d_post_bias, d_up_bias, d_router, d_qkv_bias = finish_sums(small, other_s, own)
    d_qkv = d_qkv.T
    return (
        block_out,
        input_grad,
        d_qkv,
        d_qkv_bias,
        d_out,
        d_post_bias,
        d_up,
        d_up_bias,
        d_down,
        d_gains,
        d_shifts,
        d_router,
    )


def solution(mesh):
    in_specs = (
        P("rows", None),
        P(None, "mlp"),
        P(),
        P("mlp", None),
        P(),
        P(None, "mlp"),
        P("mlp"),
        P("mlp", None),
        P(),
        P(),
        P(),
        P("rows"),
        P("rows"),
        P("rows", "mlp"),
    )
    out_specs = (
        P("rows", "mlp"),
        P("rows", None),
        P(None, "mlp"),
        P(None, "mlp"),
        P("mlp", None),
        P(),
        P(None, "mlp"),
        P("mlp"),
        P("mlp", None),
        P(),
        P(),
        P(),
    )
    body = functools.partial(local, mesh.shape["rows"], mesh.shape["mlp"])
    return jax.shard_map(body, mesh=mesh, in_specs=in_specs, out_specs=out_specs, check_vma=False)
```
